32 devices in a mesh: case: 2 (over x), space: 16 (over z, y, core).
Axes of the slice: x: 2, y: 2, z: 4, core: 2. Of those that a mesh axis runs over, the one named last changes fastest.
Arguments:
- ensemble: bfloat16 [160, 2048, 256], P('case', 'space'), parts along dimension 0, may hold values from -0.66796875 to 0.66796875
- innovation: bfloat16 [36864, 256], P(('case', 'space')), parts along dimension 0, may hold values from -6 to 6
- obs_weight: bfloat16 [36864, 256], P(('case', 'space')), parts along dimension 0, may hold values from 0.19921875 to 2
- interp_weight: float32 [8, 18432], P('case', 'space'), parts along dimension 0, may hold values from 0.1 to 0.5
- slot_of: int32 [8, 18432], P('case', 'space'), parts along dimension 0, may hold values from 0 to 2047, as said below
- intersection_list: int32 [32, 16, 128], P(('case', 'space')), parts along dimension 0, may hold values from 0 to 128, as said below
Outputs:
- control: float32 [160, 131072], P('case', 'space'), parts along dimension 0
- increment: float32 [36864, 256], P(('case', 'space')), parts along dimension 0
The draws below stay inside these ranges and needn't reach their ends.
There are 2 independent parts, one for each index of `case`. The reference program is written for one: setup_inputs(seed, part) draws one part's arguments, and reference() takes and returns one part's arrays. A program takes and returns all parts, laid end to end along the dimension named above; each array names one. Nothing has to cross between parts.
Inputs may be any that keep to these rules, and one draw needn't show every extreme that they name: `slot_of`: every slot named is live: its intersection_list entry is a column, never 128. `intersection_list`: each list of one owner and one fine device holds 0 to 128 distinct columns in its first slots, then 128; lists are nonempty only for the 16 owners o with (o - s + 8) mod 16 < 16; every live slot is named by some slot_of entry of that fine device; owner s holds a full list of 128 for fine device s.
All inputs are finite; a program needn't handle non-finite values.
Results may differ from the reference program's by a relative error of at most 0.0031.
Values may be sent and summed in bfloat16 or wider, within the bound.
No kernel may reach another device: no remote copies, remote signals or barrier semaphores. Data moves between devices by JAX's collectives and lax.ppermute only.
A program may use at most 128 MiB of HBM per device.

```python
import math
import jax
import jax.numpy as jnp
from jax import lax

VAR = 4
LEV = 64
M = 80
NB = 4
ITERS = 2
CPTS = 128
FPTS = 1152
CAP = 128
BAND = 16
COLS = 2048
FINE = 18432
N_SPACE = 16


def intersection_tables(key):
    devices = N_SPACE
    entries = NB * FPTS
    keys = jax.random.split(key, 5)
    heat = jax.random.randint(keys[0], (devices,), 1, 9)
    raw = jax.random.randint(keys[1], (devices, devices), 0, CAP)
    counts = jnp.minimum(CAP, 1 + raw * heat[None, :] // 4)
    fine_ids = jnp.arange(devices)[:, None]
    owner_ids = jnp.arange(devices)[None, :]
    offset = (owner_ids - fine_ids + BAND // 2) % devices
    counts = jnp.where(offset < BAND, counts, 0)
    counts = jnp.where(owner_ids == fine_ids, CAP, counts)
    valid = jnp.arange(CAP)[None, None, :] < counts[:, :, None]
    flat_valid = valid.reshape(devices, devices * CAP)
    ranked = jnp.where(flat_valid, 0, 1) * (devices * CAP) + jnp.arange(devices * CAP)[None, :]
    order = jnp.argsort(ranked, axis=1)
    live = jnp.sum(counts, axis=1)
    scores = jax.random.randint(keys[3], (devices, entries), 0, entries) * entries + jnp.arange(entries)[None, :]
    shuffle = jnp.argsort(scores, axis=1)
    chosen = jnp.take_along_axis(order, shuffle % live[:, None], axis=1)
    slot_table = chosen.reshape(devices, NB, FPTS).transpose(1, 0, 2).reshape(NB, devices * FPTS)
    picks = jax.random.randint(keys[4], (devices, devices, CPTS), 0, CPTS) * CPTS + jnp.arange(CPTS)[None, None, :]
    columns_drawn = jnp.argsort(picks, axis=2)[:, :, :CAP]
    intersection = jnp.where(valid, columns_drawn, CPTS).transpose(1, 0, 2)
    return (slot_table.astype(jnp.int32), intersection.astype(jnp.int32))


def draw_slot_of(key, part):
    tables = intersection_tables(key)
    return tables[0]


def draw_intersection_list(key, part):
    tables = intersection_tables(key)
    return tables[1]


def level_of(rng, dims, pieces, low, high):
    def one(dim, blocks):
        draws = jax.random.uniform(jax.random.fold_in(jax.random.fold_in(rng, 6), dim), (blocks,), jnp.float32, low / len(pieces), high / len(pieces))
        return jnp.repeat(jnp.exp(draws), dims[dim] // blocks).reshape((-1,) + (1,) * (len(dims) - dim - 1))

    factor_of = one(*pieces[0])
    for cut in pieces[1:]:
        factor_of = factor_of * one(*cut)
    return factor_of


def noise(stream_key, dims, scale, bound, cuts=(), held_as=jnp.bfloat16):
    loudness = level_of(stream_key, dims, cuts, -0.22, 0.18) if cuts else 1.0
    array = jax.random.normal(stream_key, dims, jnp.float32) * scale * loudness
    return jnp.minimum(jnp.maximum(array, -bound), bound).astype(held_as)


def setup_inputs(seed: int = 0, part: int = 0) -> dict:
    seeds = jax.random.split(jax.random.key(seed), 7)
    part_splits = jax.random.split(jax.random.fold_in(seeds[6], part), 7)
    ensemble = noise(part_splits[0], (M, COLS, VAR * LEV), (1.0 / (M ** 0.5)), 0.66796875, ((1, 16),))
    innovation = noise(part_splits[1], (FINE, VAR * LEV), 1.0, 6.0, ((0, 16),))
    obs_weight = jnp.clip(jnp.exp(math.log(2.0) - 2.306499 * jax.random.uniform(part_splits[2], (FINE, VAR * LEV), jnp.float32) ** level_of(part_splits[2], (FINE, VAR * LEV), ((0, 16),), -0.2, 0.2)), 0.19921875, 2.0).astype(jnp.bfloat16)
    interp_weight = jnp.clip(0.1 + 0.4 * jax.random.uniform(part_splits[3], (NB, FINE), jnp.float32) ** level_of(part_splits[3], (NB, FINE), ((1, 16),), -0.2, 0.2), 0.1, 0.5)
    slot_of = draw_slot_of(jax.random.fold_in(jax.random.fold_in(seeds[6], part), 71), part)
    intersection_list = draw_intersection_list(jax.random.fold_in(jax.random.fold_in(seeds[6], part), 71), part)
    return dict(ensemble=ensemble, innovation=innovation, obs_weight=obs_weight, interp_weight=interp_weight, slot_of=slot_of, intersection_list=intersection_list)


loc_scale = 3.0


def vertical_taper():
    levels = jnp.arange(LEV).astype(jnp.float32)
    spread = (levels[:, None] - levels[None, :]) / loc_scale
    return jnp.exp(-0.5 * spread * spread)


def source_columns(slot_of, intersection_list):
    owners = (slot_of // CAP).astype(jnp.int32)
    within = (slot_of % CAP).astype(jnp.int32)
    senders = (jnp.arange(FPTS * N_SPACE) // FPTS).astype(jnp.int32)
    senders = jnp.broadcast_to(senders[None, :], slot_of.shape)
    return owners * CPTS + intersection_list[owners, senders, within]


def reference(ensemble, innovation, obs_weight, interp_weight, slot_of, intersection_list):
    taper = vertical_taper()
    columns = source_columns(slot_of, intersection_list)
    width = VAR * LEV

    def inject(control):
        tapered = jnp.dot(control.reshape(M * COLS, LEV), taper.T, precision=lax.Precision.HIGHEST).reshape(M, COLS, LEV)

        def add_member(running, inputs):
            member, shaped = inputs
            return running + member.astype(jnp.float32) * jnp.tile(shaped, (1, VAR)), None

        total, unused = lax.scan(add_member, jnp.zeros((COLS, width), jnp.float32), (ensemble, tapered))
        return total

    def interpolate(coarse):
        picked = coarse[columns].astype(jnp.float32)
        return jnp.sum(interp_weight[:, :, None] * picked, axis=0)

    def interpolate_adjoint(weighted):
        spread = interp_weight[:, :, None] * weighted[None, :, :]
        return jax.ops.segment_sum(spread.reshape(-1, width), columns.reshape(-1), num_segments=COLS)

    def project(coarse_grad):
        shaped = coarse_grad.reshape(COLS, VAR, LEV)

        def per_member(member):
            inner = jnp.sum(member.astype(jnp.float32).reshape(COLS, VAR, LEV) * shaped, axis=1)
            return jnp.dot(inner, taper, precision=lax.Precision.HIGHEST).reshape(-1)

        return lax.map(per_member, ensemble)

    weight_obs = obs_weight.astype(jnp.float32)
    target = innovation.astype(jnp.float32)
    control = jnp.zeros((M, COLS * LEV), jnp.float32)
    increment = jnp.zeros((FINE, width), jnp.float32)
    for sweep in range(ITERS):
        weighted = weight_obs * (increment - target)
        gradient = control + project(interpolate_adjoint(weighted))
        image = interpolate(inject(gradient).astype(jnp.bfloat16))
        grad_norm = jnp.sum(gradient * gradient)
        image_norm = jnp.sum(weight_obs * image * image)
        length = grad_norm / (grad_norm + image_norm)
        control = control - length * gradient
        increment = increment - length * image
    return control, increment
```

```python
import functools

import jax
import jax.numpy as jnp
import ml_dtypes
import numpy as np
from jax import lax
from jax.experimental import pallas as pl
from jax.experimental.pallas import tpu as pltpu
from jax.sharding import PartitionSpec as P

VAR = 4
LOC_SCALE = 3.0
BF = jnp.bfloat16
F32 = jnp.float32
LANES = 128
GROUP = 16
VMEM = pl.BlockSpec(memory_space=pltpu.VMEM)
SMEM = pl.BlockSpec(memory_space=pltpu.SMEM)
ANY = pl.BlockSpec(memory_space=pl.ANY)


def vertical_taper(levels):
    heights = np.arange(levels).astype(np.float32)
    spread = (heights[:, None] - heights[None, :]) / np.float32(LOC_SCALE)
    return np.exp(np.float32(-0.5) * spread * spread)


def host_halves(x):
    high = x.astype(ml_dtypes.bfloat16)
    return [high, (x - high.astype(x.dtype)).astype(ml_dtypes.bfloat16)]


def params(mib):
    return pltpu.CompilerParams(vmem_limit_bytes=mib << 20)


def cost(flops, nbytes):
    return pl.CostEstimate(flops=int(flops), bytes_accessed=int(nbytes), transcendentals=0)


def dot(a, b):
    return jnp.dot(a, b, preferred_element_type=F32)


def halves(x):
    high = x.astype(BF)
    return high, (x - high.astype(F32)).astype(BF)


def shape(dims, dtype):
    return jax.ShapeDtypeStruct(dims, dtype)


def adjoint_kernel(slot_ref, weight_ref, target_ref, obs_ref, at_ref, y_ref, wh_s, wl_s, lo_s):
    step = pl.program_id(0)
    rows, fine = at_ref.shape

    @pl.when(step == 0)
    def _():
        w = -(obs_ref[...].astype(F32) * target_ref[...].astype(F32))
        wh_s[...], wl_s[...] = halves(w)

    row = lax.broadcasted_iota(jnp.int32, (rows, LANES), 0)
    for j in range(fine // LANES):
        lanes = pl.ds(j * LANES, LANES)
        total = None
        for b in range(slot_ref.shape[0]):
            slots = slot_ref[b : b + 1, lanes] - step * rows
            term = jnp.where(row == slots, weight_ref[b : b + 1, lanes], 0.0)
            total = term if total is None else total + term
        at_ref[:, lanes], lo_s[:, lanes] = halves(total)
    y_ref[...] = dot(at_ref[...], wh_s[...]) + dot(at_ref[...], wl_s[...]) + dot(lo_s[...], wh_s[...])


def adjoint_first(slot_of, weight, target, obs, slots):
    sources, fine = slot_of.shape
    width = target.shape[1]
    rows = slots // 8
    full = lambda i: (0, 0)
    return pl.pallas_call(
        adjoint_kernel,
        grid=(8,),
        in_specs=[
            pl.BlockSpec((sources, fine), full),
            pl.BlockSpec((sources, fine), full),
            pl.BlockSpec((fine, width), full),
            pl.BlockSpec((fine, width), full),
        ],
        out_specs=[
            pl.BlockSpec((rows, fine), lambda i: (i, 0)),
            pl.BlockSpec((rows, width), lambda i: (i, 0)),
        ],
        out_shape=[shape((slots, fine), BF), shape((slots, width), F32)],
        scratch_shapes=[pltpu.VMEM((fine, width), BF)] * 2 + [pltpu.VMEM((rows, fine), BF)],
        compiler_params=params(24),
        cost_estimate=cost(2 * slots * fine * width, 8e6),
        name="adjoint_first",
    )(slot_of, weight, target, obs)


PARTS = ((0, 0), (1, 0), (0, 1), (1, 1))
STEPS = 4
HEAD = 16
TOP = 32512.0


def owner(me_ref, k, dy, dc):
    z, y, c = me_ref[0], me_ref[1], me_ref[2]
    y = y if dy == 0 else 1 - y
    c = c if dc == 0 else 1 - c
    return (lax.rem(z + k, STEPS) * 2 + y) * 2 + c


def sources_of(me_ref):
    return [owner(me_ref, (STEPS - k) % STEPS, dy, dc) for dy, dc in PARTS for k in range(STEPS)]


def hits(lists_ref, o):
    column = lax.broadcasted_iota(jnp.int32, (LANES, LANES), 0)
    return jnp.where(column == lists_ref[pl.ds(o, 1), :], 1.0, 0.0)


def forward_matrix_kernel(grouped, me_ref, slot_ref, weight_ref, lists_ref, a_ref, raw_s, p_s):
    rows, slots = a_ref.shape
    if grouped:

        @pl.when(pl.program_id(0) == 0)
        def _():
            for i, o in enumerate(sources_of(me_ref)):
                p_s[i] = hits(lists_ref, o).T.astype(BF)

    out = raw_s if grouped else a_ref
    lane = lax.broadcasted_iota(jnp.int32, (32, LANES), 1)
    for r in range(rows // 32):
        some = pl.ds(r * 32, 32)
        picked = slot_ref[some, :]
        scale = weight_ref[some, :]
        ids = [jnp.broadcast_to(picked[:, b : b + 1], (32, LANES)) for b in range(picked.shape[1])]
        ws = [jnp.broadcast_to(scale[:, b : b + 1], (32, LANES)) for b in range(picked.shape[1])]
        for j in range(slots // LANES):
            here = lane + j * LANES
            total = None
            for i, w in zip(ids, ws):
                term = jnp.where(here == i, w, 0.0)
                total = term if total is None else total + term
            out[some, pl.ds(j * LANES, LANES)] = total.astype(BF)
    if grouped:
        for i, o in enumerate(sources_of(me_ref)):
            held = raw_s[:, pl.ds(pl.multiple_of(o * LANES, LANES), LANES)]
            a_ref[:, pl.ds(i * LANES, LANES)] = dot(held, p_s[i]).astype(BF)


def forward_matrix(me, slot_rows, weight_rows, lists, slots, grouped):
    fine, sources = slot_rows.shape
    rows = fine // 4 if fine % 128 == 0 and fine % 4 == 0 else fine
    return pl.pallas_call(
        functools.partial(forward_matrix_kernel, grouped),
        grid=(fine // rows,),
        in_specs=[
            SMEM,
            pl.BlockSpec((rows, sources), lambda i: (i, 0)),
            pl.BlockSpec((rows, sources), lambda i: (i, 0)),
            pl.BlockSpec(lists.shape, lambda i: (0, 0)),
        ],
        out_specs=pl.BlockSpec((rows, slots), lambda i: (i, 0)),
        out_shape=shape((fine, slots), BF),
        scratch_shapes=[
            pltpu.VMEM((rows, slots), BF),
            pltpu.VMEM((16, LANES, LANES), BF),
        ],
        compiler_params=params(16),
        cost_estimate=cost(2 * slots * fine * LANES * 16, 5e6),
        name="forward_matrix",
    )(me, slot_rows, weight_rows, lists)


def place_kernel(me_ref, lists_ref, at_ref, out_ref):
    for i, (dy, dc) in enumerate(PARTS):
        for k in range(STEPS):
            o = owner(me_ref, k, dy, dc)
            held = at_ref[pl.ds(pl.multiple_of(o * LANES, LANES), LANES), :]
            out = pl.ds((i * STEPS + k) * LANES, LANES)
            out_ref[out, :] = dot(hits(lists_ref, o).astype(BF), held).astype(BF)


def place_rows(me, lists, at):
    slots, fine = at.shape
    return pl.pallas_call(
        place_kernel,
        in_specs=[SMEM, VMEM, VMEM],
        out_specs=VMEM,
        out_shape=shape((slots, fine), BF),
        compiler_params=params(16),
        cost_estimate=cost(2 * slots * fine * LANES * 4, 1e7),
        name="place_rows",
    )(me, lists, at)


def split_kernel(me_ref, lists_ref, y_ref, *outs):
    for out, (dy, dc) in zip(outs, PARTS):
        for k in range(STEPS):
            o = owner(me_ref, k, dy, dc)
            hit = hits(lists_ref, o).astype(BF)
            high, low = halves(y_ref[pl.ds(pl.multiple_of(o * LANES, LANES), LANES), :])
            out[pl.ds(k * LANES, LANES), :] = dot(hit, high) + dot(hit, low)


def split_first(me, lists, y):
    width = y.shape[1]
    return pl.pallas_call(
        split_kernel,
        in_specs=[SMEM, VMEM, VMEM],
        out_specs=[VMEM] * 4,
        out_shape=[shape((STEPS * LANES, width), F32)] * 4,
        compiler_params=params(16),
        cost_estimate=cost(2 * y.shape[0] * LANES * width, 2e6),
        name="split_first",
    )(me, lists, y)


def exponent(m):
    return jnp.clip(jnp.ceil(jnp.log2(jnp.maximum(m, 1e-30))), -100.0, 100.0)


def whole16(x):
    return x.astype(jnp.int32).astype(jnp.int16)


def wide(x):
    return x.astype(jnp.int32).astype(F32)


def pack(out_ref, t, sums=None):
    rows, width = t.shape
    e = exponent(jnp.max(jnp.abs(t), axis=0, keepdims=True))
    out_ref[pl.ds(0, rows), :] = whole16(jnp.round(t * (jnp.exp2(-e) * TOP)))
    head = [e]
    if sums is not None:
        for i in range(2):
            v = sums[i : i + 1, :]
            f = exponent(v)
            v = v * (jnp.exp2(-f) * 16384.0)
            first = jnp.floor(v)
            head += [f, first, jnp.floor((v - first) * 16384.0)]
    row = lax.broadcasted_iota(jnp.int32, (HEAD, width), 0)
    total = jnp.zeros((HEAD, width), F32)
    for i, h in enumerate(head):
        total = jnp.where(row == i, h, total)
    out_ref[pl.ds(rows, HEAD), :] = whole16(total)


def unpack(ref):
    rows = ref.shape[0] - HEAD
    head = wide(ref[pl.ds(rows, HEAD), :])
    return wide(ref[pl.ds(0, rows), :]) * (jnp.exp2(head[0:1, :]) * (1.0 / TOP))


def unpack_sums(ref):
    head = wide(ref[pl.ds(ref.shape[0] - HEAD, HEAD), :])
    row = lax.broadcasted_iota(jnp.int32, (8, head.shape[1]), 0)
    total = jnp.zeros(row.shape, F32)
    for i in range(2):
        f, first, second = [head[1 + 3 * i + j : 2 + 3 * i + j, :] for j in range(3)]
        v = (first + second * (1.0 / 16384.0)) * (jnp.exp2(f) * (1.0 / 16384.0))
        total = jnp.where(row == i, v, total)
    return total


def merge_y_kernel(with_sums, *refs):
    if with_sums:
        a_ref, b_ref, mine_ref, out_ref, s_ref = refs
        sums = mine_ref[...] + b_ref[pl.ds(a_ref.shape[0], 8), :]
        s_ref[...] = sums
    else:
        a_ref, b_ref, out_ref = refs
        sums = None
    pack(out_ref, a_ref[...] + b_ref[pl.ds(0, a_ref.shape[0]), :], sums)


def merge_y(a, b, sums):
    rows, width = a.shape
    out = [shape((rows + HEAD, width), jnp.int16)]
    args = [a, b]
    if sums is not None:
        out.append(shape((8, width), F32))
        args.append(sums)
    return pl.pallas_call(
        functools.partial(merge_y_kernel, sums is not None),
        in_specs=[VMEM] * len(args),
        out_specs=[VMEM] * len(out),
        out_shape=out,
        compiler_params=params(8),
        cost_estimate=cost(5 * rows * width, 1e6),
        name="merge_y",
    )(*args)


def merge_z_kernel(with_sums, *refs):
    if with_sums:
        a_ref, b_ref, p_ref, mine_ref, own_ref, *outs, s_ref = refs
        sums = mine_ref[...] + unpack_sums(p_ref)
        s_ref[...] = sums
    else:
        a_ref, b_ref, p_ref, own_ref, *outs = refs
        sums = None
    t = a_ref[...] + b_ref[...] + unpack(p_ref)
    own_ref[...] = t[:LANES]
    for k in range(1, STEPS):
        pack(outs[k - 1], t[k * LANES : (k + 1) * LANES], sums)


def merge_z(a, b, p, sums):
    width = a.shape[1]
    out = [shape((LANES, width), F32)]
    out += [shape((LANES + HEAD, width), jnp.int16)] * (STEPS - 1)
    args = [a, b, p]
    if sums is not None:
        out.append(shape((8, width), F32))
        args.append(sums)
    return pl.pallas_call(
        functools.partial(merge_z_kernel, sums is not None),
        in_specs=[VMEM] * len(args),
        out_specs=[VMEM] * len(out),
        out_shape=out,
        compiler_params=params(8),
        cost_estimate=cost(5 * STEPS * LANES * width, 1e6),
        name="merge_z",
    )(*args)


def fold(a):
    return jnp.sum(a, axis=0, keepdims=True)


def length_of(sums):
    grad = jnp.sum(sums[0:1, :], axis=1, keepdims=True)
    image = jnp.sum(sums[1:2, :], axis=1, keepdims=True)
    return grad / (grad + image), image / (grad + image)


def products(e, y, held, rows):
    p = e.astype(F32) * y
    q = p[:, :LANES] + p[:, LANES:]
    q = q + pltpu.roll(q, LANES // 2, 1)
    high, low = halves(q)
    held[rows, :LANES] = high
    held[rows, LANES:] = low


BATCH = 16


def coarse_kernel(packed, second, e_ref, k_ref, *refs):
    refs = list(refs)
    y = refs.pop(0)[...]
    got = [refs.pop(0) for _ in range(packed)]
    for r in got:
        y = y + unpack(r)
    if second:
        y0_ref, s_ref = refs.pop(0), refs.pop(0)
        sums = s_ref[...]
        for r in got:
            sums = sums + unpack_sums(r)
        l0, keep = length_of(sums)
        y = keep * y0_ref[...] - l0 * y
        refs.pop(0)
        refs.pop(2)[...] = jnp.broadcast_to(l0, (8, LANES))
    else:
        refs.pop(0)
    x_ref, y_ref, sum_ref, p_s = refs
    columns, members, width = e_ref.shape
    y_ref[...] = y
    sum_ref[...] = jnp.zeros_like(sum_ref)

    @pl.loop(0, columns // BATCH)
    def _(i):
        base = pl.multiple_of(i * BATCH, BATCH)
        yb = y_ref[pl.ds(base, BATCH), :]
        for c in range(BATCH):
            products(e_ref[base + c], yb[c : c + 1, :], p_s, pl.ds(c * members, members))
        t = dot(p_s[...], k_ref[...])
        parts = []
        for c in range(BATCH):
            parts.append(fold(t[c * members : (c + 1) * members] * e_ref[base + c].astype(F32)))
        x = jnp.concatenate(parts, axis=0)
        x_ref[pl.ds(base, BATCH), :] = x.astype(BF)
        sum_ref[0:1, :] += fold(x * yb)


def coarse_image(ens, kern, own, got, after, y0=None, sums=None):
    columns, members, width = ens.shape
    second = y0 is not None
    args = [ens, kern, own, *got] + ([y0, sums] if second else []) + [after]
    out = [shape((columns, width), BF), shape((columns, width), F32)]
    out += [shape((8, LANES), F32)] if second else []
    out += [shape((8, width), F32)]
    return pl.pallas_call(
        functools.partial(coarse_kernel, len(got), second),
        in_specs=[VMEM] * (len(args) - 1) + [ANY],
        out_specs=[VMEM] * len(out),
        out_shape=out,
        scratch_shapes=[pltpu.VMEM((BATCH * members, width), BF)],
        compiler_params=params(16),
        cost_estimate=cost(2 * columns * members * width * width, 5e6),
        name="coarse_second" if second else "coarse_first",
    )(*args)


def project_kernel(e_ref, y_ref, t_ref, g_ref, even_s, odd_s):
    columns, members, width = e_ref.shape
    lanes = BATCH // 2 * LANES

    @pl.loop(0, columns // BATCH)
    def _(i):
        base = pl.multiple_of(i * BATCH, BATCH)
        yb = y_ref[pl.ds(base, BATCH), :]
        for c in range(BATCH):
            held = odd_s if c % 2 else even_s
            rows = pl.ds((c // 2) * members, members)
            products(e_ref[base + c], yb[c : c + 1, :], held, rows)
        r = dot(even_s[...], t_ref[0]) + dot(odd_s[...], t_ref[1])
        for pair in range(BATCH // 2):
            at = pl.multiple_of(i * lanes + pair * LANES, LANES)
            g_ref[:, pl.ds(at, LANES)] = r[pair * members : (pair + 1) * members]


def project(ens, y, taps):
    columns, members, width = ens.shape
    levels = width // VAR
    return pl.pallas_call(
        project_kernel,
        in_specs=[VMEM] * 3,
        out_specs=VMEM,
        out_shape=shape((members, columns * levels), F32),
        scratch_shapes=[pltpu.VMEM((BATCH // 2 * members, width), BF)] * 2,
        compiler_params=params(16),
        cost_estimate=cost(2 * columns * members * width * width, 8e6),
        name="project",
    )(ens, y, taps)


def lay_out(x_refs, xs):
    at = 0
    for x in x_refs:
        xs[pl.ds(at, x.shape[0]), :] = x[...]
        at += x.shape[0]


CUTS = 3


def image_kernel(count, n, *refs):
    x_refs, refs = refs[:count], refs[count:]
    a_ref, at_ref, obs_ref, g_ref, im_ref, sum_ref = refs[:6]
    outs, (xs, v_s) = refs[6 : 6 + n], refs[6 + n :]
    lay_out(x_refs, xs)
    fine, slots = a_ref.shape
    rows = fine // CUTS
    sums = g_ref[...]
    row = lax.broadcasted_iota(jnp.int32, sums.shape, 0)
    for i in range(CUTS):
        some = pl.ds(i * rows, rows)
        im = dot(a_ref[some, :], xs[...])
        im_ref[some, :] = im
        v = obs_ref[some, :].astype(F32) * im
        v_s[some, :] = v.astype(BF)
        sums = sums + jnp.where(row == 1, fold(v * im), 0.0)
    sum_ref[...] = sums
    rows = slots // n
    for i, out in enumerate(outs):
        out[pl.ds(0, rows), :] = dot(at_ref[pl.ds(i * rows, rows), :], v_s[...])
    if n > 1:
        outs[n - 1][pl.ds(rows, 8), :] = sums


def image_first(xs, a, at, obs, g_sums, n):
    fine, slots = a.shape
    width = obs.shape[1]
    z_rows = [slots // n] * n
    if n > 1:
        z_rows[-1] += 8
    return pl.pallas_call(
        functools.partial(image_kernel, len(xs), n),
        in_specs=[VMEM] * (len(xs) + 4),
        out_specs=[VMEM] * (2 + n),
        out_shape=[shape((fine, width), F32), shape((8, width), F32)]
        + [shape((r, width), F32) for r in z_rows],
        scratch_shapes=[pltpu.VMEM((slots, width), BF), pltpu.VMEM((fine, width), BF)],
        compiler_params=params(16),
        cost_estimate=cost(4 * slots * fine * width, 13e6),
        name="image_first",
    )(*xs, a, at, obs, g_sums)


def second_kernel(count, *refs):
    x_refs, refs = refs[:count], refs[count:]
    a_ref, obs_ref, g_ref, after_ref, im_ref, sum_ref, xs = refs
    lay_out(x_refs, xs)
    fine = a_ref.shape[0]
    rows = fine // CUTS
    sums = g_ref[...]
    row = lax.broadcasted_iota(jnp.int32, sums.shape, 0)
    for i in range(CUTS):
        some = pl.ds(i * rows, rows)
        im = dot(a_ref[some, :], xs[...])
        im_ref[some, :] = im
        v = obs_ref[some, :].astype(F32) * im
        sums = sums + jnp.where(row == 1, fold(v * im), 0.0)
    sum_ref[...] = sums


def image_second(xs, a, obs, g_sums, after):
    fine, slots = a.shape
    width = obs.shape[1]
    return pl.pallas_call(
        functools.partial(second_kernel, len(xs)),
        in_specs=[VMEM] * (len(xs) + 3) + [ANY],
        out_specs=[VMEM] * 2,
        out_shape=[shape((fine, width), F32), shape((8, width), F32)],
        scratch_shapes=[pltpu.VMEM((slots, width), BF)],
        compiler_params=params(16),
        cost_estimate=cost(2 * slots * fine * width, 8e6),
        name="image_second",
    )(*xs, a, obs, g_sums, after)


def over_core(x):
    return lax.ppermute(x, "space", [(i, i ^ 1) for i in range(GROUP)])


def over_y(x):
    return lax.ppermute(x, "space", [(i, i ^ 2) for i in range(GROUP)])


def over_z(x, k):
    return lax.ppermute(x, "space", [(i, (i + 4 * k) % GROUP) for i in range(GROUP)])


def scatter_sums(parts, sums=None):
    near, far_y, near_c, far_yc = parts
    got_yc = over_core(far_yc)
    got_c = over_core(near_c)
    out, *s = merge_y(far_y, got_yc, sums)
    got_y = over_y(out)
    own, *out = merge_z(near, got_c, got_y, s[0] if s else None)
    s = out[STEPS - 1 :]
    got = [over_z(out[k - 1], k) for k in range(1, STEPS)]
    return own, got, (s[0] if s else None)


def gather_columns(x):
    zs = [over_z(x, k) for k in range(1, STEPS)]
    y_own = over_y(x)
    c_own = over_core(x)
    rest = jnp.concatenate(zs, axis=0)
    y_rest = over_y(rest)
    c_rest = over_core(rest)
    return [x, rest, y_own, y_rest, c_own, c_rest, over_core(y_own), over_core(y_rest)]


def sum_all(x):
    x = x + over_core(x)
    x = x + over_y(x)
    return x + over_z(x, 1) + over_z(x, 2) + over_z(x, 3)


def on_device(ensemble, innovation, obs_weight, interp_weight, slot_of, intersection_list):
    members, columns, width = ensemble.shape
    levels = width // VAR
    devices = lax.axis_size("space")
    capacity = intersection_list.shape[2]
    slots = devices * capacity
    grouped = devices == GROUP and capacity == columns == LANES

    taper = vertical_taper(levels)
    both = taper.astype(np.float64) @ taper.T.astype(np.float64)
    kern = np.tile(np.concatenate(host_halves(both), axis=0), (2, VAR))
    tall = np.tile(np.concatenate(host_halves(taper), axis=0), (2, 1))
    none = np.zeros_like(tall)
    taps = np.stack(
        [np.concatenate([tall, none], axis=1), np.concatenate([none, tall], axis=1)]
    )
    kern, taps = jnp.asarray(kern), jnp.asarray(taps)

    ens = jnp.transpose(ensemble, (1, 0, 2))
    at, y_slots = adjoint_first(slot_of, interp_weight, innovation, obs_weight, slots)
    index = lax.axis_index("space").astype(jnp.int32)
    me = jnp.stack([index // 4, index // 2 % 2, index % 2, index])
    if grouped:
        lists = lax.all_to_all(
            intersection_list, "space", split_axis=1, concat_axis=0, tiled=True
        ).reshape(devices, capacity)
        scatter, gather, add_up = scatter_sums, gather_columns, sum_all
        first = split_first(me, lists, y_slots)
        at = place_rows(me, lists, at)
        n = 4
    else:
        lists = intersection_list[0]
        hit = (lists.reshape(-1, 1) == jnp.arange(columns, dtype=jnp.int32)).astype(BF)

        def swap(x):
            x = x.reshape(devices, capacity, width)
            x = lax.all_to_all(x, "space", split_axis=0, concat_axis=0, tiled=True)
            return x.reshape(slots, width)

        def scatter(parts, sums=None):
            got = swap(parts[0])
            high = lax.reduce_precision(got, 8, 7)
            high, low = high.astype(BF), (got - high).astype(BF)
            if sums is not None:
                sums = lax.psum(sums, "space")
            return dot(hit.T, high) + dot(hit.T, low), [], sums

        def gather(x):
            return [swap(dot(hit, x).astype(BF))]

        def add_up(x):
            return lax.psum(x, "space")

        first = [y_slots]
        n = 1

    a = forward_matrix(me, slot_of.T, interp_weight.T, lists, slots, grouped)
    own, got, _ = scatter(first)
    x0, y0, g_sums = coarse_image(ens, kern, own, got, at)
    im0, sums, *second = image_first(gather(x0), a, at, obs_weight, g_sums, n)
    g0 = project(ens, y0, taps)
    own, got, sums = scatter(second, sums)
    x1, y1, l0, g_sums = coarse_image(ens, kern, own, got, g0, y0, sums)
    g1 = project(ens, y1, taps)
    im1, sums = image_second(gather(x1), a, obs_weight, g_sums, g1)
    l0 = l0[:1, :1]
    l1, _ = length_of(add_up(sums))
    return (-(l0 * g0 + l1 * g1), -(l0 * im0 + l1 * im1))


def solution(mesh):
    placed = (
        P("case", "space", None),
        P(("case", "space"), None),
        P(("case", "space"), None),
        P("case", "space"),
        P("case", "space"),
        P(("case", "space"), None, None),
    )
    return jax.shard_map(
        on_device,
        mesh=mesh,
        in_specs=placed,
        out_specs=(P("case", "space"), P(("case", "space"), None)),
        check_vma=False,
    )
```

```python
import functools

import jax
import jax.numpy as jnp
import ml_dtypes
import numpy as np
from jax import lax
from jax.experimental import pallas as pl
from jax.experimental.pallas import tpu as pltpu
from jax.sharding import PartitionSpec as P

VAR = 4
LOC_SCALE = 3.0
BF = jnp.bfloat16
F32 = jnp.float32
LANES = 128
GROUP = 16
VMEM = pl.BlockSpec(memory_space=pltpu.VMEM)
SMEM = pl.BlockSpec(memory_space=pltpu.SMEM)
ANY = pl.BlockSpec(memory_space=pl.ANY)
HBM = pl.BlockSpec(memory_space=pltpu.HBM)


def vertical_taper(levels):
    heights = np.arange(levels).astype(np.float32)
    spread = (heights[:, None] - heights[None, :]) / np.float32(LOC_SCALE)
    return np.exp(np.float32(-0.5) * spread * spread)


def host_halves(x):
    high = x.astype(ml_dtypes.bfloat16)
    return [high, (x - high.astype(x.dtype)).astype(ml_dtypes.bfloat16)]


def params(mib):
    return pltpu.CompilerParams(vmem_limit_bytes=mib << 20)


def cost(flops, nbytes):
    return pl.CostEstimate(flops=int(flops), bytes_accessed=int(nbytes), transcendentals=0)


def dot(a, b):
    return jnp.dot(a, b, preferred_element_type=F32)


def halves(x):
    high = x.astype(BF)
    return high, (x - high.astype(F32)).astype(BF)


def shape(dims, dtype):
    return jax.ShapeDtypeStruct(dims, dtype)


def adjoint_kernel(*refs):
    slot_hbm, weight_hbm, obs_hbm, target_hbm, at_ref, y_ref = refs[:6]
    slot_s, weight_s, obs_s, target_s, wh_s, wl_s, lo_s, sem = refs[6:]
    copies = [
        pltpu.make_async_copy(src, dst, sem.at[i])
        for i, (src, dst) in enumerate(
            [
                (slot_hbm, slot_s),
                (weight_hbm, weight_s),
                (obs_hbm, obs_s),
                (target_hbm, target_s),
            ]
        )
    ]
    for copy in copies:
        copy.start()
    slots, fine = at_ref.shape
    rows = slots // BLOCKS
    row = lax.broadcasted_iota(jnp.int32, (rows, LANES), 0)

    def build(i):
        for j in range(fine // LANES):
            lanes = pl.ds(j * LANES, LANES)
            total = None
            for b in range(slot_s.shape[0]):
                ids = slot_s[b : b + 1, lanes] - i * rows
                term = jnp.where(row == ids, weight_s[b : b + 1, lanes], 0.0)
                total = term if total is None else total + term
            at_ref[pl.ds(i * rows, rows), lanes], lo_s[i % 2, :, lanes] = halves(total)

    copies[0].wait()
    copies[1].wait()
    build(0)
    copies[2].wait()
    copies[3].wait()
    w = -(obs_s[...].astype(F32) * target_s[...].astype(F32))
    wh_s[...], wl_s[...] = halves(w)
    for i in range(BLOCKS):
        some = pl.ds(i * rows, rows)
        y_ref[some, :] = (
            dot(at_ref[some, :], wh_s[...])
            + dot(at_ref[some, :], wl_s[...])
            + dot(lo_s[i % 2], wh_s[...])
        )
        if i + 1 < BLOCKS:
            build(i + 1)


BLOCKS = 8


def adjoint_first(slot_of, weight, target, obs, slots):
    sources, fine = slot_of.shape
    width = target.shape[1]
    rows = slots // BLOCKS
    return pl.pallas_call(
        adjoint_kernel,
        in_specs=[HBM] * 4,
        out_specs=[VMEM] * 2,
        out_shape=[shape((slots, fine), BF), shape((slots, width), F32)],
        scratch_shapes=[
            pltpu.VMEM((sources, fine), jnp.int32),
            pltpu.VMEM((sources, fine), F32),
        ]
        + [pltpu.VMEM((fine, width), BF)] * 4
        + [pltpu.VMEM((2, rows, fine), BF), pltpu.SemaphoreType.DMA((4,))],
        compiler_params=params(20),
        cost_estimate=cost(6 * slots * fine * width, 8e6),
        name="adjoint_first",
    )(slot_of, weight, obs, target)


CHIPS = GROUP // 2
HEAD = 16
TOP = 32512.0


def owners(me_ref):
    c = me_ref[0]
    return [2 * i + c for i in range(CHIPS)] + [2 * i + 1 - c for i in range(CHIPS)]


def hits(lists_ref, o):
    column = lax.broadcasted_iota(jnp.int32, (LANES, LANES), 0)
    return jnp.where(column == lists_ref[pl.ds(o, 1), :], 1.0, 0.0)


def forward_matrix_kernel(grouped, me_ref, slot_ref, weight_ref, lists_ref, a_ref, raw_s, p_s):
    rows, slots = a_ref.shape
    if grouped:

        @pl.when(pl.program_id(0) == 0)
        def _():
            for i, o in enumerate(owners(me_ref)):
                p_s[i] = hits(lists_ref, o).T.astype(BF)

    out = raw_s if grouped else a_ref
    lane = lax.broadcasted_iota(jnp.int32, (32, LANES), 1)
    for r in range(rows // 32):
        some = pl.ds(r * 32, 32)
        picked = slot_ref[some, :]
        scale = weight_ref[some, :]
        ids = [jnp.broadcast_to(picked[:, b : b + 1], (32, LANES)) for b in range(picked.shape[1])]
        ws = [jnp.broadcast_to(scale[:, b : b + 1], (32, LANES)) for b in range(picked.shape[1])]
        for j in range(slots // LANES):
            here = lane + j * LANES
            total = None
            for i, w in zip(ids, ws):
                term = jnp.where(here == i, w, 0.0)
                total = term if total is None else total + term
            out[some, pl.ds(j * LANES, LANES)] = total.astype(BF)
    if grouped:
        for i, o in enumerate(owners(me_ref)):
            held = raw_s[:, pl.ds(pl.multiple_of(o * LANES, LANES), LANES)]
            a_ref[:, pl.ds(i * LANES, LANES)] = dot(held, p_s[i]).astype(BF)


def forward_matrix(me, slot_rows, weight_rows, lists, slots, grouped):
    fine, sources = slot_rows.shape
    rows = fine // 4 if fine % 128 == 0 and fine % 4 == 0 else fine
    return pl.pallas_call(
        functools.partial(forward_matrix_kernel, grouped),
        grid=(fine // rows,),
        in_specs=[
            SMEM,
            pl.BlockSpec((rows, sources), lambda i: (i, 0)),
            pl.BlockSpec((rows, sources), lambda i: (i, 0)),
            pl.BlockSpec(lists.shape, lambda i: (0, 0)),
        ],
        out_specs=pl.BlockSpec((rows, slots), lambda i: (i, 0)),
        out_shape=shape((fine, slots), BF),
        scratch_shapes=[
            pltpu.VMEM((rows, slots), BF),
            pltpu.VMEM((16, LANES, LANES), BF),
        ],
        compiler_params=params(16),
        cost_estimate=cost(2 * slots * fine * LANES * 16, 5e6),
        name="forward_matrix",
    )(me, slot_rows, weight_rows, lists)


def place_kernel(me_ref, lists_ref, at_ref, out_ref):
    for i, o in enumerate(owners(me_ref)):
        held = at_ref[pl.ds(pl.multiple_of(o * LANES, LANES), LANES), :]
        hit = hits(lists_ref, o).astype(BF)
        out_ref[pl.ds(i * LANES, LANES), :] = dot(hit, held).astype(BF)


def place_rows(me, lists, at):
    slots, fine = at.shape
    return pl.pallas_call(
        place_kernel,
        in_specs=[SMEM, VMEM, VMEM],
        out_specs=VMEM,
        out_shape=shape((slots, fine), BF),
        compiler_params=params(16),
        cost_estimate=cost(2 * slots * fine * LANES * 4, 1e7),
        name="place_rows",
    )(me, lists, at)


def split_kernel(me_ref, lists_ref, y_ref, *outs):
    for i, o in enumerate(owners(me_ref)):
        hit = hits(lists_ref, o).astype(BF)
        high, low = halves(y_ref[pl.ds(pl.multiple_of(o * LANES, LANES), LANES), :])
        rows = pl.ds(i % CHIPS * LANES, LANES)
        outs[i // CHIPS][rows, :] = dot(hit, high) + dot(hit, low)


def split_first(me, lists, y):
    width = y.shape[1]
    return pl.pallas_call(
        split_kernel,
        in_specs=[SMEM, VMEM, VMEM],
        out_specs=[VMEM] * 2,
        out_shape=[shape((CHIPS * LANES, width), F32)] * 2,
        compiler_params=params(16),
        cost_estimate=cost(2 * y.shape[0] * LANES * width, 2e6),
        name="split_first",
    )(me, lists, y)


def exponent(m):
    return jnp.clip(jnp.ceil(jnp.log2(jnp.maximum(m, 1e-30))), -100.0, 100.0)


def whole16(x):
    return x.astype(jnp.int32).astype(jnp.int16)


def wide(x):
    return x.astype(jnp.int32).astype(F32)


def pack(out_ref, t, sums=None):
    rows, width = t.shape
    e = exponent(jnp.max(jnp.abs(t), axis=0, keepdims=True))
    out_ref[pl.ds(0, rows), :] = whole16(jnp.round(t * (jnp.exp2(-e) * TOP)))
    head = [e]
    if sums is not None:
        for i in range(2):
            v = sums[i : i + 1, :]
            f = exponent(v)
            v = v * (jnp.exp2(-f) * 16384.0)
            first = jnp.floor(v)
            head += [f, first, jnp.floor((v - first) * 16384.0)]
    row = lax.broadcasted_iota(jnp.int32, (HEAD, width), 0)
    total = jnp.zeros((HEAD, width), F32)
    for i, h in enumerate(head):
        total = jnp.where(row == i, h, total)
    out_ref[pl.ds(rows, HEAD), :] = whole16(total)


def unpack(ref):
    rows = ref.shape[0] - HEAD
    head = wide(ref[pl.ds(rows, HEAD), :])
    return wide(ref[pl.ds(0, rows), :]) * (jnp.exp2(head[0:1, :]) * (1.0 / TOP))


def unpack_sums(ref):
    head = wide(ref[pl.ds(ref.shape[0] - HEAD, HEAD), :])
    row = lax.broadcasted_iota(jnp.int32, (8, head.shape[1]), 0)
    total = jnp.zeros(row.shape, F32)
    for i in range(2):
        f, first, second = [head[1 + 3 * i + j : 2 + 3 * i + j, :] for j in range(3)]
        v = (first + second * (1.0 / 16384.0)) * (jnp.exp2(f) * (1.0 / 16384.0))
        total = jnp.where(row == i, v, total)
    return total


def merge_kernel(with_sums, a_ref, b_ref, *refs):
    out_ref = refs[-1]
    sums = refs[0][...] + b_ref[pl.ds(a_ref.shape[0], 8), :] if with_sums else None
    for i in range(CHIPS):
        rows = pl.ds(i * LANES, LANES)
        pack(out_ref.at[i], a_ref[rows, :] + b_ref[rows, :], sums)


def merge(a, b, sums):
    rows, width = a.shape
    args = [a, b] + ([] if sums is None else [sums])
    return pl.pallas_call(
        functools.partial(merge_kernel, sums is not None),
        in_specs=[VMEM] * len(args),
        out_specs=VMEM,
        out_shape=shape((CHIPS, LANES + HEAD, width), jnp.int16),
        compiler_params=params(8),
        cost_estimate=cost(5 * rows * width, 2e6),
        name="merge",
    )(*args)


def tie_kernel(x_ref, after_ref, out_ref):
    del x_ref, after_ref, out_ref


def tie(x, after):
    return pl.pallas_call(
        tie_kernel,
        in_specs=[ANY, ANY],
        out_specs=ANY,
        out_shape=shape(x.shape, x.dtype),
        input_output_aliases={0: 0},
        name="tie",
    )(x, after)


def fold(a):
    return jnp.sum(a, axis=0, keepdims=True)


def length_of(sums):
    grad = jnp.sum(sums[0:1, :], axis=1, keepdims=True)
    image = jnp.sum(sums[1:2, :], axis=1, keepdims=True)
    return grad / (grad + image), image / (grad + image)


def products(e, y, held, rows):
    p = e.astype(F32) * y
    q = p[:, :LANES] + p[:, LANES:]
    q = q + pltpu.roll(q, LANES // 2, 1)
    high, low = halves(q)
    held[rows, :LANES] = high
    held[rows, LANES:] = low


BATCH = 16


def coarse_kernel(packed, second, e_ref, k_ref, own_ref, *refs):
    refs = list(refs)
    if packed:
        got = [own_ref.at[i] for i in range(own_ref.shape[0])]
        y = sum(unpack(r) for r in got)
    else:
        y = own_ref[...]
    if second:
        y0_ref = refs.pop(0)
        if packed:
            sums = sum(unpack_sums(r) for r in got)
        else:
            sums = refs.pop(0)[...]
        l0, keep = length_of(sums)
        y = keep * y0_ref[...] - l0 * y
        refs.pop(0)
        refs.pop(2)[...] = jnp.broadcast_to(l0, (8, LANES))
    else:
        refs.pop(0)
    x_ref, y_ref, sum_ref, p_s = refs
    columns, members, width = e_ref.shape
    y_ref[...] = y
    sum_ref[...] = jnp.zeros_like(sum_ref)

    @pl.loop(0, columns // BATCH)
    def _(i):
        base = pl.multiple_of(i * BATCH, BATCH)
        yb = y_ref[pl.ds(base, BATCH), :]
        for c in range(BATCH):
            products(e_ref[base + c], yb[c : c + 1, :], p_s, pl.ds(c * members, members))
        t = dot(p_s[...], k_ref[...])
        parts = []
        for c in range(BATCH):
            parts.append(fold(t[c * members : (c + 1) * members] * e_ref[base + c].astype(F32)))
        x = jnp.concatenate(parts, axis=0)
        for copy in range(x_ref.shape[0]):
            x_ref[copy, pl.ds(base, BATCH), :] = x.astype(BF)
        sum_ref[0:1, :] += fold(x * yb)


def coarse_image(ens, kern, own, after, copies, y0=None, sums=None):
    columns, members, width = ens.shape
    second = y0 is not None
    packed = own.ndim == 3
    extra = ([y0] if packed else [y0, sums]) if second else []
    args = [ens, kern, own, *extra, after]
    out = [shape((copies, columns, width), BF), shape((columns, width), F32)]
    out += [shape((8, LANES), F32)] if second else []
    out += [shape((8, width), F32)]
    return pl.pallas_call(
        functools.partial(coarse_kernel, packed, second),
        in_specs=[VMEM] * (len(args) - 1) + [ANY],
        out_specs=[VMEM] * len(out),
        out_shape=out,
        scratch_shapes=[pltpu.VMEM((BATCH * members, width), BF)],
        compiler_params=params(16),
        cost_estimate=cost(2 * columns * members * width * width, 5e6),
        name="coarse_second" if second else "coarse_first",
    )(*args)


def project_kernel(e_ref, y_ref, t_ref, g_ref, even_s, odd_s):
    columns, members, width = e_ref.shape
    lanes = BATCH // 2 * LANES

    @pl.loop(0, columns // BATCH)
    def _(i):
        base = pl.multiple_of(i * BATCH, BATCH)
        yb = y_ref[pl.ds(base, BATCH), :]
        for c in range(BATCH):
            held = odd_s if c % 2 else even_s
            rows = pl.ds((c // 2) * members, members)
            products(e_ref[base + c], yb[c : c + 1, :], held, rows)
        r = dot(even_s[...], t_ref[0]) + dot(odd_s[...], t_ref[1])
        for pair in range(BATCH // 2):
            at = pl.multiple_of(i * lanes + pair * LANES, LANES)
            g_ref[:, pl.ds(at, LANES)] = r[pair * members : (pair + 1) * members]


def project(ens, y, taps):
    columns, members, width = ens.shape
    levels = width // VAR
    return pl.pallas_call(
        project_kernel,
        in_specs=[VMEM] * 3,
        out_specs=VMEM,
        out_shape=shape((members, columns * levels), F32),
        scratch_shapes=[pltpu.VMEM((BATCH // 2 * members, width), BF)] * 2,
        compiler_params=params(16),
        cost_estimate=cost(2 * columns * members * width * width, 8e6),
        name="project",
    )(ens, y, taps)


def lay_out(x_refs, xs):
    at = 0
    for x in x_refs:
        for part in [x] if len(x.shape) == 2 else [x.at[i] for i in range(x.shape[0])]:
            xs[pl.ds(at, part.shape[0]), :] = part[...]
            at += part.shape[0]


CUTS = 3


def image_kernel(count, n, *refs):
    x_refs, refs = refs[:count], refs[count:]
    a_ref, at_ref, obs_ref, g_ref, im_ref, sum_ref = refs[:6]
    outs, (xs, v_s) = refs[6 : 6 + n], refs[6 + n :]
    lay_out(x_refs, xs)
    fine, slots = a_ref.shape
    rows = fine // CUTS
    sums = g_ref[...]
    row = lax.broadcasted_iota(jnp.int32, sums.shape, 0)
    for i in range(CUTS):
        some = pl.ds(i * rows, rows)
        im = dot(a_ref[some, :], xs[...])
        im_ref[some, :] = im
        v = obs_ref[some, :].astype(F32) * im
        v_s[some, :] = v.astype(BF)
        sums = sums + jnp.where(row == 1, fold(v * im), 0.0)
    sum_ref[...] = sums
    rows = slots // n
    for i, out in enumerate(outs):
        out[pl.ds(0, rows), :] = dot(at_ref[pl.ds(i * rows, rows), :], v_s[...])
    if n > 1:
        outs[n - 1][pl.ds(rows, 8), :] = sums


def image_first(xs, a, at, obs, g_sums, n):
    fine, slots = a.shape
    width = obs.shape[1]
    z_rows = [slots // n] * n
    if n > 1:
        z_rows[-1] += 8
    return pl.pallas_call(
        functools.partial(image_kernel, len(xs), n),
        in_specs=[VMEM] * (len(xs) + 4),
        out_specs=[VMEM] * (2 + n),
        out_shape=[shape((fine, width), F32), shape((8, width), F32)]
        + [shape((r, width), F32) for r in z_rows],
        scratch_shapes=[pltpu.VMEM((slots, width), BF), pltpu.VMEM((fine, width), BF)],
        compiler_params=params(16),
        cost_estimate=cost(4 * slots * fine * width, 13e6),
        name="image_first",
    )(*xs, a, at, obs, g_sums)


def second_kernel(count, *refs):
    x_refs, refs = refs[:count], refs[count:]
    a_ref, obs_ref, g_ref, after_ref, im_ref, sum_ref, xs = refs
    lay_out(x_refs, xs)
    fine = a_ref.shape[0]
    rows = fine // CUTS
    sums = g_ref[...]
    row = lax.broadcasted_iota(jnp.int32, sums.shape, 0)
    for i in range(CUTS):
        some = pl.ds(i * rows, rows)
        im = dot(a_ref[some, :], xs[...])
        im_ref[some, :] = im
        v = obs_ref[some, :].astype(F32) * im
        sums = sums + jnp.where(row == 1, fold(v * im), 0.0)
    sum_ref[...] = sums


def image_second(xs, a, obs, g_sums, after):
    fine, slots = a.shape
    width = obs.shape[1]
    return pl.pallas_call(
        functools.partial(second_kernel, len(xs)),
        in_specs=[VMEM] * (len(xs) + 3) + [ANY],
        out_specs=[VMEM] * 2,
        out_shape=[shape((fine, width), F32), shape((8, width), F32)],
        scratch_shapes=[pltpu.VMEM((slots, width), BF)],
        compiler_params=params(16),
        cost_estimate=cost(2 * slots * fine * width, 8e6),
        name="image_second",
    )(*xs, a, obs, g_sums, after)


def over_core(x):
    return lax.ppermute(x, "space", [(i, i ^ 1) for i in range(GROUP)])


def over_chips(x):
    groups = [list(range(c, GROUP, 2)) for c in range(2)]
    return lax.all_to_all(
        x, "space", split_axis=0, concat_axis=0, axis_index_groups=groups, tiled=True
    )


def scatter_sums(parts, after, sums=None):
    near, far = parts
    return tie(over_chips(merge(near, over_core(far), sums)), after), None


def gather_columns(x, after):
    got = over_chips(x)
    if after is not None:
        got = tie(got, after)
    return [got, over_core(got)]


def sum_all(x):
    x = jnp.broadcast_to(x[None], (GROUP,) + x.shape)
    x = lax.all_to_all(x, "space", split_axis=0, concat_axis=0, tiled=True)
    return jnp.sum(x, axis=0)


def on_device(ensemble, innovation, obs_weight, interp_weight, slot_of, intersection_list):
    members, columns, width = ensemble.shape
    levels = width // VAR
    devices = lax.axis_size("space")
    capacity = intersection_list.shape[2]
    slots = devices * capacity
    grouped = devices == GROUP and capacity == columns == LANES

    taper = vertical_taper(levels)
    both = taper.astype(np.float64) @ taper.T.astype(np.float64)
    kern = np.tile(np.concatenate(host_halves(both), axis=0), (2, VAR))
    tall = np.tile(np.concatenate(host_halves(taper), axis=0), (2, 1))
    none = np.zeros_like(tall)
    taps = np.stack(
        [np.concatenate([tall, none], axis=1), np.concatenate([none, tall], axis=1)]
    )
    kern, taps = jnp.asarray(kern), jnp.asarray(taps)

    ens = jnp.transpose(ensemble, (1, 0, 2))
    at, y_slots = adjoint_first(slot_of, interp_weight, innovation, obs_weight, slots)
    index = lax.axis_index("space").astype(jnp.int32)
    me = jnp.stack([index % 2, index])
    if grouped:
        lists = lax.all_gather(intersection_list, "space", axis=0, tiled=True)
        lists = lax.dynamic_index_in_dim(lists, index, axis=1, keepdims=False)
        scatter, gather, add_up = scatter_sums, gather_columns, sum_all
        first = split_first(me, lists, y_slots)
        at = place_rows(me, lists, at)
        n, copies = 2, CHIPS
    else:
        lists = intersection_list[0]
        hit = (lists.reshape(-1, 1) == jnp.arange(columns, dtype=jnp.int32)).astype(BF)

        def swap(x):
            x = x.reshape(devices, capacity, width)
            x = lax.all_to_all(x, "space", split_axis=0, concat_axis=0, tiled=True)
            return x.reshape(slots, width)

        def scatter(parts, after, sums=None):
            got = swap(parts[0])
            high = lax.reduce_precision(got, 8, 7)
            high, low = high.astype(BF), (got - high).astype(BF)
            if sums is not None:
                sums = lax.psum(sums, "space")
            return dot(hit.T, high) + dot(hit.T, low), sums

        def gather(x, after):
            return [swap(dot(hit, x[0]).astype(BF))]

        def add_up(x):
            return lax.psum(x, "space")

        first = [y_slots]
        n, copies = 1, 1

    a = forward_matrix(me, slot_of.T, interp_weight.T, lists, slots, grouped)
    own, _ = scatter(first, ens)
    x0, y0, g_sums = coarse_image(ens, kern, own, at, copies)
    im0, sums, *second = image_first(gather(x0, a), a, at, obs_weight, g_sums, n)
    g0 = project(ens, y0, taps)
    own, sums = scatter(second, g0, sums)
    x1, y1, l0, g_sums = coarse_image(ens, kern, own, g0, copies, y0, sums)
    g1 = project(ens, y1, taps)
    im1, sums = image_second(gather(x1, g1), a, obs_weight, g_sums, g1)
    l0 = l0[:1, :1]
    l1, _ = length_of(add_up(sums))
    return (-(l0 * g0 + l1 * g1), -(l0 * im0 + l1 * im1))


def solution(mesh):
    placed = (
        P("case", "space", None),
        P(("case", "space"), None),
        P(("case", "space"), None),
        P("case", "space"),
        P("case", "space"),
        P(("case", "space"), None, None),
    )
    return jax.shard_map(
        on_device,
        mesh=mesh,
        in_specs=placed,
        out_specs=(P("case", "space"), P(("case", "space"), None)),
        check_vma=False,
    )
```

```python
import functools

import jax
import jax.numpy as jnp
import ml_dtypes
import numpy as np
from jax import lax
from jax.experimental import pallas as pl
from jax.experimental.pallas import tpu as pltpu
from jax.sharding import PartitionSpec as P

VAR = 4
LOC_SCALE = 3.0
BF = jnp.bfloat16
F32 = jnp.float32
LANES = 128
GROUP = 16
VMEM = pl.BlockSpec(memory_space=pltpu.VMEM)
SMEM = pl.BlockSpec(memory_space=pltpu.SMEM)
ANY = pl.BlockSpec(memory_space=pl.ANY)


def vertical_taper(levels):
    heights = np.arange(levels).astype(np.float32)
    spread = (heights[:, None] - heights[None, :]) / np.float32(LOC_SCALE)
    return np.exp(np.float32(-0.5) * spread * spread)


def host_halves(x):
    high = x.astype(ml_dtypes.bfloat16)
    return [high, (x - high.astype(x.dtype)).astype(ml_dtypes.bfloat16)]


def params(mib):
    return pltpu.CompilerParams(vmem_limit_bytes=mib << 20)


def cost(flops, nbytes):
    return pl.CostEstimate(flops=int(flops), bytes_accessed=int(nbytes), transcendentals=0)


def dot(a, b):
    return jnp.dot(a, b, preferred_element_type=F32)


def halves(x):
    high = x.astype(BF)
    return high, (x - high.astype(F32)).astype(BF)


def shape(dims, dtype):
    return jax.ShapeDtypeStruct(dims, dtype)


STEPS = 4
ORDER = (2, 1, 3, 0)
PARTS = ((0, 0), (1, 0), (0, 1), (1, 1))
HEAD = 16
TOP = 32512.0


def owner_at(me_ref, i):
    dy, dc = PARTS[i // STEPS]
    z, y, c = me_ref[0], me_ref[1], me_ref[2]
    y = y if dy == 0 else 1 - y
    c = c if dc == 0 else 1 - c
    return (lax.rem(z + ORDER[i % STEPS], STEPS) * 2 + y) * 2 + c


def places(me_ref, lists_ref, slots):
    slots = jnp.concatenate([slots, slots], axis=0)
    from_owner = jnp.right_shift(slots, 7)
    within = jnp.bitwise_and(slots, LANES - 1)
    rows = jnp.zeros(slots.shape, jnp.int32)
    for i in range(GROUP):
        o = owner_at(me_ref, i)
        row = jnp.broadcast_to(lists_ref[pl.ds(o, 1), :], slots.shape)
        column = jnp.take_along_axis(row, within, axis=1, mode="promise_in_bounds")
        rows = jnp.where(from_owner == o, column + i * LANES, rows)
    return rows[: slots.shape[0] // 2]


def build_rows(ids_ref, weight_ref, wh_ref, wl_ref, at_ref, y_refs, lo_s, base):
    sources, fine = ids_ref.shape
    rows = at_ref.shape[0] // len(y_refs)
    step = rows // 2
    row = lax.broadcasted_iota(jnp.int32, (step, LANES), 0)
    for n, y_ref in enumerate(y_refs):
        for m in range(2):
            start = n * rows + m * step
            for j in range(fine // LANES):
                lanes = pl.ds(j * LANES, LANES)
                total = None
                for b in range(sources):
                    ids = ids_ref[b : b + 1, lanes] - (base + start)
                    term = jnp.where(row == ids, weight_ref[b : b + 1, lanes], 0.0)
                    total = term if total is None else total + term
                high, low = halves(total)
                at_ref[pl.ds(start, step), lanes] = high
                lo_s[pl.ds(m * step, step), lanes] = low
        held = at_ref[pl.ds(n * rows, rows), :]
        y_ref[...] = dot(held, wh_ref[...]) + dot(held, wl_ref[...]) + dot(lo_s[...], wh_ref[...])


def far_kernel(grouped, me_ref, lists_ref, both_ref, wh_ref, wl_ref, *refs):
    ids_ref, weight_ref, at_ref, ya_ref, yb_ref, lo_s = refs
    sources = ids_ref.shape[0]
    for j in range(ids_ref.shape[1] // LANES):
        lanes = pl.ds(j * LANES, LANES)
        slots = both_ref[:sources, lanes].astype(jnp.int32)
        ids_ref[:, lanes] = places(me_ref, lists_ref, slots) if grouped else slots
        weight_ref[:, lanes] = both_ref[sources:, lanes]
    half = at_ref.shape[0]
    build_rows(ids_ref, weight_ref, wh_ref, wl_ref, at_ref, [ya_ref, yb_ref], lo_s, half)


def near_kernel(ids_ref, weight_ref, wh_ref, wl_ref, at_ref, ya_ref, yb_ref, lo_s):
    build_rows(ids_ref, weight_ref, wh_ref, wl_ref, at_ref, [ya_ref, yb_ref], lo_s, 0)


def adjoint_half(slots, args, head=None):
    fine, width = args[-1].shape
    half = slots // 2
    sources = args[0].shape[0] // (2 if head else 1)
    out = [shape((half, fine), BF)] + [shape((half // 2, width), F32)] * 2
    if head:
        grouped, me, lists = head
        kernel = functools.partial(far_kernel, grouped)
        args = [me, lists, *args]
        out = [shape((sources, fine), jnp.int32), shape((sources, fine), F32)] + out
    else:
        kernel = near_kernel
    return pl.pallas_call(
        kernel,
        in_specs=([SMEM] if head else []) + [VMEM] * (len(args) - (1 if head else 0)),
        out_specs=[VMEM] * len(out),
        out_shape=out,
        scratch_shapes=[pltpu.VMEM((half // 2, fine), BF)],
        compiler_params=params(16),
        cost_estimate=cost(3 * slots * fine * width, 4e6),
        name="adjoint_far" if head else "adjoint_near",
    )(*args)


def exponent(m):
    return jnp.clip(jnp.ceil(jnp.log2(jnp.maximum(m, 1e-30))), -100.0, 100.0)


def whole16(x):
    return x.astype(jnp.int32).astype(jnp.int16)


def wide(x):
    return x.astype(jnp.int32).astype(F32)


def pack(out_ref, t, sums=None):
    rows, width = t.shape
    e = exponent(jnp.max(jnp.abs(t), axis=0, keepdims=True))
    out_ref[pl.ds(0, rows), :] = whole16(jnp.round(t * (jnp.exp2(-e) * TOP)))
    head = [e]
    if sums is not None:
        for i in range(2):
            v = sums[i : i + 1, :]
            f = exponent(v)
            v = v * (jnp.exp2(-f) * 16384.0)
            first = jnp.floor(v)
            head += [f, first, jnp.floor((v - first) * 16384.0)]
    row = lax.broadcasted_iota(jnp.int32, (HEAD, width), 0)
    total = jnp.zeros((HEAD, width), F32)
    for i, h in enumerate(head):
        total = jnp.where(row == i, h, total)
    out_ref[pl.ds(rows, HEAD), :] = whole16(total)


def unpack(ref):
    rows = ref.shape[0] - HEAD
    head = wide(ref[pl.ds(rows, HEAD), :])
    return wide(ref[pl.ds(0, rows), :]) * (jnp.exp2(head[0:1, :]) * (1.0 / TOP))


def unpack_sums(ref):
    head = wide(ref[pl.ds(ref.shape[0] - HEAD, HEAD), :])
    row = lax.broadcasted_iota(jnp.int32, (8, head.shape[1]), 0)
    total = jnp.zeros(row.shape, F32)
    for i in range(2):
        f, first, second = [head[1 + 3 * i + j : 2 + 3 * i + j, :] for j in range(3)]
        v = (first + second * (1.0 / 16384.0)) * (jnp.exp2(f) * (1.0 / 16384.0))
        total = jnp.where(row == i, v, total)
    return total


def merge_y_kernel(with_sums, *refs):
    if with_sums:
        a_ref, b_ref, mine_ref, first_ref, second_ref, s_ref = refs
        sums = mine_ref[...] + b_ref[pl.ds(a_ref.shape[0], 8), :]
        s_ref[...] = sums
    else:
        a_ref, b_ref, first_ref, second_ref = refs
        sums = None
    half = a_ref.shape[0] // 2
    pack(first_ref, a_ref[pl.ds(0, half), :] + b_ref[pl.ds(0, half), :], sums)
    pack(second_ref, a_ref[pl.ds(half, half), :] + b_ref[pl.ds(half, half), :])


def merge_y(a, b, sums):
    rows, width = a.shape
    out = [shape((rows // 2 + HEAD, width), jnp.int16)] * 2
    args = [a, b]
    if sums is not None:
        out.append(shape((8, width), F32))
        args.append(sums)
    return pl.pallas_call(
        functools.partial(merge_y_kernel, sums is not None),
        in_specs=[VMEM] * len(args),
        out_specs=[VMEM] * len(out),
        out_shape=out,
        compiler_params=params(8),
        cost_estimate=cost(5 * rows * width, 1e6),
        name="merge_y",
    )(*args)


def merge_z_kernel(last, with_sums, a_ref, b_ref, p_ref, *refs):
    half = a_ref.shape[0] // 2
    rows = pl.ds(half if last else 0, half)
    t = a_ref[rows, :] + b_ref[rows, :] + unpack(p_ref)
    sums = None
    if with_sums:
        sums = refs[0][...]
        refs = refs[1:]
        if not last:
            sums = sums + unpack_sums(p_ref)
            refs[2][...] = sums
    pack(refs[0], t[:LANES], sums)
    if last:
        refs[1][...] = t[LANES:]
    else:
        pack(refs[1], t[LANES:], sums)


def merge_z(last, a, b, p, sums):
    width = a.shape[1]
    sent = shape((LANES + HEAD, width), jnp.int16)
    out = [sent, shape((LANES, width), F32) if last else sent]
    args = [a, b, p]
    if sums is not None:
        args.append(sums)
        if not last:
            out.append(shape((8, width), F32))
    return pl.pallas_call(
        functools.partial(merge_z_kernel, last, sums is not None),
        in_specs=[VMEM] * len(args),
        out_specs=[VMEM] * len(out),
        out_shape=out,
        compiler_params=params(8),
        cost_estimate=cost(5 * a.size, 1e6),
        name="merge_z_last" if last else "merge_z_first",
    )(*args)


def join_kernel(a_ref, b_ref, c_ref, after_ref, out_ref):
    for i, r in enumerate((a_ref, b_ref, c_ref)):
        out_ref[i] = r[...]


def join(blocks, after):
    return pl.pallas_call(
        join_kernel,
        in_specs=[VMEM] * 4,
        out_specs=VMEM,
        out_shape=shape((3,) + blocks[0].shape, BF),
        compiler_params=params(8),
        cost_estimate=cost(1e5, 4e5),
        name="join",
    )(*blocks, after)


def fold(a):
    return jnp.sum(a, axis=0, keepdims=True)


def length_of(sums):
    grad = jnp.sum(sums[0:1, :], axis=1, keepdims=True)
    image = jnp.sum(sums[1:2, :], axis=1, keepdims=True)
    return grad / (grad + image), image / (grad + image)


def products(e, y, held, rows):
    p = e.astype(F32) * y
    q = p[:, :LANES] + p[:, LANES:]
    q = q + pltpu.roll(q, LANES // 2, 1)
    high, low = halves(q)
    held[rows, :LANES] = high
    held[rows, LANES:] = low


BATCH = 16
SOME = 8


def coarse_kernel(packed, second, e_ref, k_ref, own_ref, *refs):
    refs = list(refs)
    got = [refs.pop(0) for _ in range(packed)]
    y = own_ref[...]
    for r in got:
        y = y + unpack(r)
    if second:
        y0_ref, s_ref = refs.pop(0), refs.pop(0)
        sums = s_ref[...]
        for r in got:
            sums = sums + unpack_sums(r)
        l0, keep = length_of(sums)
        y = keep * y0_ref[...] - l0 * y
        refs.pop(2)[...] = jnp.broadcast_to(l0, (8, LANES))
    x_ref, y_ref, sum_ref, p_s, x_s = refs
    members, columns, width = e_ref.shape
    y_ref[...] = y
    x_s[...] = jnp.zeros_like(x_s)

    @pl.loop(0, members // SOME)
    def _(i):
        for m in range(SOME):
            products(e_ref[i * SOME + m], y_ref[...], p_s, pl.ds(m * columns, columns))
        t = dot(p_s[...], k_ref[...])
        total = x_s[...]
        for m in range(SOME):
            total = total + t[m * columns : (m + 1) * columns] * e_ref[i * SOME + m].astype(F32)
        x_s[...] = total

    x = x_s[...]
    x_ref[...] = x.T.astype(BF)
    sum_ref[...] = jnp.zeros_like(sum_ref)
    sum_ref[0:1, :] = fold(x * y_ref[...])


def coarse_image(ensemble, kern, own, got, y0=None, sums=None):
    members, columns, width = ensemble.shape
    second = y0 is not None
    args = [ensemble, kern, own, *got] + ([y0, sums] if second else [])
    out = [shape((width, columns), BF), shape((columns, width), F32)]
    out += [shape((8, LANES), F32)] if second else []
    out += [shape((8, width), F32)]
    return pl.pallas_call(
        functools.partial(coarse_kernel, len(got), second),
        in_specs=[VMEM] * len(args),
        out_specs=[VMEM] * len(out),
        out_shape=out,
        scratch_shapes=[
            pltpu.VMEM((SOME * columns, width), BF),
            pltpu.VMEM((columns, width), F32),
        ],
        compiler_params=params(16),
        cost_estimate=cost(2 * columns * members * width * width, 5e6),
        name="coarse_second" if second else "coarse_first",
    )(*args)


def project_kernel(e_ref, y_ref, t_ref, g_ref, token_ref, even_s, odd_s):
    columns, members, width = e_ref.shape
    lanes = BATCH // 2 * LANES
    token_ref[...] = jnp.zeros_like(token_ref)

    @pl.loop(0, columns // BATCH)
    def _(i):
        base = pl.multiple_of(i * BATCH, BATCH)
        yb = y_ref[pl.ds(base, BATCH), :]
        for c in range(BATCH):
            held = odd_s if c % 2 else even_s
            rows = pl.ds((c // 2) * members, members)
            products(e_ref[base + c], yb[c : c + 1, :], held, rows)
        r = dot(even_s[...], t_ref[0]) + dot(odd_s[...], t_ref[1])
        for pair in range(BATCH // 2):
            at = pl.multiple_of(i * lanes + pair * LANES, LANES)
            g_ref[:, pl.ds(at, LANES)] = r[pair * members : (pair + 1) * members]


def project(ens, y, taps):
    columns, members, width = ens.shape
    levels = width // VAR
    return pl.pallas_call(
        project_kernel,
        in_specs=[VMEM] * 3,
        out_specs=[VMEM] * 2,
        out_shape=[shape((members, columns * levels), F32), shape((8, LANES), F32)],
        scratch_shapes=[pltpu.VMEM((BATCH // 2 * members, width), BF)] * 2,
        compiler_params=params(16),
        cost_estimate=cost(2 * columns * members * width * width, 8e6),
        name="project",
    )(ens, y, taps)


def lay_out(x_refs, xs):
    if len(x_refs) == 1:
        xs[...] = x_refs[0][...]
        return
    own, rest = x_refs[0::2], x_refs[1::2]
    for part in range(STEPS):
        at = part * STEPS * LANES
        for i in range(STEPS - 1):
            xs[:, pl.ds(at + i * LANES, LANES)] = rest[part][i]
        xs[:, pl.ds(at + (STEPS - 1) * LANES, LANES)] = own[part][...]


CUTS = 3


def images(x_refs, near_ref, far_ref, obs_ref, im_ref, xs):
    lay_out(x_refs, xs)
    half, fine = near_ref.shape
    rows = fine // CUTS
    for i in range(CUTS):
        some = pl.ds(i * rows, rows)
        turned = dot(xs[:, :half], near_ref[:, some]) + dot(xs[:, half:], far_ref[:, some])
        im = turned.T
        im_ref[some, :] = im
        yield some, im, obs_ref[some, :].astype(F32) * im


def image_kernel(count, *refs):
    x_refs, refs = refs[:count], refs[count:]
    near_ref, far_ref, obs_ref, g_ref, im_ref, sum_ref = refs[:6]
    outs, (xs, v_s) = refs[6:10], refs[10:]
    sums = g_ref[...]
    row = lax.broadcasted_iota(jnp.int32, sums.shape, 0)
    for some, im, v in images(x_refs, near_ref, far_ref, obs_ref, im_ref, xs):
        v_s[some, :] = v.astype(BF)
        sums = sums + jnp.where(row == 1, fold(v * im), 0.0)
    sum_ref[...] = sums
    rows = near_ref.shape[0] // 2
    for i, out in enumerate(outs):
        at_ref = far_ref if i > 1 else near_ref
        out[pl.ds(0, rows), :] = dot(at_ref[pl.ds(i % 2 * rows, rows), :], v_s[...])
    outs[3][pl.ds(rows, 8), :] = sums


def image_first(xs, near, far, obs, g_sums):
    half, fine = near.shape
    width = obs.shape[1]
    z_rows = [half // 2] * 3 + [half // 2 + 8]
    return pl.pallas_call(
        functools.partial(image_kernel, len(xs)),
        in_specs=[VMEM] * (len(xs) + 4),
        out_specs=[VMEM] * 6,
        out_shape=[shape((fine, width), F32), shape((8, width), F32)]
        + [shape((r, width), F32) for r in z_rows],
        scratch_shapes=[pltpu.VMEM((width, 2 * half), BF), pltpu.VMEM((fine, width), BF)],
        compiler_params=params(16),
        cost_estimate=cost(8 * half * fine * width, 13e6),
        name="image_first",
    )(*xs, near, far, obs, g_sums)


def second_kernel(count, *refs):
    x_refs, refs = refs[:count], refs[count:]
    near_ref, far_ref, obs_ref, g_ref, im_ref, sum_ref, xs = refs
    sums = g_ref[...]
    row = lax.broadcasted_iota(jnp.int32, sums.shape, 0)
    for _, im, v in images(x_refs, near_ref, far_ref, obs_ref, im_ref, xs):
        sums = sums + jnp.where(row == 1, fold(v * im), 0.0)
    sum_ref[...] = sums


def image_second(xs, near, far, obs, g_sums):
    half, fine = near.shape
    width = obs.shape[1]
    return pl.pallas_call(
        functools.partial(second_kernel, len(xs)),
        in_specs=[VMEM] * (len(xs) + 4),
        out_specs=[VMEM] * 2,
        out_shape=[shape((fine, width), F32), shape((8, width), F32)],
        scratch_shapes=[pltpu.VMEM((width, 2 * half), BF)],
        compiler_params=params(16),
        cost_estimate=cost(4 * half * fine * width, 8e6),
        name="image_second",
    )(*xs, near, far, obs, g_sums)


def result_kernel(count, l0_ref, *refs):
    sums = refs[0][...]
    for r in refs[1:count]:
        sums = sums + r[...]
    g0_ref, g1_ref, i0_ref, i1_ref, control_ref, increment_ref = refs[count:]
    l0 = -l0_ref[0:1, 0:1]
    l1, _ = length_of(sums)
    control_ref[...] = l0 * g0_ref[...] - l1 * g1_ref[...]
    increment_ref[...] = l0 * i0_ref[...] - l1 * i1_ref[...]


def result(l0, sums, g0, g1, im0, im1):
    cuts = 4
    whole = lambda i: (0, 0)
    g_spec = pl.BlockSpec((g0.shape[0], g0.shape[1] // cuts), lambda i: (0, i))
    i_spec = pl.BlockSpec((im0.shape[0] // cuts, im0.shape[1]), lambda i: (i, 0))
    return pl.pallas_call(
        functools.partial(result_kernel, len(sums)),
        grid=(cuts,),
        in_specs=[pl.BlockSpec(l0.shape, whole)]
        + [pl.BlockSpec(r.shape, whole) for r in sums]
        + [g_spec, g_spec, i_spec, i_spec],
        out_specs=[g_spec, i_spec],
        out_shape=[shape(g0.shape, F32), shape(im0.shape, F32)],
        compiler_params=params(24),
        cost_estimate=cost(3 * g0.size, 1e7),
        name="result",
    )(l0, *sums, g0, g1, im0, im1)


def over_core(x):
    return lax.ppermute(x, "space", [(i, i ^ 1) for i in range(GROUP)])


def over_y(x):
    return lax.ppermute(x, "space", [(i, i ^ 2) for i in range(GROUP)])


def over_z(x, k):
    return lax.ppermute(x, "space", [(i, (i + 4 * k) % GROUP) for i in range(GROUP)])


def scatter_sums(parts, sums=None):
    near, far_y, near_c, far_yc = parts
    got_yc = over_core(far_yc)
    got_c = over_core(near_c)
    first, second, *s = merge_y(far_y, got_yc, sums)
    first, second = over_y(first), over_y(second)
    two, one, *s = merge_z(False, near, got_c, first, s[0] if s else None)
    got = [over_z(two, 2), over_z(one, 1)]
    three, own = merge_z(True, near, got_c, second, s[0] if s else None)
    return own, got + [over_z(three, 3)], (s[0] if s else None)


def gather_columns(x, after):
    two, three, one = over_z(x, 2), over_z(x, 3), over_z(x, 1)
    y_own = over_y(x)
    c_own = over_core(x)
    rest = join([two, three, one], after)
    y_rest = over_y(rest)
    c_rest = over_core(rest)
    return [x, rest, y_own, y_rest, c_own, c_rest, over_core(y_own), over_core(y_rest)]


def sum_all(x):
    x = x + over_core(x)
    x = x + over_y(x)
    return [x] + [over_z(x, k) for k in range(1, STEPS)]


def on_device(ensemble, innovation, obs_weight, interp_weight, slot_of, intersection_list):
    members, columns, width = ensemble.shape
    levels = width // VAR
    devices = lax.axis_size("space")
    capacity = intersection_list.shape[2]
    slots = devices * capacity
    grouped = devices == GROUP and capacity == columns == LANES

    taper = vertical_taper(levels)
    both = taper.astype(np.float64) @ taper.T.astype(np.float64)
    kern = np.tile(np.concatenate(host_halves(both), axis=0), (2, VAR))
    tall = np.tile(np.concatenate(host_halves(taper), axis=0), (2, 1))
    none = np.zeros_like(tall)
    taps = np.stack(
        [np.concatenate([tall, none], axis=1), np.concatenate([none, tall], axis=1)]
    )
    kern, taps = jnp.asarray(kern), jnp.asarray(taps)

    index = lax.axis_index("space").astype(jnp.int32)
    me = jnp.stack([index // 4, index // 2 % 2, index % 2, index])
    w = -(obs_weight.astype(F32) * innovation.astype(F32))
    high = lax.reduce_precision(w, 8, 7)
    wh, wl = high.astype(BF), (w - high).astype(BF)
    named = jnp.concatenate([slot_of.astype(F32), interp_weight], axis=0)
    if grouped:
        lists = lax.all_to_all(
            intersection_list, "space", split_axis=1, concat_axis=0, tiled=True
        ).reshape(devices, capacity)
        scatter, gather, add_up = scatter_sums, gather_columns, sum_all
    else:
        lists = intersection_list[0]
        hit = (lists.reshape(-1, 1) == jnp.arange(columns, dtype=jnp.int32)).astype(BF)

        def swap(x):
            x = x.reshape(devices, capacity, width)
            x = lax.all_to_all(x, "space", split_axis=0, concat_axis=0, tiled=True)
            return x.reshape(slots, width)

        def scatter(parts, sums=None):
            got = swap(jnp.concatenate([p[: slots // 4] for p in parts], axis=0))
            high = lax.reduce_precision(got, 8, 7)
            high, low = high.astype(BF), (got - high).astype(BF)
            if sums is not None:
                sums = lax.psum(sums, "space")
            return dot(hit.T, high) + dot(hit.T, low), [], sums

        def gather(x, after):
            return [swap(dot(hit, x.T).astype(BF)).T]

        def add_up(x):
            return [lax.psum(x, "space")]

    ids, weight, far, c0, c1 = adjoint_half(slots, [named, wh, wl], (grouped, me, lists))
    near, n0, n1 = adjoint_half(slots, [ids, weight, wh, wl])
    own, got, _ = scatter([n0, n1, c0, c1])
    x0, y0, g_sums = coarse_image(ensemble, kern, own, got)
    ens = jnp.transpose(ensemble, (1, 0, 2))
    g0, token = project(ens, y0, taps)
    im0, sums, *second = image_first(gather(x0, token), near, far, obs_weight, g_sums)
    own, got, sums = scatter(second, sums)
    x1, y1, l0, g_sums = coarse_image(ensemble, kern, own, got, y0, sums)
    g1, token = project(ens, y1, taps)
    im1, sums = image_second(gather(x1, token), near, far, obs_weight, g_sums)
    return tuple(result(l0, add_up(sums), g0, g1, im0, im1))


def solution(mesh):
    placed = (
        P("case", "space", None),
        P(("case", "space"), None),
        P(("case", "space"), None),
        P("case", "space"),
        P("case", "space"),
        P(("case", "space"), None, None),
    )
    return jax.shard_map(
        on_device,
        mesh=mesh,
        in_specs=placed,
        out_specs=(P("case", "space"), P(("case", "space"), None)),
        check_vma=False,
    )
```

```python
import functools

import jax
import jax.numpy as jnp
import ml_dtypes
import numpy as np
from jax import lax
from jax.experimental import pallas as pl
from jax.experimental.pallas import tpu as pltpu
from jax.sharding import PartitionSpec as P

VAR = 4
LOC_SCALE = 3.0
BF = jnp.bfloat16
F32 = jnp.float32
LANES = 128
GROUP = 16
VMEM = pl.BlockSpec(memory_space=pltpu.VMEM)
SMEM = pl.BlockSpec(memory_space=pltpu.SMEM)
ANY = pl.BlockSpec(memory_space=pl.ANY)


def vertical_taper(levels):
    heights = np.arange(levels).astype(np.float32)
    spread = (heights[:, None] - heights[None, :]) / np.float32(LOC_SCALE)
    return np.exp(np.float32(-0.5) * spread * spread)


def host_halves(x):
    high = x.astype(ml_dtypes.bfloat16)
    return [high, (x - high.astype(x.dtype)).astype(ml_dtypes.bfloat16)]


def params(mib):
    return pltpu.CompilerParams(vmem_limit_bytes=mib << 20)


def cost(flops, nbytes):
    return pl.CostEstimate(flops=int(flops), bytes_accessed=int(nbytes), transcendentals=0)


def dot(a, b):
    return jnp.dot(a, b, preferred_element_type=F32)


def halves(x):
    high = x.astype(BF)
    return high, (x - high.astype(F32)).astype(BF)


def shape(dims, dtype):
    return jax.ShapeDtypeStruct(dims, dtype)


STEPS = 4
ORDER = (2, 1, 3, 0)
PARTS = ((0, 0), (1, 0), (0, 1), (1, 1))
HEAD = 16
TOP = 32512.0


def owner_at(me_ref, i):
    dy, dc = PARTS[i // STEPS]
    z, y, c = me_ref[0], me_ref[1], me_ref[2]
    y = y if dy == 0 else 1 - y
    c = c if dc == 0 else 1 - c
    return (lax.rem(z + ORDER[i % STEPS], STEPS) * 2 + y) * 2 + c


def places(me_ref, list_refs, slots):
    slots = jnp.concatenate([slots, slots], axis=0)
    from_owner = jnp.right_shift(slots, 7)
    within = jnp.bitwise_and(slots, LANES - 1)
    rows = jnp.zeros(slots.shape, jnp.int32)
    for i in range(GROUP):
        o = owner_at(me_ref, i)
        dy, dc = PARTS[i // STEPS]
        held = list_refs[-ORDER[i % STEPS] % STEPS]
        row = jnp.broadcast_to(held[2 * dy + dc : 2 * dy + dc + 1, :], slots.shape)
        column = jnp.take_along_axis(row, within, axis=1, mode="promise_in_bounds")
        rows = jnp.where(from_owner == o, column + i * LANES, rows)
    return rows[: slots.shape[0] // 2]


def build_rows(ids_ref, weight_ref, wh_ref, wl_ref, at_ref, y_refs, lo_s, base):
    sources, fine = ids_ref.shape
    rows = at_ref.shape[0] // len(y_refs)
    step = rows // 2
    row = lax.broadcasted_iota(jnp.int32, (step, LANES), 0)
    for n, y_ref in enumerate(y_refs):
        for m in range(2):
            start = n * rows + m * step
            for j in range(fine // LANES):
                lanes = pl.ds(j * LANES, LANES)
                total = None
                for b in range(sources):
                    ids = ids_ref[b : b + 1, lanes] - (base + start)
                    term = jnp.where(row == ids, weight_ref[b : b + 1, lanes], 0.0)
                    total = term if total is None else total + term
                high, low = halves(total)
                at_ref[pl.ds(start, step), lanes] = high
                lo_s[pl.ds(m * step, step), lanes] = low
        held = at_ref[pl.ds(n * rows, rows), :]
        y_ref[...] = dot(held, wh_ref[...]) + dot(held, wl_ref[...]) + dot(lo_s[...], wh_ref[...])


def far_kernel(grouped, me_ref, *refs):
    list_refs, refs = refs[: 4 * grouped], refs[4 * grouped :]
    both_ref, wh_ref, wl_ref, *refs = refs
    ids_ref, weight_ref, at_ref, ya_ref, yb_ref, lo_s = refs
    sources = ids_ref.shape[0]
    for j in range(ids_ref.shape[1] // LANES):
        lanes = pl.ds(j * LANES, LANES)
        slots = both_ref[:sources, lanes].astype(jnp.int32)
        ids_ref[:, lanes] = places(me_ref, list_refs, slots) if grouped else slots
        weight_ref[:, lanes] = both_ref[sources:, lanes]
    half = at_ref.shape[0]
    build_rows(ids_ref, weight_ref, wh_ref, wl_ref, at_ref, [ya_ref, yb_ref], lo_s, half)


def near_kernel(ids_ref, weight_ref, wh_ref, wl_ref, at_ref, ya_ref, yb_ref, lo_s):
    build_rows(ids_ref, weight_ref, wh_ref, wl_ref, at_ref, [ya_ref, yb_ref], lo_s, 0)


def adjoint_half(slots, args, head=None):
    fine, width = args[-1].shape
    half = slots // 2
    sources = args[0].shape[0] // (2 if head else 1)
    out = [shape((half, fine), BF)] + [shape((half // 2, width), F32)] * 2
    if head:
        grouped, me, lists = head
        kernel = functools.partial(far_kernel, grouped)
        args = [me, *lists, *args]
        out = [shape((sources, fine), jnp.int32), shape((sources, fine), F32)] + out
    else:
        kernel = near_kernel
    return pl.pallas_call(
        kernel,
        in_specs=([SMEM] if head else []) + [VMEM] * (len(args) - (1 if head else 0)),
        out_specs=[VMEM] * len(out),
        out_shape=out,
        scratch_shapes=[pltpu.VMEM((half // 2, fine), BF)],
        compiler_params=params(16),
        cost_estimate=cost(3 * slots * fine * width, 4e6),
        name="adjoint_far" if head else "adjoint_near",
    )(*args)


def pick_kernel(me_ref, lists_ref, near_ref, far_ref):
    z, y, c = me_ref[0], me_ref[1], me_ref[2]
    for dy in range(2):
        for k in range(STEPS):
            there = (lax.rem(z + k, STEPS) * 2 + (y if dy == 0 else 1 - y)) * 2
            row = slice(dy * STEPS + k, dy * STEPS + k + 1)
            near_ref[row, :] = lists_ref[pl.ds(there + c, 1), :]
            far_ref[row, :] = lists_ref[pl.ds(there + 1 - c, 1), :]


def mix_y_kernel(near_ref, got_ref, near_y_ref, far_y_ref):
    for i, held in enumerate((near_ref, got_ref)):
        rows = slice(i * STEPS, (i + 1) * STEPS)
        near_y_ref[rows, :] = held[:STEPS, :]
        far_y_ref[rows, :] = held[STEPS:, :]


def mix_z_kernel(near_ref, got_ref, *outs):
    for k, out in enumerate(outs):
        out[...] = jnp.zeros_like(out)
        for i, held in enumerate((near_ref, got_ref)):
            for c in range(2):
                row = c * STEPS + k
                out[2 * i + c : 2 * i + c + 1, :] = held[row : row + 1, :]


def small(kernel, n, name, *args, scalars=0):
    return pl.pallas_call(
        kernel,
        in_specs=[SMEM] * scalars + [VMEM] * (len(args) - scalars),
        out_specs=[VMEM] * n,
        out_shape=[shape((8, LANES), jnp.int32)] * n,
        compiler_params=params(8),
        cost_estimate=cost(1e4, 3e4),
        name=name,
    )(*args)


def exchange_lists(me, lists):
    near, far = small(pick_kernel, 2, "pick", me, lists, scalars=1)
    near, far = small(mix_y_kernel, 2, "mix_y", near, over_core(far))
    own, *sent = small(mix_z_kernel, STEPS, "mix_z", near, over_y(far))
    return [own] + [over_z(sent[k - 1], k) for k in range(1, STEPS)]


def exponent(m):
    return jnp.clip(jnp.ceil(jnp.log2(jnp.maximum(m, 1e-30))), -100.0, 100.0)


def whole16(x):
    return x.astype(jnp.int32).astype(jnp.int16)


def wide(x):
    return x.astype(jnp.int32).astype(F32)


def pack(out_ref, t, sums=None):
    rows, width = t.shape
    e = exponent(jnp.max(jnp.abs(t), axis=0, keepdims=True))
    out_ref[pl.ds(0, rows), :] = whole16(jnp.round(t * (jnp.exp2(-e) * TOP)))
    head = [e]
    if sums is not None:
        for i in range(2):
            v = sums[i : i + 1, :]
            f = exponent(v)
            v = v * (jnp.exp2(-f) * 16384.0)
            first = jnp.floor(v)
            head += [f, first, jnp.floor((v - first) * 16384.0)]
    row = lax.broadcasted_iota(jnp.int32, (HEAD, width), 0)
    total = jnp.zeros((HEAD, width), F32)
    for i, h in enumerate(head):
        total = jnp.where(row == i, h, total)
    out_ref[pl.ds(rows, HEAD), :] = whole16(total)


def unpack(ref):
    rows = ref.shape[0] - HEAD
    head = wide(ref[pl.ds(rows, HEAD), :])
    return wide(ref[pl.ds(0, rows), :]) * (jnp.exp2(head[0:1, :]) * (1.0 / TOP))


def unpack_sums(ref):
    head = wide(ref[pl.ds(ref.shape[0] - HEAD, HEAD), :])
    row = lax.broadcasted_iota(jnp.int32, (8, head.shape[1]), 0)
    total = jnp.zeros(row.shape, F32)
    for i in range(2):
        f, first, second = [head[1 + 3 * i + j : 2 + 3 * i + j, :] for j in range(3)]
        v = (first + second * (1.0 / 16384.0)) * (jnp.exp2(f) * (1.0 / 16384.0))
        total = jnp.where(row == i, v, total)
    return total


def merge_y_kernel(with_sums, *refs):
    if with_sums:
        a_ref, b_ref, mine_ref, first_ref, second_ref, s_ref = refs
        sums = mine_ref[...] + b_ref[pl.ds(a_ref.shape[0], 8), :]
        s_ref[...] = sums
    else:
        a_ref, b_ref, first_ref, second_ref = refs
        sums = None
    half = a_ref.shape[0] // 2
    pack(first_ref, a_ref[pl.ds(0, half), :] + b_ref[pl.ds(0, half), :], sums)
    pack(second_ref, a_ref[pl.ds(half, half), :] + b_ref[pl.ds(half, half), :])


def merge_y(a, b, sums):
    rows, width = a.shape
    out = [shape((rows // 2 + HEAD, width), jnp.int16)] * 2
    args = [a, b]
    if sums is not None:
        out.append(shape((8, width), F32))
        args.append(sums)
    return pl.pallas_call(
        functools.partial(merge_y_kernel, sums is not None),
        in_specs=[VMEM] * len(args),
        out_specs=[VMEM] * len(out),
        out_shape=out,
        compiler_params=params(8),
        cost_estimate=cost(5 * rows * width, 1e6),
        name="merge_y",
    )(*args)


def merge_z_kernel(last, with_sums, a_ref, b_ref, p_ref, *refs):
    half = a_ref.shape[0] // 2
    rows = pl.ds(half if last else 0, half)
    t = a_ref[rows, :] + b_ref[rows, :] + unpack(p_ref)
    sums = None
    if with_sums:
        sums = refs[0][...]
        refs = refs[1:]
        if not last:
            sums = sums + unpack_sums(p_ref)
            refs[2][...] = sums
    pack(refs[0], t[:LANES], sums)
    if last:
        refs[1][...] = t[LANES:]
    else:
        pack(refs[1], t[LANES:], sums)


def merge_z(last, a, b, p, sums):
    width = a.shape[1]
    sent = shape((LANES + HEAD, width), jnp.int16)
    out = [sent, shape((LANES, width), F32) if last else sent]
    args = [a, b, p]
    if sums is not None:
        args.append(sums)
        if not last:
            out.append(shape((8, width), F32))
    return pl.pallas_call(
        functools.partial(merge_z_kernel, last, sums is not None),
        in_specs=[VMEM] * len(args),
        out_specs=[VMEM] * len(out),
        out_shape=out,
        compiler_params=params(8),
        cost_estimate=cost(5 * a.size, 1e6),
        name="merge_z_last" if last else "merge_z_first",
    )(*args)


def join_kernel(*refs):
    out_ref = refs[-1]
    for i, r in enumerate(refs[:3]):
        out_ref[i] = r[...]


def join(blocks, *after):
    return pl.pallas_call(
        join_kernel,
        in_specs=[VMEM] * (3 + len(after)),
        out_specs=VMEM,
        out_shape=shape((3,) + blocks[0].shape, BF),
        compiler_params=params(8),
        cost_estimate=cost(1e5, 4e5),
        name="join",
    )(*blocks, *after)


def fold(a):
    return jnp.sum(a, axis=0, keepdims=True)


def length_of(sums):
    grad = jnp.sum(sums[0:1, :], axis=1, keepdims=True)
    image = jnp.sum(sums[1:2, :], axis=1, keepdims=True)
    return grad / (grad + image), image / (grad + image)


def products(e, y, held, rows):
    p = e.astype(F32) * y
    q = p[:, :LANES] + p[:, LANES:]
    q = q + pltpu.roll(q, LANES // 2, 1)
    high, low = halves(q)
    held[rows, :LANES] = high
    held[rows, LANES:] = low


BATCH = 16
SOME = 8


def coarse_kernel(packed, second, e_ref, k_ref, own_ref, *refs):
    refs = list(refs)
    got = [refs.pop(0) for _ in range(packed)]
    y = own_ref[...]
    for r in got:
        y = y + unpack(r)
    if second:
        y0_ref, s_ref = refs.pop(0), refs.pop(0)
        sums = s_ref[...]
        for r in got:
            sums = sums + unpack_sums(r)
        l0, keep = length_of(sums)
        y = keep * y0_ref[...] - l0 * y
        refs.pop(2)[...] = jnp.broadcast_to(l0, (8, LANES))
    x_ref, y_ref, sum_ref, even_s, odd_s, x_s = refs
    members, columns, width = e_ref.shape
    y_ref[...] = y
    x_s[...] = jnp.zeros_like(x_s)

    def build(i, held):
        for m in range(SOME):
            products(e_ref[i * SOME + m], y_ref[...], held, pl.ds(m * columns, columns))

    def add_in(i, t):
        total = x_s[...]
        for m in range(SOME):
            total = total + t[m * columns : (m + 1) * columns] * e_ref[i * SOME + m].astype(F32)
        x_s[...] = total

    pairs = members // SOME // 2
    build(0, even_s)

    @pl.loop(0, pairs - 1)
    def _(i):
        t = dot(even_s[...], k_ref[...])
        build(2 * i + 1, odd_s)
        add_in(2 * i, t)
        t = dot(odd_s[...], k_ref[...])
        build(2 * i + 2, even_s)
        add_in(2 * i + 1, t)

    t = dot(even_s[...], k_ref[...])
    build(2 * pairs - 1, odd_s)
    add_in(2 * pairs - 2, t)
    add_in(2 * pairs - 1, dot(odd_s[...], k_ref[...]))

    x = x_s[...]
    x_ref[...] = x.T.astype(BF)
    sum_ref[...] = jnp.zeros_like(sum_ref)
    sum_ref[0:1, :] = fold(x * y_ref[...])


def coarse_image(ensemble, kern, own, got, y0=None, sums=None):
    members, columns, width = ensemble.shape
    second = y0 is not None
    args = [ensemble, kern, own, *got] + ([y0, sums] if second else [])
    out = [shape((width, columns), BF), shape((columns, width), F32)]
    out += [shape((8, LANES), F32)] if second else []
    out += [shape((8, width), F32)]
    return pl.pallas_call(
        functools.partial(coarse_kernel, len(got), second),
        in_specs=[VMEM] * len(args),
        out_specs=[VMEM] * len(out),
        out_shape=out,
        scratch_shapes=[
            pltpu.VMEM((SOME * columns, width), BF),
            pltpu.VMEM((SOME * columns, width), BF),
            pltpu.VMEM((columns, width), F32),
        ],
        compiler_params=params(16),
        cost_estimate=cost(2 * columns * members * width * width, 5e6),
        name="coarse_second" if second else "coarse_first",
    )(*args)


def project_kernel(e_ref, y_ref, t_ref, g_ref, token_ref, even_s, odd_s):
    columns, members, width = e_ref.shape
    lanes = BATCH // 2 * LANES
    token_ref[...] = jnp.zeros_like(token_ref)

    @pl.loop(0, columns // BATCH)
    def _(i):
        base = pl.multiple_of(i * BATCH, BATCH)
        yb = y_ref[pl.ds(base, BATCH), :]
        for c in range(BATCH):
            held = odd_s if c % 2 else even_s
            rows = pl.ds((c // 2) * members, members)
            products(e_ref[base + c], yb[c : c + 1, :], held, rows)
        r = dot(even_s[...], t_ref[0]) + dot(odd_s[...], t_ref[1])
        for pair in range(BATCH // 2):
            at = pl.multiple_of(i * lanes + pair * LANES, LANES)
            g_ref[:, pl.ds(at, LANES)] = r[pair * members : (pair + 1) * members]


def project(ens, y, taps):
    columns, members, width = ens.shape
    levels = width // VAR
    return pl.pallas_call(
        project_kernel,
        in_specs=[VMEM] * 3,
        out_specs=[VMEM] * 2,
        out_shape=[shape((members, columns * levels), F32), shape((8, LANES), F32)],
        scratch_shapes=[pltpu.VMEM((BATCH // 2 * members, width), BF)] * 2,
        compiler_params=params(16),
        cost_estimate=cost(2 * columns * members * width * width, 8e6),
        name="project",
    )(ens, y, taps)


def lay_out(x_refs, xs):
    if len(x_refs) == 1:
        xs[...] = x_refs[0][...]
        return
    own, rest = x_refs[0::2], x_refs[1::2]
    for part in range(STEPS):
        at = part * STEPS * LANES
        for i in range(STEPS - 1):
            xs[:, pl.ds(at + i * LANES, LANES)] = rest[part][i]
        xs[:, pl.ds(at + (STEPS - 1) * LANES, LANES)] = own[part][...]


CUTS = 3


def images(x_refs, near_ref, far_ref, obs_ref, im_ref, xs):
    lay_out(x_refs, xs)
    half, fine = near_ref.shape
    rows = fine // CUTS
    for i in range(CUTS):
        some = pl.ds(i * rows, rows)
        turned = dot(xs[:, :half], near_ref[:, some]) + dot(xs[:, half:], far_ref[:, some])
        im = turned.T
        im_ref[some, :] = im
        yield some, im, obs_ref[some, :].astype(F32) * im


def image_kernel(count, *refs):
    x_refs, refs = refs[:count], refs[count:]
    near_ref, far_ref, obs_ref, g_ref, im_ref, sum_ref = refs[:6]
    outs, (xs, v_s) = refs[6:10], refs[10:]
    sums = g_ref[...]
    row = lax.broadcasted_iota(jnp.int32, sums.shape, 0)
    for some, im, v in images(x_refs, near_ref, far_ref, obs_ref, im_ref, xs):
        v_s[some, :] = v.astype(BF)
        sums = sums + jnp.where(row == 1, fold(v * im), 0.0)
    sum_ref[...] = sums
    rows = near_ref.shape[0] // 2
    for i, out in enumerate(outs):
        at_ref = far_ref if i > 1 else near_ref
        out[pl.ds(0, rows), :] = dot(at_ref[pl.ds(i % 2 * rows, rows), :], v_s[...])
    outs[3][pl.ds(rows, 8), :] = sums


def image_first(xs, near, far, obs, g_sums):
    half, fine = near.shape
    width = obs.shape[1]
    z_rows = [half // 2] * 3 + [half // 2 + 8]
    return pl.pallas_call(
        functools.partial(image_kernel, len(xs)),
        in_specs=[VMEM] * (len(xs) + 4),
        out_specs=[VMEM] * 6,
        out_shape=[shape((fine, width), F32), shape((8, width), F32)]
        + [shape((r, width), F32) for r in z_rows],
        scratch_shapes=[pltpu.VMEM((width, 2 * half), BF), pltpu.VMEM((fine, width), BF)],
        compiler_params=params(16),
        cost_estimate=cost(8 * half * fine * width, 13e6),
        name="image_first",
    )(*xs, near, far, obs, g_sums)


def second_kernel(count, *refs):
    x_refs, refs = refs[:count], refs[count:]
    near_ref, far_ref, obs_ref, g_ref, im_ref, sum_ref, xs = refs
    sums = g_ref[...]
    row = lax.broadcasted_iota(jnp.int32, sums.shape, 0)
    for _, im, v in images(x_refs, near_ref, far_ref, obs_ref, im_ref, xs):
        sums = sums + jnp.where(row == 1, fold(v * im), 0.0)
    sum_ref[...] = sums


def image_second(xs, near, far, obs, g_sums):
    half, fine = near.shape
    width = obs.shape[1]
    return pl.pallas_call(
        functools.partial(second_kernel, len(xs)),
        in_specs=[VMEM] * (len(xs) + 4),
        out_specs=[VMEM] * 2,
        out_shape=[shape((fine, width), F32), shape((8, width), F32)],
        scratch_shapes=[pltpu.VMEM((width, 2 * half), BF)],
        compiler_params=params(16),
        cost_estimate=cost(4 * half * fine * width, 8e6),
        name="image_second",
    )(*xs, near, far, obs, g_sums)


OUT_CUTS = 4


def result_kernel(count, l0_ref, *refs):
    sums = refs[0][...]
    for r in refs[1:count]:
        sums = sums + r[...]
    g0_ref, g1_ref, i0_ref, i1_ref, control_hbm, increment_hbm, c_s, i_s, sem = refs[count:]
    l0 = -l0_ref[0:1, 0:1]
    l1, _ = length_of(sums)
    lanes = c_s.shape[1] // OUT_CUTS
    rows = i_s.shape[0] // OUT_CUTS
    copies = []
    for i in range(OUT_CUTS):
        some = pl.ds(i * lanes, lanes)
        c_s[:, some] = l0 * g0_ref[:, some] - l1 * g1_ref[:, some]
        copies.append(
            pltpu.make_async_copy(c_s.at[:, some], control_hbm.at[:, some], sem.at[2 * i])
        )
        copies[-1].start()
        some = pl.ds(i * rows, rows)
        i_s[some, :] = l0 * i0_ref[some, :] - l1 * i1_ref[some, :]
        copies.append(
            pltpu.make_async_copy(i_s.at[some, :], increment_hbm.at[some, :], sem.at[2 * i + 1])
        )
        copies[-1].start()
    for copy in copies:
        copy.wait()


def result(l0, sums, g0, g1, im0, im1):
    return pl.pallas_call(
        functools.partial(result_kernel, len(sums)),
        in_specs=[VMEM] * (5 + len(sums)),
        out_specs=[ANY] * 2,
        out_shape=[shape(g0.shape, F32), shape(im0.shape, F32)],
        scratch_shapes=[
            pltpu.VMEM(g0.shape, F32),
            pltpu.VMEM(im0.shape, F32),
            pltpu.SemaphoreType.DMA((2 * OUT_CUTS,)),
        ],
        compiler_params=params(16),
        cost_estimate=cost(3 * g0.size, 1e7),
        name="result",
    )(l0, *sums, g0, g1, im0, im1)


def over_core(x):
    return lax.ppermute(x, "space", [(i, i ^ 1) for i in range(GROUP)])


def over_y(x):
    return lax.ppermute(x, "space", [(i, i ^ 2) for i in range(GROUP)])


def over_z(x, k):
    return lax.ppermute(x, "space", [(i, (i + 4 * k) % GROUP) for i in range(GROUP)])


def scatter_sums(parts, sums=None):
    near, far_y, near_c, far_yc = parts
    got_yc = over_core(far_yc)
    got_c = over_core(near_c)
    first, second, *s = merge_y(far_y, got_yc, sums)
    first, second = over_y(first), over_y(second)
    two, one, *s = merge_z(False, near, got_c, first, s[0] if s else None)
    got = [over_z(two, 2), over_z(one, 1)]
    three, own = merge_z(True, near, got_c, second, s[0] if s else None)
    return own, got + [over_z(three, 3)], (s[0] if s else None)


def gather_columns(x, after):
    two, three, one = over_z(x, 2), over_z(x, 3), over_z(x, 1)
    y_own = over_y(x)
    c_own = over_core(x)
    rest = join([two, three, one], y_own, c_own, after)
    y_rest = over_y(rest)
    c_rest = over_core(rest)
    return [x, rest, y_own, y_rest, c_own, c_rest, over_core(y_own), over_core(y_rest)]


def sum_all(x):
    x = x + over_core(x)
    x = x + over_y(x)
    return [x] + [over_z(x, k) for k in range(1, STEPS)]


def on_device(ensemble, innovation, obs_weight, interp_weight, slot_of, intersection_list):
    members, columns, width = ensemble.shape
    levels = width // VAR
    devices = lax.axis_size("space")
    capacity = intersection_list.shape[2]
    slots = devices * capacity
    grouped = devices == GROUP and capacity == columns == LANES

    taper = vertical_taper(levels)
    both = taper.astype(np.float64) @ taper.T.astype(np.float64)
    kern = np.tile(np.concatenate(host_halves(both), axis=0), (2, VAR))
    tall = np.tile(np.concatenate(host_halves(taper), axis=0), (2, 1))
    none = np.zeros_like(tall)
    taps = np.stack(
        [np.concatenate([tall, none], axis=1), np.concatenate([none, tall], axis=1)]
    )
    kern, taps = jnp.asarray(kern), jnp.asarray(taps)

    index = lax.axis_index("space").astype(jnp.int32)
    me = jnp.stack([index // 4, index // 2 % 2, index % 2, index])
    w = -(obs_weight.astype(F32) * innovation.astype(F32))
    high = lax.reduce_precision(w, 8, 7)
    wh, wl = high.astype(BF), (w - high).astype(BF)
    named = jnp.concatenate([slot_of.astype(F32), interp_weight], axis=0)
    if grouped:
        lists = exchange_lists(me, intersection_list[0])
        scatter, gather, add_up = scatter_sums, gather_columns, sum_all
    else:
        lists = intersection_list[0]
        hit = (lists.reshape(-1, 1) == jnp.arange(columns, dtype=jnp.int32)).astype(BF)

        def swap(x):
            x = x.reshape(devices, capacity, width)
            x = lax.all_to_all(x, "space", split_axis=0, concat_axis=0, tiled=True)
            return x.reshape(slots, width)

        def scatter(parts, sums=None):
            got = swap(jnp.concatenate([p[: slots // 4] for p in parts], axis=0))
            high = lax.reduce_precision(got, 8, 7)
            high, low = high.astype(BF), (got - high).astype(BF)
            if sums is not None:
                sums = lax.psum(sums, "space")
            return dot(hit.T, high) + dot(hit.T, low), [], sums

        def gather(x, after):
            return [swap(dot(hit, x.T).astype(BF)).T]

        def add_up(x):
            return [lax.psum(x, "space")]

    ids, weight, far, c0, c1 = adjoint_half(slots, [named, wh, wl], (grouped, me, lists if grouped else []))
    near, n0, n1 = adjoint_half(slots, [ids, weight, wh, wl])
    own, got, _ = scatter([n0, n1, c0, c1])
    x0, y0, g_sums = coarse_image(ensemble, kern, own, got)
    ens = jnp.transpose(ensemble, (1, 0, 2))
    g0, token = project(ens, y0, taps)
    im0, sums, *second = image_first(gather(x0, token), near, far, obs_weight, g_sums)
    own, got, sums = scatter(second, sums)
    x1, y1, l0, g_sums = coarse_image(ensemble, kern, own, got, y0, sums)
    g1, token = project(ens, y1, taps)
    im1, sums = image_second(gather(x1, token), near, far, obs_weight, g_sums)
    return tuple(result(l0, add_up(sums), g0, g1, im0, im1))


def solution(mesh):
    placed = (
        P("case", "space", None),
        P(("case", "space"), None),
        P(("case", "space"), None),
        P("case", "space"),
        P("case", "space"),
        P(("case", "space"), None, None),
    )
    return jax.shard_map(
        on_device,
        mesh=mesh,
        in_specs=placed,
        out_specs=(P("case", "space"), P(("case", "space"), None)),
        check_vma=False,
    )
```

```python
import functools

import jax
import jax.numpy as jnp
import ml_dtypes
import numpy as np
from jax import lax
from jax.experimental import pallas as pl
from jax.experimental.pallas import tpu as pltpu
from jax.sharding import PartitionSpec as P

VAR = 4
LOC_SCALE = 3.0
BF = jnp.bfloat16
F32 = jnp.float32
LANES = 128
GROUP = 16
VMEM = pl.BlockSpec(memory_space=pltpu.VMEM)
SMEM = pl.BlockSpec(memory_space=pltpu.SMEM)
ANY = pl.BlockSpec(memory_space=pl.ANY)


def vertical_taper(levels):
    heights = np.arange(levels).astype(np.float32)
    spread = (heights[:, None] - heights[None, :]) / np.float32(LOC_SCALE)
    return np.exp(np.float32(-0.5) * spread * spread)


def host_halves(x):
    high = x.astype(ml_dtypes.bfloat16)
    return [high, (x - high.astype(x.dtype)).astype(ml_dtypes.bfloat16)]


def params(mib):
    return pltpu.CompilerParams(vmem_limit_bytes=mib << 20)


def cost(flops, nbytes):
    return pl.CostEstimate(flops=int(flops), bytes_accessed=int(nbytes), transcendentals=0)


def dot(a, b):
    return jnp.dot(a, b, preferred_element_type=F32)


def halves(x):
    high = x.astype(BF)
    return high, (x - high.astype(F32)).astype(BF)


def shape(dims, dtype):
    return jax.ShapeDtypeStruct(dims, dtype)


STEPS = 4
CHIPS = GROUP // 2
ORDER = (2, 1, 3, 0)
PARTS = ((0, 0), (1, 0), (0, 1), (1, 1))
HEAD = 16
TOP = 32512.0


def owner_at(me_ref, i):
    dy, dc = PARTS[i // STEPS]
    z, y, c = me_ref[0], me_ref[1], me_ref[2]
    y = y if dy == 0 else 1 - y
    c = c if dc == 0 else 1 - c
    return (lax.rem(z + ORDER[i % STEPS], STEPS) * 2 + y) * 2 + c


def places(me_ref, lists_ref, slots):
    slots = jnp.concatenate([slots, slots], axis=0)
    from_owner = jnp.right_shift(slots, 7)
    within = jnp.bitwise_and(slots, LANES - 1)
    rows = jnp.zeros(slots.shape, jnp.int32)
    for i in range(GROUP):
        o = owner_at(me_ref, i)
        dc = PARTS[i // STEPS][1]
        row = jnp.broadcast_to(lists_ref[jnp.right_shift(o, 1), dc : dc + 1, :], slots.shape)
        column = jnp.take_along_axis(row, within, axis=1, mode="promise_in_bounds")
        rows = jnp.where(from_owner == o, column + i * LANES, rows)
    return rows[: slots.shape[0] // 2]


def build_rows(ids_ref, weight_ref, wh_ref, wl_ref, at_ref, y_refs, lo_s, base):
    sources, fine = ids_ref.shape
    rows = at_ref.shape[0] // len(y_refs)
    step = rows // 2
    row = lax.broadcasted_iota(jnp.int32, (step, LANES), 0)
    for n, y_ref in enumerate(y_refs):
        for m in range(2):
            start = n * rows + m * step
            for j in range(fine // LANES):
                lanes = pl.ds(j * LANES, LANES)
                total = None
                for b in range(sources):
                    ids = ids_ref[b : b + 1, lanes] - (base + start)
                    term = jnp.where(row == ids, weight_ref[b : b + 1, lanes], 0.0)
                    total = term if total is None else total + term
                high, low = halves(total)
                at_ref[pl.ds(start, step), lanes] = high
                lo_s[pl.ds(m * step, step), lanes] = low
        held = at_ref[pl.ds(n * rows, rows), :]
        y_ref[...] = dot(held, wh_ref[...]) + dot(held, wl_ref[...]) + dot(lo_s[...], wh_ref[...])


def far_kernel(grouped, me_ref, *refs):
    lists_ref, refs = (refs[0], refs[1:]) if grouped else (None, refs)
    both_ref, wh_ref, wl_ref, *refs = refs
    ids_ref, weight_ref, at_ref, ya_ref, yb_ref, lo_s = refs
    sources = ids_ref.shape[0]
    for j in range(ids_ref.shape[1] // LANES):
        lanes = pl.ds(j * LANES, LANES)
        slots = both_ref[:sources, lanes].astype(jnp.int32)
        ids_ref[:, lanes] = places(me_ref, lists_ref, slots) if grouped else slots
        weight_ref[:, lanes] = both_ref[sources:, lanes]
    half = at_ref.shape[0]
    build_rows(ids_ref, weight_ref, wh_ref, wl_ref, at_ref, [ya_ref, yb_ref], lo_s, half)


def near_kernel(ids_ref, weight_ref, wh_ref, wl_ref, at_ref, ya_ref, yb_ref, lo_s):
    build_rows(ids_ref, weight_ref, wh_ref, wl_ref, at_ref, [ya_ref, yb_ref], lo_s, 0)


def adjoint_half(slots, args, head=None):
    fine, width = args[-1].shape
    half = slots // 2
    sources = args[0].shape[0] // (2 if head else 1)
    out = [shape((half, fine), BF)] + [shape((half // 2, width), F32)] * 2
    if head:
        grouped, me, lists = head
        kernel = functools.partial(far_kernel, grouped)
        args = [me, *lists, *args]
        out = [shape((sources, fine), jnp.int32), shape((sources, fine), F32)] + out
    else:
        kernel = near_kernel
    return pl.pallas_call(
        kernel,
        in_specs=([SMEM] if head else []) + [VMEM] * (len(args) - (1 if head else 0)),
        out_specs=[VMEM] * len(out),
        out_shape=out,
        scratch_shapes=[pltpu.VMEM((half // 2, fine), BF)],
        compiler_params=params(16),
        cost_estimate=cost(3 * slots * fine * width, 4e6),
        name="adjoint_far" if head else "adjoint_near",
    )(*args)


def pick_kernel(me_ref, lists_ref, near_ref, far_ref):
    c = me_ref[2]
    for chip in range(CHIPS):
        row = slice(chip, chip + 1)
        near_ref[row, :] = lists_ref[pl.ds(2 * chip + c, 1), :]
        far_ref[row, :] = lists_ref[pl.ds(2 * chip + 1 - c, 1), :]


def mix_kernel(near_ref, got_ref, out_ref):
    out_ref[...] = jnp.zeros_like(out_ref)
    for chip in range(CHIPS):
        for i, held in enumerate((near_ref, got_ref)):
            out_ref[chip, i : i + 1, :] = held[chip : chip + 1, :]


def spread_kernel(a_ref, b_ref, out_ref):
    total = a_ref[...] + b_ref[...]
    for chip in range(CHIPS):
        out_ref[chip] = total


def small(kernel, out, name, *args, scalars=0):
    return pl.pallas_call(
        kernel,
        in_specs=[SMEM] * scalars + [VMEM] * (len(args) - scalars),
        out_specs=[VMEM] * len(out),
        out_shape=out,
        compiler_params=params(8),
        cost_estimate=cost(1e4, 3e4),
        name=name,
    )(*args)


def over_chips(x):
    groups = [list(range(c, GROUP, 2)) for c in range(2)]
    return lax.all_to_all(
        x, "space", split_axis=0, concat_axis=0, axis_index_groups=groups, tiled=True
    )


def exchange_lists(me, lists):
    one = shape((CHIPS, LANES), jnp.int32)
    near, far = small(pick_kernel, [one, one], "pick", me, lists, scalars=1)
    out = shape((CHIPS, 8, LANES), jnp.int32)
    (both,) = small(mix_kernel, [out], "mix", near, over_core(far))
    return [over_chips(both)]


def exponent(m):
    return jnp.clip(jnp.ceil(jnp.log2(jnp.maximum(m, 1e-30))), -100.0, 100.0)


def whole16(x):
    return x.astype(jnp.int32).astype(jnp.int16)


def wide(x):
    return x.astype(jnp.int32).astype(F32)


def pack(out_ref, t, sums=None):
    rows, width = t.shape
    e = exponent(jnp.max(jnp.abs(t), axis=0, keepdims=True))
    out_ref[pl.ds(0, rows), :] = whole16(jnp.round(t * (jnp.exp2(-e) * TOP)))
    head = [e]
    if sums is not None:
        for i in range(2):
            v = sums[i : i + 1, :]
            f = exponent(v)
            v = v * (jnp.exp2(-f) * 16384.0)
            first = jnp.floor(v)
            head += [f, first, jnp.floor((v - first) * 16384.0)]
    row = lax.broadcasted_iota(jnp.int32, (HEAD, width), 0)
    total = jnp.zeros((HEAD, width), F32)
    for i, h in enumerate(head):
        total = jnp.where(row == i, h, total)
    out_ref[pl.ds(rows, HEAD), :] = whole16(total)


def unpack(ref):
    rows = ref.shape[0] - HEAD
    head = wide(ref[pl.ds(rows, HEAD), :])
    return wide(ref[pl.ds(0, rows), :]) * (jnp.exp2(head[0:1, :]) * (1.0 / TOP))


def unpack_sums(ref):
    head = wide(ref[pl.ds(ref.shape[0] - HEAD, HEAD), :])
    row = lax.broadcasted_iota(jnp.int32, (8, head.shape[1]), 0)
    total = jnp.zeros(row.shape, F32)
    for i in range(2):
        f, first, second = [head[1 + 3 * i + j : 2 + 3 * i + j, :] for j in range(3)]
        v = (first + second * (1.0 / 16384.0)) * (jnp.exp2(f) * (1.0 / 16384.0))
        total = jnp.where(row == i, v, total)
    return total


def merge_y_kernel(with_sums, *refs):
    if with_sums:
        a_ref, b_ref, mine_ref, first_ref, second_ref, s_ref = refs
        sums = mine_ref[...] + b_ref[pl.ds(a_ref.shape[0], 8), :]
        s_ref[...] = sums
    else:
        a_ref, b_ref, first_ref, second_ref = refs
        sums = None
    half = a_ref.shape[0] // 2
    pack(first_ref, a_ref[pl.ds(0, half), :] + b_ref[pl.ds(0, half), :], sums)
    pack(second_ref, a_ref[pl.ds(half, half), :] + b_ref[pl.ds(half, half), :])


def merge_y(a, b, sums):
    rows, width = a.shape
    out = [shape((rows // 2 + HEAD, width), jnp.int16)] * 2
    args = [a, b]
    if sums is not None:
        out.append(shape((8, width), F32))
        args.append(sums)
    return pl.pallas_call(
        functools.partial(merge_y_kernel, sums is not None),
        in_specs=[VMEM] * len(args),
        out_specs=[VMEM] * len(out),
        out_shape=out,
        compiler_params=params(8),
        cost_estimate=cost(5 * rows * width, 1e6),
        name="merge_y",
    )(*args)


def merge_z_kernel(last, with_sums, a_ref, b_ref, p_ref, *refs):
    half = a_ref.shape[0] // 2
    rows = pl.ds(half if last else 0, half)
    t = a_ref[rows, :] + b_ref[rows, :] + unpack(p_ref)
    sums = None
    if with_sums:
        sums = refs[0][...]
        refs = refs[1:]
        if not last:
            sums = sums + unpack_sums(p_ref)
            refs[2][...] = sums
    pack(refs[0], t[:LANES], sums)
    if last:
        refs[1][...] = t[LANES:]
    else:
        pack(refs[1], t[LANES:], sums)


def merge_z(last, a, b, p, sums):
    width = a.shape[1]
    sent = shape((LANES + HEAD, width), jnp.int16)
    out = [sent, shape((LANES, width), F32) if last else sent]
    args = [a, b, p]
    if sums is not None:
        args.append(sums)
        if not last:
            out.append(shape((8, width), F32))
    return pl.pallas_call(
        functools.partial(merge_z_kernel, last, sums is not None),
        in_specs=[VMEM] * len(args),
        out_specs=[VMEM] * len(out),
        out_shape=out,
        compiler_params=params(8),
        cost_estimate=cost(5 * a.size, 1e6),
        name="merge_z_last" if last else "merge_z_first",
    )(*args)


def join_kernel(*refs):
    out_ref = refs[-1]
    for i, r in enumerate(refs[:3]):
        out_ref[i] = r[...]


def join(blocks, *after):
    return pl.pallas_call(
        join_kernel,
        in_specs=[VMEM] * (3 + len(after)),
        out_specs=VMEM,
        out_shape=shape((3,) + blocks[0].shape, BF),
        compiler_params=params(8),
        cost_estimate=cost(1e5, 4e5),
        name="join",
    )(*blocks, *after)


def fold(a):
    return jnp.sum(a, axis=0, keepdims=True)


def length_of(sums):
    grad = jnp.sum(sums[0:1, :], axis=1, keepdims=True)
    image = jnp.sum(sums[1:2, :], axis=1, keepdims=True)
    return grad / (grad + image), image / (grad + image)


def products(e, y, held, rows):
    p = e.astype(F32) * y
    q = p[:, :LANES] + p[:, LANES:]
    q = q + pltpu.roll(q, LANES // 2, 1)
    high, low = halves(q)
    held[rows, :LANES] = high
    held[rows, LANES:] = low


BATCH = 16
SOME = 8


def coarse_kernel(packed, second, e_ref, k_ref, own_ref, *refs):
    refs = list(refs)
    got = [refs.pop(0) for _ in range(packed)]
    y = own_ref[...]
    for r in got:
        y = y + unpack(r)
    if second:
        y0_ref, s_ref = refs.pop(0), refs.pop(0)
        sums = s_ref[...]
        for r in got:
            sums = sums + unpack_sums(r)
        l0, keep = length_of(sums)
        y = keep * y0_ref[...] - l0 * y
        refs.pop(2)[...] = jnp.broadcast_to(l0, (8, LANES))
    x_ref, y_ref, sum_ref, even_s, odd_s, x_s = refs
    members, columns, width = e_ref.shape
    y_ref[...] = y
    x_s[...] = jnp.zeros_like(x_s)

    def build(i, held):
        for m in range(SOME):
            products(e_ref[i * SOME + m], y_ref[...], held, pl.ds(m * columns, columns))

    def add_in(i, t):
        total = x_s[...]
        for m in range(SOME):
            total = total + t[m * columns : (m + 1) * columns] * e_ref[i * SOME + m].astype(F32)
        x_s[...] = total

    pairs = members // SOME // 2
    build(0, even_s)

    @pl.loop(0, pairs - 1)
    def _(i):
        t = dot(even_s[...], k_ref[...])
        build(2 * i + 1, odd_s)
        add_in(2 * i, t)
        t = dot(odd_s[...], k_ref[...])
        build(2 * i + 2, even_s)
        add_in(2 * i + 1, t)

    t = dot(even_s[...], k_ref[...])
    build(2 * pairs - 1, odd_s)
    add_in(2 * pairs - 2, t)
    add_in(2 * pairs - 1, dot(odd_s[...], k_ref[...]))

    x = x_s[...]
    x_ref[...] = x.T.astype(BF)
    sum_ref[...] = jnp.zeros_like(sum_ref)
    sum_ref[0:1, :] = fold(x * y_ref[...])


def coarse_image(ensemble, kern, own, got, y0=None, sums=None):
    members, columns, width = ensemble.shape
    second = y0 is not None
    args = [ensemble, kern, own, *got] + ([y0, sums] if second else [])
    out = [shape((width, columns), BF), shape((columns, width), F32)]
    out += [shape((8, LANES), F32)] if second else []
    out += [shape((8, width), F32)]
    return pl.pallas_call(
        functools.partial(coarse_kernel, len(got), second),
        in_specs=[VMEM] * len(args),
        out_specs=[VMEM] * len(out),
        out_shape=out,
        scratch_shapes=[
            pltpu.VMEM((SOME * columns, width), BF),
            pltpu.VMEM((SOME * columns, width), BF),
            pltpu.VMEM((columns, width), F32),
        ],
        compiler_params=params(16),
        cost_estimate=cost(2 * columns * members * width * width, 5e6),
        name="coarse_second" if second else "coarse_first",
    )(*args)


def project_kernel(e_ref, y_ref, t_ref, after_ref, g_ref, token_ref, even_s, odd_s):
    columns, members, width = e_ref.shape
    lanes = BATCH // 2 * LANES
    token_ref[...] = jnp.zeros_like(token_ref)

    @pl.loop(0, columns // BATCH)
    def _(i):
        base = pl.multiple_of(i * BATCH, BATCH)
        yb = y_ref[pl.ds(base, BATCH), :]
        for c in range(BATCH):
            held = odd_s if c % 2 else even_s
            rows = pl.ds((c // 2) * members, members)
            products(e_ref[base + c], yb[c : c + 1, :], held, rows)
        r = dot(even_s[...], t_ref[0]) + dot(odd_s[...], t_ref[1])
        for pair in range(BATCH // 2):
            at = pl.multiple_of(i * lanes + pair * LANES, LANES)
            g_ref[:, pl.ds(at, LANES)] = r[pair * members : (pair + 1) * members]


def project(ens, y, taps, after):
    columns, members, width = ens.shape
    levels = width // VAR
    return pl.pallas_call(
        project_kernel,
        in_specs=[VMEM] * 4,
        out_specs=[VMEM] * 2,
        out_shape=[shape((members, columns * levels), F32), shape((8, LANES), F32)],
        scratch_shapes=[pltpu.VMEM((BATCH // 2 * members, width), BF)] * 2,
        compiler_params=params(16),
        cost_estimate=cost(2 * columns * members * width * width, 8e6),
        name="project",
    )(ens, y, taps, after)


def lay_out(x_refs, xs):
    if len(x_refs) == 1:
        xs[...] = x_refs[0][...]
        return
    own, rest = x_refs[0::2], x_refs[1::2]
    for part in range(STEPS):
        at = part * STEPS * LANES
        for i in range(STEPS - 1):
            xs[:, pl.ds(at + i * LANES, LANES)] = rest[part][i]
        xs[:, pl.ds(at + (STEPS - 1) * LANES, LANES)] = own[part][...]


CUTS = 3


def images(x_refs, near_ref, far_ref, obs_ref, im_ref, xs):
    lay_out(x_refs, xs)
    half, fine = near_ref.shape
    rows = fine // CUTS
    for i in range(CUTS):
        some = pl.ds(i * rows, rows)
        turned = dot(xs[:, :half], near_ref[:, some]) + dot(xs[:, half:], far_ref[:, some])
        im = turned.T
        im_ref[some, :] = im
        yield some, im, obs_ref[some, :].astype(F32) * im


def image_kernel(count, *refs):
    x_refs, refs = refs[:count], refs[count:]
    near_ref, far_ref, obs_ref, g_ref, im_ref, sum_ref = refs[:6]
    outs, (xs, v_s) = refs[6:10], refs[10:]
    sums = g_ref[...]
    row = lax.broadcasted_iota(jnp.int32, sums.shape, 0)
    for some, im, v in images(x_refs, near_ref, far_ref, obs_ref, im_ref, xs):
        v_s[some, :] = v.astype(BF)
        sums = sums + jnp.where(row == 1, fold(v * im), 0.0)
    sum_ref[...] = sums
    rows = near_ref.shape[0] // 2
    for i, out in enumerate(outs):
        at_ref = far_ref if i > 1 else near_ref
        out[pl.ds(0, rows), :] = dot(at_ref[pl.ds(i % 2 * rows, rows), :], v_s[...])
    outs[3][pl.ds(rows, 8), :] = sums


def image_first(xs, near, far, obs, g_sums):
    half, fine = near.shape
    width = obs.shape[1]
    z_rows = [half // 2] * 3 + [half // 2 + 8]
    return pl.pallas_call(
        functools.partial(image_kernel, len(xs)),
        in_specs=[VMEM] * (len(xs) + 4),
        out_specs=[VMEM] * 6,
        out_shape=[shape((fine, width), F32), shape((8, width), F32)]
        + [shape((r, width), F32) for r in z_rows],
        scratch_shapes=[pltpu.VMEM((width, 2 * half), BF), pltpu.VMEM((fine, width), BF)],
        compiler_params=params(16),
        cost_estimate=cost(8 * half * fine * width, 13e6),
        name="image_first",
    )(*xs, near, far, obs, g_sums)


def second_kernel(count, *refs):
    x_refs, refs = refs[:count], refs[count:]
    near_ref, far_ref, obs_ref, g_ref, im_ref, sum_ref, xs = refs
    sums = g_ref[...]
    row = lax.broadcasted_iota(jnp.int32, sums.shape, 0)
    for _, im, v in images(x_refs, near_ref, far_ref, obs_ref, im_ref, xs):
        sums = sums + jnp.where(row == 1, fold(v * im), 0.0)
    sum_ref[...] = sums


def image_second(xs, near, far, obs, g_sums):
    half, fine = near.shape
    width = obs.shape[1]
    return pl.pallas_call(
        functools.partial(second_kernel, len(xs)),
        in_specs=[VMEM] * (len(xs) + 4),
        out_specs=[VMEM] * 2,
        out_shape=[shape((fine, width), F32), shape((8, width), F32)],
        scratch_shapes=[pltpu.VMEM((width, 2 * half), BF)],
        compiler_params=params(16),
        cost_estimate=cost(4 * half * fine * width, 8e6),
        name="image_second",
    )(*xs, near, far, obs, g_sums)


OUT_CUTS = 4


def result_kernel(l0_ref, sums_ref, *refs):
    sums = sums_ref[0]
    for i in range(1, sums_ref.shape[0]):
        sums = sums + sums_ref[i]
    g0_ref, g1_ref, i0_ref, i1_ref, control_hbm, increment_hbm, c_s, i_s, sem = refs
    l0 = -l0_ref[0:1, 0:1]
    l1, _ = length_of(sums)
    lanes = c_s.shape[1] // OUT_CUTS
    rows = i_s.shape[0] // OUT_CUTS
    copies = []
    for i in range(OUT_CUTS):
        some = pl.ds(i * lanes, lanes)
        c_s[:, some] = l0 * g0_ref[:, some] - l1 * g1_ref[:, some]
        copies.append(
            pltpu.make_async_copy(c_s.at[:, some], control_hbm.at[:, some], sem.at[2 * i])
        )
        copies[-1].start()
        some = pl.ds(i * rows, rows)
        i_s[some, :] = l0 * i0_ref[some, :] - l1 * i1_ref[some, :]
        copies.append(
            pltpu.make_async_copy(i_s.at[some, :], increment_hbm.at[some, :], sem.at[2 * i + 1])
        )
        copies[-1].start()
    for copy in copies:
        copy.wait()


def result(l0, sums, g0, g1, im0, im1):
    return pl.pallas_call(
        result_kernel,
        in_specs=[VMEM] * 6,
        out_specs=[ANY] * 2,
        out_shape=[shape(g0.shape, F32), shape(im0.shape, F32)],
        scratch_shapes=[
            pltpu.VMEM(g0.shape, F32),
            pltpu.VMEM(im0.shape, F32),
            pltpu.SemaphoreType.DMA((2 * OUT_CUTS,)),
        ],
        compiler_params=params(16),
        cost_estimate=cost(3 * g0.size, 1e7),
        name="result",
    )(l0, sums, g0, g1, im0, im1)


def over_core(x):
    return lax.ppermute(x, "space", [(i, i ^ 1) for i in range(GROUP)])


def over_y(x):
    return lax.ppermute(x, "space", [(i, i ^ 2) for i in range(GROUP)])


def over_z(x, k):
    return lax.ppermute(x, "space", [(i, (i + 4 * k) % GROUP) for i in range(GROUP)])


def scatter_sums(parts, sums=None):
    near, far_y, near_c, far_yc = parts
    got_yc = over_core(far_yc)
    got_c = over_core(near_c)
    first, second, *s = merge_y(far_y, got_yc, sums)
    first, second = over_y(first), over_y(second)
    two, one, *s = merge_z(False, near, got_c, first, s[0] if s else None)
    got = [over_z(two, 2), over_z(one, 1)]
    three, own = merge_z(True, near, got_c, second, s[0] if s else None)
    return own, got + [over_z(three, 3)], (s[0] if s else None)


def relay_kernel(x_ref, after_ref, out_ref):
    out_ref[...] = x_ref[...]


def gather_columns(x, work):
    two, three, one = over_z(x, 2), over_z(x, 3), over_z(x, 1)
    y_own = over_y(x)
    c_own = over_core(x)
    rest = join([two, three, one], y_own, c_own)
    y_rest = over_y(rest)
    c_rest = over_core(rest)
    cy_own = over_core(y_own)
    done, token = work(rest)
    (y_rest,) = small(relay_kernel, [shape(rest.shape, BF)], "relay", y_rest, token)
    return [x, rest, y_own, y_rest, c_own, c_rest, cy_own, over_core(y_rest)], done


def sum_all(x):
    out = shape((CHIPS,) + x.shape, F32)
    (both,) = small(spread_kernel, [out], "spread", x, over_core(x))
    return over_chips(both)


def on_device(ensemble, innovation, obs_weight, interp_weight, slot_of, intersection_list):
    members, columns, width = ensemble.shape
    levels = width // VAR
    devices = lax.axis_size("space")
    capacity = intersection_list.shape[2]
    slots = devices * capacity
    grouped = devices == GROUP and capacity == columns == LANES

    taper = vertical_taper(levels)
    both = taper.astype(np.float64) @ taper.T.astype(np.float64)
    kern = np.tile(np.concatenate(host_halves(both), axis=0), (2, VAR))
    tall = np.tile(np.concatenate(host_halves(taper), axis=0), (2, 1))
    none = np.zeros_like(tall)
    taps = np.stack(
        [np.concatenate([tall, none], axis=1), np.concatenate([none, tall], axis=1)]
    )
    kern, taps = jnp.asarray(kern), jnp.asarray(taps)

    index = lax.axis_index("space").astype(jnp.int32)
    me = jnp.stack([index // 4, index // 2 % 2, index % 2, index])
    w = -(obs_weight.astype(F32) * innovation.astype(F32))
    high = lax.reduce_precision(w, 8, 7)
    wh, wl = high.astype(BF), (w - high).astype(BF)
    named = jnp.concatenate([slot_of.astype(F32), interp_weight], axis=0)
    if grouped:
        lists = exchange_lists(me, intersection_list[0])
        scatter, gather, add_up = scatter_sums, gather_columns, sum_all
    else:
        lists = intersection_list[0]
        hit = (lists.reshape(-1, 1) == jnp.arange(columns, dtype=jnp.int32)).astype(BF)

        def swap(x):
            x = x.reshape(devices, capacity, width)
            x = lax.all_to_all(x, "space", split_axis=0, concat_axis=0, tiled=True)
            return x.reshape(slots, width)

        def scatter(parts, sums=None):
            got = swap(jnp.concatenate([p[: slots // 4] for p in parts], axis=0))
            high = lax.reduce_precision(got, 8, 7)
            high, low = high.astype(BF), (got - high).astype(BF)
            if sums is not None:
                sums = lax.psum(sums, "space")
            return dot(hit.T, high) + dot(hit.T, low), [], sums

        def gather(x, work):
            return [swap(dot(hit, x.T).astype(BF)).T], work(x)[0]

        def add_up(x):
            return lax.psum(x, "space")[None]

    ids, weight, far, c0, c1 = adjoint_half(slots, [named, wh, wl], (grouped, me, lists if grouped else []))
    near, n0, n1 = adjoint_half(slots, [ids, weight, wh, wl])
    own, got, _ = scatter([n0, n1, c0, c1])
    x0, y0, g_sums = coarse_image(ensemble, kern, own, got)
    ens = jnp.transpose(ensemble, (1, 0, 2))
    xs, g0 = gather(x0, lambda after: project(ens, y0, taps, after))
    im0, sums, *second = image_first(xs, near, far, obs_weight, g_sums)
    own, got, sums = scatter(second, sums)
    x1, y1, l0, g_sums = coarse_image(ensemble, kern, own, got, y0, sums)
    xs, g1 = gather(x1, lambda after: project(ens, y1, taps, after))
    im1, sums = image_second(xs, near, far, obs_weight, g_sums)
    return tuple(result(l0, add_up(sums), g0, g1, im0, im1))


def solution(mesh):
    placed = (
        P("case", "space", None),
        P(("case", "space"), None),
        P(("case", "space"), None),
        P("case", "space"),
        P("case", "space"),
        P(("case", "space"), None, None),
    )
    return jax.shard_map(
        on_device,
        mesh=mesh,
        in_specs=placed,
        out_specs=(P("case", "space"), P(("case", "space"), None)),
        check_vma=False,
    )
```

```python
import functools

import jax
import jax.numpy as jnp
import ml_dtypes
import numpy as np
from jax import lax
from jax.experimental import pallas as pl
from jax.experimental.pallas import tpu as pltpu
from jax.sharding import PartitionSpec as P

VAR = 4
LOC_SCALE = 3.0
BF = jnp.bfloat16
F32 = jnp.float32
LANES = 128
GROUP = 16
VMEM = pl.BlockSpec(memory_space=pltpu.VMEM)
SMEM = pl.BlockSpec(memory_space=pltpu.SMEM)
ANY = pl.BlockSpec(memory_space=pl.ANY)


def vertical_taper(levels):
    heights = np.arange(levels).astype(np.float32)
    spread = (heights[:, None] - heights[None, :]) / np.float32(LOC_SCALE)
    return np.exp(np.float32(-0.5) * spread * spread)


def host_halves(x):
    high = x.astype(ml_dtypes.bfloat16)
    return [high, (x - high.astype(x.dtype)).astype(ml_dtypes.bfloat16)]


def params(mib):
    return pltpu.CompilerParams(vmem_limit_bytes=mib << 20)


def cost(flops, nbytes):
    return pl.CostEstimate(flops=int(flops), bytes_accessed=int(nbytes), transcendentals=0)


def dot(a, b):
    return jnp.dot(a, b, preferred_element_type=F32)


def halves(x):
    high = x.astype(BF)
    return high, (x - high.astype(F32)).astype(BF)


def shape(dims, dtype):
    return jax.ShapeDtypeStruct(dims, dtype)


STEPS = 4
ORDER = (1, 3, 0, 2)
PARTS = ((0, 0), (1, 0), (0, 1), (1, 1))
HEAD = 16
TOP = 32512.0


def owner_at(me_ref, i):
    dy, dc = PARTS[i // STEPS]
    z, y, c = me_ref[0], me_ref[1], me_ref[2]
    y = y if dy == 0 else 1 - y
    c = c if dc == 0 else 1 - c
    return (jnp.bitwise_xor(z, ORDER[i % STEPS]) * 2 + y) * 2 + c


def places(me_ref, list_refs, slots):
    slots = jnp.concatenate([slots, slots], axis=0)
    from_owner = jnp.right_shift(slots, 7)
    within = jnp.bitwise_and(slots, LANES - 1)
    rows = jnp.zeros(slots.shape, jnp.int32)
    for i in range(GROUP):
        o = owner_at(me_ref, i)
        dy, dc = PARTS[i // STEPS]
        k = ORDER[i % STEPS]
        row = k % 2 * STEPS + 2 * dy + dc
        row = jnp.broadcast_to(list_refs[k // 2][row : row + 1, :], slots.shape)
        column = jnp.take_along_axis(row, within, axis=1, mode="promise_in_bounds")
        rows = jnp.where(from_owner == o, column + i * LANES, rows)
    return rows[: slots.shape[0] // 2]


PIECES = 4


def build_rows(ids_ref, weight_ref, wh_ref, wl_ref, at_ref, y_refs, held, base):
    sources, fine = ids_ref.shape
    rows = at_ref.shape[0] // PIECES
    row = lax.broadcasted_iota(jnp.int32, (rows, LANES), 0)

    def build(n):
        high_s, low_s = held[2 * (n % 2) : 2 * (n % 2) + 2]
        for j in range(fine // LANES):
            lanes = pl.ds(j * LANES, LANES)
            total = None
            for b in range(sources):
                ids = ids_ref[b : b + 1, lanes] - (base + n * rows)
                term = jnp.where(row == ids, weight_ref[b : b + 1, lanes], 0.0)
                total = term if total is None else total + term
            high, low = halves(total)
            at_ref[pl.ds(n * rows, rows), lanes] = high
            high_s[:, lanes] = high
            low_s[:, lanes] = low

    build(0)
    for n in range(PIECES):
        high_s, low_s = held[2 * (n % 2) : 2 * (n % 2) + 2]
        y = dot(high_s[...], wh_ref[...]) + dot(high_s[...], wl_ref[...])
        y = y + dot(low_s[...], wh_ref[...])
        if n + 1 < PIECES:
            build(n + 1)
        y_refs[n // 2][pl.ds(n % 2 * rows, rows), :] = y


def far_kernel(grouped, me_ref, *refs):
    list_refs, refs = refs[: 2 * grouped], refs[2 * grouped :]
    both_ref, wh_ref, wl_ref, *refs = refs
    ids_ref, weight_ref, at_ref, ya_ref, yb_ref, *held = refs
    sources = ids_ref.shape[0]
    for j in range(ids_ref.shape[1] // LANES):
        lanes = pl.ds(j * LANES, LANES)
        slots = both_ref[:sources, lanes].astype(jnp.int32)
        ids_ref[:, lanes] = places(me_ref, list_refs, slots) if grouped else slots
        weight_ref[:, lanes] = both_ref[sources:, lanes]
    half = at_ref.shape[0]
    build_rows(ids_ref, weight_ref, wh_ref, wl_ref, at_ref, [ya_ref, yb_ref], held, half)


def near_kernel(ids_ref, weight_ref, wh_ref, wl_ref, at_ref, ya_ref, yb_ref, *held):
    build_rows(ids_ref, weight_ref, wh_ref, wl_ref, at_ref, [ya_ref, yb_ref], held, 0)


def adjoint_half(slots, args, head=None):
    fine, width = args[-1].shape
    half = slots // 2
    sources = args[0].shape[0] // (2 if head else 1)
    out = [shape((half, fine), BF)] + [shape((half // 2, width), F32)] * 2
    if head:
        grouped, me, lists = head
        kernel = functools.partial(far_kernel, grouped)
        args = [me, *lists, *args]
        out = [shape((sources, fine), jnp.int32), shape((sources, fine), F32)] + out
    else:
        kernel = near_kernel
    return pl.pallas_call(
        kernel,
        in_specs=([SMEM] if head else []) + [VMEM] * (len(args) - (1 if head else 0)),
        out_specs=[VMEM] * len(out),
        out_shape=out,
        scratch_shapes=[pltpu.VMEM((half // PIECES, fine), BF)] * 4,
        compiler_params=params(16),
        cost_estimate=cost(3 * slots * fine * width, 4e6),
        name="adjoint_far" if head else "adjoint_near",
    )(*args)


def pick_kernel(me_ref, lists_ref, near_ref, far_ref):
    z, y, c = me_ref[0], me_ref[1], me_ref[2]
    for dy in range(2):
        for p, k in enumerate(ORDER):
            there = (jnp.bitwise_xor(z, k) * 2 + (y if dy == 0 else 1 - y)) * 2
            row = slice(dy * STEPS + p, dy * STEPS + p + 1)
            near_ref[row, :] = lists_ref[pl.ds(there + c, 1), :]
            far_ref[row, :] = lists_ref[pl.ds(there + 1 - c, 1), :]


def mix_y_kernel(near_ref, got_ref, near_y_ref, far_y_ref):
    for i, held in enumerate((near_ref, got_ref)):
        rows = slice(i * STEPS, (i + 1) * STEPS)
        near_y_ref[rows, :] = held[:STEPS, :]
        far_y_ref[rows, :] = held[STEPS:, :]


def mix_z_kernel(near_ref, got_ref, near_z_ref, far_z_ref):
    for i, held in enumerate((near_ref, got_ref)):
        for c in range(2):
            rows = slice(4 * i + 2 * c, 4 * i + 2 * c + 2)
            far_z_ref[rows, :] = held[c * STEPS : c * STEPS + 2, :]
            near_z_ref[rows, :] = held[c * STEPS + 2 : c * STEPS + 4, :]


def mix_end_kernel(near_ref, got_ref, own_ref, sent_ref):
    for i, held in enumerate((near_ref, got_ref)):
        for n in range(STEPS):
            row = slice(i * STEPS + n, i * STEPS + n + 1)
            own_ref[row, :] = held[2 * n : 2 * n + 1, :]
            sent_ref[row, :] = held[2 * n + 1 : 2 * n + 2, :]


def small(kernel, n, name, *args, scalars=0):
    return pl.pallas_call(
        kernel,
        in_specs=[SMEM] * scalars + [VMEM] * (len(args) - scalars),
        out_specs=[VMEM] * n,
        out_shape=[shape((8, LANES), jnp.int32)] * n,
        compiler_params=params(8),
        cost_estimate=cost(1e4, 3e4),
        name=name,
    )(*args)


def exchange_lists(me, lists):
    near, far = small(pick_kernel, 2, "pick", me, lists, scalars=1)
    near, far = small(mix_y_kernel, 2, "mix_y", near, over_core(far))
    near, far = small(mix_z_kernel, 2, "mix_z", near, over_y(far))
    own, sent = small(mix_end_kernel, 2, "mix_end", near, over_z(far, 1))
    return [own, over_z(sent, 2)]


def exponent(m):
    return jnp.clip(jnp.ceil(jnp.log2(jnp.maximum(m, 1e-30))), -100.0, 100.0)


def whole16(x):
    return x.astype(jnp.int32).astype(jnp.int16)


def wide(x):
    return x.astype(jnp.int32).astype(F32)


def pack(out_ref, t, sums=None):
    rows, width = t.shape
    e = exponent(jnp.max(jnp.abs(t), axis=0, keepdims=True))
    out_ref[pl.ds(0, rows), :] = whole16(jnp.round(t * (jnp.exp2(-e) * TOP)))
    head = [e]
    if sums is not None:
        for i in range(2):
            v = sums[i : i + 1, :]
            f = exponent(v)
            v = v * (jnp.exp2(-f) * 16384.0)
            first = jnp.floor(v)
            head += [f, first, jnp.floor((v - first) * 16384.0)]
    row = lax.broadcasted_iota(jnp.int32, (HEAD, width), 0)
    total = jnp.zeros((HEAD, width), F32)
    for i, h in enumerate(head):
        total = jnp.where(row == i, h, total)
    out_ref[pl.ds(rows, HEAD), :] = whole16(total)


def unpack(ref):
    rows = ref.shape[0] - HEAD
    head = wide(ref[pl.ds(rows, HEAD), :])
    return wide(ref[pl.ds(0, rows), :]) * (jnp.exp2(head[0:1, :]) * (1.0 / TOP))


def unpack_sums(ref):
    head = wide(ref[pl.ds(ref.shape[0] - HEAD, HEAD), :])
    row = lax.broadcasted_iota(jnp.int32, (8, head.shape[1]), 0)
    total = jnp.zeros(row.shape, F32)
    for i in range(2):
        f, first, second = [head[1 + 3 * i + j : 2 + 3 * i + j, :] for j in range(3)]
        v = (first + second * (1.0 / 16384.0)) * (jnp.exp2(f) * (1.0 / 16384.0))
        total = jnp.where(row == i, v, total)
    return total


def half_of(ref, second):
    half = ref.shape[0] // 2 // LANES * LANES
    return ref[pl.ds(half if second else 0, half), :]


def merge_a_kernel(with_sums, a_ref, b_ref, *refs):
    sums = None
    if with_sums:
        sums = refs[0][...] + b_ref[pl.ds(a_ref.shape[0], 8), :]
        refs[2][...] = sums
    pack(refs[1 if with_sums else 0], half_of(a_ref, False) + half_of(b_ref, False), sums)


def merge_b_kernel(a_ref, b_ref, after_ref, out_ref):
    pack(out_ref, half_of(a_ref, True) + half_of(b_ref, True))


def merge_c_kernel(with_sums, a_ref, b_ref, p_ref, *refs):
    sums = None
    if with_sums:
        sums = refs[0][...] + unpack_sums(p_ref)
        refs[2][...] = sums
    t = half_of(a_ref, False) + half_of(b_ref, False) + unpack(p_ref)
    pack(refs[1 if with_sums else 0], t, sums)


def merge_d_kernel(with_sums, a_ref, b_ref, p_ref, q_ref, *refs):
    sums = None
    if with_sums:
        sums = refs[0][...] + unpack_sums(q_ref)
        refs[3][...] = sums
        refs = refs[1:]
    t = half_of(a_ref, True) + half_of(b_ref, True) + unpack(p_ref) + unpack(q_ref)
    refs[0][...] = t[:LANES]
    pack(refs[1], t[LANES:], sums)


def merge(kernel, name, out, *args, sums=None):
    if sums is not None:
        out = out + [shape(sums.shape, F32)]
        args = args + (sums,)
    return pl.pallas_call(
        kernel if kernel is merge_b_kernel else functools.partial(kernel, sums is not None),
        in_specs=[VMEM] * len(args),
        out_specs=[VMEM] * len(out),
        out_shape=out,
        compiler_params=params(8),
        cost_estimate=cost(5e5, 1e6),
        name=name,
    )(*args)


def join_kernel(a_ref, b_ref, out_ref):
    out_ref[0] = a_ref[...]
    out_ref[1] = b_ref[...]


def relay_kernel(x_ref, after_ref, out_ref):
    out_ref[...] = x_ref[...]


def pair_of(kernel, name, out, *args):
    return pl.pallas_call(
        kernel,
        in_specs=[VMEM] * len(args),
        out_specs=VMEM,
        out_shape=out,
        compiler_params=params(8),
        cost_estimate=cost(1e5, 4e5),
        name=name,
    )(*args)


def fold(a):
    return jnp.sum(a, axis=0, keepdims=True)


def length_of(sums):
    grad = jnp.sum(sums[0:1, :], axis=1, keepdims=True)
    image = jnp.sum(sums[1:2, :], axis=1, keepdims=True)
    return grad / (grad + image), image / (grad + image)


def products(e, y, held, rows):
    p = e.astype(F32) * y
    q = p[:, :LANES] + p[:, LANES:]
    q = q + pltpu.roll(q, LANES // 2, 1)
    high, low = halves(q)
    held[rows, :LANES] = high
    held[rows, LANES:] = low


BATCH = 16
SOME = 8


def coarse_kernel(packed, second, after, e_ref, k_ref, own_ref, *refs):
    refs = list(refs)
    got = [refs.pop(0) for _ in range(packed)]
    y = own_ref[...]
    for r in got:
        y = y + unpack(r)
    if second:
        y0_ref, s_ref = refs.pop(0), refs.pop(0)
        sums = s_ref[...]
        for r in got:
            sums = sums + unpack_sums(r)
        l0, keep = length_of(sums)
        y = keep * y0_ref[...] - l0 * y
        refs.pop(after + 2)[...] = jnp.broadcast_to(l0, (8, LANES))
    x_ref, y_ref, sum_ref, even_s, odd_s, x_s = refs[after:]
    members, columns, width = e_ref.shape
    y_ref[...] = y
    x_s[...] = jnp.zeros_like(x_s)

    def build(i, held):
        for m in range(SOME):
            products(e_ref[i * SOME + m], y_ref[...], held, pl.ds(m * columns, columns))

    def add_in(i, t):
        total = x_s[...]
        for m in range(SOME):
            total = total + t[m * columns : (m + 1) * columns] * e_ref[i * SOME + m].astype(F32)
        x_s[...] = total

    pairs = members // SOME // 2
    build(0, even_s)

    @pl.loop(0, pairs - 1)
    def _(i):
        t = dot(even_s[...], k_ref[...])
        build(2 * i + 1, odd_s)
        add_in(2 * i, t)
        t = dot(odd_s[...], k_ref[...])
        build(2 * i + 2, even_s)
        add_in(2 * i + 1, t)

    t = dot(even_s[...], k_ref[...])
    build(2 * pairs - 1, odd_s)
    add_in(2 * pairs - 2, t)
    add_in(2 * pairs - 1, dot(odd_s[...], k_ref[...]))

    x = x_s[...]
    x_ref[...] = x.T.astype(BF)
    sum_ref[...] = jnp.zeros_like(sum_ref)
    sum_ref[0:1, :] = fold(x * y_ref[...])


def coarse_image(ensemble, kern, own, got, y0=None, sums=None, after=()):
    members, columns, width = ensemble.shape
    second = y0 is not None
    args = [ensemble, kern, own, *got] + ([y0, sums] if second else []) + list(after)
    out = [shape((width, columns), BF), shape((columns, width), F32)]
    out += [shape((8, LANES), F32)] if second else []
    out += [shape((8, width), F32)]
    return pl.pallas_call(
        functools.partial(coarse_kernel, len(got), second, len(after)),
        in_specs=[VMEM] * (len(args) - len(after)) + [ANY] * len(after),
        out_specs=[VMEM] * len(out),
        out_shape=out,
        scratch_shapes=[
            pltpu.VMEM((SOME * columns, width), BF),
            pltpu.VMEM((SOME * columns, width), BF),
            pltpu.VMEM((columns, width), F32),
        ],
        compiler_params=params(16),
        cost_estimate=cost(2 * columns * members * width * width, 5e6),
        name="coarse_second" if second else "coarse_first",
    )(*args)


def project_kernel(e_ref, y_ref, t_ref, after_ref, g_ref, token_ref, even_s, odd_s):
    columns, members, width = e_ref.shape
    lanes = BATCH // 2 * LANES
    token_ref[...] = jnp.zeros_like(token_ref)

    @pl.loop(0, columns // BATCH)
    def _(i):
        base = pl.multiple_of(i * BATCH, BATCH)
        yb = y_ref[pl.ds(base, BATCH), :]
        for c in range(BATCH):
            held = odd_s if c % 2 else even_s
            rows = pl.ds((c // 2) * members, members)
            products(e_ref[base + c], yb[c : c + 1, :], held, rows)
        r = dot(even_s[...], t_ref[0]) + dot(odd_s[...], t_ref[1])
        for pair in range(BATCH // 2):
            at = pl.multiple_of(i * lanes + pair * LANES, LANES)
            g_ref[:, pl.ds(at, LANES)] = r[pair * members : (pair + 1) * members]


def project(ens, y, taps, after):
    columns, members, width = ens.shape
    levels = width // VAR
    return pl.pallas_call(
        project_kernel,
        in_specs=[VMEM] * 4,
        out_specs=[VMEM] * 2,
        out_shape=[shape((members, columns * levels), F32), shape((8, LANES), F32)],
        scratch_shapes=[pltpu.VMEM((BATCH // 2 * members, width), BF)] * 2,
        compiler_params=params(16),
        cost_estimate=cost(2 * columns * members * width * width, 8e6),
        name="project",
    )(ens, y, taps, after)


def lay_out(x_refs, xs):
    if len(x_refs) == 1:
        xs[...] = x_refs[0][...]
        return
    for i, x in enumerate(x_refs):
        for n in range(2):
            xs[:, pl.ds((2 * i + n) * LANES, LANES)] = x[n]


CUTS = 3


def images(x_refs, near_ref, far_ref, obs_ref, im_ref, xs):
    lay_out(x_refs, xs)
    half, fine = near_ref.shape
    rows = fine // CUTS
    for i in range(CUTS):
        some = pl.ds(i * rows, rows)
        turned = dot(xs[:, :half], near_ref[:, some]) + dot(xs[:, half:], far_ref[:, some])
        im = turned.T
        im_ref[some, :] = im
        yield some, im, obs_ref[some, :].astype(F32) * im


def image_kernel(count, *refs):
    x_refs, refs = refs[:count], refs[count:]
    near_ref, far_ref, obs_ref, g_ref, im_ref, sum_ref = refs[:6]
    outs, (xs, v_s) = refs[6:10], refs[10:]
    sums = g_ref[...]
    row = lax.broadcasted_iota(jnp.int32, sums.shape, 0)
    for some, im, v in images(x_refs, near_ref, far_ref, obs_ref, im_ref, xs):
        v_s[some, :] = v.astype(BF)
        sums = sums + jnp.where(row == 1, fold(v * im), 0.0)
    sum_ref[...] = sums
    rows = near_ref.shape[0] // 2
    for i, out in enumerate(outs):
        at_ref = far_ref if i > 1 else near_ref
        out[pl.ds(0, rows), :] = dot(at_ref[pl.ds(i % 2 * rows, rows), :], v_s[...])
    outs[3][pl.ds(rows, 8), :] = sums


def image_first(xs, near, far, obs, g_sums):
    half, fine = near.shape
    width = obs.shape[1]
    z_rows = [half // 2] * 3 + [half // 2 + 8]
    return pl.pallas_call(
        functools.partial(image_kernel, len(xs)),
        in_specs=[VMEM] * (len(xs) + 4),
        out_specs=[VMEM] * 6,
        out_shape=[shape((fine, width), F32), shape((8, width), F32)]
        + [shape((r, width), F32) for r in z_rows],
        scratch_shapes=[pltpu.VMEM((width, 2 * half), BF), pltpu.VMEM((fine, width), BF)],
        compiler_params=params(16),
        cost_estimate=cost(8 * half * fine * width, 13e6),
        name="image_first",
    )(*xs, near, far, obs, g_sums)


def second_kernel(count, *refs):
    x_refs, refs = refs[:count], refs[count:]
    near_ref, far_ref, obs_ref, g_ref, im_ref, sum_ref, xs = refs
    sums = g_ref[...]
    row = lax.broadcasted_iota(jnp.int32, sums.shape, 0)
    for _, im, v in images(x_refs, near_ref, far_ref, obs_ref, im_ref, xs):
        sums = sums + jnp.where(row == 1, fold(v * im), 0.0)
    sum_ref[...] = sums


def image_second(xs, near, far, obs, g_sums):
    half, fine = near.shape
    width = obs.shape[1]
    return pl.pallas_call(
        functools.partial(second_kernel, len(xs)),
        in_specs=[VMEM] * (len(xs) + 4),
        out_specs=[VMEM] * 2,
        out_shape=[shape((fine, width), F32), shape((8, width), F32)],
        scratch_shapes=[pltpu.VMEM((width, 2 * half), BF)],
        compiler_params=params(16),
        cost_estimate=cost(4 * half * fine * width, 8e6),
        name="image_second",
    )(*xs, near, far, obs, g_sums)


OUT_CUTS = 4


def result_kernel(count, l0_ref, *refs):
    sums = refs[0][...]
    for r in refs[1:count]:
        sums = sums + r[...]
    g0_ref, g1_ref, i0_ref, i1_ref, control_hbm, increment_hbm, c_s, i_s, sem = refs[count:]
    l0 = -l0_ref[0:1, 0:1]
    l1, _ = length_of(sums)
    lanes = c_s.shape[1] // OUT_CUTS
    rows = i_s.shape[0] // OUT_CUTS
    copies = []
    for i in range(OUT_CUTS):
        some = pl.ds(i * lanes, lanes)
        c_s[:, some] = l0 * g0_ref[:, some] - l1 * g1_ref[:, some]
        copies.append(
            pltpu.make_async_copy(c_s.at[:, some], control_hbm.at[:, some], sem.at[2 * i])
        )
        copies[-1].start()
        some = pl.ds(i * rows, rows)
        i_s[some, :] = l0 * i0_ref[some, :] - l1 * i1_ref[some, :]
        copies.append(
            pltpu.make_async_copy(i_s.at[some, :], increment_hbm.at[some, :], sem.at[2 * i + 1])
        )
        copies[-1].start()
    for copy in copies:
        copy.wait()


def result(l0, sums, g0, g1, im0, im1):
    return pl.pallas_call(
        functools.partial(result_kernel, len(sums)),
        in_specs=[VMEM] * (5 + len(sums)),
        out_specs=[ANY] * 2,
        out_shape=[shape(g0.shape, F32), shape(im0.shape, F32)],
        scratch_shapes=[
            pltpu.VMEM(g0.shape, F32),
            pltpu.VMEM(im0.shape, F32),
            pltpu.SemaphoreType.DMA((2 * OUT_CUTS,)),
        ],
        compiler_params=params(16),
        cost_estimate=cost(3 * g0.size, 1e7),
        name="result",
    )(l0, *sums, g0, g1, im0, im1)


def over_core(x):
    return lax.ppermute(x, "space", [(i, i ^ 1) for i in range(GROUP)])


def over_y(x):
    return lax.ppermute(x, "space", [(i, i ^ 2) for i in range(GROUP)])


def over_z(x, k):
    return lax.ppermute(x, "space", [(i, i ^ (4 * k)) for i in range(GROUP)])


def scatter_sums(parts, sums=None):
    near, far_y, near_c, far_yc = parts
    width = near.shape[1]
    two = shape((2 * LANES + HEAD, width), jnp.int16)
    one = shape((LANES + HEAD, width), jnp.int16)
    got_yc = over_core(far_yc)
    got_c = over_core(near_c)
    p, *s = merge(merge_a_kernel, "merge_a", [two], far_y, got_yc, sums=sums)
    p = over_y(p)
    (q,) = merge(merge_b_kernel, "merge_b", [two], far_y, got_yc, p)
    z, *s = merge(merge_c_kernel, "merge_c", [two], near, got_c, p, sums=s[0] if s else None)
    z, q = over_z(z, 1), over_y(q)
    out = [shape((LANES, width), F32), one]
    own, z, *s = merge(merge_d_kernel, "merge_d", out, near, got_c, q, z, sums=s[0] if s else None)
    return own, [over_z(z, 2)], (s[0] if s else None)


def gather_columns(x, work):
    two = shape((2,) + x.shape, BF)
    a = pair_of(join_kernel, "join", two, x, over_z(x, 2))
    b, ya, ca = over_z(a, 1), over_y(a), over_core(a)
    cya = over_core(ya)
    cb, yb = over_core(b), over_y(b)
    done, token = work(b)
    yb = pair_of(relay_kernel, "relay", two, yb, token)
    return [b, a, yb, ya, cb, ca, over_core(yb), cya], done


def sum_all(x):
    x = x + over_core(x)
    x = x + over_y(x)
    x = x + over_z(x, 1)
    return [x, over_z(x, 2)]


def on_device(ensemble, innovation, obs_weight, interp_weight, slot_of, intersection_list):
    members, columns, width = ensemble.shape
    levels = width // VAR
    devices = lax.axis_size("space")
    capacity = intersection_list.shape[2]
    slots = devices * capacity
    grouped = devices == GROUP and capacity == columns == LANES

    taper = vertical_taper(levels)
    both = taper.astype(np.float64) @ taper.T.astype(np.float64)
    kern = np.tile(np.concatenate(host_halves(both), axis=0), (2, VAR))
    tall = np.tile(np.concatenate(host_halves(taper), axis=0), (2, 1))
    none = np.zeros_like(tall)
    taps = np.stack(
        [np.concatenate([tall, none], axis=1), np.concatenate([none, tall], axis=1)]
    )
    kern, taps = jnp.asarray(kern), jnp.asarray(taps)

    index = lax.axis_index("space").astype(jnp.int32)
    me = jnp.stack([index // 4, index // 2 % 2, index % 2, index])
    w = -(obs_weight.astype(F32) * innovation.astype(F32))
    high = lax.reduce_precision(w, 8, 7)
    wh, wl = high.astype(BF), (w - high).astype(BF)
    named = jnp.concatenate([slot_of.astype(F32), interp_weight], axis=0)
    if grouped:
        lists = exchange_lists(me, intersection_list[0])
        scatter, gather, add_up = scatter_sums, gather_columns, sum_all
    else:
        lists = intersection_list[0]
        hit = (lists.reshape(-1, 1) == jnp.arange(columns, dtype=jnp.int32)).astype(BF)

        def swap(x):
            x = x.reshape(devices, capacity, width)
            x = lax.all_to_all(x, "space", split_axis=0, concat_axis=0, tiled=True)
            return x.reshape(slots, width)

        def scatter(parts, sums=None):
            got = swap(jnp.concatenate([p[: slots // 4] for p in parts], axis=0))
            high = lax.reduce_precision(got, 8, 7)
            high, low = high.astype(BF), (got - high).astype(BF)
            if sums is not None:
                sums = lax.psum(sums, "space")
            return dot(hit.T, high) + dot(hit.T, low), [], sums

        def gather(x, work):
            return [swap(dot(hit, x.T).astype(BF)).T], work(x)[0]

        def add_up(x):
            return [lax.psum(x, "space")]

    ids, weight, far, c0, c1 = adjoint_half(slots, [named, wh, wl], (grouped, me, lists if grouped else []))
    near, n0, n1 = adjoint_half(slots, [ids, weight, wh, wl])
    own, got, _ = scatter([n0, n1, c0, c1])
    ens = jnp.transpose(ensemble, (1, 0, 2))
    x0, y0, g_sums = coarse_image(ensemble, kern, own, got, after=[ens])
    xs, g0 = gather(x0, lambda after: project(ens, y0, taps, after))
    im0, sums, *second = image_first(xs, near, far, obs_weight, g_sums)
    own, got, sums = scatter(second, sums)
    x1, y1, l0, g_sums = coarse_image(ensemble, kern, own, got, y0, sums)
    xs, g1 = gather(x1, lambda after: project(ens, y1, taps, after))
    im1, sums = image_second(xs, near, far, obs_weight, g_sums)
    return tuple(result(l0, add_up(sums), g0, g1, im0, im1))


def solution(mesh):
    placed = (
        P("case", "space", None),
        P(("case", "space"), None),
        P(("case", "space"), None),
        P("case", "space"),
        P("case", "space"),
        P(("case", "space"), None, None),
    )
    return jax.shard_map(
        on_device,
        mesh=mesh,
        in_specs=placed,
        out_specs=(P("case", "space"), P(("case", "space"), None)),
        check_vma=False,
    )
```

```python
import functools

import jax
import jax.numpy as jnp
import ml_dtypes
import numpy as np
from jax import lax
from jax.experimental import pallas as pl
from jax.experimental.pallas import tpu as pltpu
from jax.sharding import PartitionSpec as P

VAR = 4
LOC_SCALE = 3.0
BF = jnp.bfloat16
F32 = jnp.float32
LANES = 128
GROUP = 16
VMEM = pl.BlockSpec(memory_space=pltpu.VMEM)
SMEM = pl.BlockSpec(memory_space=pltpu.SMEM)
ANY = pl.BlockSpec(memory_space=pl.ANY)


def vertical_taper(levels):
    heights = np.arange(levels).astype(np.float32)
    spread = (heights[:, None] - heights[None, :]) / np.float32(LOC_SCALE)
    return np.exp(np.float32(-0.5) * spread * spread)


def host_halves(x):
    high = x.astype(ml_dtypes.bfloat16)
    return [high, (x - high.astype(x.dtype)).astype(ml_dtypes.bfloat16)]


def params(mib):
    return pltpu.CompilerParams(vmem_limit_bytes=mib << 20)


def cost(flops, nbytes):
    return pl.CostEstimate(flops=int(flops), bytes_accessed=int(nbytes), transcendentals=0)


def dot(a, b):
    return jnp.dot(a, b, preferred_element_type=F32)


def halves(x):
    high = x.astype(BF)
    return high, (x - high.astype(F32)).astype(BF)


def shape(dims, dtype):
    return jax.ShapeDtypeStruct(dims, dtype)


STEPS = 4
ORDER = (2, 3, 1, 0)
PARTS = ((0, 0), (1, 0), (0, 1), (1, 1))
HEAD = 16
TOP = 32512.0


def owner_at(me_ref, i):
    dy, dc = PARTS[i // STEPS]
    z, y, c = me_ref[0], me_ref[1], me_ref[2]
    y = y if dy == 0 else 1 - y
    c = c if dc == 0 else 1 - c
    return (jnp.bitwise_xor(z, ORDER[i % STEPS]) * 2 + y) * 2 + c


def places(me_ref, list_refs, slots):
    slots = jnp.concatenate([slots, slots], axis=0)
    from_owner = jnp.right_shift(slots, 7)
    within = jnp.bitwise_and(slots, LANES - 1)
    rows = jnp.zeros(slots.shape, jnp.int32)
    for i in range(GROUP):
        o = owner_at(me_ref, i)
        dy, dc = PARTS[i // STEPS]
        held = list_refs[ORDER[i % STEPS]]
        row = jnp.broadcast_to(held[2 * dy + dc : 2 * dy + dc + 1, :], slots.shape)
        column = jnp.take_along_axis(row, within, axis=1, mode="promise_in_bounds")
        rows = jnp.where(from_owner == o, column + i * LANES, rows)
    return rows[: slots.shape[0] // 2]


def build_rows(ids_ref, weight_ref, wh_ref, wl_ref, at_ref, y_refs, lo_s, base):
    sources, fine = ids_ref.shape
    rows = at_ref.shape[0] // len(y_refs)
    step = rows // 2
    row = lax.broadcasted_iota(jnp.int32, (step, LANES), 0)
    for n, y_ref in enumerate(y_refs):
        for m in range(2):
            start = n * rows + m * step
            for j in range(fine // LANES):
                lanes = pl.ds(j * LANES, LANES)
                total = None
                for b in range(sources):
                    ids = ids_ref[b : b + 1, lanes] - (base + start)
                    term = jnp.where(row == ids, weight_ref[b : b + 1, lanes], 0.0)
                    total = term if total is None else total + term
                high, low = halves(total)
                at_ref[pl.ds(start, step), lanes] = high
                lo_s[pl.ds(m * step, step), lanes] = low
        held = at_ref[pl.ds(n * rows, rows), :]
        y_ref[...] = dot(held, wh_ref[...]) + dot(held, wl_ref[...]) + dot(lo_s[...], wh_ref[...])


def far_kernel(grouped, me_ref, *refs):
    list_refs, refs = refs[: 4 * grouped], refs[4 * grouped :]
    both_ref, wh_ref, wl_ref, *refs = refs
    ids_ref, weight_ref, at_ref, ya_ref, yb_ref, lo_s = refs
    sources = ids_ref.shape[0]
    for j in range(ids_ref.shape[1] // LANES):
        lanes = pl.ds(j * LANES, LANES)
        slots = both_ref[:sources, lanes].astype(jnp.int32)
        ids_ref[:, lanes] = places(me_ref, list_refs, slots) if grouped else slots
        weight_ref[:, lanes] = both_ref[sources:, lanes]
    half = at_ref.shape[0]
    build_rows(ids_ref, weight_ref, wh_ref, wl_ref, at_ref, [ya_ref, yb_ref], lo_s, half)


def near_kernel(ids_ref, weight_ref, wh_ref, wl_ref, at_ref, ya_ref, yb_ref, lo_s):
    build_rows(ids_ref, weight_ref, wh_ref, wl_ref, at_ref, [ya_ref, yb_ref], lo_s, 0)


def adjoint_half(slots, args, head=None):
    fine, width = args[-1].shape
    half = slots // 2
    sources = args[0].shape[0] // (2 if head else 1)
    out = [shape((half, fine), BF)] + [shape((half // 2, width), F32)] * 2
    if head:
        grouped, me, lists = head
        kernel = functools.partial(far_kernel, grouped)
        args = [me, *lists, *args]
        out = [shape((sources, fine), jnp.int32), shape((sources, fine), F32)] + out
    else:
        kernel = near_kernel
    return pl.pallas_call(
        kernel,
        in_specs=([SMEM] if head else []) + [VMEM] * (len(args) - (1 if head else 0)),
        out_specs=[VMEM] * len(out),
        out_shape=out,
        scratch_shapes=[pltpu.VMEM((half // 2, fine), BF)],
        compiler_params=params(16),
        cost_estimate=cost(3 * slots * fine * width, 4e6),
        name="adjoint_far" if head else "adjoint_near",
    )(*args)


def pick_kernel(me_ref, lists_ref, near_ref, far_ref):
    z, y, c = me_ref[0], me_ref[1], me_ref[2]
    for dy in range(2):
        for k in range(STEPS):
            there = (jnp.bitwise_xor(z, k) * 2 + (y if dy == 0 else 1 - y)) * 2
            row = slice(dy * STEPS + k, dy * STEPS + k + 1)
            near_ref[row, :] = lists_ref[pl.ds(there + c, 1), :]
            far_ref[row, :] = lists_ref[pl.ds(there + 1 - c, 1), :]


def mix_y_kernel(near_ref, got_ref, near_y_ref, far_y_ref):
    for i, held in enumerate((near_ref, got_ref)):
        rows = slice(i * STEPS, (i + 1) * STEPS)
        near_y_ref[rows, :] = held[:STEPS, :]
        far_y_ref[rows, :] = held[STEPS:, :]


def mix_z_kernel(near_ref, got_ref, *outs):
    for k, out in enumerate(outs):
        out[...] = jnp.zeros_like(out)
        for i, held in enumerate((near_ref, got_ref)):
            for c in range(2):
                row = c * STEPS + k
                out[2 * i + c : 2 * i + c + 1, :] = held[row : row + 1, :]


def small(kernel, n, name, *args, scalars=0):
    return pl.pallas_call(
        kernel,
        in_specs=[SMEM] * scalars + [VMEM] * (len(args) - scalars),
        out_specs=[VMEM] * n,
        out_shape=[shape((8, LANES), jnp.int32)] * n,
        compiler_params=params(8),
        cost_estimate=cost(1e4, 3e4),
        name=name,
    )(*args)


def exchange_lists(me, lists):
    near, far = small(pick_kernel, 2, "pick", me, lists, scalars=1)
    near, far = small(mix_y_kernel, 2, "mix_y", near, over_core(far))
    own, *sent = small(mix_z_kernel, STEPS, "mix_z", near, over_y(far))
    return [own] + [over_z(sent[k - 1], k) for k in range(1, STEPS)], own


def exponent(m):
    return jnp.clip(jnp.ceil(jnp.log2(jnp.maximum(m, 1e-30))), -100.0, 100.0)


def whole16(x):
    return x.astype(jnp.int32).astype(jnp.int16)


def wide(x):
    return x.astype(jnp.int32).astype(F32)


def pack(out_ref, t, sums=None):
    rows, width = t.shape
    e = exponent(jnp.max(jnp.abs(t), axis=0, keepdims=True))
    out_ref[pl.ds(0, rows), :] = whole16(jnp.round(t * (jnp.exp2(-e) * TOP)))
    head = [e]
    if sums is not None:
        for i in range(2):
            v = sums[i : i + 1, :]
            f = exponent(v)
            v = v * (jnp.exp2(-f) * 16384.0)
            first = jnp.floor(v)
            head += [f, first, jnp.floor((v - first) * 16384.0)]
    row = lax.broadcasted_iota(jnp.int32, (HEAD, width), 0)
    total = jnp.zeros((HEAD, width), F32)
    for i, h in enumerate(head):
        total = jnp.where(row == i, h, total)
    out_ref[pl.ds(rows, HEAD), :] = whole16(total)


def unpack(ref):
    rows = ref.shape[0] - HEAD
    head = wide(ref[pl.ds(rows, HEAD), :])
    return wide(ref[pl.ds(0, rows), :]) * (jnp.exp2(head[0:1, :]) * (1.0 / TOP))


def unpack_sums(ref):
    head = wide(ref[pl.ds(ref.shape[0] - HEAD, HEAD), :])
    row = lax.broadcasted_iota(jnp.int32, (8, head.shape[1]), 0)
    total = jnp.zeros(row.shape, F32)
    for i in range(2):
        f, first, second = [head[1 + 3 * i + j : 2 + 3 * i + j, :] for j in range(3)]
        v = (first + second * (1.0 / 16384.0)) * (jnp.exp2(f) * (1.0 / 16384.0))
        total = jnp.where(row == i, v, total)
    return total


def merge_y_kernel(with_sums, *refs):
    if with_sums:
        a_ref, b_ref, mine_ref, first_ref, second_ref, s_ref = refs
        sums = mine_ref[...] + b_ref[pl.ds(a_ref.shape[0], 8), :]
        s_ref[...] = sums
    else:
        a_ref, b_ref, first_ref, second_ref = refs
        sums = None
    half = a_ref.shape[0] // 2
    pack(first_ref, a_ref[pl.ds(0, half), :] + b_ref[pl.ds(0, half), :], sums)
    pack(second_ref, a_ref[pl.ds(half, half), :] + b_ref[pl.ds(half, half), :])


def merge_y(a, b, sums):
    rows, width = a.shape
    out = [shape((rows // 2 + HEAD, width), jnp.int16)] * 2
    args = [a, b]
    if sums is not None:
        out.append(shape((8, width), F32))
        args.append(sums)
    return pl.pallas_call(
        functools.partial(merge_y_kernel, sums is not None),
        in_specs=[VMEM] * len(args),
        out_specs=[VMEM] * len(out),
        out_shape=out,
        compiler_params=params(8),
        cost_estimate=cost(5 * rows * width, 1e6),
        name="merge_y",
    )(*args)


def merge_z_kernel(last, with_sums, a_ref, b_ref, p_ref, *refs):
    half = a_ref.shape[0] // 2
    rows = pl.ds(half if last else 0, half)
    t = a_ref[rows, :] + b_ref[rows, :] + unpack(p_ref)
    sums = None
    if with_sums:
        sums = refs[0][...]
        refs = refs[1:]
        if not last:
            sums = sums + unpack_sums(p_ref)
            refs[2][...] = sums
    pack(refs[0], t[:LANES], sums)
    if last:
        refs[1][...] = t[LANES:]
    else:
        pack(refs[1], t[LANES:], sums)


def merge_z(last, a, b, p, sums):
    width = a.shape[1]
    sent = shape((LANES + HEAD, width), jnp.int16)
    out = [sent, shape((LANES, width), F32) if last else sent]
    args = [a, b, p]
    if sums is not None:
        args.append(sums)
        if not last:
            out.append(shape((8, width), F32))
    return pl.pallas_call(
        functools.partial(merge_z_kernel, last, sums is not None),
        in_specs=[VMEM] * len(args),
        out_specs=[VMEM] * len(out),
        out_shape=out,
        compiler_params=params(8),
        cost_estimate=cost(5 * a.size, 1e6),
        name="merge_z_last" if last else "merge_z_first",
    )(*args)


def join_kernel(*refs):
    for i, r in enumerate(refs[:-1]):
        refs[-1][i] = r[...]


def relay_kernel(x_ref, after_ref, out_ref):
    out_ref[...] = x_ref[...]


def copy_of(kernel, name, out, *args):
    return pl.pallas_call(
        kernel,
        in_specs=[VMEM] * len(args),
        out_specs=VMEM,
        out_shape=out,
        compiler_params=params(8),
        cost_estimate=cost(1e5, 5e5),
        name=name,
    )(*args)


def fold(a):
    return jnp.sum(a, axis=0, keepdims=True)


def length_of(sums):
    grad = jnp.sum(sums[0:1, :], axis=1, keepdims=True)
    image = jnp.sum(sums[1:2, :], axis=1, keepdims=True)
    return grad / (grad + image), image / (grad + image)


def products(e, y, held, rows):
    p = e.astype(F32) * y
    q = p[:, :LANES] + p[:, LANES:]
    q = q + pltpu.roll(q, LANES // 2, 1)
    high, low = halves(q)
    held[rows, :LANES] = high
    held[rows, LANES:] = low


BATCH = 16
SOME = 8


def coarse_kernel(packed, second, after, e_ref, k_ref, own_ref, *refs):
    refs = list(refs)
    got = [refs.pop(0) for _ in range(packed)]
    y = own_ref[...]
    for r in got:
        y = y + unpack(r)
    if second:
        y0_ref, s_ref = refs.pop(0), refs.pop(0)
        sums = s_ref[...]
        for r in got:
            sums = sums + unpack_sums(r)
        l0, keep = length_of(sums)
        y = keep * y0_ref[...] - l0 * y
        refs.pop(after + 2)[...] = jnp.broadcast_to(l0, (8, LANES))
    x_ref, y_ref, sum_ref, even_s, odd_s, x_s = refs[after:]
    members, columns, width = e_ref.shape
    y_ref[...] = y
    x_s[...] = jnp.zeros_like(x_s)

    def build(i, held):
        for m in range(SOME):
            products(e_ref[i * SOME + m], y_ref[...], held, pl.ds(m * columns, columns))

    def add_in(i, t):
        total = x_s[...]
        for m in range(SOME):
            total = total + t[m * columns : (m + 1) * columns] * e_ref[i * SOME + m].astype(F32)
        x_s[...] = total

    pairs = members // SOME // 2
    build(0, even_s)

    @pl.loop(0, pairs - 1)
    def _(i):
        t = dot(even_s[...], k_ref[...])
        build(2 * i + 1, odd_s)
        add_in(2 * i, t)
        t = dot(odd_s[...], k_ref[...])
        build(2 * i + 2, even_s)
        add_in(2 * i + 1, t)

    t = dot(even_s[...], k_ref[...])
    build(2 * pairs - 1, odd_s)
    add_in(2 * pairs - 2, t)
    add_in(2 * pairs - 1, dot(odd_s[...], k_ref[...]))

    x = x_s[...]
    x_ref[...] = x.T.astype(BF)
    sum_ref[...] = jnp.zeros_like(sum_ref)
    sum_ref[0:1, :] = fold(x * y_ref[...])


def coarse_image(ensemble, kern, own, got, y0=None, sums=None, after=()):
    members, columns, width = ensemble.shape
    second = y0 is not None
    args = [ensemble, kern, own, *got] + ([y0, sums] if second else []) + list(after)
    out = [shape((width, columns), BF), shape((columns, width), F32)]
    out += [shape((8, LANES), F32)] if second else []
    out += [shape((8, width), F32)]
    return pl.pallas_call(
        functools.partial(coarse_kernel, len(got), second, len(after)),
        in_specs=[VMEM] * (len(args) - len(after)) + [ANY] * len(after),
        out_specs=[VMEM] * len(out),
        out_shape=out,
        scratch_shapes=[
            pltpu.VMEM((SOME * columns, width), BF),
            pltpu.VMEM((SOME * columns, width), BF),
            pltpu.VMEM((columns, width), F32),
        ],
        compiler_params=params(16),
        cost_estimate=cost(2 * columns * members * width * width, 5e6),
        name="coarse_second" if second else "coarse_first",
    )(*args)


def project_kernel(e_ref, y_ref, t_ref, after_ref, g_ref, token_ref, even_s, odd_s):
    columns, members, width = e_ref.shape
    lanes = BATCH // 2 * LANES
    token_ref[...] = jnp.zeros_like(token_ref)

    @pl.loop(0, columns // BATCH)
    def _(i):
        base = pl.multiple_of(i * BATCH, BATCH)
        yb = y_ref[pl.ds(base, BATCH), :]
        for c in range(BATCH):
            held = odd_s if c % 2 else even_s
            rows = pl.ds((c // 2) * members, members)
            products(e_ref[base + c], yb[c : c + 1, :], held, rows)
        r = dot(even_s[...], t_ref[0]) + dot(odd_s[...], t_ref[1])
        for pair in range(BATCH // 2):
            at = pl.multiple_of(i * lanes + pair * LANES, LANES)
            g_ref[:, pl.ds(at, LANES)] = r[pair * members : (pair + 1) * members]


def project(ens, y, taps, after):
    columns, members, width = ens.shape
    levels = width // VAR
    return pl.pallas_call(
        project_kernel,
        in_specs=[VMEM] * 4,
        out_specs=[VMEM] * 2,
        out_shape=[shape((members, columns * levels), F32), shape((8, LANES), F32)],
        scratch_shapes=[pltpu.VMEM((BATCH // 2 * members, width), BF)] * 2,
        compiler_params=params(16),
        cost_estimate=cost(2 * columns * members * width * width, 8e6),
        name="project",
    )(ens, y, taps, after)


def lay_out(x_refs, xs):
    if len(x_refs) == 1:
        xs[...] = x_refs[0][...]
        return
    for i, x in enumerate(x_refs):
        for n in range(STEPS):
            xs[:, pl.ds((i * STEPS + n) * LANES, LANES)] = x[n]


CUTS = 3


def images(x_refs, near_ref, far_ref, obs_ref, im_ref, xs):
    lay_out(x_refs, xs)
    half, fine = near_ref.shape
    rows = fine // CUTS
    for i in range(CUTS):
        some = pl.ds(i * rows, rows)
        turned = dot(xs[:, :half], near_ref[:, some]) + dot(xs[:, half:], far_ref[:, some])
        im = turned.T
        im_ref[some, :] = im
        yield some, im, obs_ref[some, :].astype(F32) * im


def image_kernel(count, *refs):
    x_refs, refs = refs[:count], refs[count:]
    near_ref, far_ref, obs_ref, g_ref, im_ref, sum_ref = refs[:6]
    outs, (xs, v_s) = refs[6:10], refs[10:]
    sums = g_ref[...]
    row = lax.broadcasted_iota(jnp.int32, sums.shape, 0)
    for some, im, v in images(x_refs, near_ref, far_ref, obs_ref, im_ref, xs):
        v_s[some, :] = v.astype(BF)
        sums = sums + jnp.where(row == 1, fold(v * im), 0.0)
    sum_ref[...] = sums
    rows = near_ref.shape[0] // 2
    for i, out in enumerate(outs):
        at_ref = far_ref if i > 1 else near_ref
        out[pl.ds(0, rows), :] = dot(at_ref[pl.ds(i % 2 * rows, rows), :], v_s[...])
    outs[3][pl.ds(rows, 8), :] = sums


def image_first(xs, near, far, obs, g_sums):
    half, fine = near.shape
    width = obs.shape[1]
    z_rows = [half // 2] * 3 + [half // 2 + 8]
    return pl.pallas_call(
        functools.partial(image_kernel, len(xs)),
        in_specs=[VMEM] * (len(xs) + 4),
        out_specs=[VMEM] * 6,
        out_shape=[shape((fine, width), F32), shape((8, width), F32)]
        + [shape((r, width), F32) for r in z_rows],
        scratch_shapes=[pltpu.VMEM((width, 2 * half), BF), pltpu.VMEM((fine, width), BF)],
        compiler_params=params(16),
        cost_estimate=cost(8 * half * fine * width, 13e6),
        name="image_first",
    )(*xs, near, far, obs, g_sums)


def second_kernel(count, *refs):
    x_refs, refs = refs[:count], refs[count:]
    near_ref, far_ref, obs_ref, g_ref, im_ref, sum_ref, xs = refs
    sums = g_ref[...]
    row = lax.broadcasted_iota(jnp.int32, sums.shape, 0)
    for _, im, v in images(x_refs, near_ref, far_ref, obs_ref, im_ref, xs):
        sums = sums + jnp.where(row == 1, fold(v * im), 0.0)
    sum_ref[...] = sums


def image_second(xs, near, far, obs, g_sums):
    half, fine = near.shape
    width = obs.shape[1]
    return pl.pallas_call(
        functools.partial(second_kernel, len(xs)),
        in_specs=[VMEM] * (len(xs) + 4),
        out_specs=[VMEM] * 2,
        out_shape=[shape((fine, width), F32), shape((8, width), F32)],
        scratch_shapes=[pltpu.VMEM((width, 2 * half), BF)],
        compiler_params=params(16),
        cost_estimate=cost(4 * half * fine * width, 8e6),
        name="image_second",
    )(*xs, near, far, obs, g_sums)


OUT_CUTS = 4


def result_kernel(count, l0_ref, *refs):
    sums = refs[0][...]
    for r in refs[1:count]:
        sums = sums + r[...]
    g0_ref, g1_ref, i0_ref, i1_ref, control_hbm, increment_hbm, c_s, i_s, sem = refs[count:]
    l0 = -l0_ref[0:1, 0:1]
    l1, _ = length_of(sums)
    lanes = c_s.shape[1] // OUT_CUTS
    rows = i_s.shape[0] // OUT_CUTS
    copies = []
    for i in range(OUT_CUTS):
        some = pl.ds(i * lanes, lanes)
        c_s[:, some] = l0 * g0_ref[:, some] - l1 * g1_ref[:, some]
        copies.append(
            pltpu.make_async_copy(c_s.at[:, some], control_hbm.at[:, some], sem.at[2 * i])
        )
        copies[-1].start()
        some = pl.ds(i * rows, rows)
        i_s[some, :] = l0 * i0_ref[some, :] - l1 * i1_ref[some, :]
        copies.append(
            pltpu.make_async_copy(i_s.at[some, :], increment_hbm.at[some, :], sem.at[2 * i + 1])
        )
        copies[-1].start()
    for copy in copies:
        copy.wait()


def result(l0, sums, g0, g1, im0, im1):
    return pl.pallas_call(
        functools.partial(result_kernel, len(sums)),
        in_specs=[VMEM] * (5 + len(sums)),
        out_specs=[ANY] * 2,
        out_shape=[shape(g0.shape, F32), shape(im0.shape, F32)],
        scratch_shapes=[
            pltpu.VMEM(g0.shape, F32),
            pltpu.VMEM(im0.shape, F32),
            pltpu.SemaphoreType.DMA((2 * OUT_CUTS,)),
        ],
        compiler_params=params(16),
        cost_estimate=cost(3 * g0.size, 1e7),
        name="result",
    )(l0, *sums, g0, g1, im0, im1)


def over_core(x):
    return lax.ppermute(x, "space", [(i, i ^ 1) for i in range(GROUP)])


def over_y(x):
    return lax.ppermute(x, "space", [(i, i ^ 2) for i in range(GROUP)])


def over_z(x, k):
    return lax.ppermute(x, "space", [(i, i ^ (4 * k)) for i in range(GROUP)])


def scatter_sums(parts, sums=None):
    near, far_y, near_c, far_yc = parts
    got_yc = over_core(far_yc)
    got_c = over_core(near_c)
    first, second, *s = merge_y(far_y, got_yc, sums)
    first, second = over_y(first), over_y(second)
    two, three, *s = merge_z(False, near, got_c, first, s[0] if s else None)
    got = [over_z(two, 2), over_z(three, 3)]
    one, own = merge_z(True, near, got_c, second, s[0] if s else None)
    return own, got + [over_z(one, 1)], (s[0] if s else None)


def gather_columns(x, work):
    four = shape((STEPS,) + x.shape, BF)
    a = copy_of(join_kernel, "join", four, *[over_z(x, k) for k in ORDER[:3]], x)
    ya, ca = over_y(a), over_core(a)
    done, token = work(a)
    ya = copy_of(relay_kernel, "relay", four, ya, token)
    return [a, ya, ca, over_core(ya)], done


def sum_all(x):
    x = x + over_core(x)
    x = x + over_y(x)
    return [x] + [over_z(x, k) for k in range(1, STEPS)]


def on_device(ensemble, innovation, obs_weight, interp_weight, slot_of, intersection_list):
    members, columns, width = ensemble.shape
    levels = width // VAR
    devices = lax.axis_size("space")
    capacity = intersection_list.shape[2]
    slots = devices * capacity
    grouped = devices == GROUP and capacity == columns == LANES

    taper = vertical_taper(levels)
    both = taper.astype(np.float64) @ taper.T.astype(np.float64)
    kern = np.tile(np.concatenate(host_halves(both), axis=0), (2, VAR))
    tall = np.tile(np.concatenate(host_halves(taper), axis=0), (2, 1))
    none = np.zeros_like(tall)
    taps = np.stack(
        [np.concatenate([tall, none], axis=1), np.concatenate([none, tall], axis=1)]
    )
    kern, taps = jnp.asarray(kern), jnp.asarray(taps)

    index = lax.axis_index("space").astype(jnp.int32)
    me = jnp.stack([index // 4, index // 2 % 2, index % 2, index])
    named = jnp.concatenate([slot_of.astype(F32), interp_weight], axis=0)
    if grouped:
        lists, after = exchange_lists(me, intersection_list[0])
        late = 0.0 * after[:1, :1].astype(F32)
        scatter, gather, add_up = scatter_sums, gather_columns, sum_all
    else:
        lists, late = intersection_list[0], 0.0
        hit = (lists.reshape(-1, 1) == jnp.arange(columns, dtype=jnp.int32)).astype(BF)

        def swap(x):
            x = x.reshape(devices, capacity, width)
            x = lax.all_to_all(x, "space", split_axis=0, concat_axis=0, tiled=True)
            return x.reshape(slots, width)

        def scatter(parts, sums=None):
            got = swap(jnp.concatenate([p[: slots // 4] for p in parts], axis=0))
            high = lax.reduce_precision(got, 8, 7)
            high, low = high.astype(BF), (got - high).astype(BF)
            if sums is not None:
                sums = lax.psum(sums, "space")
            return dot(hit.T, high) + dot(hit.T, low), [], sums

        def gather(x, work):
            return [swap(dot(hit, x.T).astype(BF)).T], work(x)[0]

        def add_up(x):
            return [lax.psum(x, "space")]

    w = late - obs_weight.astype(F32) * innovation.astype(F32)
    high = lax.reduce_precision(w, 8, 7)
    wh, wl = high.astype(BF), (w - high).astype(BF)
    ids, weight, far, c0, c1 = adjoint_half(slots, [named, wh, wl], (grouped, me, lists if grouped else []))
    near, n0, n1 = adjoint_half(slots, [ids, weight, wh, wl])
    own, got, _ = scatter([n0, n1, c0, c1])
    ens = jnp.transpose(ensemble, (1, 0, 2))
    x0, y0, g_sums = coarse_image(ensemble, kern, own, got, after=[ens])
    xs, g0 = gather(x0, lambda after: project(ens, y0, taps, after))
    im0, sums, *second = image_first(xs, near, far, obs_weight, g_sums)
    own, got, sums = scatter(second, sums)
    x1, y1, l0, g_sums = coarse_image(ensemble, kern, own, got, y0, sums)
    xs, g1 = gather(x1, lambda after: project(ens, y1, taps, after))
    im1, sums = image_second(xs, near, far, obs_weight, g_sums)
    return tuple(result(l0, add_up(sums), g0, g1, im0, im1))


def solution(mesh):
    placed = (
        P("case", "space", None),
        P(("case", "space"), None),
        P(("case", "space"), None),
        P("case", "space"),
        P("case", "space"),
        P(("case", "space"), None, None),
    )
    return jax.shard_map(
        on_device,
        mesh=mesh,
        in_specs=placed,
        out_specs=(P("case", "space"), P(("case", "space"), None)),
        check_vma=False,
    )
```

```python
import functools

import jax
import jax.numpy as jnp
import ml_dtypes
import numpy as np
from jax import lax
from jax.experimental import pallas as pl
from jax.experimental.pallas import tpu as pltpu
from jax.sharding import PartitionSpec as P

VAR = 4
LOC_SCALE = 3.0
BF = jnp.bfloat16
F32 = jnp.float32
LANES = 128
GROUP = 16
VMEM = pl.BlockSpec(memory_space=pltpu.VMEM)
SMEM = pl.BlockSpec(memory_space=pltpu.SMEM)
ANY = pl.BlockSpec(memory_space=pl.ANY)


def vertical_taper(levels):
    heights = np.arange(levels).astype(np.float32)
    spread = (heights[:, None] - heights[None, :]) / np.float32(LOC_SCALE)
    return np.exp(np.float32(-0.5) * spread * spread)


def host_halves(x):
    high = x.astype(ml_dtypes.bfloat16)
    return [high, (x - high.astype(x.dtype)).astype(ml_dtypes.bfloat16)]


def params(mib):
    return pltpu.CompilerParams(vmem_limit_bytes=mib << 20)


def cost(flops, nbytes):
    return pl.CostEstimate(flops=int(flops), bytes_accessed=int(nbytes), transcendentals=0)


def dot(a, b):
    return jnp.dot(a, b, preferred_element_type=F32)


def halves(x):
    high = x.astype(BF)
    return high, (x - high.astype(F32)).astype(BF)


def shape(dims, dtype):
    return jax.ShapeDtypeStruct(dims, dtype)


STEPS = 4
ORDER = (2, 3, 1, 0)
PARTS = ((0, 0), (1, 0), (0, 1), (1, 1))
HEAD = 16
TOP = 32512.0


def owner_at(me_ref, i):
    dy, dc = PARTS[i // STEPS]
    z, y, c = me_ref[0], me_ref[1], me_ref[2]
    y = y if dy == 0 else 1 - y
    c = c if dc == 0 else 1 - c
    return (jnp.bitwise_xor(z, ORDER[i % STEPS]) * 2 + y) * 2 + c


def places(me_ref, list_refs, slots):
    slots = jnp.concatenate([slots, slots], axis=0)
    from_owner = jnp.right_shift(slots, 7)
    within = jnp.bitwise_and(slots, LANES - 1)
    rows = jnp.zeros(slots.shape, jnp.int32)
    for i in range(GROUP):
        o = owner_at(me_ref, i)
        dy, dc = PARTS[i // STEPS]
        held = list_refs[ORDER[i % STEPS]]
        row = jnp.broadcast_to(held[2 * dy + dc : 2 * dy + dc + 1, :], slots.shape)
        column = jnp.take_along_axis(row, within, axis=1, mode="promise_in_bounds")
        rows = jnp.where(from_owner == o, column + i * LANES, rows)
    return rows[: slots.shape[0] // 2]


def build_rows(ids_ref, weight_ref, wh_ref, wl_ref, at_ref, y_refs, lo_s, base):
    sources, fine = ids_ref.shape
    rows = at_ref.shape[0] // len(y_refs)
    step = rows // 2
    row = lax.broadcasted_iota(jnp.int32, (step, LANES), 0)
    for n, y_ref in enumerate(y_refs):
        for m in range(2):
            start = n * rows + m * step
            for j in range(fine // LANES):
                lanes = pl.ds(j * LANES, LANES)
                total = None
                for b in range(sources):
                    ids = ids_ref[b : b + 1, lanes] - (base + start)
                    term = jnp.where(row == ids, weight_ref[b : b + 1, lanes], 0.0)
                    total = term if total is None else total + term
                high, low = halves(total)
                at_ref[pl.ds(start, step), lanes] = high
                lo_s[pl.ds(m * step, step), lanes] = low
        held = at_ref[pl.ds(n * rows, rows), :]
        y_ref[...] = dot(held, wh_ref[...]) + dot(held, wl_ref[...]) + dot(lo_s[...], wh_ref[...])


def far_kernel(grouped, me_ref, *refs):
    list_refs, refs = refs[: 4 * grouped], refs[4 * grouped :]
    both_ref, wh_ref, wl_ref, *refs = refs
    ids_ref, weight_ref, at_ref, ya_ref, yb_ref, lo_s = refs
    sources = ids_ref.shape[0]
    for j in range(ids_ref.shape[1] // LANES):
        lanes = pl.ds(j * LANES, LANES)
        slots = both_ref[:sources, lanes].astype(jnp.int32)
        ids_ref[:, lanes] = places(me_ref, list_refs, slots) if grouped else slots
        weight_ref[:, lanes] = both_ref[sources:, lanes]
    half = at_ref.shape[0]
    build_rows(ids_ref, weight_ref, wh_ref, wl_ref, at_ref, [ya_ref, yb_ref], lo_s, half)


def near_kernel(ids_ref, weight_ref, wh_ref, wl_ref, at_ref, ya_ref, yb_ref, lo_s):
    build_rows(ids_ref, weight_ref, wh_ref, wl_ref, at_ref, [ya_ref, yb_ref], lo_s, 0)


def adjoint_half(slots, args, head=None):
    fine, width = args[-1].shape
    half = slots // 2
    sources = args[0].shape[0] // (2 if head else 1)
    out = [shape((half, fine), BF)] + [shape((half // 2, width), F32)] * 2
    if head:
        grouped, me, lists = head
        kernel = functools.partial(far_kernel, grouped)
        args = [me, *lists, *args]
        out = [shape((sources, fine), jnp.int32), shape((sources, fine), F32)] + out
    else:
        kernel = near_kernel
    return pl.pallas_call(
        kernel,
        in_specs=([SMEM] if head else []) + [VMEM] * (len(args) - (1 if head else 0)),
        out_specs=[VMEM] * len(out),
        out_shape=out,
        scratch_shapes=[pltpu.VMEM((half // 2, fine), BF)],
        compiler_params=params(16),
        cost_estimate=cost(3 * slots * fine * width, 4e6),
        name="adjoint_far" if head else "adjoint_near",
    )(*args)


def pick_kernel(me_ref, lists_ref, near_ref, far_ref):
    z, y, c = me_ref[0], me_ref[1], me_ref[2]
    for dy in range(2):
        for k in range(STEPS):
            there = (jnp.bitwise_xor(z, k) * 2 + (y if dy == 0 else 1 - y)) * 2
            row = slice(dy * STEPS + k, dy * STEPS + k + 1)
            near_ref[row, :] = lists_ref[pl.ds(there + c, 1), :]
            far_ref[row, :] = lists_ref[pl.ds(there + 1 - c, 1), :]


def mix_y_kernel(near_ref, got_ref, near_y_ref, far_y_ref):
    for i, held in enumerate((near_ref, got_ref)):
        rows = slice(i * STEPS, (i + 1) * STEPS)
        near_y_ref[rows, :] = held[:STEPS, :]
        far_y_ref[rows, :] = held[STEPS:, :]


def mix_z_kernel(near_ref, got_ref, *outs):
    for k, out in enumerate(outs):
        out[...] = jnp.zeros_like(out)
        for i, held in enumerate((near_ref, got_ref)):
            for c in range(2):
                row = c * STEPS + k
                out[2 * i + c : 2 * i + c + 1, :] = held[row : row + 1, :]


def small(kernel, n, name, *args, scalars=0):
    return pl.pallas_call(
        kernel,
        in_specs=[SMEM] * scalars + [VMEM] * (len(args) - scalars),
        out_specs=[VMEM] * n,
        out_shape=[shape((8, LANES), jnp.int32)] * n,
        compiler_params=params(8),
        cost_estimate=cost(1e4, 3e4),
        name=name,
    )(*args)


def exchange_lists(me, lists):
    near, far = small(pick_kernel, 2, "pick", me, lists, scalars=1)
    near, far = small(mix_y_kernel, 2, "mix_y", near, over_core(far))
    own, *sent = small(mix_z_kernel, STEPS, "mix_z", near, over_y(far))
    return [own] + [over_z(sent[k - 1], k) for k in range(1, STEPS)]


def exponent(m):
    return jnp.clip(jnp.ceil(jnp.log2(jnp.maximum(m, 1e-30))), -100.0, 100.0)


def whole16(x):
    return x.astype(jnp.int32).astype(jnp.int16)


def wide(x):
    return x.astype(jnp.int32).astype(F32)


def pack(out_ref, t, sums=None):
    rows, width = t.shape
    e = exponent(jnp.max(jnp.abs(t), axis=0, keepdims=True))
    out_ref[pl.ds(0, rows), :] = whole16(jnp.round(t * (jnp.exp2(-e) * TOP)))
    head = [e]
    if sums is not None:
        for i in range(2):
            v = sums[i : i + 1, :]
            f = exponent(v)
            v = v * (jnp.exp2(-f) * 16384.0)
            first = jnp.floor(v)
            head += [f, first, jnp.floor((v - first) * 16384.0)]
    row = lax.broadcasted_iota(jnp.int32, (HEAD, width), 0)
    total = jnp.zeros((HEAD, width), F32)
    for i, h in enumerate(head):
        total = jnp.where(row == i, h, total)
    out_ref[pl.ds(rows, HEAD), :] = whole16(total)


def unpack(ref):
    rows = ref.shape[0] - HEAD
    head = wide(ref[pl.ds(rows, HEAD), :])
    return wide(ref[pl.ds(0, rows), :]) * (jnp.exp2(head[0:1, :]) * (1.0 / TOP))


def unpack_sums(ref):
    head = wide(ref[pl.ds(ref.shape[0] - HEAD, HEAD), :])
    row = lax.broadcasted_iota(jnp.int32, (8, head.shape[1]), 0)
    total = jnp.zeros(row.shape, F32)
    for i in range(2):
        f, first, second = [head[1 + 3 * i + j : 2 + 3 * i + j, :] for j in range(3)]
        v = (first + second * (1.0 / 16384.0)) * (jnp.exp2(f) * (1.0 / 16384.0))
        total = jnp.where(row == i, v, total)
    return total


def merge_y_kernel(with_sums, *refs):
    if with_sums:
        a_ref, b_ref, mine_ref, first_ref, second_ref, s_ref = refs
        sums = mine_ref[...] + b_ref[pl.ds(a_ref.shape[0], 8), :]
        s_ref[...] = sums
    else:
        a_ref, b_ref, first_ref, second_ref = refs
        sums = None
    half = a_ref.shape[0] // 2
    pack(first_ref, a_ref[pl.ds(0, half), :] + b_ref[pl.ds(0, half), :], sums)
    pack(second_ref, a_ref[pl.ds(half, half), :] + b_ref[pl.ds(half, half), :])


def merge_y(a, b, sums):
    rows, width = a.shape
    out = [shape((rows // 2 + HEAD, width), jnp.int16)] * 2
    args = [a, b]
    if sums is not None:
        out.append(shape((8, width), F32))
        args.append(sums)
    return pl.pallas_call(
        functools.partial(merge_y_kernel, sums is not None),
        in_specs=[VMEM] * len(args),
        out_specs=[VMEM] * len(out),
        out_shape=out,
        compiler_params=params(8),
        cost_estimate=cost(5 * rows * width, 1e6),
        name="merge_y",
    )(*args)


def merge_z_kernel(last, with_sums, a_ref, b_ref, p_ref, *refs):
    half = a_ref.shape[0] // 2
    rows = pl.ds(half if last else 0, half)
    t = a_ref[rows, :] + b_ref[rows, :] + unpack(p_ref)
    sums = None
    if with_sums:
        sums = refs[0][...]
        refs = refs[1:]
        if not last:
            sums = sums + unpack_sums(p_ref)
            refs[2][...] = sums
    pack(refs[0], t[:LANES], sums)
    if last:
        refs[1][...] = t[LANES:]
    else:
        pack(refs[1], t[LANES:], sums)


def merge_z(last, a, b, p, sums):
    width = a.shape[1]
    sent = shape((LANES + HEAD, width), jnp.int16)
    out = [sent, shape((LANES, width), F32) if last else sent]
    args = [a, b, p]
    if sums is not None:
        args.append(sums)
        if not last:
            out.append(shape((8, width), F32))
    return pl.pallas_call(
        functools.partial(merge_z_kernel, last, sums is not None),
        in_specs=[VMEM] * len(args),
        out_specs=[VMEM] * len(out),
        out_shape=out,
        compiler_params=params(8),
        cost_estimate=cost(5 * a.size, 1e6),
        name="merge_z_last" if last else "merge_z_first",
    )(*args)


def join_kernel(*refs):
    for i, r in enumerate(refs[:-1]):
        refs[-1][i] = r[...]


def relay_kernel(x_ref, after_ref, out_ref):
    out_ref[...] = x_ref[...]


def copy_of(kernel, name, out, *args):
    return pl.pallas_call(
        kernel,
        in_specs=[VMEM] * len(args),
        out_specs=VMEM,
        out_shape=out,
        compiler_params=params(8),
        cost_estimate=cost(1e5, 5e5),
        name=name,
    )(*args)


def fold(a):
    return jnp.sum(a, axis=0, keepdims=True)


def length_of(sums):
    grad = jnp.sum(sums[0:1, :], axis=1, keepdims=True)
    image = jnp.sum(sums[1:2, :], axis=1, keepdims=True)
    return grad / (grad + image), image / (grad + image)


def products(e, y, held, rows):
    p = e.astype(F32) * y
    q = p[:, :LANES] + p[:, LANES:]
    q = q + pltpu.roll(q, LANES // 2, 1)
    high, low = halves(q)
    held[rows, :LANES] = high
    held[rows, LANES:] = low


BATCH = 16
SOME = 8


def coarse_kernel(packed, second, after, e_ref, k_ref, own_ref, *refs):
    refs = list(refs)
    got = [refs.pop(0) for _ in range(packed)]
    y = own_ref[...]
    for r in got:
        y = y + unpack(r)
    if second:
        y0_ref, s_ref = refs.pop(0), refs.pop(0)
        sums = s_ref[...]
        for r in got:
            sums = sums + unpack_sums(r)
        l0, keep = length_of(sums)
        y = keep * y0_ref[...] - l0 * y
        refs.pop(after + 2)[...] = jnp.broadcast_to(l0, (8, LANES))
    x_ref, y_ref, sum_ref, even_s, odd_s, x_s = refs[after:]
    members, columns, width = e_ref.shape
    y_ref[...] = y
    x_s[...] = jnp.zeros_like(x_s)

    def build(i, held):
        for m in range(SOME):
            products(e_ref[i * SOME + m], y_ref[...], held, pl.ds(m * columns, columns))

    def add_in(i, t):
        total = x_s[...]
        for m in range(SOME):
            total = total + t[m * columns : (m + 1) * columns] * e_ref[i * SOME + m].astype(F32)
        x_s[...] = total

    pairs = members // SOME // 2
    build(0, even_s)

    @pl.loop(0, pairs - 1)
    def _(i):
        t = dot(even_s[...], k_ref[...])
        build(2 * i + 1, odd_s)
        add_in(2 * i, t)
        t = dot(odd_s[...], k_ref[...])
        build(2 * i + 2, even_s)
        add_in(2 * i + 1, t)

    t = dot(even_s[...], k_ref[...])
    build(2 * pairs - 1, odd_s)
    add_in(2 * pairs - 2, t)
    add_in(2 * pairs - 1, dot(odd_s[...], k_ref[...]))

    x = x_s[...]
    x_ref[...] = x.T.astype(BF)
    sum_ref[...] = jnp.zeros_like(sum_ref)
    sum_ref[0:1, :] = fold(x * y_ref[...])


def coarse_image(ensemble, kern, own, got, y0=None, sums=None, after=()):
    members, columns, width = ensemble.shape
    second = y0 is not None
    args = [ensemble, kern, own, *got] + ([y0, sums] if second else []) + list(after)
    out = [shape((width, columns), BF), shape((columns, width), F32)]
    out += [shape((8, LANES), F32)] if second else []
    out += [shape((8, width), F32)]
    return pl.pallas_call(
        functools.partial(coarse_kernel, len(got), second, len(after)),
        in_specs=[VMEM] * (len(args) - len(after)) + [ANY] * len(after),
        out_specs=[VMEM] * len(out),
        out_shape=out,
        scratch_shapes=[
            pltpu.VMEM((SOME * columns, width), BF),
            pltpu.VMEM((SOME * columns, width), BF),
            pltpu.VMEM((columns, width), F32),
        ],
        compiler_params=params(16),
        cost_estimate=cost(2 * columns * members * width * width, 5e6),
        name="coarse_second" if second else "coarse_first",
    )(*args)


def project_kernel(e_ref, y_ref, t_ref, after_ref, g_ref, token_ref, even_s, odd_s):
    columns, members, width = e_ref.shape
    lanes = BATCH // 2 * LANES
    token_ref[...] = jnp.zeros_like(token_ref)

    @pl.loop(0, columns // BATCH)
    def _(i):
        base = pl.multiple_of(i * BATCH, BATCH)
        yb = y_ref[pl.ds(base, BATCH), :]
        for c in range(BATCH):
            held = odd_s if c % 2 else even_s
            rows = pl.ds((c // 2) * members, members)
            products(e_ref[base + c], yb[c : c + 1, :], held, rows)
        r = dot(even_s[...], t_ref[0]) + dot(odd_s[...], t_ref[1])
        for pair in range(BATCH // 2):
            at = pl.multiple_of(i * lanes + pair * LANES, LANES)
            g_ref[:, pl.ds(at, LANES)] = r[pair * members : (pair + 1) * members]


def project(ens, y, taps, after):
    columns, members, width = ens.shape
    levels = width // VAR
    return pl.pallas_call(
        project_kernel,
        in_specs=[VMEM] * 4,
        out_specs=[VMEM] * 2,
        out_shape=[shape((members, columns * levels), F32), shape((8, LANES), F32)],
        scratch_shapes=[pltpu.VMEM((BATCH // 2 * members, width), BF)] * 2,
        compiler_params=params(16),
        cost_estimate=cost(2 * columns * members * width * width, 8e6),
        name="project",
    )(ens, y, taps, after)


def lay_out(x_refs, xs):
    if len(x_refs[0].shape) == 2:
        xs[...] = x_refs[0][...]
        return
    for i, x in enumerate(x_refs):
        for n in range(STEPS):
            xs[:, pl.ds((i * STEPS + n) * LANES, LANES)] = x[n]


CUTS = 3


def part_kernel(*refs):
    *x_refs, near_ref, far_ref, out_ref, xs = refs
    lay_out(x_refs, xs)
    half, fine = near_ref.shape
    rows = fine // CUTS
    for i in range(CUTS):
        some = pl.ds(i * rows, rows)
        out_ref[:, some] = dot(xs[:, :half], near_ref[:, some]) + dot(
            xs[:, half:], far_ref[pl.ds(0, xs.shape[1] - half), some]
        )


def image_part(xs, near, far, width):
    half, fine = near.shape
    return pl.pallas_call(
        part_kernel,
        in_specs=[VMEM] * (len(xs) + 2),
        out_specs=VMEM,
        out_shape=shape((width, fine), F32),
        scratch_shapes=[pltpu.VMEM((width, len(xs) * STEPS * LANES), BF)],
        compiler_params=params(16),
        cost_estimate=cost(3 * half * fine * width, 4e6),
        name="image_part",
    )(*xs, near, far)


def images(x_ref, part_ref, near_ref, far_ref, obs_ref, im_ref, xs):
    lay_out([x_ref], xs)
    half, fine = near_ref.shape
    rows = fine // CUTS
    for i in range(CUTS):
        some = pl.ds(i * rows, rows)
        if part_ref is None:
            turned = dot(xs[:, :half], near_ref[:, some]) + dot(xs[:, half:], far_ref[:, some])
        else:
            last = xs.shape[1]
            turned = dot(xs[...], far_ref[pl.ds(half - last, last), some]) + part_ref[:, some]
        im = turned.T
        im_ref[some, :] = im
        yield some, im, obs_ref[some, :].astype(F32) * im


def image_kernel(parts, first, x_ref, *refs):
    part_ref, refs = (refs[0], refs[1:]) if parts else (None, refs)
    near_ref, far_ref, obs_ref, g_ref, im_ref, sum_ref, *refs = refs
    if first:
        v_ref, *outs, xs = refs
    else:
        (xs,) = refs
    sums = g_ref[...]
    row = lax.broadcasted_iota(jnp.int32, sums.shape, 0)
    for some, im, v in images(x_ref, part_ref, near_ref, far_ref, obs_ref, im_ref, xs):
        if first:
            v_ref[some, :] = v.astype(BF)
        sums = sums + jnp.where(row == 1, fold(v * im), 0.0)
    sum_ref[...] = sums
    if first:
        rows = near_ref.shape[0] // 2
        for i in (1, 0):
            outs[i][pl.ds(0, rows), :] = dot(far_ref[pl.ds(i * rows, rows), :], v_ref[...])
        outs[1][pl.ds(rows, 8), :] = sums


def image_of(xs, near, far, obs, g_sums, first):
    half, fine = near.shape
    width = obs.shape[1]
    part = [image_part(xs[:-1], near, far, width)] if len(xs) > 1 else []
    out = [shape((fine, width), F32), shape((8, width), F32)]
    if first:
        out += [shape((fine, width), BF)]
        out += [shape((half // 2, width), F32), shape((half // 2 + 8, width), F32)]
    last = STEPS * LANES if part else 2 * half
    return pl.pallas_call(
        functools.partial(image_kernel, bool(part), first),
        in_specs=[VMEM] * (5 + len(part)),
        out_specs=[VMEM] * len(out),
        out_shape=out,
        scratch_shapes=[pltpu.VMEM((width, last), BF)],
        compiler_params=params(16),
        cost_estimate=cost(3 * half * fine * width, 8e6),
        name="image_first" if first else "image_second",
    )(xs[-1], *part, near, far, obs, g_sums)


def back_kernel(near_ref, v_ref, *outs):
    rows = near_ref.shape[0] // 2
    for i, out in enumerate(outs):
        out[...] = dot(near_ref[pl.ds(i * rows, rows), :], v_ref[...])


def back_near(near, v):
    half, fine = near.shape
    width = v.shape[1]
    return pl.pallas_call(
        back_kernel,
        in_specs=[VMEM] * 2,
        out_specs=[VMEM] * 2,
        out_shape=[shape((half // 2, width), F32)] * 2,
        compiler_params=params(16),
        cost_estimate=cost(2 * half * fine * width, 4e6),
        name="back_near",
    )(near, v)


OUT_CUTS = 4


def result_kernel(count, l0_ref, *refs):
    sums = refs[0][...]
    for r in refs[1:count]:
        sums = sums + r[...]
    g0_ref, g1_ref, i0_ref, i1_ref, control_hbm, increment_hbm, c_s, i_s, sem = refs[count:]
    l0 = -l0_ref[0:1, 0:1]
    l1, _ = length_of(sums)
    lanes = c_s.shape[1] // OUT_CUTS
    rows = i_s.shape[0] // OUT_CUTS
    copies = []
    for i in range(OUT_CUTS):
        some = pl.ds(i * lanes, lanes)
        c_s[:, some] = l0 * g0_ref[:, some] - l1 * g1_ref[:, some]
        copies.append(
            pltpu.make_async_copy(c_s.at[:, some], control_hbm.at[:, some], sem.at[2 * i])
        )
        copies[-1].start()
        some = pl.ds(i * rows, rows)
        i_s[some, :] = l0 * i0_ref[some, :] - l1 * i1_ref[some, :]
        copies.append(
            pltpu.make_async_copy(i_s.at[some, :], increment_hbm.at[some, :], sem.at[2 * i + 1])
        )
        copies[-1].start()
    for copy in copies:
        copy.wait()


def result(l0, sums, g0, g1, im0, im1):
    return pl.pallas_call(
        functools.partial(result_kernel, len(sums)),
        in_specs=[VMEM] * (5 + len(sums)),
        out_specs=[ANY] * 2,
        out_shape=[shape(g0.shape, F32), shape(im0.shape, F32)],
        scratch_shapes=[
            pltpu.VMEM(g0.shape, F32),
            pltpu.VMEM(im0.shape, F32),
            pltpu.SemaphoreType.DMA((2 * OUT_CUTS,)),
        ],
        compiler_params=params(16),
        cost_estimate=cost(3 * g0.size, 1e7),
        name="result",
    )(l0, *sums, g0, g1, im0, im1)


def over_core(x):
    return lax.ppermute(x, "space", [(i, i ^ 1) for i in range(GROUP)])


def over_y(x):
    return lax.ppermute(x, "space", [(i, i ^ 2) for i in range(GROUP)])


def over_z(x, k):
    return lax.ppermute(x, "space", [(i, i ^ (4 * k)) for i in range(GROUP)])


def scatter_sums(parts, sums=None):
    near, far_y, near_c, far_yc = parts
    got_yc = over_core(far_yc)
    got_c = over_core(near_c)
    first, second, *s = merge_y(far_y, got_yc, sums)
    first, second = over_y(first), over_y(second)
    two, three, *s = merge_z(False, near, got_c, first, s[0] if s else None)
    got = [over_z(two, 2), over_z(three, 3)]
    one, own = merge_z(True, near, got_c, second, s[0] if s else None)
    return own, got + [over_z(one, 1)], (s[0] if s else None)


def gather_columns(x, work):
    four = shape((STEPS,) + x.shape, BF)
    a = copy_of(join_kernel, "join", four, *[over_z(x, k) for k in ORDER[:3]], x)
    ya, ca = over_y(a), over_core(a)
    done, token = work(a)
    ya = copy_of(relay_kernel, "relay", four, ya, token)
    return [a, ya, ca, over_core(ya)], done


def sum_all(x):
    x = x + over_core(x)
    x = x + over_y(x)
    return [x] + [over_z(x, k) for k in range(1, STEPS)]


def on_device(ensemble, innovation, obs_weight, interp_weight, slot_of, intersection_list):
    members, columns, width = ensemble.shape
    levels = width // VAR
    devices = lax.axis_size("space")
    capacity = intersection_list.shape[2]
    slots = devices * capacity
    grouped = devices == GROUP and capacity == columns == LANES

    taper = vertical_taper(levels)
    both = taper.astype(np.float64) @ taper.T.astype(np.float64)
    kern = np.tile(np.concatenate(host_halves(both), axis=0), (2, VAR))
    tall = np.tile(np.concatenate(host_halves(taper), axis=0), (2, 1))
    none = np.zeros_like(tall)
    taps = np.stack(
        [np.concatenate([tall, none], axis=1), np.concatenate([none, tall], axis=1)]
    )
    kern, taps = jnp.asarray(kern), jnp.asarray(taps)

    index = lax.axis_index("space").astype(jnp.int32)
    me = jnp.stack([index // 4, index // 2 % 2, index % 2, index])
    w = -(obs_weight.astype(F32) * innovation.astype(F32))
    high = lax.reduce_precision(w, 8, 7)
    wh, wl = high.astype(BF), (w - high).astype(BF)
    named = jnp.concatenate([slot_of.astype(F32), interp_weight], axis=0)
    if grouped:
        lists = exchange_lists(me, intersection_list[0])
        scatter, gather, add_up = scatter_sums, gather_columns, sum_all
    else:
        lists = intersection_list[0]
        hit = (lists.reshape(-1, 1) == jnp.arange(columns, dtype=jnp.int32)).astype(BF)

        def swap(x):
            x = x.reshape(devices, capacity, width)
            x = lax.all_to_all(x, "space", split_axis=0, concat_axis=0, tiled=True)
            return x.reshape(slots, width)

        def scatter(parts, sums=None):
            got = swap(jnp.concatenate([p[: slots // 4] for p in parts], axis=0))
            high = lax.reduce_precision(got, 8, 7)
            high, low = high.astype(BF), (got - high).astype(BF)
            if sums is not None:
                sums = lax.psum(sums, "space")
            return dot(hit.T, high) + dot(hit.T, low), [], sums

        def gather(x, work):
            return [swap(dot(hit, x.T).astype(BF)).T], work(x)[0]

        def add_up(x):
            return [lax.psum(x, "space")]

    ids, weight, far, c0, c1 = adjoint_half(slots, [named, wh, wl], (grouped, me, lists if grouped else []))
    near, n0, n1 = adjoint_half(slots, [ids, weight, wh, wl])
    own, got, _ = scatter([n0, n1, c0, c1])
    ens = jnp.transpose(ensemble, (1, 0, 2))
    x0, y0, g_sums = coarse_image(ensemble, kern, own, got, after=[ens])
    xs, g0 = gather(x0, lambda after: project(ens, y0, taps, after))
    im0, sums, v, c0, c1 = image_of(xs, near, far, obs_weight, g_sums, True)
    own, got, sums = scatter([*back_near(near, v), c0, c1], sums)
    x1, y1, l0, g_sums = coarse_image(ensemble, kern, own, got, y0, sums)
    xs, g1 = gather(x1, lambda after: project(ens, y1, taps, after))
    im1, sums = image_of(xs, near, far, obs_weight, g_sums, False)
    return tuple(result(l0, add_up(sums), g0, g1, im0, im1))


def solution(mesh):
    placed = (
        P("case", "space", None),
        P(("case", "space"), None),
        P(("case", "space"), None),
        P("case", "space"),
        P("case", "space"),
        P(("case", "space"), None, None),
    )
    return jax.shard_map(
        on_device,
        mesh=mesh,
        in_specs=placed,
        out_specs=(P("case", "space"), P(("case", "space"), None)),
        check_vma=False,
    )
```

```python
import functools

import jax
import jax.numpy as jnp
import ml_dtypes
import numpy as np
from jax import lax
from jax.experimental import pallas as pl
from jax.experimental.pallas import tpu as pltpu
from jax.sharding import PartitionSpec as P

VAR = 4
LOC_SCALE = 3.0
BF = jnp.bfloat16
F32 = jnp.float32
LANES = 128
GROUP = 16
VMEM = pl.BlockSpec(memory_space=pltpu.VMEM)
SMEM = pl.BlockSpec(memory_space=pltpu.SMEM)
ANY = pl.BlockSpec(memory_space=pl.ANY)


def vertical_taper(levels):
    heights = np.arange(levels).astype(np.float32)
    spread = (heights[:, None] - heights[None, :]) / np.float32(LOC_SCALE)
    return np.exp(np.float32(-0.5) * spread * spread)


def host_halves(x):
    high = x.astype(ml_dtypes.bfloat16)
    return [high, (x - high.astype(x.dtype)).astype(ml_dtypes.bfloat16)]


def params(mib):
    return pltpu.CompilerParams(vmem_limit_bytes=mib << 20)


def cost(flops, nbytes):
    return pl.CostEstimate(flops=int(flops), bytes_accessed=int(nbytes), transcendentals=0)


def dot(a, b):
    return jnp.dot(a, b, preferred_element_type=F32)


def halves(x):
    high = x.astype(BF)
    return high, (x - high.astype(F32)).astype(BF)


def shape(dims, dtype):
    return jax.ShapeDtypeStruct(dims, dtype)


STEPS = 4
ORDER = (2, 3, 1, 0)
PARTS = ((0, 0), (1, 0), (0, 1), (1, 1))
HEAD = 16
TOP = 32512.0


def owner_at(me_ref, i):
    dy, dc = PARTS[i // STEPS]
    z, y, c = me_ref[0], me_ref[1], me_ref[2]
    y = y if dy == 0 else 1 - y
    c = c if dc == 0 else 1 - c
    return (jnp.bitwise_xor(z, ORDER[i % STEPS]) * 2 + y) * 2 + c


def places(me_ref, list_refs, slots):
    slots = jnp.concatenate([slots, slots], axis=0)
    from_owner = jnp.right_shift(slots, 7)
    within = jnp.bitwise_and(slots, LANES - 1)
    rows = jnp.zeros(slots.shape, jnp.int32)
    for i in range(GROUP):
        o = owner_at(me_ref, i)
        dy, dc = PARTS[i // STEPS]
        held = list_refs[ORDER[i % STEPS]]
        row = jnp.broadcast_to(held[2 * dy + dc : 2 * dy + dc + 1, :], slots.shape)
        column = jnp.take_along_axis(row, within, axis=1, mode="promise_in_bounds")
        rows = jnp.where(from_owner == o, column + i * LANES, rows)
    return rows[: slots.shape[0] // 2]


def build_rows(ids_ref, weight_ref, wh_ref, wl_ref, at_ref, y_refs, lo_s, base):
    sources, fine = ids_ref.shape
    rows = at_ref.shape[0] // len(y_refs)
    step = rows // 2
    row = lax.broadcasted_iota(jnp.int32, (step, LANES), 0)
    for n, y_ref in enumerate(y_refs):
        for m in range(2):
            start = n * rows + m * step
            for j in range(fine // LANES):
                lanes = pl.ds(j * LANES, LANES)
                total = None
                for b in range(sources):
                    ids = ids_ref[b : b + 1, lanes] - (base + start)
                    term = jnp.where(row == ids, weight_ref[b : b + 1, lanes], 0.0)
                    total = term if total is None else total + term
                high, low = halves(total)
                at_ref[pl.ds(start, step), lanes] = high
                lo_s[pl.ds(m * step, step), lanes] = low
        held = at_ref[pl.ds(n * rows, rows), :]
        y_ref[...] = dot(held, wh_ref[...]) + dot(held, wl_ref[...]) + dot(lo_s[...], wh_ref[...])


def far_kernel(grouped, me_ref, *refs):
    list_refs, refs = refs[: 4 * grouped], refs[4 * grouped :]
    both_ref, wh_ref, wl_ref, *refs = refs
    ids_ref, weight_ref, at_ref, ya_ref, yb_ref, lo_s = refs
    sources = ids_ref.shape[0]
    for j in range(ids_ref.shape[1] // LANES):
        lanes = pl.ds(j * LANES, LANES)
        slots = both_ref[:sources, lanes].astype(jnp.int32)
        ids_ref[:, lanes] = places(me_ref, list_refs, slots) if grouped else slots
        weight_ref[:, lanes] = both_ref[sources:, lanes]
    half = at_ref.shape[0]
    build_rows(ids_ref, weight_ref, wh_ref, wl_ref, at_ref, [ya_ref, yb_ref], lo_s, half)


def near_kernel(ids_ref, weight_ref, wh_ref, wl_ref, at_ref, ya_ref, yb_ref, lo_s):
    build_rows(ids_ref, weight_ref, wh_ref, wl_ref, at_ref, [ya_ref, yb_ref], lo_s, 0)


def adjoint_half(slots, args, head=None):
    fine, width = args[-1].shape
    half = slots // 2
    sources = args[0].shape[0] // (2 if head else 1)
    out = [shape((half, fine), BF)] + [shape((half // 2, width), F32)] * 2
    if head:
        grouped, me, lists = head
        kernel = functools.partial(far_kernel, grouped)
        args = [me, *lists, *args]
        out = [shape((sources, fine), jnp.int32), shape((sources, fine), F32)] + out
    else:
        kernel = near_kernel
    return pl.pallas_call(
        kernel,
        in_specs=([SMEM] if head else []) + [VMEM] * (len(args) - (1 if head else 0)),
        out_specs=[VMEM] * len(out),
        out_shape=out,
        scratch_shapes=[pltpu.VMEM((half // 2, fine), BF)],
        compiler_params=params(16),
        cost_estimate=cost(3 * slots * fine * width, 4e6),
        name="adjoint_far" if head else "adjoint_near",
    )(*args)


def pick_kernel(me_ref, lists_ref, near_ref, far_ref):
    z, y, c = me_ref[0], me_ref[1], me_ref[2]
    for dy in range(2):
        for k in range(STEPS):
            there = (jnp.bitwise_xor(z, k) * 2 + (y if dy == 0 else 1 - y)) * 2
            row = slice(dy * STEPS + k, dy * STEPS + k + 1)
            near_ref[row, :] = lists_ref[pl.ds(there + c, 1), :]
            far_ref[row, :] = lists_ref[pl.ds(there + 1 - c, 1), :]


def mix_y_kernel(near_ref, got_ref, near_y_ref, far_y_ref):
    for i, held in enumerate((near_ref, got_ref)):
        rows = slice(i * STEPS, (i + 1) * STEPS)
        near_y_ref[rows, :] = held[:STEPS, :]
        far_y_ref[rows, :] = held[STEPS:, :]


def mix_z_kernel(near_ref, got_ref, *outs):
    for k, out in enumerate(outs):
        out[...] = jnp.zeros_like(out)
        for i, held in enumerate((near_ref, got_ref)):
            for c in range(2):
                row = c * STEPS + k
                out[2 * i + c : 2 * i + c + 1, :] = held[row : row + 1, :]


def small(kernel, n, name, *args, scalars=0):
    return pl.pallas_call(
        kernel,
        in_specs=[SMEM] * scalars + [VMEM] * (len(args) - scalars),
        out_specs=[VMEM] * n,
        out_shape=[shape((8, LANES), jnp.int32)] * n,
        compiler_params=params(8),
        cost_estimate=cost(1e4, 3e4),
        name=name,
    )(*args)


def exchange_lists(me, lists):
    near, far = small(pick_kernel, 2, "pick", me, lists, scalars=1)
    near, far = small(mix_y_kernel, 2, "mix_y", near, over_core(far))
    own, *sent = small(mix_z_kernel, STEPS, "mix_z", near, over_y(far))
    three, two, one = [over_z(sent[k - 1], k) for k in (3, 2, 1)]
    return [own, one, two, three]


def exponent(m):
    return jnp.clip(jnp.ceil(jnp.log2(jnp.maximum(m, 1e-30))), -100.0, 100.0)


def whole16(x):
    return x.astype(jnp.int32).astype(jnp.int16)


def wide(x):
    return x.astype(jnp.int32).astype(F32)


def pack(out_ref, t, sums=None):
    rows, width = t.shape
    e = exponent(jnp.max(jnp.abs(t), axis=0, keepdims=True))
    out_ref[pl.ds(0, rows), :] = whole16(jnp.round(t * (jnp.exp2(-e) * TOP)))
    head = [e]
    if sums is not None:
        for i in range(2):
            v = sums[i : i + 1, :]
            f = exponent(v)
            v = v * (jnp.exp2(-f) * 16384.0)
            first = jnp.floor(v)
            head += [f, first, jnp.floor((v - first) * 16384.0)]
    row = lax.broadcasted_iota(jnp.int32, (HEAD, width), 0)
    total = jnp.zeros((HEAD, width), F32)
    for i, h in enumerate(head):
        total = jnp.where(row == i, h, total)
    out_ref[pl.ds(rows, HEAD), :] = whole16(total)


def unpack(ref):
    rows = ref.shape[0] - HEAD
    head = wide(ref[pl.ds(rows, HEAD), :])
    return wide(ref[pl.ds(0, rows), :]) * (jnp.exp2(head[0:1, :]) * (1.0 / TOP))


def unpack_sums(ref):
    head = wide(ref[pl.ds(ref.shape[0] - HEAD, HEAD), :])
    row = lax.broadcasted_iota(jnp.int32, (8, head.shape[1]), 0)
    total = jnp.zeros(row.shape, F32)
    for i in range(2):
        f, first, second = [head[1 + 3 * i + j : 2 + 3 * i + j, :] for j in range(3)]
        v = (first + second * (1.0 / 16384.0)) * (jnp.exp2(f) * (1.0 / 16384.0))
        total = jnp.where(row == i, v, total)
    return total


def merge_y_kernel(with_sums, *refs):
    if with_sums:
        a_ref, b_ref, mine_ref, first_ref, second_ref, s_ref = refs
        sums = mine_ref[...] + b_ref[pl.ds(a_ref.shape[0], 8), :]
        s_ref[...] = sums
    else:
        a_ref, b_ref, first_ref, second_ref = refs
        sums = None
    half = a_ref.shape[0] // 2
    pack(first_ref, a_ref[pl.ds(0, half), :] + b_ref[pl.ds(0, half), :], sums)
    pack(second_ref, a_ref[pl.ds(half, half), :] + b_ref[pl.ds(half, half), :])


def merge_y(a, b, sums):
    rows, width = a.shape
    out = [shape((rows // 2 + HEAD, width), jnp.int16)] * 2
    args = [a, b]
    if sums is not None:
        out.append(shape((8, width), F32))
        args.append(sums)
    return pl.pallas_call(
        functools.partial(merge_y_kernel, sums is not None),
        in_specs=[VMEM] * len(args),
        out_specs=[VMEM] * len(out),
        out_shape=out,
        compiler_params=params(8),
        cost_estimate=cost(5 * rows * width, 1e6),
        name="merge_y",
    )(*args)


def merge_z_kernel(last, with_sums, a_ref, b_ref, p_ref, *refs):
    half = a_ref.shape[0] // 2
    rows = pl.ds(half if last else 0, half)
    t = a_ref[rows, :] + b_ref[rows, :] + unpack(p_ref)
    sums = None
    if with_sums:
        sums = refs[0][...]
        refs = refs[1:]
        if not last:
            sums = sums + unpack_sums(p_ref)
            refs[2][...] = sums
    pack(refs[0], t[:LANES], sums)
    if last:
        refs[1][...] = t[LANES:]
    else:
        pack(refs[1], t[LANES:], sums)


def merge_z(last, a, b, p, sums):
    width = a.shape[1]
    sent = shape((LANES + HEAD, width), jnp.int16)
    out = [sent, shape((LANES, width), F32) if last else sent]
    args = [a, b, p]
    if sums is not None:
        args.append(sums)
        if not last:
            out.append(shape((8, width), F32))
    return pl.pallas_call(
        functools.partial(merge_z_kernel, last, sums is not None),
        in_specs=[VMEM] * len(args),
        out_specs=[VMEM] * len(out),
        out_shape=out,
        compiler_params=params(8),
        cost_estimate=cost(5 * a.size, 1e6),
        name="merge_z_last" if last else "merge_z_first",
    )(*args)


def join_kernel(*refs):
    for i, r in enumerate(refs[:2]):
        refs[-1][i] = r[...]


def relay_kernel(x_ref, after_ref, out_ref):
    out_ref[...] = x_ref[...]


def copy_of(kernel, name, out, *args):
    return pl.pallas_call(
        kernel,
        in_specs=[VMEM] * len(args),
        out_specs=VMEM,
        out_shape=out,
        compiler_params=params(8),
        cost_estimate=cost(1e5, 5e5),
        name=name,
    )(*args)


def fold(a):
    return jnp.sum(a, axis=0, keepdims=True)


def length_of(sums):
    grad = jnp.sum(sums[0:1, :], axis=1, keepdims=True)
    image = jnp.sum(sums[1:2, :], axis=1, keepdims=True)
    return grad / (grad + image), image / (grad + image)


def products(e, y, held, rows):
    p = e.astype(F32) * y
    q = p[:, :LANES] + p[:, LANES:]
    q = q + pltpu.roll(q, LANES // 2, 1)
    high, low = halves(q)
    held[rows, :LANES] = high
    held[rows, LANES:] = low


BATCH = 16
SOME = 8


def coarse_kernel(packed, second, after, e_ref, k_ref, own_ref, *refs):
    refs = list(refs)
    got = [refs.pop(0) for _ in range(packed)]
    y = own_ref[...]
    for r in got:
        y = y + unpack(r)
    if second:
        y0_ref, s_ref = refs.pop(0), refs.pop(0)
        sums = s_ref[...]
        for r in got:
            sums = sums + unpack_sums(r)
        l0, keep = length_of(sums)
        y = keep * y0_ref[...] - l0 * y
        refs.pop(after + 2)[...] = jnp.broadcast_to(l0, (8, LANES))
    x_ref, y_ref, sum_ref, even_s, odd_s, x_s = refs[after:]
    members, columns, width = e_ref.shape
    y_ref[...] = y
    x_s[...] = jnp.zeros_like(x_s)

    def build(i, held):
        for m in range(SOME):
            products(e_ref[i * SOME + m], y_ref[...], held, pl.ds(m * columns, columns))

    def add_in(i, t):
        total = x_s[...]
        for m in range(SOME):
            total = total + t[m * columns : (m + 1) * columns] * e_ref[i * SOME + m].astype(F32)
        x_s[...] = total

    pairs = members // SOME // 2
    build(0, even_s)

    @pl.loop(0, pairs - 1)
    def _(i):
        t = dot(even_s[...], k_ref[...])
        build(2 * i + 1, odd_s)
        add_in(2 * i, t)
        t = dot(odd_s[...], k_ref[...])
        build(2 * i + 2, even_s)
        add_in(2 * i + 1, t)

    t = dot(even_s[...], k_ref[...])
    build(2 * pairs - 1, odd_s)
    add_in(2 * pairs - 2, t)
    add_in(2 * pairs - 1, dot(odd_s[...], k_ref[...]))

    x = x_s[...]
    x_ref[...] = x.T.astype(BF)
    sum_ref[...] = jnp.zeros_like(sum_ref)
    sum_ref[0:1, :] = fold(x * y_ref[...])


def coarse_image(ensemble, kern, own, got, y0=None, sums=None, after=()):
    members, columns, width = ensemble.shape
    second = y0 is not None
    args = [ensemble, kern, own, *got] + ([y0, sums] if second else []) + list(after)
    out = [shape((width, columns), BF), shape((columns, width), F32)]
    out += [shape((8, LANES), F32)] if second else []
    out += [shape((8, width), F32)]
    return pl.pallas_call(
        functools.partial(coarse_kernel, len(got), second, len(after)),
        in_specs=[VMEM] * (len(args) - len(after)) + [ANY] * len(after),
        out_specs=[VMEM] * len(out),
        out_shape=out,
        scratch_shapes=[
            pltpu.VMEM((SOME * columns, width), BF),
            pltpu.VMEM((SOME * columns, width), BF),
            pltpu.VMEM((columns, width), F32),
        ],
        compiler_params=params(16),
        cost_estimate=cost(2 * columns * members * width * width, 5e6),
        name="coarse_second" if second else "coarse_first",
    )(*args)


def project_kernel(e_ref, y_ref, t_ref, after_ref, g_ref, token_ref, even_s, odd_s):
    columns, members, width = e_ref.shape
    lanes = BATCH // 2 * LANES
    token_ref[...] = jnp.zeros_like(token_ref)

    @pl.loop(0, columns // BATCH)
    def _(i):
        base = pl.multiple_of(i * BATCH, BATCH)
        yb = y_ref[pl.ds(base, BATCH), :]
        for c in range(BATCH):
            held = odd_s if c % 2 else even_s
            rows = pl.ds((c // 2) * members, members)
            products(e_ref[base + c], yb[c : c + 1, :], held, rows)
        r = dot(even_s[...], t_ref[0]) + dot(odd_s[...], t_ref[1])
        for pair in range(BATCH // 2):
            at = pl.multiple_of(i * lanes + pair * LANES, LANES)
            g_ref[:, pl.ds(at, LANES)] = r[pair * members : (pair + 1) * members]


def project(ens, y, taps, after):
    columns, members, width = ens.shape
    levels = width // VAR
    return pl.pallas_call(
        project_kernel,
        in_specs=[VMEM] * 4,
        out_specs=[VMEM] * 2,
        out_shape=[shape((members, columns * levels), F32), shape((8, LANES), F32)],
        scratch_shapes=[pltpu.VMEM((BATCH // 2 * members, width), BF)] * 2,
        compiler_params=params(16),
        cost_estimate=cost(2 * columns * members * width * width, 8e6),
        name="project",
    )(ens, y, taps, after)


def lay_out(x_refs, xs):
    if len(x_refs[0].shape) == 2:
        xs[...] = x_refs[0][...]
        return
    for i, x in enumerate(x_refs):
        for n in range(2):
            xs[:, pl.ds((i * 2 + n) * LANES, LANES)] = x[n]


CUTS = 3
PAIR = 2 * LANES


def part_kernel(*refs):
    *x_refs, near_ref, far_ref, out_ref, xs = refs
    lay_out(x_refs, xs)
    half, fine = near_ref.shape
    split = half // 2
    rows = fine // CUTS
    for i in range(CUTS):
        some = pl.ds(i * rows, rows)
        out_ref[:, some] = (
            dot(xs[:, :half], near_ref[:, some])
            + dot(xs[:, half : half + split], far_ref[pl.ds(0, split), some])
            + dot(xs[:, half + split :], far_ref[pl.ds(split + PAIR, half - split - PAIR), some])
        )


def image_part(xs, near, far, width):
    half, fine = near.shape
    return pl.pallas_call(
        part_kernel,
        in_specs=[VMEM] * (len(xs) + 2),
        out_specs=VMEM,
        out_shape=shape((width, fine), F32),
        scratch_shapes=[pltpu.VMEM((width, len(xs) * PAIR), BF)],
        compiler_params=params(16),
        cost_estimate=cost(3 * half * fine * width, 4e6),
        name="image_part",
    )(*xs, near, far)


def images(x_ref, part_ref, near_ref, far_ref, obs_ref, im_ref, xs):
    lay_out([x_ref], xs)
    half, fine = near_ref.shape
    rows = fine // CUTS
    for i in range(CUTS):
        some = pl.ds(i * rows, rows)
        if part_ref is None:
            turned = dot(xs[:, :half], near_ref[:, some]) + dot(xs[:, half:], far_ref[:, some])
        else:
            turned = dot(xs[...], far_ref[pl.ds(half // 2, PAIR), some]) + part_ref[:, some]
        im = turned.T
        im_ref[some, :] = im
        yield some, im, obs_ref[some, :].astype(F32) * im


def image_kernel(parts, first, x_ref, *refs):
    part_ref, refs = (refs[0], refs[1:]) if parts else (None, refs)
    near_ref, far_ref, obs_ref, g_ref, im_ref, sum_ref, *refs = refs
    if first:
        v_ref, *outs, xs = refs
    else:
        (xs,) = refs
    sums = g_ref[...]
    row = lax.broadcasted_iota(jnp.int32, sums.shape, 0)
    for some, im, v in images(x_ref, part_ref, near_ref, far_ref, obs_ref, im_ref, xs):
        if first:
            v_ref[some, :] = v.astype(BF)
        sums = sums + jnp.where(row == 1, fold(v * im), 0.0)
    sum_ref[...] = sums
    if first:
        rows = near_ref.shape[0] // 2
        for i in (1, 0):
            outs[i][pl.ds(0, rows), :] = dot(far_ref[pl.ds(i * rows, rows), :], v_ref[...])
        outs[1][pl.ds(rows, 8), :] = sums


def image_of(xs, near, far, obs, g_sums, first):
    half, fine = near.shape
    width = obs.shape[1]
    part = [image_part(xs[:-1], near, far, width)] if len(xs) > 1 else []
    out = [shape((fine, width), F32), shape((8, width), F32)]
    if first:
        out += [shape((fine, width), BF)]
        out += [shape((half // 2, width), F32), shape((half // 2 + 8, width), F32)]
    last = PAIR if part else 2 * half
    return pl.pallas_call(
        functools.partial(image_kernel, bool(part), first),
        in_specs=[VMEM] * (5 + len(part)),
        out_specs=[VMEM] * len(out),
        out_shape=out,
        scratch_shapes=[pltpu.VMEM((width, last), BF)],
        compiler_params=params(16),
        cost_estimate=cost(3 * half * fine * width, 8e6),
        name="image_first" if first else "image_second",
    )(xs[-1], *part, near, far, obs, g_sums)


def back_kernel(near_ref, v_ref, *outs):
    rows = near_ref.shape[0] // 2
    for i, out in enumerate(outs):
        out[...] = dot(near_ref[pl.ds(i * rows, rows), :], v_ref[...])


def back_near(near, v):
    half, fine = near.shape
    width = v.shape[1]
    return pl.pallas_call(
        back_kernel,
        in_specs=[VMEM] * 2,
        out_specs=[VMEM] * 2,
        out_shape=[shape((half // 2, width), F32)] * 2,
        compiler_params=params(16),
        cost_estimate=cost(2 * half * fine * width, 4e6),
        name="back_near",
    )(near, v)


OUT_CUTS = 4


def result_kernel(count, l0_ref, *refs):
    sums = refs[0][...]
    for r in refs[1:count]:
        sums = sums + r[...]
    g0_ref, g1_ref, i0_ref, i1_ref, control_hbm, increment_hbm, c_s, i_s, sem = refs[count:]
    l0 = -l0_ref[0:1, 0:1]
    l1, _ = length_of(sums)
    lanes = c_s.shape[1] // OUT_CUTS
    rows = i_s.shape[0] // OUT_CUTS
    copies = []
    for i in range(OUT_CUTS):
        some = pl.ds(i * lanes, lanes)
        c_s[:, some] = l0 * g0_ref[:, some] - l1 * g1_ref[:, some]
        copies.append(
            pltpu.make_async_copy(c_s.at[:, some], control_hbm.at[:, some], sem.at[2 * i])
        )
        copies[-1].start()
        some = pl.ds(i * rows, rows)
        i_s[some, :] = l0 * i0_ref[some, :] - l1 * i1_ref[some, :]
        copies.append(
            pltpu.make_async_copy(i_s.at[some, :], increment_hbm.at[some, :], sem.at[2 * i + 1])
        )
        copies[-1].start()
    for copy in copies:
        copy.wait()


def result(l0, sums, g0, g1, im0, im1):
    return pl.pallas_call(
        functools.partial(result_kernel, len(sums)),
        in_specs=[VMEM] * (5 + len(sums)),
        out_specs=[ANY] * 2,
        out_shape=[shape(g0.shape, F32), shape(im0.shape, F32)],
        scratch_shapes=[
            pltpu.VMEM(g0.shape, F32),
            pltpu.VMEM(im0.shape, F32),
            pltpu.SemaphoreType.DMA((2 * OUT_CUTS,)),
        ],
        compiler_params=params(16),
        cost_estimate=cost(3 * g0.size, 1e7),
        name="result",
    )(l0, *sums, g0, g1, im0, im1)


def over_core(x):
    return lax.ppermute(x, "space", [(i, i ^ 1) for i in range(GROUP)])


def over_y(x):
    return lax.ppermute(x, "space", [(i, i ^ 2) for i in range(GROUP)])


def over_z(x, k):
    return lax.ppermute(x, "space", [(i, i ^ (4 * k)) for i in range(GROUP)])


def scatter_sums(parts, sums=None):
    near, far_y, near_c, far_yc = parts
    got_yc = over_core(far_yc)
    got_c = over_core(near_c)
    first, second, *s = merge_y(far_y, got_yc, sums)
    first, second = over_y(first), over_y(second)
    two, three, *s = merge_z(False, near, got_c, first, s[0] if s else None)
    got = [over_z(two, 2), over_z(three, 3)]
    one, own = merge_z(True, near, got_c, second, s[0] if s else None)
    return own, got + [over_z(one, 1)], (s[0] if s else None)


def gather_columns(x, work):
    two = shape((2,) + x.shape, BF)
    a = copy_of(join_kernel, "join_first", two, over_z(x, 1), x)
    ya, ca = over_y(a), over_core(a)
    b = copy_of(join_kernel, "join_second", two, over_z(x, 2), over_z(x, 3), ya)
    yb, cb, cya = over_y(b), over_core(b), over_core(ya)
    done, token = work(b)
    yb = copy_of(relay_kernel, "relay", two, yb, token)
    return [b, a, yb, ya, cb, ca, cya, over_core(yb)], done


def sum_all(x):
    x = x + over_core(x)
    x = x + over_y(x)
    return [x] + [over_z(x, k) for k in range(1, STEPS)]


def on_device(ensemble, innovation, obs_weight, interp_weight, slot_of, intersection_list):
    members, columns, width = ensemble.shape
    levels = width // VAR
    devices = lax.axis_size("space")
    capacity = intersection_list.shape[2]
    slots = devices * capacity
    grouped = devices == GROUP and capacity == columns == LANES

    taper = vertical_taper(levels)
    both = taper.astype(np.float64) @ taper.T.astype(np.float64)
    kern = np.tile(np.concatenate(host_halves(both), axis=0), (2, VAR))
    tall = np.tile(np.concatenate(host_halves(taper), axis=0), (2, 1))
    none = np.zeros_like(tall)
    taps = np.stack(
        [np.concatenate([tall, none], axis=1), np.concatenate([none, tall], axis=1)]
    )
    kern, taps = jnp.asarray(kern), jnp.asarray(taps)

    index = lax.axis_index("space").astype(jnp.int32)
    me = jnp.stack([index // 4, index // 2 % 2, index % 2, index])
    w = -(obs_weight.astype(F32) * innovation.astype(F32))
    high = lax.reduce_precision(w, 8, 7)
    wh, wl = high.astype(BF), (w - high).astype(BF)
    named = jnp.concatenate([slot_of.astype(F32), interp_weight], axis=0)
    if grouped:
        lists = exchange_lists(me, intersection_list[0])
        scatter, gather, add_up = scatter_sums, gather_columns, sum_all
    else:
        lists = intersection_list[0]
        hit = (lists.reshape(-1, 1) == jnp.arange(columns, dtype=jnp.int32)).astype(BF)

        def swap(x):
            x = x.reshape(devices, capacity, width)
            x = lax.all_to_all(x, "space", split_axis=0, concat_axis=0, tiled=True)
            return x.reshape(slots, width)

        def scatter(parts, sums=None):
            got = swap(jnp.concatenate([p[: slots // 4] for p in parts], axis=0))
            high = lax.reduce_precision(got, 8, 7)
            high, low = high.astype(BF), (got - high).astype(BF)
            if sums is not None:
                sums = lax.psum(sums, "space")
            return dot(hit.T, high) + dot(hit.T, low), [], sums

        def gather(x, work):
            return [swap(dot(hit, x.T).astype(BF)).T], work(x)[0]

        def add_up(x):
            return [lax.psum(x, "space")]

    ids, weight, far, c0, c1 = adjoint_half(slots, [named, wh, wl], (grouped, me, lists if grouped else []))
    near, n0, n1 = adjoint_half(slots, [ids, weight, wh, wl])
    own, got, _ = scatter([n0, n1, c0, c1])
    ens = jnp.transpose(ensemble, (1, 0, 2))
    x0, y0, g_sums = coarse_image(ensemble, kern, own, got, after=[ens])
    xs, g0 = gather(x0, lambda after: project(ens, y0, taps, after))
    im0, sums, v, c0, c1 = image_of(xs, near, far, obs_weight, g_sums, True)
    own, got, sums = scatter([*back_near(near, v), c0, c1], sums)
    x1, y1, l0, g_sums = coarse_image(ensemble, kern, own, got, y0, sums)
    xs, g1 = gather(x1, lambda after: project(ens, y1, taps, after))
    im1, sums = image_of(xs, near, far, obs_weight, g_sums, False)
    return tuple(result(l0, add_up(sums), g0, g1, im0, im1))


def solution(mesh):
    placed = (
        P("case", "space", None),
        P(("case", "space"), None),
        P(("case", "space"), None),
        P("case", "space"),
        P("case", "space"),
        P(("case", "space"), None, None),
    )
    return jax.shard_map(
        on_device,
        mesh=mesh,
        in_specs=placed,
        out_specs=(P("case", "space"), P(("case", "space"), None)),
        check_vma=False,
    )
```

```python
import functools

import jax
import jax.numpy as jnp
import ml_dtypes
import numpy as np
from jax import lax
from jax.experimental import pallas as pl
from jax.experimental.pallas import tpu as pltpu
from jax.sharding import PartitionSpec as P

VAR = 4
LOC_SCALE = 3.0
BF = jnp.bfloat16
F32 = jnp.float32
LANES = 128
GROUP = 16
VMEM = pl.BlockSpec(memory_space=pltpu.VMEM)
SMEM = pl.BlockSpec(memory_space=pltpu.SMEM)
ANY = pl.BlockSpec(memory_space=pl.ANY)


def vertical_taper(levels):
    heights = np.arange(levels).astype(np.float32)
    spread = (heights[:, None] - heights[None, :]) / np.float32(LOC_SCALE)
    return np.exp(np.float32(-0.5) * spread * spread)


def host_halves(x):
    high = x.astype(ml_dtypes.bfloat16)
    return [high, (x - high.astype(x.dtype)).astype(ml_dtypes.bfloat16)]


def params(mib):
    return pltpu.CompilerParams(vmem_limit_bytes=mib << 20)


def cost(flops, nbytes):
    return pl.CostEstimate(flops=int(flops), bytes_accessed=int(nbytes), transcendentals=0)


def dot(a, b):
    return jnp.dot(a, b, preferred_element_type=F32)


def halves(x):
    high = x.astype(BF)
    return high, (x - high.astype(F32)).astype(BF)


def shape(dims, dtype):
    return jax.ShapeDtypeStruct(dims, dtype)


STEPS = 4
ORDER = (2, 3, 1, 0)
LIST_ORDER = (1, 3, 0, 2)
PARTS = ((0, 0), (1, 0), (0, 1), (1, 1))
HEAD = 16
TOP = 32512.0


def owner_at(me_ref, i):
    dy, dc = PARTS[i // STEPS]
    z, y, c = me_ref[0], me_ref[1], me_ref[2]
    y = y if dy == 0 else 1 - y
    c = c if dc == 0 else 1 - c
    return (jnp.bitwise_xor(z, ORDER[i % STEPS]) * 2 + y) * 2 + c


def places(me_ref, list_refs, slots):
    slots = jnp.concatenate([slots, slots], axis=0)
    from_owner = jnp.right_shift(slots, 7)
    within = jnp.bitwise_and(slots, LANES - 1)
    rows = jnp.zeros(slots.shape, jnp.int32)
    for i in range(GROUP):
        o = owner_at(me_ref, i)
        dy, dc = PARTS[i // STEPS]
        k = ORDER[i % STEPS]
        row = k % 2 * STEPS + 2 * dy + dc
        row = jnp.broadcast_to(list_refs[k // 2][row : row + 1, :], slots.shape)
        column = jnp.take_along_axis(row, within, axis=1, mode="promise_in_bounds")
        rows = jnp.where(from_owner == o, column + i * LANES, rows)
    return rows[: slots.shape[0] // 2]


def build_rows(ids_ref, weight_ref, wh_ref, wl_ref, at_ref, y_refs, lo_s, base):
    sources, fine = ids_ref.shape
    rows = at_ref.shape[0] // len(y_refs)
    step = rows // 2
    row = lax.broadcasted_iota(jnp.int32, (step, LANES), 0)
    for n, y_ref in enumerate(y_refs):
        for m in range(2):
            start = n * rows + m * step
            for j in range(fine // LANES):
                lanes = pl.ds(j * LANES, LANES)
                total = None
                for b in range(sources):
                    ids = ids_ref[b : b + 1, lanes] - (base + start)
                    term = jnp.where(row == ids, weight_ref[b : b + 1, lanes], 0.0)
                    total = term if total is None else total + term
                high, low = halves(total)
                at_ref[pl.ds(start, step), lanes] = high
                lo_s[pl.ds(m * step, step), lanes] = low
        held = at_ref[pl.ds(n * rows, rows), :]
        y_ref[...] = dot(held, wh_ref[...]) + dot(held, wl_ref[...]) + dot(lo_s[...], wh_ref[...])


def far_kernel(grouped, me_ref, *refs):
    list_refs, refs = refs[: 2 * grouped], refs[2 * grouped :]
    both_ref, wh_ref, wl_ref, *refs = refs
    ids_ref, weight_ref, at_ref, ya_ref, yb_ref, lo_s = refs
    sources = ids_ref.shape[0]
    for j in range(ids_ref.shape[1] // LANES):
        lanes = pl.ds(j * LANES, LANES)
        slots = both_ref[:sources, lanes].astype(jnp.int32)
        ids_ref[:, lanes] = places(me_ref, list_refs, slots) if grouped else slots
        weight_ref[:, lanes] = both_ref[sources:, lanes]
    half = at_ref.shape[0]
    build_rows(ids_ref, weight_ref, wh_ref, wl_ref, at_ref, [ya_ref, yb_ref], lo_s, half)


def near_kernel(base, ids_ref, weight_ref, wh_ref, wl_ref, at_ref, y_ref, lo_s):
    build_rows(ids_ref, weight_ref, wh_ref, wl_ref, at_ref, [y_ref], lo_s, base)


def adjoint_far(slots, args, grouped, me, lists):
    fine, width = args[-1].shape
    half = slots // 2
    sources = args[0].shape[0] // 2
    out = [shape((sources, fine), jnp.int32), shape((sources, fine), F32)]
    out += [shape((half, fine), BF)] + [shape((half // 2, width), F32)] * 2
    args = [me, *lists, *args]
    return pl.pallas_call(
        functools.partial(far_kernel, grouped),
        in_specs=[SMEM] + [VMEM] * (len(args) - 1),
        out_specs=[VMEM] * len(out),
        out_shape=out,
        scratch_shapes=[pltpu.VMEM((half // 2, fine), BF)],
        compiler_params=params(16),
        cost_estimate=cost(3 * slots * fine * width, 4e6),
        name="adjoint_far",
    )(*args)


def adjoint_near(slots, args, base):
    fine, width = args[-1].shape
    rows = slots // 4
    return pl.pallas_call(
        functools.partial(near_kernel, base),
        in_specs=[VMEM] * len(args),
        out_specs=[VMEM] * 2,
        out_shape=[shape((rows, fine), BF), shape((rows, width), F32)],
        scratch_shapes=[pltpu.VMEM((rows, fine), BF)],
        compiler_params=params(16),
        cost_estimate=cost(1.5 * slots * fine * width, 2e6),
        name="adjoint_near" if base else "adjoint_stay",
    )(*args)


def pick_kernel(me_ref, lists_ref, near_ref, far_ref):
    z, y, c = me_ref[0], me_ref[1], me_ref[2]
    for dy in range(2):
        for p, k in enumerate(LIST_ORDER):
            there = (jnp.bitwise_xor(z, k) * 2 + (y if dy == 0 else 1 - y)) * 2
            row = slice(dy * STEPS + p, dy * STEPS + p + 1)
            near_ref[row, :] = lists_ref[pl.ds(there + c, 1), :]
            far_ref[row, :] = lists_ref[pl.ds(there + 1 - c, 1), :]


def mix_y_kernel(near_ref, got_ref, near_y_ref, far_y_ref):
    for i, held in enumerate((near_ref, got_ref)):
        rows = slice(i * STEPS, (i + 1) * STEPS)
        near_y_ref[rows, :] = held[:STEPS, :]
        far_y_ref[rows, :] = held[STEPS:, :]


def mix_z_kernel(near_ref, got_ref, near_z_ref, far_z_ref):
    for i, held in enumerate((near_ref, got_ref)):
        for c in range(2):
            rows = slice(4 * i + 2 * c, 4 * i + 2 * c + 2)
            far_z_ref[rows, :] = held[c * STEPS : c * STEPS + 2, :]
            near_z_ref[rows, :] = held[c * STEPS + 2 : c * STEPS + 4, :]


def mix_end_kernel(near_ref, got_ref, own_ref, sent_ref):
    for i, held in enumerate((near_ref, got_ref)):
        for n in range(STEPS):
            row = slice(i * STEPS + n, i * STEPS + n + 1)
            own_ref[row, :] = held[2 * n : 2 * n + 1, :]
            sent_ref[row, :] = held[2 * n + 1 : 2 * n + 2, :]


def small(kernel, n, name, *args, scalars=0):
    return pl.pallas_call(
        kernel,
        in_specs=[SMEM] * scalars + [VMEM] * (len(args) - scalars),
        out_specs=[VMEM] * n,
        out_shape=[shape((8, LANES), jnp.int32)] * n,
        compiler_params=params(8),
        cost_estimate=cost(1e4, 3e4),
        name=name,
    )(*args)


def exchange_lists(me, lists):
    near, far = small(pick_kernel, 2, "pick", me, lists, scalars=1)
    near, far = small(mix_y_kernel, 2, "mix_y", near, over_core(far))
    near, far = small(mix_z_kernel, 2, "mix_z", near, over_y(far))
    own, sent = small(mix_end_kernel, 2, "mix_end", near, over_z(far, 1))
    return [own, over_z(sent, 2)]


def exponent(m):
    return jnp.clip(jnp.ceil(jnp.log2(jnp.maximum(m, 1e-30))), -100.0, 100.0)


def whole16(x):
    return x.astype(jnp.int32).astype(jnp.int16)


def wide(x):
    return x.astype(jnp.int32).astype(F32)


def pack(out_ref, t, sums=None):
    rows, width = t.shape
    e = exponent(jnp.max(jnp.abs(t), axis=0, keepdims=True))
    out_ref[pl.ds(0, rows), :] = whole16(jnp.round(t * (jnp.exp2(-e) * TOP)))
    head = [e]
    if sums is not None:
        for i in range(2):
            v = sums[i : i + 1, :]
            f = exponent(v)
            v = v * (jnp.exp2(-f) * 16384.0)
            first = jnp.floor(v)
            head += [f, first, jnp.floor((v - first) * 16384.0)]
    row = lax.broadcasted_iota(jnp.int32, (HEAD, width), 0)
    total = jnp.zeros((HEAD, width), F32)
    for i, h in enumerate(head):
        total = jnp.where(row == i, h, total)
    out_ref[pl.ds(rows, HEAD), :] = whole16(total)


def unpack(ref):
    rows = ref.shape[0] - HEAD
    head = wide(ref[pl.ds(rows, HEAD), :])
    return wide(ref[pl.ds(0, rows), :]) * (jnp.exp2(head[0:1, :]) * (1.0 / TOP))


def unpack_sums(ref):
    head = wide(ref[pl.ds(ref.shape[0] - HEAD, HEAD), :])
    row = lax.broadcasted_iota(jnp.int32, (8, head.shape[1]), 0)
    total = jnp.zeros(row.shape, F32)
    for i in range(2):
        f, first, second = [head[1 + 3 * i + j : 2 + 3 * i + j, :] for j in range(3)]
        v = (first + second * (1.0 / 16384.0)) * (jnp.exp2(f) * (1.0 / 16384.0))
        total = jnp.where(row == i, v, total)
    return total


def merge_y_kernel(with_sums, *refs):
    if with_sums:
        a_ref, b_ref, mine_ref, first_ref, second_ref, s_ref = refs
        sums = mine_ref[...] + b_ref[pl.ds(a_ref.shape[0], 8), :]
        s_ref[...] = sums
    else:
        a_ref, b_ref, first_ref, second_ref = refs
        sums = None
    half = a_ref.shape[0] // 2
    pack(first_ref, a_ref[pl.ds(0, half), :] + b_ref[pl.ds(0, half), :], sums)
    pack(second_ref, a_ref[pl.ds(half, half), :] + b_ref[pl.ds(half, half), :])


def merge_y(a, b, sums):
    rows, width = a.shape
    out = [shape((rows // 2 + HEAD, width), jnp.int16)] * 2
    args = [a, b]
    if sums is not None:
        out.append(shape((8, width), F32))
        args.append(sums)
    return pl.pallas_call(
        functools.partial(merge_y_kernel, sums is not None),
        in_specs=[VMEM] * len(args),
        out_specs=[VMEM] * len(out),
        out_shape=out,
        compiler_params=params(8),
        cost_estimate=cost(5 * rows * width, 1e6),
        name="merge_y",
    )(*args)


def merge_z_kernel(last, with_sums, a_ref, b_ref, p_ref, *refs):
    half = a_ref.shape[0] // 2
    rows = pl.ds(half if last else 0, half)
    t = a_ref[rows, :] + b_ref[rows, :] + unpack(p_ref)
    sums = None
    if with_sums:
        sums = refs[0][...]
        refs = refs[1:]
        if not last:
            sums = sums + unpack_sums(p_ref)
            refs[2][...] = sums
    pack(refs[0], t[:LANES], sums)
    if last:
        refs[1][...] = t[LANES:]
    else:
        pack(refs[1], t[LANES:], sums)


def merge_z(last, a, b, p, sums):
    width = a.shape[1]
    sent = shape((LANES + HEAD, width), jnp.int16)
    out = [sent, shape((LANES, width), F32) if last else sent]
    args = [a, b, p]
    if sums is not None:
        args.append(sums)
        if not last:
            out.append(shape((8, width), F32))
    return pl.pallas_call(
        functools.partial(merge_z_kernel, last, sums is not None),
        in_specs=[VMEM] * len(args),
        out_specs=[VMEM] * len(out),
        out_shape=out,
        compiler_params=params(8),
        cost_estimate=cost(5 * a.size, 1e6),
        name="merge_z_last" if last else "merge_z_first",
    )(*args)


def join_kernel(*refs):
    for i, r in enumerate(refs[:-1]):
        refs[-1][i] = r[...]


def relay_kernel(x_ref, after_ref, out_ref):
    out_ref[...] = x_ref[...]


def copy_of(kernel, name, out, *args):
    return pl.pallas_call(
        kernel,
        in_specs=[VMEM] * len(args),
        out_specs=VMEM,
        out_shape=out,
        compiler_params=params(8),
        cost_estimate=cost(1e5, 5e5),
        name=name,
    )(*args)


def fold(a):
    return jnp.sum(a, axis=0, keepdims=True)


def length_of(sums):
    grad = jnp.sum(sums[0:1, :], axis=1, keepdims=True)
    image = jnp.sum(sums[1:2, :], axis=1, keepdims=True)
    return grad / (grad + image), image / (grad + image)


def products(e, y, held, rows):
    p = e.astype(F32) * y
    q = p[:, :LANES] + p[:, LANES:]
    q = q + pltpu.roll(q, LANES // 2, 1)
    high, low = halves(q)
    held[rows, :LANES] = high
    held[rows, LANES:] = low


BATCH = 16
SOME = 8


def coarse_kernel(packed, second, after, e_ref, k_ref, own_ref, *refs):
    refs = list(refs)
    got = [refs.pop(0) for _ in range(packed)]
    y = own_ref[...]
    for r in got:
        y = y + unpack(r)
    if second:
        y0_ref, s_ref = refs.pop(0), refs.pop(0)
        sums = s_ref[...]
        for r in got:
            sums = sums + unpack_sums(r)
        l0, keep = length_of(sums)
        y = keep * y0_ref[...] - l0 * y
        refs.pop(after + 2)[...] = jnp.broadcast_to(l0, (8, LANES))
    x_ref, y_ref, sum_ref, even_s, odd_s, x_s = refs[after:]
    members, columns, width = e_ref.shape
    y_ref[...] = y
    x_s[...] = jnp.zeros_like(x_s)

    def build(i, held):
        for m in range(SOME):
            products(e_ref[i * SOME + m], y_ref[...], held, pl.ds(m * columns, columns))

    def add_in(i, t):
        total = x_s[...]
        for m in range(SOME):
            total = total + t[m * columns : (m + 1) * columns] * e_ref[i * SOME + m].astype(F32)
        x_s[...] = total

    pairs = members // SOME // 2
    build(0, even_s)

    @pl.loop(0, pairs - 1)
    def _(i):
        t = dot(even_s[...], k_ref[...])
        build(2 * i + 1, odd_s)
        add_in(2 * i, t)
        t = dot(odd_s[...], k_ref[...])
        build(2 * i + 2, even_s)
        add_in(2 * i + 1, t)

    t = dot(even_s[...], k_ref[...])
    build(2 * pairs - 1, odd_s)
    add_in(2 * pairs - 2, t)
    add_in(2 * pairs - 1, dot(odd_s[...], k_ref[...]))

    x = x_s[...]
    x_ref[...] = x.T.astype(BF)
    sum_ref[...] = jnp.zeros_like(sum_ref)
    sum_ref[0:1, :] = fold(x * y_ref[...])


def coarse_image(ensemble, kern, own, got, y0=None, sums=None, after=()):
    members, columns, width = ensemble.shape
    second = y0 is not None
    args = [ensemble, kern, own, *got] + ([y0, sums] if second else []) + list(after)
    out = [shape((width, columns), BF), shape((columns, width), F32)]
    out += [shape((8, LANES), F32)] if second else []
    out += [shape((8, width), F32)]
    return pl.pallas_call(
        functools.partial(coarse_kernel, len(got), second, len(after)),
        in_specs=[VMEM] * (len(args) - len(after)) + [ANY] * len(after),
        out_specs=[VMEM] * len(out),
        out_shape=out,
        scratch_shapes=[
            pltpu.VMEM((SOME * columns, width), BF),
            pltpu.VMEM((SOME * columns, width), BF),
            pltpu.VMEM((columns, width), F32),
        ],
        compiler_params=params(16),
        cost_estimate=cost(2 * columns * members * width * width, 5e6),
        name="coarse_second" if second else "coarse_first",
    )(*args)


def project_kernel(e_ref, y_ref, t_ref, after_ref, g_ref, token_ref, even_s, odd_s):
    columns, members, width = e_ref.shape
    lanes = BATCH // 2 * LANES
    token_ref[...] = jnp.zeros_like(token_ref)

    @pl.loop(0, columns // BATCH)
    def _(i):
        base = pl.multiple_of(i * BATCH, BATCH)
        yb = y_ref[pl.ds(base, BATCH), :]
        for c in range(BATCH):
            held = odd_s if c % 2 else even_s
            rows = pl.ds((c // 2) * members, members)
            products(e_ref[base + c], yb[c : c + 1, :], held, rows)
        r = dot(even_s[...], t_ref[0]) + dot(odd_s[...], t_ref[1])
        for pair in range(BATCH // 2):
            at = pl.multiple_of(i * lanes + pair * LANES, LANES)
            g_ref[:, pl.ds(at, LANES)] = r[pair * members : (pair + 1) * members]


def project(ens, y, taps, after):
    columns, members, width = ens.shape
    levels = width // VAR
    return pl.pallas_call(
        project_kernel,
        in_specs=[VMEM] * 4,
        out_specs=[VMEM] * 2,
        out_shape=[shape((members, columns * levels), F32), shape((8, LANES), F32)],
        scratch_shapes=[pltpu.VMEM((BATCH // 2 * members, width), BF)] * 2,
        compiler_params=params(16),
        cost_estimate=cost(2 * columns * members * width * width, 8e6),
        name="project",
    )(ens, y, taps, after)


def lay_out(x_refs, xs):
    if len(x_refs[0].shape) == 2:
        xs[...] = x_refs[0][...]
        return
    for i, x in enumerate(x_refs):
        for n in range(STEPS):
            xs[:, pl.ds((i * STEPS + n) * LANES, LANES)] = x[n]


CUTS = 3


def part_kernel(*refs):
    *x_refs, stay_ref, near_ref, far_ref, out_ref, xs = refs
    lay_out(x_refs, xs)
    half, fine = far_ref.shape
    split = half // 2
    rows = fine // CUTS
    for i in range(CUTS):
        some = pl.ds(i * rows, rows)
        out_ref[:, some] = (
            dot(xs[:, :split], stay_ref[:, some])
            + dot(xs[:, split:half], near_ref[:, some])
            + dot(xs[:, half:], far_ref[pl.ds(0, xs.shape[1] - half), some])
        )


def image_part(xs, stay, near, far, width):
    half, fine = far.shape
    return pl.pallas_call(
        part_kernel,
        in_specs=[VMEM] * (len(xs) + 3),
        out_specs=VMEM,
        out_shape=shape((width, fine), F32),
        scratch_shapes=[pltpu.VMEM((width, len(xs) * STEPS * LANES), BF)],
        compiler_params=params(16),
        cost_estimate=cost(3 * half * fine * width, 4e6),
        name="image_part",
    )(*xs, stay, near, far)


def images(x_ref, refs, far_ref, obs_ref, im_ref, xs):
    lay_out([x_ref], xs)
    half, fine = far_ref.shape
    split = half // 2
    rows = fine // CUTS
    for i in range(CUTS):
        some = pl.ds(i * rows, rows)
        if len(refs) > 1:
            turned = (
                dot(xs[:, :split], refs[0][:, some])
                + dot(xs[:, split:half], refs[1][:, some])
                + dot(xs[:, half:], far_ref[:, some])
            )
        else:
            last = xs.shape[1]
            turned = dot(xs[...], far_ref[pl.ds(half - last, last), some]) + refs[0][:, some]
        im = turned.T
        im_ref[some, :] = im
        yield some, im, obs_ref[some, :].astype(F32) * im


def image_kernel(parts, first, x_ref, *refs):
    part_refs, refs = refs[:parts], refs[parts:]
    far_ref, obs_ref, g_ref, im_ref, sum_ref, *refs = refs
    if first:
        v_ref, *outs, xs = refs
    else:
        (xs,) = refs
    sums = g_ref[...]
    row = lax.broadcasted_iota(jnp.int32, sums.shape, 0)
    for some, im, v in images(x_ref, part_refs, far_ref, obs_ref, im_ref, xs):
        if first:
            v_ref[some, :] = v.astype(BF)
        sums = sums + jnp.where(row == 1, fold(v * im), 0.0)
    sum_ref[...] = sums
    if first:
        rows = far_ref.shape[0] // 2
        for i in (1, 0):
            outs[i][pl.ds(0, rows), :] = dot(far_ref[pl.ds(i * rows, rows), :], v_ref[...])
        outs[1][pl.ds(rows, 8), :] = sums


def image_of(xs, stay, near, far, obs, g_sums, first):
    half, fine = far.shape
    width = obs.shape[1]
    whole = len(xs) == 1
    part = [stay, near] if whole else [image_part(xs[:-1], stay, near, far, width)]
    out = [shape((fine, width), F32), shape((8, width), F32)]
    if first:
        out += [shape((fine, width), BF)]
        out += [shape((half // 2, width), F32), shape((half // 2 + 8, width), F32)]
    last = 2 * half if whole else STEPS * LANES
    return pl.pallas_call(
        functools.partial(image_kernel, len(part), first),
        in_specs=[VMEM] * (4 + len(part)),
        out_specs=[VMEM] * len(out),
        out_shape=out,
        scratch_shapes=[pltpu.VMEM((width, last), BF)],
        compiler_params=params(16),
        cost_estimate=cost(3 * half * fine * width, 8e6),
        name="image_first" if first else "image_second",
    )(xs[-1], *part, far, obs, g_sums)


def back_kernel(at_ref, v_ref, out_ref):
    out_ref[...] = dot(at_ref[...], v_ref[...])


def back(at, v, name):
    rows, fine = at.shape
    width = v.shape[1]
    return pl.pallas_call(
        back_kernel,
        in_specs=[VMEM] * 2,
        out_specs=VMEM,
        out_shape=shape((rows, width), F32),
        compiler_params=params(16),
        cost_estimate=cost(2 * rows * fine * width, 2e6),
        name=name,
    )(at, v)


OUT_CUTS = 4


def result_kernel(count, l0_ref, *refs):
    sums = refs[0][...]
    for r in refs[1:count]:
        sums = sums + r[...]
    g0_ref, g1_ref, i0_ref, i1_ref, control_hbm, increment_hbm, c_s, i_s, sem = refs[count:]
    l0 = -l0_ref[0:1, 0:1]
    l1, _ = length_of(sums)
    lanes = c_s.shape[1] // OUT_CUTS
    rows = i_s.shape[0] // OUT_CUTS
    copies = []
    for i in range(OUT_CUTS):
        some = pl.ds(i * lanes, lanes)
        c_s[:, some] = l0 * g0_ref[:, some] - l1 * g1_ref[:, some]
        copies.append(
            pltpu.make_async_copy(c_s.at[:, some], control_hbm.at[:, some], sem.at[2 * i])
        )
        copies[-1].start()
        some = pl.ds(i * rows, rows)
        i_s[some, :] = l0 * i0_ref[some, :] - l1 * i1_ref[some, :]
        copies.append(
            pltpu.make_async_copy(i_s.at[some, :], increment_hbm.at[some, :], sem.at[2 * i + 1])
        )
        copies[-1].start()
    for copy in copies:
        copy.wait()


def result(l0, sums, g0, g1, im0, im1):
    return pl.pallas_call(
        functools.partial(result_kernel, len(sums)),
        in_specs=[VMEM] * (5 + len(sums)),
        out_specs=[ANY] * 2,
        out_shape=[shape(g0.shape, F32), shape(im0.shape, F32)],
        scratch_shapes=[
            pltpu.VMEM(g0.shape, F32),
            pltpu.VMEM(im0.shape, F32),
            pltpu.SemaphoreType.DMA((2 * OUT_CUTS,)),
        ],
        compiler_params=params(16),
        cost_estimate=cost(3 * g0.size, 1e7),
        name="result",
    )(l0, *sums, g0, g1, im0, im1)


def over_core(x):
    return lax.ppermute(x, "space", [(i, i ^ 1) for i in range(GROUP)])


def over_y(x):
    return lax.ppermute(x, "space", [(i, i ^ 2) for i in range(GROUP)])


def over_z(x, k):
    return lax.ppermute(x, "space", [(i, i ^ (4 * k)) for i in range(GROUP)])


def scatter_sums(parts, sums=None):
    near, far_y, near_c, far_yc = parts
    got_yc = over_core(far_yc)
    got_c = over_core(near_c)
    first, second, *s = merge_y(far_y, got_yc, sums)
    first, second = over_y(first), over_y(second)
    two, three, *s = merge_z(False, near, got_c, first, s[0] if s else None)
    got = [over_z(two, 2), over_z(three, 3)]
    one, own = merge_z(True, near, got_c, second, s[0] if s else None)
    return own, got + [over_z(one, 1)], (s[0] if s else None)


def gather_columns(x, work):
    four = shape((STEPS,) + x.shape, BF)
    a = copy_of(join_kernel, "join", four, *[over_z(x, k) for k in ORDER[:3]], x)
    ya, ca = over_y(a), over_core(a)
    done, token = work(a)
    ya = copy_of(relay_kernel, "relay", four, ya, token)
    return [a, ya, ca, over_core(ya)], done


def sum_all(x):
    x = x + over_core(x)
    x = x + over_y(x)
    return [x] + [over_z(x, k) for k in range(1, STEPS)]


def on_device(ensemble, innovation, obs_weight, interp_weight, slot_of, intersection_list):
    members, columns, width = ensemble.shape
    levels = width // VAR
    devices = lax.axis_size("space")
    capacity = intersection_list.shape[2]
    slots = devices * capacity
    grouped = devices == GROUP and capacity == columns == LANES

    taper = vertical_taper(levels)
    both = taper.astype(np.float64) @ taper.T.astype(np.float64)
    kern = np.tile(np.concatenate(host_halves(both), axis=0), (2, VAR))
    tall = np.tile(np.concatenate(host_halves(taper), axis=0), (2, 1))
    none = np.zeros_like(tall)
    taps = np.stack(
        [np.concatenate([tall, none], axis=1), np.concatenate([none, tall], axis=1)]
    )
    kern, taps = jnp.asarray(kern), jnp.asarray(taps)

    index = lax.axis_index("space").astype(jnp.int32)
    me = jnp.stack([index // 4, index // 2 % 2, index % 2, index])
    w = -(obs_weight.astype(F32) * innovation.astype(F32))
    high = lax.reduce_precision(w, 8, 7)
    wh, wl = high.astype(BF), (w - high).astype(BF)
    named = jnp.concatenate([slot_of.astype(F32), interp_weight], axis=0)
    if grouped:
        lists = exchange_lists(me, intersection_list[0])
        scatter, gather, add_up = scatter_sums, gather_columns, sum_all
    else:
        lists = intersection_list[0]
        hit = (lists.reshape(-1, 1) == jnp.arange(columns, dtype=jnp.int32)).astype(BF)

        def swap(x):
            x = x.reshape(devices, capacity, width)
            x = lax.all_to_all(x, "space", split_axis=0, concat_axis=0, tiled=True)
            return x.reshape(slots, width)

        def scatter(parts, sums=None):
            got = swap(jnp.concatenate([p[: slots // 4] for p in parts], axis=0))
            high = lax.reduce_precision(got, 8, 7)
            high, low = high.astype(BF), (got - high).astype(BF)
            if sums is not None:
                sums = lax.psum(sums, "space")
            return dot(hit.T, high) + dot(hit.T, low), [], sums

        def gather(x, work):
            return [swap(dot(hit, x.T).astype(BF)).T], work(x)[0]

        def add_up(x):
            return [lax.psum(x, "space")]

    ids, weight, far, c0, c1 = adjoint_far(
        slots, [named, wh, wl], grouped, me, lists if grouped else []
    )
    near, n1 = adjoint_near(slots, [ids, weight, wh, wl], slots // 4)
    stay, n0 = adjoint_near(slots, [ids, weight, wh, wl], 0)
    own, got, _ = scatter([n0, n1, c0, c1])
    ens = jnp.transpose(ensemble, (1, 0, 2))
    x0, y0, g_sums = coarse_image(ensemble, kern, own, got, after=[ens])
    xs, g0 = gather(x0, lambda after: project(ens, y0, taps, after))
    im0, sums, v, c0, c1 = image_of(xs, stay, near, far, obs_weight, g_sums, True)
    n1, n0 = back(near, v, "back_near"), back(stay, v, "back_stay")
    own, got, sums = scatter([n0, n1, c0, c1], sums)
    x1, y1, l0, g_sums = coarse_image(ensemble, kern, own, got, y0, sums)
    xs, g1 = gather(x1, lambda after: project(ens, y1, taps, after))
    im1, sums = image_of(xs, stay, near, far, obs_weight, g_sums, False)
    return tuple(result(l0, add_up(sums), g0, g1, im0, im1))


def solution(mesh):
    placed = (
        P("case", "space", None),
        P(("case", "space"), None),
        P(("case", "space"), None),
        P("case", "space"),
        P("case", "space"),
        P(("case", "space"), None, None),
    )
    return jax.shard_map(
        on_device,
        mesh=mesh,
        in_specs=placed,
        out_specs=(P("case", "space"), P(("case", "space"), None)),
        check_vma=False,
    )
```

```python
import functools

import jax
import jax.numpy as jnp
import ml_dtypes
import numpy as np
from jax import lax
from jax.experimental import pallas as pl
from jax.experimental.pallas import tpu as pltpu
from jax.sharding import PartitionSpec as P

VAR = 4
LOC_SCALE = 3.0
BF = jnp.bfloat16
F32 = jnp.float32
LANES = 128
GROUP = 16
VMEM = pl.BlockSpec(memory_space=pltpu.VMEM)
SMEM = pl.BlockSpec(memory_space=pltpu.SMEM)
ANY = pl.BlockSpec(memory_space=pl.ANY)


def vertical_taper(levels):
    heights = np.arange(levels).astype(np.float32)
    spread = (heights[:, None] - heights[None, :]) / np.float32(LOC_SCALE)
    return np.exp(np.float32(-0.5) * spread * spread)


def host_halves(x):
    high = x.astype(ml_dtypes.bfloat16)
    return [high, (x - high.astype(x.dtype)).astype(ml_dtypes.bfloat16)]


def params(mib):
    return pltpu.CompilerParams(vmem_limit_bytes=mib << 20)


def cost(flops, nbytes):
    return pl.CostEstimate(flops=int(flops), bytes_accessed=int(nbytes), transcendentals=0)


def dot(a, b):
    return jnp.dot(a, b, preferred_element_type=F32)


def halves(x):
    high = x.astype(BF)
    return high, (x - high.astype(F32)).astype(BF)


def shape(dims, dtype):
    return jax.ShapeDtypeStruct(dims, dtype)


STEPS = 4
ORDER = (2, 3, 1, 0)
LIST_ORDER = (1, 3, 0, 2)
PARTS = ((0, 0), (1, 0), (0, 1), (1, 1))
HEAD = 16
TOP = 32512.0


def owner_at(me_ref, i):
    dy, dc = PARTS[i // STEPS]
    z, y, c = me_ref[0], me_ref[1], me_ref[2]
    y = y if dy == 0 else 1 - y
    c = c if dc == 0 else 1 - c
    return (jnp.bitwise_xor(z, ORDER[i % STEPS]) * 2 + y) * 2 + c


def places(me_ref, list_refs, slots):
    slots = jnp.concatenate([slots, slots], axis=0)
    from_owner = jnp.right_shift(slots, 7)
    within = jnp.bitwise_and(slots, LANES - 1)
    rows = jnp.zeros(slots.shape, jnp.int32)
    for i in range(GROUP):
        o = owner_at(me_ref, i)
        dy, dc = PARTS[i // STEPS]
        k = ORDER[i % STEPS]
        row = k % 2 * STEPS + 2 * dy + dc
        row = jnp.broadcast_to(list_refs[k // 2][row : row + 1, :], slots.shape)
        column = jnp.take_along_axis(row, within, axis=1, mode="promise_in_bounds")
        rows = jnp.where(from_owner == o, column + i * LANES, rows)
    return rows[: slots.shape[0] // 2]


def build_rows(ids_ref, weight_ref, wh_ref, wl_ref, at_ref, y_refs, lo_s, base):
    sources, fine = ids_ref.shape
    rows = at_ref.shape[0] // len(y_refs)
    step = rows // 2
    row = lax.broadcasted_iota(jnp.int32, (step, LANES), 0)
    for n, y_ref in enumerate(y_refs):
        for m in range(2):
            start = n * rows + m * step
            for j in range(fine // LANES):
                lanes = pl.ds(j * LANES, LANES)
                total = None
                for b in range(sources):
                    ids = ids_ref[b : b + 1, lanes] - (base + start)
                    term = jnp.where(row == ids, weight_ref[b : b + 1, lanes], 0.0)
                    total = term if total is None else total + term
                high, low = halves(total)
                at_ref[pl.ds(start, step), lanes] = high
                lo_s[pl.ds(m * step, step), lanes] = low
        held = at_ref[pl.ds(n * rows, rows), :]
        y_ref[...] = dot(held, wh_ref[...]) + dot(held, wl_ref[...]) + dot(lo_s[...], wh_ref[...])


def far_kernel(grouped, me_ref, *refs):
    list_refs, refs = refs[: 2 * grouped], refs[2 * grouped :]
    both_ref, wh_ref, wl_ref, *refs = refs
    ids_ref, weight_ref, at_ref, y_ref, lo_s = refs
    sources = ids_ref.shape[0]
    for j in range(ids_ref.shape[1] // LANES):
        lanes = pl.ds(j * LANES, LANES)
        slots = both_ref[:sources, lanes].astype(jnp.int32)
        ids_ref[:, lanes] = places(me_ref, list_refs, slots) if grouped else slots
        weight_ref[:, lanes] = both_ref[sources:, lanes]
    base = 3 * at_ref.shape[0]
    build_rows(ids_ref, weight_ref, wh_ref, wl_ref, at_ref, [y_ref], lo_s, base)


def near_kernel(base, ids_ref, weight_ref, wh_ref, wl_ref, at_ref, y_ref, lo_s):
    build_rows(ids_ref, weight_ref, wh_ref, wl_ref, at_ref, [y_ref], lo_s, base)


def adjoint_far(slots, args, grouped, me, lists):
    fine, width = args[-1].shape
    rows = slots // 4
    sources = args[0].shape[0] // 2
    out = [shape((sources, fine), jnp.int32), shape((sources, fine), F32)]
    out += [shape((rows, fine), BF), shape((rows, width), F32)]
    args = [me, *lists, *args]
    return pl.pallas_call(
        functools.partial(far_kernel, grouped),
        in_specs=[SMEM] + [VMEM] * (len(args) - 1),
        out_specs=[VMEM] * len(out),
        out_shape=out,
        scratch_shapes=[pltpu.VMEM((rows, fine), BF)],
        compiler_params=params(16),
        cost_estimate=cost(1.5 * slots * fine * width, 2e6),
        name="adjoint_far",
    )(*args)


def adjoint_near(slots, args, base):
    fine, width = args[-1].shape
    rows = slots // 4
    return pl.pallas_call(
        functools.partial(near_kernel, base),
        in_specs=[VMEM] * len(args),
        out_specs=[VMEM] * 2,
        out_shape=[shape((rows, fine), BF), shape((rows, width), F32)],
        scratch_shapes=[pltpu.VMEM((rows, fine), BF)],
        compiler_params=params(16),
        cost_estimate=cost(1.5 * slots * fine * width, 2e6),
        name=("adjoint_stay", "adjoint_near", "adjoint_side")[base // rows],
    )(*args)


def pick_kernel(me_ref, lists_ref, near_ref, far_ref):
    z, y, c = me_ref[0], me_ref[1], me_ref[2]
    for dy in range(2):
        for p, k in enumerate(LIST_ORDER):
            there = (jnp.bitwise_xor(z, k) * 2 + (y if dy == 0 else 1 - y)) * 2
            row = slice(dy * STEPS + p, dy * STEPS + p + 1)
            near_ref[row, :] = lists_ref[pl.ds(there + c, 1), :]
            far_ref[row, :] = lists_ref[pl.ds(there + 1 - c, 1), :]


def mix_y_kernel(near_ref, got_ref, near_y_ref, far_y_ref):
    for i, held in enumerate((near_ref, got_ref)):
        rows = slice(i * STEPS, (i + 1) * STEPS)
        near_y_ref[rows, :] = held[:STEPS, :]
        far_y_ref[rows, :] = held[STEPS:, :]


def mix_z_kernel(near_ref, got_ref, near_z_ref, far_z_ref):
    for i, held in enumerate((near_ref, got_ref)):
        for c in range(2):
            rows = slice(4 * i + 2 * c, 4 * i + 2 * c + 2)
            far_z_ref[rows, :] = held[c * STEPS : c * STEPS + 2, :]
            near_z_ref[rows, :] = held[c * STEPS + 2 : c * STEPS + 4, :]


def mix_end_kernel(near_ref, got_ref, own_ref, sent_ref):
    for i, held in enumerate((near_ref, got_ref)):
        for n in range(STEPS):
            row = slice(i * STEPS + n, i * STEPS + n + 1)
            own_ref[row, :] = held[2 * n : 2 * n + 1, :]
            sent_ref[row, :] = held[2 * n + 1 : 2 * n + 2, :]


def small(kernel, n, name, *args, scalars=0):
    return pl.pallas_call(
        kernel,
        in_specs=[SMEM] * scalars + [VMEM] * (len(args) - scalars),
        out_specs=[VMEM] * n,
        out_shape=[shape((8, LANES), jnp.int32)] * n,
        compiler_params=params(8),
        cost_estimate=cost(1e4, 3e4),
        name=name,
    )(*args)


def exchange_lists(me, lists):
    near, far = small(pick_kernel, 2, "pick", me, lists, scalars=1)
    near, far = small(mix_y_kernel, 2, "mix_y", near, over_core(far))
    near, far = small(mix_z_kernel, 2, "mix_z", near, over_y(far))
    own, sent = small(mix_end_kernel, 2, "mix_end", near, over_z(far, 1))
    return [own, over_z(sent, 2)]


def exponent(m):
    return jnp.clip(jnp.ceil(jnp.log2(jnp.maximum(m, 1e-30))), -100.0, 100.0)


def whole16(x):
    return x.astype(jnp.int32).astype(jnp.int16)


def wide(x):
    return x.astype(jnp.int32).astype(F32)


def pack(out_ref, t, sums=None):
    rows, width = t.shape
    e = exponent(jnp.max(jnp.abs(t), axis=0, keepdims=True))
    out_ref[pl.ds(0, rows), :] = whole16(jnp.round(t * (jnp.exp2(-e) * TOP)))
    head = [e]
    if sums is not None:
        for i in range(2):
            v = sums[i : i + 1, :]
            f = exponent(v)
            v = v * (jnp.exp2(-f) * 16384.0)
            first = jnp.floor(v)
            head += [f, first, jnp.floor((v - first) * 16384.0)]
    row = lax.broadcasted_iota(jnp.int32, (HEAD, width), 0)
    total = jnp.zeros((HEAD, width), F32)
    for i, h in enumerate(head):
        total = jnp.where(row == i, h, total)
    out_ref[pl.ds(rows, HEAD), :] = whole16(total)


def unpack(ref):
    rows = ref.shape[0] - HEAD
    head = wide(ref[pl.ds(rows, HEAD), :])
    return wide(ref[pl.ds(0, rows), :]) * (jnp.exp2(head[0:1, :]) * (1.0 / TOP))


def unpack_sums(ref):
    head = wide(ref[pl.ds(ref.shape[0] - HEAD, HEAD), :])
    row = lax.broadcasted_iota(jnp.int32, (8, head.shape[1]), 0)
    total = jnp.zeros(row.shape, F32)
    for i in range(2):
        f, first, second = [head[1 + 3 * i + j : 2 + 3 * i + j, :] for j in range(3)]
        v = (first + second * (1.0 / 16384.0)) * (jnp.exp2(f) * (1.0 / 16384.0))
        total = jnp.where(row == i, v, total)
    return total


def merge_y_kernel(with_sums, *refs):
    if with_sums:
        a_ref, b_ref, mine_ref, first_ref, second_ref, s_ref = refs
        sums = mine_ref[...] + b_ref[pl.ds(a_ref.shape[0], 8), :]
        s_ref[...] = sums
    else:
        a_ref, b_ref, first_ref, second_ref = refs
        sums = None
    half = a_ref.shape[0] // 2
    pack(first_ref, a_ref[pl.ds(0, half), :] + b_ref[pl.ds(0, half), :], sums)
    pack(second_ref, a_ref[pl.ds(half, half), :] + b_ref[pl.ds(half, half), :])


def merge_y(a, b, sums):
    rows, width = a.shape
    out = [shape((rows // 2 + HEAD, width), jnp.int16)] * 2
    args = [a, b]
    if sums is not None:
        out.append(shape((8, width), F32))
        args.append(sums)
    return pl.pallas_call(
        functools.partial(merge_y_kernel, sums is not None),
        in_specs=[VMEM] * len(args),
        out_specs=[VMEM] * len(out),
        out_shape=out,
        compiler_params=params(8),
        cost_estimate=cost(5 * rows * width, 1e6),
        name="merge_y",
    )(*args)


def merge_z_kernel(last, with_sums, a_ref, b_ref, p_ref, *refs):
    half = a_ref.shape[0] // 2
    rows = pl.ds(half if last else 0, half)
    t = a_ref[rows, :] + b_ref[rows, :] + unpack(p_ref)
    sums = None
    if with_sums:
        sums = refs[0][...]
        refs = refs[1:]
        if not last:
            sums = sums + unpack_sums(p_ref)
            refs[2][...] = sums
    pack(refs[0], t[:LANES], sums)
    if last:
        refs[1][...] = t[LANES:]
    else:
        pack(refs[1], t[LANES:], sums)


def merge_z(last, a, b, p, sums):
    width = a.shape[1]
    sent = shape((LANES + HEAD, width), jnp.int16)
    out = [sent, shape((LANES, width), F32) if last else sent]
    args = [a, b, p]
    if sums is not None:
        args.append(sums)
        if not last:
            out.append(shape((8, width), F32))
    return pl.pallas_call(
        functools.partial(merge_z_kernel, last, sums is not None),
        in_specs=[VMEM] * len(args),
        out_specs=[VMEM] * len(out),
        out_shape=out,
        compiler_params=params(8),
        cost_estimate=cost(5 * a.size, 1e6),
        name="merge_z_last" if last else "merge_z_first",
    )(*args)


def join_kernel(*refs):
    for i, r in enumerate(refs[:-1]):
        refs[-1][i] = r[...]


def relay_kernel(x_ref, after_ref, out_ref):
    out_ref[...] = x_ref[...]


def copy_of(kernel, name, out, *args):
    return pl.pallas_call(
        kernel,
        in_specs=[VMEM] * len(args),
        out_specs=VMEM,
        out_shape=out,
        compiler_params=params(8),
        cost_estimate=cost(1e5, 5e5),
        name=name,
    )(*args)


def fold(a):
    return jnp.sum(a, axis=0, keepdims=True)


def length_of(sums):
    grad = jnp.sum(sums[0:1, :], axis=1, keepdims=True)
    image = jnp.sum(sums[1:2, :], axis=1, keepdims=True)
    return grad / (grad + image), image / (grad + image)


def products(e, y, held, rows):
    p = e.astype(F32) * y
    q = p[:, :LANES] + p[:, LANES:]
    q = q + pltpu.roll(q, LANES // 2, 1)
    high, low = halves(q)
    held[rows, :LANES] = high
    held[rows, LANES:] = low


BATCH = 16
SOME = 8


def coarse_kernel(packed, second, after, e_ref, k_ref, own_ref, *refs):
    refs = list(refs)
    got = [refs.pop(0) for _ in range(packed)]
    y = own_ref[...]
    for r in got:
        y = y + unpack(r)
    if second:
        y0_ref, s_ref = refs.pop(0), refs.pop(0)
        sums = s_ref[...]
        for r in got:
            sums = sums + unpack_sums(r)
        l0, keep = length_of(sums)
        y = keep * y0_ref[...] - l0 * y
        refs.pop(after + 2)[...] = jnp.broadcast_to(l0, (8, LANES))
    x_ref, y_ref, sum_ref, even_s, odd_s, x_s = refs[after:]
    members, columns, width = e_ref.shape
    y_ref[...] = y
    x_s[...] = jnp.zeros_like(x_s)

    def build(i, held):
        for m in range(SOME):
            products(e_ref[i * SOME + m], y_ref[...], held, pl.ds(m * columns, columns))

    def add_in(i, t):
        total = x_s[...]
        for m in range(SOME):
            total = total + t[m * columns : (m + 1) * columns] * e_ref[i * SOME + m].astype(F32)
        x_s[...] = total

    pairs = members // SOME // 2
    build(0, even_s)

    @pl.loop(0, pairs - 1)
    def _(i):
        t = dot(even_s[...], k_ref[...])
        build(2 * i + 1, odd_s)
        add_in(2 * i, t)
        t = dot(odd_s[...], k_ref[...])
        build(2 * i + 2, even_s)
        add_in(2 * i + 1, t)

    t = dot(even_s[...], k_ref[...])
    build(2 * pairs - 1, odd_s)
    add_in(2 * pairs - 2, t)
    add_in(2 * pairs - 1, dot(odd_s[...], k_ref[...]))

    x = x_s[...]
    x_ref[...] = x.T.astype(BF)
    sum_ref[...] = jnp.zeros_like(sum_ref)
    sum_ref[0:1, :] = fold(x * y_ref[...])


def coarse_image(ensemble, kern, own, got, y0=None, sums=None, after=()):
    members, columns, width = ensemble.shape
    second = y0 is not None
    args = [ensemble, kern, own, *got] + ([y0, sums] if second else []) + list(after)
    out = [shape((width, columns), BF), shape((columns, width), F32)]
    out += [shape((8, LANES), F32)] if second else []
    out += [shape((8, width), F32)]
    return pl.pallas_call(
        functools.partial(coarse_kernel, len(got), second, len(after)),
        in_specs=[VMEM] * (len(args) - len(after)) + [ANY] * len(after),
        out_specs=[VMEM] * len(out),
        out_shape=out,
        scratch_shapes=[
            pltpu.VMEM((SOME * columns, width), BF),
            pltpu.VMEM((SOME * columns, width), BF),
            pltpu.VMEM((columns, width), F32),
        ],
        compiler_params=params(16),
        cost_estimate=cost(2 * columns * members * width * width, 5e6),
        name="coarse_second" if second else "coarse_first",
    )(*args)


def project_kernel(e_ref, y_ref, t_ref, after_ref, g_ref, token_ref, even_s, odd_s):
    columns, members, width = e_ref.shape
    lanes = BATCH // 2 * LANES
    token_ref[...] = jnp.zeros_like(token_ref)

    @pl.loop(0, columns // BATCH)
    def _(i):
        base = pl.multiple_of(i * BATCH, BATCH)
        yb = y_ref[pl.ds(base, BATCH), :]
        for c in range(BATCH):
            held = odd_s if c % 2 else even_s
            rows = pl.ds((c // 2) * members, members)
            products(e_ref[base + c], yb[c : c + 1, :], held, rows)
        r = dot(even_s[...], t_ref[0]) + dot(odd_s[...], t_ref[1])
        for pair in range(BATCH // 2):
            at = pl.multiple_of(i * lanes + pair * LANES, LANES)
            g_ref[:, pl.ds(at, LANES)] = r[pair * members : (pair + 1) * members]


def project(ens, y, taps, after):
    columns, members, width = ens.shape
    levels = width // VAR
    return pl.pallas_call(
        project_kernel,
        in_specs=[VMEM] * 4,
        out_specs=[VMEM] * 2,
        out_shape=[shape((members, columns * levels), F32), shape((8, LANES), F32)],
        scratch_shapes=[pltpu.VMEM((BATCH // 2 * members, width), BF)] * 2,
        compiler_params=params(16),
        cost_estimate=cost(2 * columns * members * width * width, 8e6),
        name="project",
    )(ens, y, taps, after)


def lay_out(x_refs, xs):
    if len(x_refs[0].shape) == 2:
        xs[...] = x_refs[0][...]
        return
    for i, x in enumerate(x_refs):
        for n in range(STEPS):
            xs[:, pl.ds((i * STEPS + n) * LANES, LANES)] = x[n]


CUTS = 3


def part_kernel(*refs):
    *x_refs, a_ref, b_ref, c_ref, out_ref, xs = refs
    lay_out(x_refs, xs)
    quarter, fine = a_ref.shape
    rows = fine // CUTS
    for i in range(CUTS):
        some = pl.ds(i * rows, rows)
        total = None
        for n, m in enumerate((a_ref, b_ref, c_ref)):
            term = dot(xs[:, n * quarter : (n + 1) * quarter], m[:, some])
            total = term if total is None else total + term
        out_ref[:, some] = total


def image_part(xs, quarters, width):
    quarter, fine = quarters[0].shape
    return pl.pallas_call(
        part_kernel,
        in_specs=[VMEM] * 6,
        out_specs=VMEM,
        out_shape=shape((width, fine), F32),
        scratch_shapes=[pltpu.VMEM((width, 3 * quarter), BF)],
        compiler_params=params(16),
        cost_estimate=cost(6 * quarter * fine * width, 4e6),
        name="image_part",
    )(*xs, *quarters)


def images(x_ref, refs, last_ref, obs_ref, im_ref, xs):
    lay_out([x_ref], xs)
    quarter, fine = last_ref.shape
    rows = fine // CUTS
    for i in range(CUTS):
        some = pl.ds(i * rows, rows)
        if len(refs) > 1:
            turned = dot(xs[:, 3 * quarter :], last_ref[:, some])
            for n, m in enumerate(refs):
                turned = turned + dot(xs[:, n * quarter : (n + 1) * quarter], m[:, some])
        else:
            turned = dot(xs[...], last_ref[:, some]) + refs[0][:, some]
        im = turned.T
        im_ref[some, :] = im
        yield some, im, obs_ref[some, :].astype(F32) * im


def image_kernel(parts, first, x_ref, *refs):
    part_refs, refs = refs[:parts], refs[parts:]
    far_ref, obs_ref, g_ref, im_ref, sum_ref, *refs = refs
    if first:
        v_ref, out_ref, xs = refs
    else:
        (xs,) = refs
    sums = g_ref[...]
    row = lax.broadcasted_iota(jnp.int32, sums.shape, 0)
    for some, im, v in images(x_ref, part_refs, far_ref, obs_ref, im_ref, xs):
        if first:
            v_ref[some, :] = v.astype(BF)
        sums = sums + jnp.where(row == 1, fold(v * im), 0.0)
    sum_ref[...] = sums
    if first:
        rows = far_ref.shape[0]
        out_ref[pl.ds(0, rows), :] = dot(far_ref[...], v_ref[...])
        out_ref[pl.ds(rows, 8), :] = sums


def image_of(xs, quarters, far, obs, g_sums, first):
    quarter, fine = far.shape
    width = obs.shape[1]
    whole = len(xs) == 1
    part = quarters if whole else [image_part(xs[:-1], quarters, width)]
    out = [shape((fine, width), F32), shape((8, width), F32)]
    if first:
        out += [shape((fine, width), BF)]
        out += [shape((quarter + 8, width), F32)]
    last = 4 * quarter if whole else quarter
    return pl.pallas_call(
        functools.partial(image_kernel, len(part), first),
        in_specs=[VMEM] * (4 + len(part)),
        out_specs=[VMEM] * len(out),
        out_shape=out,
        scratch_shapes=[pltpu.VMEM((width, last), BF)],
        compiler_params=params(16),
        cost_estimate=cost(4 * quarter * fine * width, 6e6),
        name="image_first" if first else "image_second",
    )(xs[-1], *part, far, obs, g_sums)


def back_kernel(at_ref, v_ref, out_ref):
    out_ref[...] = dot(at_ref[...], v_ref[...])


def back(at, v, name):
    rows, fine = at.shape
    width = v.shape[1]
    return pl.pallas_call(
        back_kernel,
        in_specs=[VMEM] * 2,
        out_specs=VMEM,
        out_shape=shape((rows, width), F32),
        compiler_params=params(16),
        cost_estimate=cost(2 * rows * fine * width, 2e6),
        name=name,
    )(at, v)


OUT_CUTS = 4


def result_kernel(count, l0_ref, *refs):
    sums = refs[0][...]
    for r in refs[1:count]:
        sums = sums + r[...]
    g0_ref, g1_ref, i0_ref, i1_ref, control_hbm, increment_hbm, c_s, i_s, sem = refs[count:]
    l0 = -l0_ref[0:1, 0:1]
    l1, _ = length_of(sums)
    lanes = c_s.shape[1] // OUT_CUTS
    rows = i_s.shape[0] // OUT_CUTS
    copies = []
    for i in range(OUT_CUTS):
        some = pl.ds(i * lanes, lanes)
        c_s[:, some] = l0 * g0_ref[:, some] - l1 * g1_ref[:, some]
        copies.append(
            pltpu.make_async_copy(c_s.at[:, some], control_hbm.at[:, some], sem.at[2 * i])
        )
        copies[-1].start()
        some = pl.ds(i * rows, rows)
        i_s[some, :] = l0 * i0_ref[some, :] - l1 * i1_ref[some, :]
        copies.append(
            pltpu.make_async_copy(i_s.at[some, :], increment_hbm.at[some, :], sem.at[2 * i + 1])
        )
        copies[-1].start()
    for copy in copies:
        copy.wait()


def result(l0, sums, g0, g1, im0, im1):
    return pl.pallas_call(
        functools.partial(result_kernel, len(sums)),
        in_specs=[VMEM] * (5 + len(sums)),
        out_specs=[ANY] * 2,
        out_shape=[shape(g0.shape, F32), shape(im0.shape, F32)],
        scratch_shapes=[
            pltpu.VMEM(g0.shape, F32),
            pltpu.VMEM(im0.shape, F32),
            pltpu.SemaphoreType.DMA((2 * OUT_CUTS,)),
        ],
        compiler_params=params(16),
        cost_estimate=cost(3 * g0.size, 1e7),
        name="result",
    )(l0, *sums, g0, g1, im0, im1)


def over_core(x):
    return lax.ppermute(x, "space", [(i, i ^ 1) for i in range(GROUP)])


def over_y(x):
    return lax.ppermute(x, "space", [(i, i ^ 2) for i in range(GROUP)])


def over_z(x, k):
    return lax.ppermute(x, "space", [(i, i ^ (4 * k)) for i in range(GROUP)])


def scatter_sums(parts, sums=None):
    near, far_y, near_c, far_yc = parts
    got_yc = over_core(far_yc)
    got_c = over_core(near_c)
    first, second, *s = merge_y(far_y, got_yc, sums)
    first, second = over_y(first), over_y(second)
    two, three, *s = merge_z(False, near, got_c, first, s[0] if s else None)
    got = [over_z(two, 2), over_z(three, 3)]
    one, own = merge_z(True, near, got_c, second, s[0] if s else None)
    return own, got + [over_z(one, 1)], (s[0] if s else None)


def gather_columns(x, work):
    four = shape((STEPS,) + x.shape, BF)
    a = copy_of(join_kernel, "join", four, *[over_z(x, k) for k in ORDER[:3]], x)
    ya, ca = over_y(a), over_core(a)
    done, token = work(a)
    ya = copy_of(relay_kernel, "relay", four, ya, token)
    return [a, ya, ca, over_core(ya)], done


def sum_all(x):
    x = x + over_core(x)
    x = x + over_y(x)
    return [x] + [over_z(x, k) for k in range(1, STEPS)]


def on_device(ensemble, innovation, obs_weight, interp_weight, slot_of, intersection_list):
    members, columns, width = ensemble.shape
    levels = width // VAR
    devices = lax.axis_size("space")
    capacity = intersection_list.shape[2]
    slots = devices * capacity
    grouped = devices == GROUP and capacity == columns == LANES

    taper = vertical_taper(levels)
    both = taper.astype(np.float64) @ taper.T.astype(np.float64)
    kern = np.tile(np.concatenate(host_halves(both), axis=0), (2, VAR))
    tall = np.tile(np.concatenate(host_halves(taper), axis=0), (2, 1))
    none = np.zeros_like(tall)
    taps = np.stack(
        [np.concatenate([tall, none], axis=1), np.concatenate([none, tall], axis=1)]
    )
    kern, taps = jnp.asarray(kern), jnp.asarray(taps)

    index = lax.axis_index("space").astype(jnp.int32)
    me = jnp.stack([index // 4, index // 2 % 2, index % 2, index])
    w = -(obs_weight.astype(F32) * innovation.astype(F32))
    high = lax.reduce_precision(w, 8, 7)
    wh, wl = high.astype(BF), (w - high).astype(BF)
    named = jnp.concatenate([slot_of.astype(F32), interp_weight], axis=0)
    if grouped:
        lists = exchange_lists(me, intersection_list[0])
        scatter, gather, add_up = scatter_sums, gather_columns, sum_all
    else:
        lists = intersection_list[0]
        hit = (lists.reshape(-1, 1) == jnp.arange(columns, dtype=jnp.int32)).astype(BF)

        def swap(x):
            x = x.reshape(devices, capacity, width)
            x = lax.all_to_all(x, "space", split_axis=0, concat_axis=0, tiled=True)
            return x.reshape(slots, width)

        def scatter(parts, sums=None):
            got = swap(jnp.concatenate([p[: slots // 4] for p in parts], axis=0))
            high = lax.reduce_precision(got, 8, 7)
            high, low = high.astype(BF), (got - high).astype(BF)
            if sums is not None:
                sums = lax.psum(sums, "space")
            return dot(hit.T, high) + dot(hit.T, low), [], sums

        def gather(x, work):
            return [swap(dot(hit, x.T).astype(BF)).T], work(x)[0]

        def add_up(x):
            return [lax.psum(x, "space")]

    ids, weight, far, c1 = adjoint_far(
        slots, [named, wh, wl], grouped, me, lists if grouped else []
    )
    built = [ids, weight, wh, wl]
    near, n1 = adjoint_near(slots, built, slots // 4)
    side, c0 = adjoint_near(slots, built, slots // 2)
    stay, n0 = adjoint_near(slots, built, 0)
    quarters = [stay, near, side]
    own, got, _ = scatter([n0, n1, c0, c1])
    ens = jnp.transpose(ensemble, (1, 0, 2))
    x0, y0, g_sums = coarse_image(ensemble, kern, own, got, after=[ens])
    xs, g0 = gather(x0, lambda after: project(ens, y0, taps, after))
    im0, sums, v, c1 = image_of(xs, quarters, far, obs_weight, g_sums, True)
    c0 = back(side, v, "back_side")
    n1, n0 = back(near, v, "back_near"), back(stay, v, "back_stay")
    own, got, sums = scatter([n0, n1, c0, c1], sums)
    x1, y1, l0, g_sums = coarse_image(ensemble, kern, own, got, y0, sums)
    xs, g1 = gather(x1, lambda after: project(ens, y1, taps, after))
    im1, sums = image_of(xs, quarters, far, obs_weight, g_sums, False)
    return tuple(result(l0, add_up(sums), g0, g1, im0, im1))


def solution(mesh):
    placed = (
        P("case", "space", None),
        P(("case", "space"), None),
        P(("case", "space"), None),
        P("case", "space"),
        P("case", "space"),
        P(("case", "space"), None, None),
    )
    return jax.shard_map(
        on_device,
        mesh=mesh,
        in_specs=placed,
        out_specs=(P("case", "space"), P(("case", "space"), None)),
        check_vma=False,
    )
```

```python
import functools

import jax
import jax.numpy as jnp
import ml_dtypes
import numpy as np
from jax import lax
from jax.experimental import pallas as pl
from jax.experimental.pallas import tpu as pltpu
from jax.sharding import PartitionSpec as P

VAR = 4
LOC_SCALE = 3.0
BF = jnp.bfloat16
F32 = jnp.float32
LANES = 128
GROUP = 16
VMEM = pl.BlockSpec(memory_space=pltpu.VMEM)
SMEM = pl.BlockSpec(memory_space=pltpu.SMEM)
ANY = pl.BlockSpec(memory_space=pl.ANY)


def vertical_taper(levels):
    heights = np.arange(levels).astype(np.float32)
    spread = (heights[:, None] - heights[None, :]) / np.float32(LOC_SCALE)
    return np.exp(np.float32(-0.5) * spread * spread)


def host_halves(x):
    high = x.astype(ml_dtypes.bfloat16)
    return [high, (x - high.astype(x.dtype)).astype(ml_dtypes.bfloat16)]


def params(mib):
    return pltpu.CompilerParams(vmem_limit_bytes=mib << 20)


def cost(flops, nbytes):
    return pl.CostEstimate(flops=int(flops), bytes_accessed=int(nbytes), transcendentals=0)


def dot(a, b):
    return jnp.dot(a, b, preferred_element_type=F32)


def halves(x):
    high = x.astype(BF)
    return high, (x - high.astype(F32)).astype(BF)


def shape(dims, dtype):
    return jax.ShapeDtypeStruct(dims, dtype)


STEPS = 4
ORDER = (2, 3, 1, 0)
LIST_ORDER = (1, 3, 0, 2)
PARTS = ((0, 0), (1, 0), (0, 1), (1, 1))
HEAD = 16
TOP = 32512.0


def owner_at(me_ref, i):
    dy, dc = PARTS[i // STEPS]
    z, y, c = me_ref[0], me_ref[1], me_ref[2]
    y = y if dy == 0 else 1 - y
    c = c if dc == 0 else 1 - c
    return (jnp.bitwise_xor(z, ORDER[i % STEPS]) * 2 + y) * 2 + c


def places(me_ref, list_refs, slots):
    slots = jnp.concatenate([slots, slots], axis=0)
    from_owner = jnp.right_shift(slots, 7)
    within = jnp.bitwise_and(slots, LANES - 1)
    rows = jnp.zeros(slots.shape, jnp.int32)
    for i in range(GROUP):
        o = owner_at(me_ref, i)
        dy, dc = PARTS[i // STEPS]
        k = ORDER[i % STEPS]
        row = k % 2 * STEPS + 2 * dy + dc
        row = jnp.broadcast_to(list_refs[k // 2][row : row + 1, :], slots.shape)
        column = jnp.take_along_axis(row, within, axis=1, mode="promise_in_bounds")
        rows = jnp.where(from_owner == o, column + i * LANES, rows)
    return rows[: slots.shape[0] // 2]


def build_rows(ids_ref, weight_ref, wh_ref, wl_ref, at_ref, y_refs, lo_s, base):
    sources, fine = ids_ref.shape
    rows = at_ref.shape[0] // len(y_refs)
    step = rows // 2
    row = lax.broadcasted_iota(jnp.int32, (step, LANES), 0)
    for n, y_ref in enumerate(y_refs):
        for m in range(2):
            start = n * rows + m * step
            for j in range(fine // LANES):
                lanes = pl.ds(j * LANES, LANES)
                total = None
                for b in range(sources):
                    ids = ids_ref[b : b + 1, lanes] - (base + start)
                    term = jnp.where(row == ids, weight_ref[b : b + 1, lanes], 0.0)
                    total = term if total is None else total + term
                high, low = halves(total)
                at_ref[pl.ds(start, step), lanes] = high
                lo_s[pl.ds(m * step, step), lanes] = low
        held = at_ref[pl.ds(n * rows, rows), :]
        y_ref[...] = dot(held, wh_ref[...]) + dot(held, wl_ref[...]) + dot(lo_s[...], wh_ref[...])


def far_kernel(grouped, me_ref, *refs):
    list_refs, refs = refs[: 2 * grouped], refs[2 * grouped :]
    both_ref, wh_ref, wl_ref, *refs = refs
    ids_ref, weight_ref, at_ref, y_ref, lo_s = refs
    sources = ids_ref.shape[0]
    for j in range(ids_ref.shape[1] // LANES):
        lanes = pl.ds(j * LANES, LANES)
        slots = both_ref[:sources, lanes].astype(jnp.int32)
        ids_ref[:, lanes] = places(me_ref, list_refs, slots) if grouped else slots
        weight_ref[:, lanes] = both_ref[sources:, lanes]
    base = 3 * at_ref.shape[0]
    build_rows(ids_ref, weight_ref, wh_ref, wl_ref, at_ref, [y_ref], lo_s, base)


def near_kernel(base, ids_ref, weight_ref, wh_ref, wl_ref, *refs):
    at_ref, y_ref, lo_s = refs[-3:]
    build_rows(ids_ref, weight_ref, wh_ref, wl_ref, at_ref, [y_ref], lo_s, base)


def adjoint_far(slots, args, grouped, me, lists):
    fine, width = args[-1].shape
    rows = slots // 4
    sources = args[0].shape[0] // 2
    out = [shape((sources, fine), jnp.int32), shape((sources, fine), F32)]
    out += [shape((rows, fine), BF), shape((rows, width), F32)]
    args = [me, *lists, *args]
    return pl.pallas_call(
        functools.partial(far_kernel, grouped),
        in_specs=[SMEM] + [VMEM] * (len(args) - 1),
        out_specs=[VMEM] * len(out),
        out_shape=out,
        scratch_shapes=[pltpu.VMEM((rows, fine), BF)],
        compiler_params=params(16),
        cost_estimate=cost(1.5 * slots * fine * width, 2e6),
        name="adjoint_far",
    )(*args)


def adjoint_near(slots, args, base):
    fine, width = args[2].shape
    rows = slots // 4
    return pl.pallas_call(
        functools.partial(near_kernel, base),
        in_specs=[VMEM] * len(args),
        out_specs=[VMEM] * 2,
        out_shape=[shape((rows, fine), BF), shape((rows, width), F32)],
        scratch_shapes=[pltpu.VMEM((rows, fine), BF)],
        compiler_params=params(16),
        cost_estimate=cost(1.5 * slots * fine * width, 2e6),
        name=("adjoint_stay", "adjoint_near", "adjoint_side")[base // rows],
    )(*args)


def pick_kernel(me_ref, lists_ref, near_ref, far_ref):
    z, y, c = me_ref[0], me_ref[1], me_ref[2]
    for dy in range(2):
        for p, k in enumerate(LIST_ORDER):
            there = (jnp.bitwise_xor(z, k) * 2 + (y if dy == 0 else 1 - y)) * 2
            row = slice(dy * STEPS + p, dy * STEPS + p + 1)
            near_ref[row, :] = lists_ref[pl.ds(there + c, 1), :]
            far_ref[row, :] = lists_ref[pl.ds(there + 1 - c, 1), :]


def mix_y_kernel(near_ref, got_ref, near_y_ref, far_y_ref):
    for i, held in enumerate((near_ref, got_ref)):
        rows = slice(i * STEPS, (i + 1) * STEPS)
        near_y_ref[rows, :] = held[:STEPS, :]
        far_y_ref[rows, :] = held[STEPS:, :]


def mix_z_kernel(near_ref, got_ref, near_z_ref, far_z_ref):
    for i, held in enumerate((near_ref, got_ref)):
        for c in range(2):
            rows = slice(4 * i + 2 * c, 4 * i + 2 * c + 2)
            far_z_ref[rows, :] = held[c * STEPS : c * STEPS + 2, :]
            near_z_ref[rows, :] = held[c * STEPS + 2 : c * STEPS + 4, :]


def mix_end_kernel(near_ref, got_ref, own_ref, sent_ref):
    for i, held in enumerate((near_ref, got_ref)):
        for n in range(STEPS):
            row = slice(i * STEPS + n, i * STEPS + n + 1)
            own_ref[row, :] = held[2 * n : 2 * n + 1, :]
            sent_ref[row, :] = held[2 * n + 1 : 2 * n + 2, :]


def small(kernel, n, name, *args, scalars=0):
    return pl.pallas_call(
        kernel,
        in_specs=[SMEM] * scalars + [VMEM] * (len(args) - scalars),
        out_specs=[VMEM] * n,
        out_shape=[shape((8, LANES), jnp.int32)] * n,
        compiler_params=params(8),
        cost_estimate=cost(1e4, 3e4),
        name=name,
    )(*args)


def exchange_lists(me, lists):
    near, far = small(pick_kernel, 2, "pick", me, lists, scalars=1)
    near, far = small(mix_y_kernel, 2, "mix_y", near, over_core(far))
    near, far = small(mix_z_kernel, 2, "mix_z", near, over_y(far))
    own, sent = small(mix_end_kernel, 2, "mix_end", near, over_z(far, 1))
    return [own, over_z(sent, 2)]


def exponent(m):
    return jnp.clip(jnp.ceil(jnp.log2(jnp.maximum(m, 1e-30))), -100.0, 100.0)


def whole16(x):
    return x.astype(jnp.int32).astype(jnp.int16)


def wide(x):
    return x.astype(jnp.int32).astype(F32)


def pack(out_ref, t, sums=None):
    rows, width = t.shape
    e = exponent(jnp.max(jnp.abs(t), axis=0, keepdims=True))
    out_ref[pl.ds(0, rows), :] = whole16(jnp.round(t * (jnp.exp2(-e) * TOP)))
    head = [e]
    if sums is not None:
        for i in range(2):
            v = sums[i : i + 1, :]
            f = exponent(v)
            v = v * (jnp.exp2(-f) * 16384.0)
            first = jnp.floor(v)
            head += [f, first, jnp.floor((v - first) * 16384.0)]
    row = lax.broadcasted_iota(jnp.int32, (HEAD, width), 0)
    total = jnp.zeros((HEAD, width), F32)
    for i, h in enumerate(head):
        total = jnp.where(row == i, h, total)
    out_ref[pl.ds(rows, HEAD), :] = whole16(total)


def unpack(ref):
    rows = ref.shape[0] - HEAD
    head = wide(ref[pl.ds(rows, HEAD), :])
    return wide(ref[pl.ds(0, rows), :]) * (jnp.exp2(head[0:1, :]) * (1.0 / TOP))


def unpack_sums(ref):
    head = wide(ref[pl.ds(ref.shape[0] - HEAD, HEAD), :])
    row = lax.broadcasted_iota(jnp.int32, (8, head.shape[1]), 0)
    total = jnp.zeros(row.shape, F32)
    for i in range(2):
        f, first, second = [head[1 + 3 * i + j : 2 + 3 * i + j, :] for j in range(3)]
        v = (first + second * (1.0 / 16384.0)) * (jnp.exp2(f) * (1.0 / 16384.0))
        total = jnp.where(row == i, v, total)
    return total


def merge_y_kernel(with_sums, *refs):
    if with_sums:
        a_ref, b_ref, mine_ref, first_ref, second_ref, s_ref = refs
        sums = mine_ref[...] + b_ref[pl.ds(a_ref.shape[0], 8), :]
        s_ref[...] = sums
    else:
        a_ref, b_ref, first_ref, second_ref = refs
        sums = None
    half = a_ref.shape[0] // 2
    pack(first_ref, a_ref[pl.ds(0, half), :] + b_ref[pl.ds(0, half), :], sums)
    pack(second_ref, a_ref[pl.ds(half, half), :] + b_ref[pl.ds(half, half), :])


def merge_y(a, b, sums):
    rows, width = a.shape
    out = [shape((rows // 2 + HEAD, width), jnp.int16)] * 2
    args = [a, b]
    if sums is not None:
        out.append(shape((8, width), F32))
        args.append(sums)
    return pl.pallas_call(
        functools.partial(merge_y_kernel, sums is not None),
        in_specs=[VMEM] * len(args),
        out_specs=[VMEM] * len(out),
        out_shape=out,
        compiler_params=params(8),
        cost_estimate=cost(5 * rows * width, 1e6),
        name="merge_y",
    )(*args)


def merge_z_kernel(last, with_sums, a_ref, b_ref, p_ref, *refs):
    half = a_ref.shape[0] // 2
    rows = pl.ds(half if last else 0, half)
    t = a_ref[rows, :] + b_ref[rows, :] + unpack(p_ref)
    sums = None
    if with_sums:
        sums = refs[0][...]
        refs = refs[1:]
        if not last:
            sums = sums + unpack_sums(p_ref)
            refs[2][...] = sums
    pack(refs[0], t[:LANES], sums)
    if last:
        refs[1][...] = t[LANES:]
    else:
        pack(refs[1], t[LANES:], sums)


def merge_z(last, a, b, p, sums):
    width = a.shape[1]
    sent = shape((LANES + HEAD, width), jnp.int16)
    out = [sent, shape((LANES, width), F32) if last else sent]
    args = [a, b, p]
    if sums is not None:
        args.append(sums)
        if not last:
            out.append(shape((8, width), F32))
    return pl.pallas_call(
        functools.partial(merge_z_kernel, last, sums is not None),
        in_specs=[VMEM] * len(args),
        out_specs=[VMEM] * len(out),
        out_shape=out,
        compiler_params=params(8),
        cost_estimate=cost(5 * a.size, 1e6),
        name="merge_z_last" if last else "merge_z_first",
    )(*args)


def join_kernel(*refs):
    for i, r in enumerate(refs[:-1]):
        refs[-1][i] = r[...]


def relay_kernel(x_ref, after_ref, out_ref):
    out_ref[...] = x_ref[...]


def copy_of(kernel, name, out, *args):
    return pl.pallas_call(
        kernel,
        in_specs=[VMEM] * len(args),
        out_specs=VMEM,
        out_shape=out,
        compiler_params=params(8),
        cost_estimate=cost(1e5, 5e5),
        name=name,
    )(*args)


def fold(a):
    return jnp.sum(a, axis=0, keepdims=True)


def length_of(sums):
    grad = jnp.sum(sums[0:1, :], axis=1, keepdims=True)
    image = jnp.sum(sums[1:2, :], axis=1, keepdims=True)
    return grad / (grad + image), image / (grad + image)


def products(e, y, held, rows):
    p = e.astype(F32) * y
    q = p[:, :LANES] + p[:, LANES:]
    q = q + pltpu.roll(q, LANES // 2, 1)
    high, low = halves(q)
    held[rows, :LANES] = high
    held[rows, LANES:] = low


BATCH = 16
SOME = 8


def coarse_kernel(packed, second, after, e_ref, k_ref, own_ref, *refs):
    refs = list(refs)
    got = [refs.pop(0) for _ in range(packed)]
    y = own_ref[...]
    for r in got:
        y = y + unpack(r)
    if second:
        y0_ref, s_ref = refs.pop(0), refs.pop(0)
        sums = s_ref[...]
        for r in got:
            sums = sums + unpack_sums(r)
        l0, keep = length_of(sums)
        y = keep * y0_ref[...] - l0 * y
        refs.pop(after + 2)[...] = jnp.broadcast_to(l0, (8, LANES))
    x_ref, y_ref, sum_ref, even_s, odd_s, x_s = refs[after:]
    members, columns, width = e_ref.shape
    y_ref[...] = y
    x_s[...] = jnp.zeros_like(x_s)

    def build(i, held):
        for m in range(SOME):
            products(e_ref[i * SOME + m], y_ref[...], held, pl.ds(m * columns, columns))

    def add_in(i, t):
        total = x_s[...]
        for m in range(SOME):
            total = total + t[m * columns : (m + 1) * columns] * e_ref[i * SOME + m].astype(F32)
        x_s[...] = total

    pairs = members // SOME // 2
    build(0, even_s)

    @pl.loop(0, pairs - 1)
    def _(i):
        t = dot(even_s[...], k_ref[...])
        build(2 * i + 1, odd_s)
        add_in(2 * i, t)
        t = dot(odd_s[...], k_ref[...])
        build(2 * i + 2, even_s)
        add_in(2 * i + 1, t)

    t = dot(even_s[...], k_ref[...])
    build(2 * pairs - 1, odd_s)
    add_in(2 * pairs - 2, t)
    add_in(2 * pairs - 1, dot(odd_s[...], k_ref[...]))

    x = x_s[...]
    x_ref[...] = x.T.astype(BF)
    sum_ref[...] = jnp.zeros_like(sum_ref)
    sum_ref[0:1, :] = fold(x * y_ref[...])


def coarse_image(ensemble, kern, own, got, y0=None, sums=None, after=()):
    members, columns, width = ensemble.shape
    second = y0 is not None
    args = [ensemble, kern, own, *got] + ([y0, sums] if second else []) + list(after)
    out = [shape((width, columns), BF), shape((columns, width), F32)]
    out += [shape((8, LANES), F32)] if second else []
    out += [shape((8, width), F32)]
    return pl.pallas_call(
        functools.partial(coarse_kernel, len(got), second, len(after)),
        in_specs=[VMEM] * (len(args) - len(after)) + [ANY] * len(after),
        out_specs=[VMEM] * len(out),
        out_shape=out,
        scratch_shapes=[
            pltpu.VMEM((SOME * columns, width), BF),
            pltpu.VMEM((SOME * columns, width), BF),
            pltpu.VMEM((columns, width), F32),
        ],
        compiler_params=params(16),
        cost_estimate=cost(2 * columns * members * width * width, 5e6),
        name="coarse_second" if second else "coarse_first",
    )(*args)


def project_kernel(e_ref, y_ref, t_ref, after_ref, g_ref, token_ref, even_s, odd_s):
    columns, members, width = e_ref.shape
    lanes = BATCH // 2 * LANES
    token_ref[...] = jnp.zeros_like(token_ref)

    @pl.loop(0, columns // BATCH)
    def _(i):
        base = pl.multiple_of(i * BATCH, BATCH)
        yb = y_ref[pl.ds(base, BATCH), :]
        for c in range(BATCH):
            held = odd_s if c % 2 else even_s
            rows = pl.ds((c // 2) * members, members)
            products(e_ref[base + c], yb[c : c + 1, :], held, rows)
        r = dot(even_s[...], t_ref[0]) + dot(odd_s[...], t_ref[1])
        for pair in range(BATCH // 2):
            at = pl.multiple_of(i * lanes + pair * LANES, LANES)
            g_ref[:, pl.ds(at, LANES)] = r[pair * members : (pair + 1) * members]


def project(ens, y, taps, after):
    columns, members, width = ens.shape
    levels = width // VAR
    return pl.pallas_call(
        project_kernel,
        in_specs=[VMEM] * 4,
        out_specs=[VMEM] * 2,
        out_shape=[shape((members, columns * levels), F32), shape((8, LANES), F32)],
        scratch_shapes=[pltpu.VMEM((BATCH // 2 * members, width), BF)] * 2,
        compiler_params=params(16),
        cost_estimate=cost(2 * columns * members * width * width, 8e6),
        name="project",
    )(ens, y, taps, after)


def lay_out(x_refs, xs):
    if len(x_refs[0].shape) == 2:
        xs[...] = x_refs[0][...]
        return
    for i, x in enumerate(x_refs):
        for n in range(STEPS):
            xs[:, pl.ds((i * STEPS + n) * LANES, LANES)] = x[n]


CUTS = 3


def part_kernel(*refs):
    *x_refs, a_ref, b_ref, c_ref, out_ref, xs = refs
    lay_out(x_refs, xs)
    quarter, fine = a_ref.shape
    rows = fine // CUTS
    for i in range(CUTS):
        some = pl.ds(i * rows, rows)
        total = None
        for n, m in enumerate((a_ref, b_ref, c_ref)):
            term = dot(xs[:, n * quarter : (n + 1) * quarter], m[:, some])
            total = term if total is None else total + term
        out_ref[:, some] = total


def image_part(xs, quarters, width):
    quarter, fine = quarters[0].shape
    return pl.pallas_call(
        part_kernel,
        in_specs=[VMEM] * 6,
        out_specs=VMEM,
        out_shape=shape((width, fine), F32),
        scratch_shapes=[pltpu.VMEM((width, 3 * quarter), BF)],
        compiler_params=params(16),
        cost_estimate=cost(6 * quarter * fine * width, 4e6),
        name="image_part",
    )(*xs, *quarters)


def images(x_ref, refs, last_ref, obs_ref, im_ref, xs):
    lay_out([x_ref], xs)
    quarter, fine = last_ref.shape
    rows = fine // CUTS
    for i in range(CUTS):
        some = pl.ds(i * rows, rows)
        if len(refs) > 1:
            turned = dot(xs[:, 3 * quarter :], last_ref[:, some])
            for n, m in enumerate(refs):
                turned = turned + dot(xs[:, n * quarter : (n + 1) * quarter], m[:, some])
        else:
            turned = dot(xs[...], last_ref[:, some]) + refs[0][:, some]
        im = turned.T
        im_ref[some, :] = im
        yield some, im, obs_ref[some, :].astype(F32) * im


def image_kernel(parts, first, x_ref, *refs):
    part_refs, refs = refs[:parts], refs[parts:]
    far_ref, obs_ref, g_ref, im_ref, sum_ref, *refs = refs
    if first:
        v_ref, out_ref, xs = refs
    else:
        (xs,) = refs
    sums = g_ref[...]
    row = lax.broadcasted_iota(jnp.int32, sums.shape, 0)
    for some, im, v in images(x_ref, part_refs, far_ref, obs_ref, im_ref, xs):
        if first:
            v_ref[some, :] = v.astype(BF)
        sums = sums + jnp.where(row == 1, fold(v * im), 0.0)
    sum_ref[...] = sums
    if first:
        rows = far_ref.shape[0]
        out_ref[pl.ds(0, rows), :] = dot(far_ref[...], v_ref[...])
        out_ref[pl.ds(rows, 8), :] = sums


def image_of(xs, quarters, far, obs, g_sums, first):
    quarter, fine = far.shape
    width = obs.shape[1]
    whole = len(xs) == 1
    part = quarters if whole else [image_part(xs[:-1], quarters, width)]
    out = [shape((fine, width), F32), shape((8, width), F32)]
    if first:
        out += [shape((fine, width), BF)]
        out += [shape((quarter + 8, width), F32)]
    last = 4 * quarter if whole else quarter
    return pl.pallas_call(
        functools.partial(image_kernel, len(part), first),
        in_specs=[VMEM] * (4 + len(part)),
        out_specs=[VMEM] * len(out),
        out_shape=out,
        scratch_shapes=[pltpu.VMEM((width, last), BF)],
        compiler_params=params(16),
        cost_estimate=cost(4 * quarter * fine * width, 6e6),
        name="image_first" if first else "image_second",
    )(xs[-1], *part, far, obs, g_sums)


def back_kernel(at_ref, v_ref, *refs):
    refs[-1][...] = dot(at_ref[...], v_ref[...])


def back(at, v, name, *after):
    rows, fine = at.shape
    width = v.shape[1]
    return pl.pallas_call(
        back_kernel,
        in_specs=[VMEM] * (2 + len(after)),
        out_specs=VMEM,
        out_shape=shape((rows, width), F32),
        compiler_params=params(16),
        cost_estimate=cost(2 * rows * fine * width, 2e6),
        name=name,
    )(at, v, *after)


OUT_CUTS = 4


def result_kernel(count, l0_ref, *refs):
    sums = refs[0][...]
    for r in refs[1:count]:
        sums = sums + r[...]
    g0_ref, g1_ref, i0_ref, i1_ref, control_hbm, increment_hbm, c_s, i_s, sem = refs[count:]
    l0 = -l0_ref[0:1, 0:1]
    l1, _ = length_of(sums)
    lanes = c_s.shape[1] // OUT_CUTS
    rows = i_s.shape[0] // OUT_CUTS
    copies = []
    for i in range(OUT_CUTS):
        some = pl.ds(i * lanes, lanes)
        c_s[:, some] = l0 * g0_ref[:, some] - l1 * g1_ref[:, some]
        copies.append(
            pltpu.make_async_copy(c_s.at[:, some], control_hbm.at[:, some], sem.at[2 * i])
        )
        copies[-1].start()
        some = pl.ds(i * rows, rows)
        i_s[some, :] = l0 * i0_ref[some, :] - l1 * i1_ref[some, :]
        copies.append(
            pltpu.make_async_copy(i_s.at[some, :], increment_hbm.at[some, :], sem.at[2 * i + 1])
        )
        copies[-1].start()
    for copy in copies:
        copy.wait()


def result(l0, sums, g0, g1, im0, im1):
    return pl.pallas_call(
        functools.partial(result_kernel, len(sums)),
        in_specs=[VMEM] * (5 + len(sums)),
        out_specs=[ANY] * 2,
        out_shape=[shape(g0.shape, F32), shape(im0.shape, F32)],
        scratch_shapes=[
            pltpu.VMEM(g0.shape, F32),
            pltpu.VMEM(im0.shape, F32),
            pltpu.SemaphoreType.DMA((2 * OUT_CUTS,)),
        ],
        compiler_params=params(16),
        cost_estimate=cost(3 * g0.size, 1e7),
        name="result",
    )(l0, *sums, g0, g1, im0, im1)


def over_core(x):
    return lax.ppermute(x, "space", [(i, i ^ 1) for i in range(GROUP)])


def over_y(x):
    return lax.ppermute(x, "space", [(i, i ^ 2) for i in range(GROUP)])


def over_z(x, k):
    return lax.ppermute(x, "space", [(i, i ^ (4 * k)) for i in range(GROUP)])


def scatter_sums(parts, sums=None):
    near, far_y, near_c, far_yc = parts
    got_yc = over_core(far_yc)
    first, second, *s = merge_y(far_y, got_yc, sums)
    got_c = over_core(near_c(first))
    first, second = over_y(first), over_y(second)
    two, three, *s = merge_z(False, near, got_c, first, s[0] if s else None)
    got = [over_z(two, 2), over_z(three, 3)]
    one, own = merge_z(True, near, got_c, second, s[0] if s else None)
    return own, got + [over_z(one, 1)], (s[0] if s else None)


def gather_columns(x, work):
    four = shape((STEPS,) + x.shape, BF)
    a = copy_of(join_kernel, "join", four, *[over_z(x, k) for k in ORDER[:3]], x)
    ya, ca = over_y(a), over_core(a)
    done, token = work(a)
    ya = copy_of(relay_kernel, "relay", four, ya, token)
    return [a, ya, ca, over_core(ya)], done


def sum_all(x):
    x = x + over_core(x)
    x = x + over_y(x)
    return [x] + [over_z(x, k) for k in range(1, STEPS)]


def on_device(ensemble, innovation, obs_weight, interp_weight, slot_of, intersection_list):
    members, columns, width = ensemble.shape
    levels = width // VAR
    devices = lax.axis_size("space")
    capacity = intersection_list.shape[2]
    slots = devices * capacity
    grouped = devices == GROUP and capacity == columns == LANES

    taper = vertical_taper(levels)
    both = taper.astype(np.float64) @ taper.T.astype(np.float64)
    kern = np.tile(np.concatenate(host_halves(both), axis=0), (2, VAR))
    tall = np.tile(np.concatenate(host_halves(taper), axis=0), (2, 1))
    none = np.zeros_like(tall)
    taps = np.stack(
        [np.concatenate([tall, none], axis=1), np.concatenate([none, tall], axis=1)]
    )
    kern, taps = jnp.asarray(kern), jnp.asarray(taps)

    index = lax.axis_index("space").astype(jnp.int32)
    me = jnp.stack([index // 4, index // 2 % 2, index % 2, index])
    w = -(obs_weight.astype(F32) * innovation.astype(F32))
    high = lax.reduce_precision(w, 8, 7)
    wh, wl = high.astype(BF), (w - high).astype(BF)
    named = jnp.concatenate([slot_of.astype(F32), interp_weight], axis=0)
    if grouped:
        lists = exchange_lists(me, intersection_list[0])
        scatter, gather, add_up = scatter_sums, gather_columns, sum_all
    else:
        lists = intersection_list[0]
        hit = (lists.reshape(-1, 1) == jnp.arange(columns, dtype=jnp.int32)).astype(BF)

        def swap(x):
            x = x.reshape(devices, capacity, width)
            x = lax.all_to_all(x, "space", split_axis=0, concat_axis=0, tiled=True)
            return x.reshape(slots, width)

        def scatter(parts, sums=None):
            parts = [p(parts[0]) if callable(p) else p for p in parts]
            got = swap(jnp.concatenate([p[: slots // 4] for p in parts], axis=0))
            high = lax.reduce_precision(got, 8, 7)
            high, low = high.astype(BF), (got - high).astype(BF)
            if sums is not None:
                sums = lax.psum(sums, "space")
            return dot(hit.T, high) + dot(hit.T, low), [], sums

        def gather(x, work):
            return [swap(dot(hit, x.T).astype(BF)).T], work(x)[0]

        def add_up(x):
            return [lax.psum(x, "space")]

    ids, weight, far, c1 = adjoint_far(
        slots, [named, wh, wl], grouped, me, lists if grouped else []
    )
    built = [ids, weight, wh, wl]
    near, n1 = adjoint_near(slots, built, slots // 4)
    stay, n0 = adjoint_near(slots, built, 0)
    quarters = [stay, near]

    def first_side(after):
        side, c0 = adjoint_near(slots, built + [after], slots // 2)
        quarters.append(side)
        return c0

    own, got, _ = scatter([n0, n1, first_side, c1])
    ens = jnp.transpose(ensemble, (1, 0, 2))
    x0, y0, g_sums = coarse_image(ensemble, kern, own, got, after=[ens])
    xs, g0 = gather(x0, lambda after: project(ens, y0, taps, after))
    im0, sums, v, c1 = image_of(xs, quarters, far, obs_weight, g_sums, True)
    c0 = lambda after: back(quarters[2], v, "back_side", after)
    n1, n0 = back(near, v, "back_near"), back(stay, v, "back_stay")
    own, got, sums = scatter([n0, n1, c0, c1], sums)
    x1, y1, l0, g_sums = coarse_image(ensemble, kern, own, got, y0, sums)
    xs, g1 = gather(x1, lambda after: project(ens, y1, taps, after))
    im1, sums = image_of(xs, quarters, far, obs_weight, g_sums, False)
    return tuple(result(l0, add_up(sums), g0, g1, im0, im1))


def solution(mesh):
    placed = (
        P("case", "space", None),
        P(("case", "space"), None),
        P(("case", "space"), None),
        P("case", "space"),
        P("case", "space"),
        P(("case", "space"), None, None),
    )
    return jax.shard_map(
        on_device,
        mesh=mesh,
        in_specs=placed,
        out_specs=(P("case", "space"), P(("case", "space"), None)),
        check_vma=False,
    )
```

```python
import functools

import jax
import jax.numpy as jnp
import ml_dtypes
import numpy as np
from jax import lax
from jax.experimental import pallas as pl
from jax.experimental.pallas import tpu as pltpu
from jax.sharding import PartitionSpec as P

VAR = 4
LOC_SCALE = 3.0
BF = jnp.bfloat16
F32 = jnp.float32
LANES = 128
GROUP = 16
VMEM = pl.BlockSpec(memory_space=pltpu.VMEM)
SMEM = pl.BlockSpec(memory_space=pltpu.SMEM)
ANY = pl.BlockSpec(memory_space=pl.ANY)


def vertical_taper(levels):
    heights = np.arange(levels).astype(np.float32)
    spread = (heights[:, None] - heights[None, :]) / np.float32(LOC_SCALE)
    return np.exp(np.float32(-0.5) * spread * spread)


def host_halves(x):
    high = x.astype(ml_dtypes.bfloat16)
    return [high, (x - high.astype(x.dtype)).astype(ml_dtypes.bfloat16)]


def params(mib):
    return pltpu.CompilerParams(vmem_limit_bytes=mib << 20)


def cost(flops, nbytes):
    return pl.CostEstimate(flops=int(flops), bytes_accessed=int(nbytes), transcendentals=0)


def dot(a, b):
    return jnp.dot(a, b, preferred_element_type=F32)


def halves(x):
    high = x.astype(BF)
    return high, (x - high.astype(F32)).astype(BF)


def shape(dims, dtype):
    return jax.ShapeDtypeStruct(dims, dtype)


STEPS = 4
ORDER = (2, 3, 1, 0)
LIST_ORDER = (1, 3, 0, 2)
PARTS = ((0, 0), (1, 0), (0, 1), (1, 1))
HEAD = 16
TOP = 32512.0


def owner_at(me_ref, i):
    dy, dc = PARTS[i // STEPS]
    z, y, c = me_ref[0], me_ref[1], me_ref[2]
    y = y if dy == 0 else 1 - y
    c = c if dc == 0 else 1 - c
    return (jnp.bitwise_xor(z, ORDER[i % STEPS]) * 2 + y) * 2 + c


def places(me_ref, list_refs, slots):
    slots = jnp.concatenate([slots, slots], axis=0)
    from_owner = jnp.right_shift(slots, 7)
    within = jnp.bitwise_and(slots, LANES - 1)
    rows = jnp.zeros(slots.shape, jnp.int32)
    for i in range(GROUP):
        o = owner_at(me_ref, i)
        dy, dc = PARTS[i // STEPS]
        k = ORDER[i % STEPS]
        row = k % 2 * STEPS + 2 * dy + dc
        row = jnp.broadcast_to(list_refs[k // 2][row : row + 1, :], slots.shape)
        column = jnp.take_along_axis(row, within, axis=1, mode="promise_in_bounds")
        rows = jnp.where(from_owner == o, column + i * LANES, rows)
    return rows[: slots.shape[0] // 2]


def build_rows(ids_ref, weight_ref, wh_ref, wl_ref, at_ref, y_refs, lo_s, base):
    sources, fine = ids_ref.shape
    rows = at_ref.shape[0] // len(y_refs)
    step = rows // 2
    row = lax.broadcasted_iota(jnp.int32, (step, LANES), 0)
    for n, y_ref in enumerate(y_refs):
        for m in range(2):
            start = n * rows + m * step
            for j in range(fine // LANES):
                lanes = pl.ds(j * LANES, LANES)
                total = None
                for b in range(sources):
                    ids = ids_ref[b : b + 1, lanes] - (base + start)
                    term = jnp.where(row == ids, weight_ref[b : b + 1, lanes], 0.0)
                    total = term if total is None else total + term
                high, low = halves(total)
                at_ref[pl.ds(start, step), lanes] = high
                lo_s[pl.ds(m * step, step), lanes] = low
        held = at_ref[pl.ds(n * rows, rows), :]
        y_ref[...] = dot(held, wh_ref[...]) + dot(held, wl_ref[...]) + dot(lo_s[...], wh_ref[...])


def far_kernel(grouped, me_ref, *refs):
    list_refs, refs = refs[: 2 * grouped], refs[2 * grouped :]
    both_ref, wh_ref, wl_ref, *refs = refs
    ids_ref, weight_ref, at_ref, y_ref, lo_s = refs
    sources = ids_ref.shape[0]
    for j in range(ids_ref.shape[1] // LANES):
        lanes = pl.ds(j * LANES, LANES)
        slots = both_ref[:sources, lanes].astype(jnp.int32)
        ids_ref[:, lanes] = places(me_ref, list_refs, slots) if grouped else slots
        weight_ref[:, lanes] = both_ref[sources:, lanes]
    base = 3 * at_ref.shape[0]
    build_rows(ids_ref, weight_ref, wh_ref, wl_ref, at_ref, [y_ref], lo_s, base)


def near_kernel(base, ids_ref, weight_ref, wh_ref, wl_ref, *refs):
    at_ref, y_ref, lo_s = refs[-3:]
    build_rows(ids_ref, weight_ref, wh_ref, wl_ref, at_ref, [y_ref], lo_s, base)


def adjoint_far(slots, args, grouped, me, lists):
    fine, width = args[-1].shape
    rows = slots // 4
    sources = args[0].shape[0] // 2
    out = [shape((sources, fine), jnp.int32), shape((sources, fine), F32)]
    out += [shape((rows, fine), BF), shape((rows, width), F32)]
    args = [me, *lists, *args]
    return pl.pallas_call(
        functools.partial(far_kernel, grouped),
        in_specs=[SMEM] + [VMEM] * (len(args) - 1),
        out_specs=[VMEM] * len(out),
        out_shape=out,
        scratch_shapes=[pltpu.VMEM((rows, fine), BF)],
        compiler_params=params(16),
        cost_estimate=cost(1.5 * slots * fine * width, 2e6),
        name="adjoint_far",
    )(*args)


def adjoint_near(slots, args, base):
    fine, width = args[2].shape
    rows = slots // 4
    return pl.pallas_call(
        functools.partial(near_kernel, base),
        in_specs=[VMEM] * len(args),
        out_specs=[VMEM] * 2,
        out_shape=[shape((rows, fine), BF), shape((rows, width), F32)],
        scratch_shapes=[pltpu.VMEM((rows, fine), BF)],
        compiler_params=params(16),
        cost_estimate=cost(1.5 * slots * fine * width, 2e6),
        name=("adjoint_stay", "adjoint_near", "adjoint_side")[base // rows],
    )(*args)


def pick_kernel(me_ref, lists_ref, near_ref, far_ref):
    z, y, c = me_ref[0], me_ref[1], me_ref[2]
    for dy in range(2):
        for p, k in enumerate(LIST_ORDER):
            there = (jnp.bitwise_xor(z, k) * 2 + (y if dy == 0 else 1 - y)) * 2
            row = slice(dy * STEPS + p, dy * STEPS + p + 1)
            near_ref[row, :] = lists_ref[pl.ds(there + c, 1), :]
            far_ref[row, :] = lists_ref[pl.ds(there + 1 - c, 1), :]


def mix_y_kernel(near_ref, got_ref, near_y_ref, far_y_ref):
    for i, held in enumerate((near_ref, got_ref)):
        rows = slice(i * STEPS, (i + 1) * STEPS)
        near_y_ref[rows, :] = held[:STEPS, :]
        far_y_ref[rows, :] = held[STEPS:, :]


def mix_z_kernel(near_ref, got_ref, near_z_ref, far_z_ref):
    for i, held in enumerate((near_ref, got_ref)):
        for c in range(2):
            rows = slice(4 * i + 2 * c, 4 * i + 2 * c + 2)
            far_z_ref[rows, :] = held[c * STEPS : c * STEPS + 2, :]
            near_z_ref[rows, :] = held[c * STEPS + 2 : c * STEPS + 4, :]


def mix_end_kernel(near_ref, got_ref, own_ref, sent_ref):
    for i, held in enumerate((near_ref, got_ref)):
        for n in range(STEPS):
            row = slice(i * STEPS + n, i * STEPS + n + 1)
            own_ref[row, :] = held[2 * n : 2 * n + 1, :]
            sent_ref[row, :] = held[2 * n + 1 : 2 * n + 2, :]


def small(kernel, n, name, *args, scalars=0):
    return pl.pallas_call(
        kernel,
        in_specs=[SMEM] * scalars + [VMEM] * (len(args) - scalars),
        out_specs=[VMEM] * n,
        out_shape=[shape((8, LANES), jnp.int32)] * n,
        compiler_params=params(8),
        cost_estimate=cost(1e4, 3e4),
        name=name,
    )(*args)


def exchange_lists(me, lists):
    near, far = small(pick_kernel, 2, "pick", me, lists, scalars=1)
    near, far = small(mix_y_kernel, 2, "mix_y", near, over_core(far))
    near, far = small(mix_z_kernel, 2, "mix_z", near, over_y(far))
    own, sent = small(mix_end_kernel, 2, "mix_end", near, over_z(far, 1))
    return [own, over_z(sent, 2)]


def exponent(m):
    return jnp.clip(jnp.ceil(jnp.log2(jnp.maximum(m, 1e-30))), -100.0, 100.0)


def whole16(x):
    return x.astype(jnp.int32).astype(jnp.int16)


def wide(x):
    return x.astype(jnp.int32).astype(F32)


def pack(out_ref, t, sums=None):
    rows, width = t.shape
    e = exponent(jnp.max(jnp.abs(t), axis=0, keepdims=True))
    out_ref[pl.ds(0, rows), :] = whole16(jnp.round(t * (jnp.exp2(-e) * TOP)))
    head = [e]
    if sums is not None:
        for i in range(2):
            v = sums[i : i + 1, :]
            f = exponent(v)
            v = v * (jnp.exp2(-f) * 16384.0)
            first = jnp.floor(v)
            head += [f, first, jnp.floor((v - first) * 16384.0)]
    row = lax.broadcasted_iota(jnp.int32, (HEAD, width), 0)
    total = jnp.zeros((HEAD, width), F32)
    for i, h in enumerate(head):
        total = jnp.where(row == i, h, total)
    out_ref[pl.ds(rows, HEAD), :] = whole16(total)


def unpack(ref):
    rows = ref.shape[0] - HEAD
    head = wide(ref[pl.ds(rows, HEAD), :])
    return wide(ref[pl.ds(0, rows), :]) * (jnp.exp2(head[0:1, :]) * (1.0 / TOP))


def unpack_sums(ref):
    head = wide(ref[pl.ds(ref.shape[0] - HEAD, HEAD), :])
    row = lax.broadcasted_iota(jnp.int32, (8, head.shape[1]), 0)
    total = jnp.zeros(row.shape, F32)
    for i in range(2):
        f, first, second = [head[1 + 3 * i + j : 2 + 3 * i + j, :] for j in range(3)]
        v = (first + second * (1.0 / 16384.0)) * (jnp.exp2(f) * (1.0 / 16384.0))
        total = jnp.where(row == i, v, total)
    return total


def merge_y_kernel(with_sums, *refs):
    if with_sums:
        a_ref, b_ref, mine_ref, first_ref, second_ref, s_ref = refs
        sums = mine_ref[...] + b_ref[pl.ds(a_ref.shape[0], 8), :]
        s_ref[...] = sums
    else:
        a_ref, b_ref, first_ref, second_ref = refs
        sums = None
    half = a_ref.shape[0] // 2
    pack(first_ref, a_ref[pl.ds(0, half), :] + b_ref[pl.ds(0, half), :], sums)
    pack(second_ref, a_ref[pl.ds(half, half), :] + b_ref[pl.ds(half, half), :])


def merge_y(a, b, sums):
    rows, width = a.shape
    out = [shape((rows // 2 + HEAD, width), jnp.int16)] * 2
    args = [a, b]
    if sums is not None:
        out.append(shape((8, width), F32))
        args.append(sums)
    return pl.pallas_call(
        functools.partial(merge_y_kernel, sums is not None),
        in_specs=[VMEM] * len(args),
        out_specs=[VMEM] * len(out),
        out_shape=out,
        compiler_params=params(8),
        cost_estimate=cost(5 * rows * width, 1e6),
        name="merge_y",
    )(*args)


def merge_z_kernel(last, with_sums, a_ref, b_ref, p_ref, *refs):
    half = a_ref.shape[0] // 2
    rows = pl.ds(half if last else 0, half)
    t = a_ref[rows, :] + b_ref[rows, :] + unpack(p_ref)
    sums = None
    if with_sums:
        sums = refs[0][...]
        refs = refs[1:]
        if not last:
            sums = sums + unpack_sums(p_ref)
            refs[2][...] = sums
    pack(refs[0], t[:LANES], sums)
    if last:
        refs[1][...] = t[LANES:]
    else:
        pack(refs[1], t[LANES:], sums)


def merge_z(last, a, b, p, sums):
    width = a.shape[1]
    sent = shape((LANES + HEAD, width), jnp.int16)
    out = [sent, shape((LANES, width), F32) if last else sent]
    args = [a, b, p]
    if sums is not None:
        args.append(sums)
        if not last:
            out.append(shape((8, width), F32))
    return pl.pallas_call(
        functools.partial(merge_z_kernel, last, sums is not None),
        in_specs=[VMEM] * len(args),
        out_specs=[VMEM] * len(out),
        out_shape=out,
        compiler_params=params(8),
        cost_estimate=cost(5 * a.size, 1e6),
        name="merge_z_last" if last else "merge_z_first",
    )(*args)


def join_kernel(*refs):
    for i, r in enumerate(refs[:-1]):
        refs[-1][i] = r[...]


def relay_kernel(x_ref, after_ref, out_ref):
    out_ref[...] = x_ref[...]


def copy_of(kernel, name, out, *args):
    return pl.pallas_call(
        kernel,
        in_specs=[VMEM] * len(args),
        out_specs=VMEM,
        out_shape=out,
        compiler_params=params(8),
        cost_estimate=cost(1e5, 5e5),
        name=name,
    )(*args)


def fold(a):
    return jnp.sum(a, axis=0, keepdims=True)


def length_of(sums):
    grad = jnp.sum(sums[0:1, :], axis=1, keepdims=True)
    image = jnp.sum(sums[1:2, :], axis=1, keepdims=True)
    return grad / (grad + image), image / (grad + image)


def products(e, y, held, rows):
    p = e.astype(F32) * y
    q = p[:, :LANES] + p[:, LANES:]
    q = q + pltpu.roll(q, LANES // 2, 1)
    high, low = halves(q)
    held[rows, :LANES] = high
    held[rows, LANES:] = low


BATCH = 16
SOME = 10


def coarse_kernel(packed, second, after, e_ref, k_ref, own_ref, *refs):
    refs = list(refs)
    got = [refs.pop(0) for _ in range(packed)]
    y = own_ref[...]
    for r in got:
        y = y + unpack(r)
    if second:
        y0_ref, s_ref = refs.pop(0), refs.pop(0)
        sums = s_ref[...]
        for r in got:
            sums = sums + unpack_sums(r)
        l0, keep = length_of(sums)
        y = keep * y0_ref[...] - l0 * y
        refs.pop(after + 2)[...] = jnp.broadcast_to(l0, (8, LANES))
    x_ref, y_ref, sum_ref, even_s, odd_s, x_s = refs[after:]
    members, columns, width = e_ref.shape
    y_ref[...] = y
    x_s[...] = jnp.zeros_like(x_s)

    def build(i, held):
        for m in range(SOME):
            products(e_ref[i * SOME + m], y_ref[...], held, pl.ds(m * columns, columns))

    def add_in(i, t):
        total = x_s[...]
        for m in range(SOME):
            total = total + t[m * columns : (m + 1) * columns] * e_ref[i * SOME + m].astype(F32)
        x_s[...] = total

    pairs = members // SOME // 2
    build(0, even_s)

    @pl.loop(0, pairs - 1)
    def _(i):
        t = dot(even_s[...], k_ref[...])
        build(2 * i + 1, odd_s)
        add_in(2 * i, t)
        t = dot(odd_s[...], k_ref[...])
        build(2 * i + 2, even_s)
        add_in(2 * i + 1, t)

    t = dot(even_s[...], k_ref[...])
    build(2 * pairs - 1, odd_s)
    add_in(2 * pairs - 2, t)
    add_in(2 * pairs - 1, dot(odd_s[...], k_ref[...]))

    x = x_s[...]
    x_ref[...] = x.T.astype(BF)
    sum_ref[...] = jnp.zeros_like(sum_ref)
    sum_ref[0:1, :] = fold(x * y_ref[...])


def coarse_image(ensemble, kern, own, got, y0=None, sums=None, after=()):
    members, columns, width = ensemble.shape
    second = y0 is not None
    args = [ensemble, kern, own, *got] + ([y0, sums] if second else []) + list(after)
    out = [shape((width, columns), BF), shape((columns, width), F32)]
    out += [shape((8, LANES), F32)] if second else []
    out += [shape((8, width), F32)]
    return pl.pallas_call(
        functools.partial(coarse_kernel, len(got), second, len(after)),
        in_specs=[VMEM] * (len(args) - len(after)) + [ANY] * len(after),
        out_specs=[VMEM] * len(out),
        out_shape=out,
        scratch_shapes=[
            pltpu.VMEM((SOME * columns, width), BF),
            pltpu.VMEM((SOME * columns, width), BF),
            pltpu.VMEM((columns, width), F32),
        ],
        compiler_params=params(16),
        cost_estimate=cost(2 * columns * members * width * width, 5e6),
        name="coarse_second" if second else "coarse_first",
    )(*args)


def project_kernel(e_ref, y_ref, t_ref, after_ref, g_ref, token_ref, even_s, odd_s):
    columns, members, width = e_ref.shape
    lanes = BATCH // 2 * LANES
    token_ref[...] = jnp.zeros_like(token_ref)

    @pl.loop(0, columns // BATCH)
    def _(i):
        base = pl.multiple_of(i * BATCH, BATCH)
        yb = y_ref[pl.ds(base, BATCH), :]
        for c in range(BATCH):
            held = odd_s if c % 2 else even_s
            rows = pl.ds((c // 2) * members, members)
            products(e_ref[base + c], yb[c : c + 1, :], held, rows)
        r = dot(even_s[...], t_ref[0]) + dot(odd_s[...], t_ref[1])
        for pair in range(BATCH // 2):
            at = pl.multiple_of(i * lanes + pair * LANES, LANES)
            g_ref[:, pl.ds(at, LANES)] = r[pair * members : (pair + 1) * members]


def project(ens, y, taps, after):
    columns, members, width = ens.shape
    levels = width // VAR
    return pl.pallas_call(
        project_kernel,
        in_specs=[VMEM] * 4,
        out_specs=[VMEM] * 2,
        out_shape=[shape((members, columns * levels), F32), shape((8, LANES), F32)],
        scratch_shapes=[pltpu.VMEM((BATCH // 2 * members, width), BF)] * 2,
        compiler_params=params(16),
        cost_estimate=cost(2 * columns * members * width * width, 8e6),
        name="project",
    )(ens, y, taps, after)


def lay_out(x_refs, xs):
    if len(x_refs[0].shape) == 2:
        xs[...] = x_refs[0][...]
        return
    for i, x in enumerate(x_refs):
        for n in range(STEPS):
            xs[:, pl.ds((i * STEPS + n) * LANES, LANES)] = x[n]


CUTS = 3


def part_kernel(*refs):
    *x_refs, a_ref, b_ref, c_ref, out_ref, xs = refs
    lay_out(x_refs, xs)
    quarter, fine = a_ref.shape
    rows = fine // CUTS
    for i in range(CUTS):
        some = pl.ds(i * rows, rows)
        total = None
        for n, m in enumerate((a_ref, b_ref, c_ref)):
            term = dot(xs[:, n * quarter : (n + 1) * quarter], m[:, some])
            total = term if total is None else total + term
        out_ref[:, some] = total


def image_part(xs, quarters, width):
    quarter, fine = quarters[0].shape
    return pl.pallas_call(
        part_kernel,
        in_specs=[VMEM] * 6,
        out_specs=VMEM,
        out_shape=shape((width, fine), F32),
        scratch_shapes=[pltpu.VMEM((width, 3 * quarter), BF)],
        compiler_params=params(16),
        cost_estimate=cost(6 * quarter * fine * width, 4e6),
        name="image_part",
    )(*xs, *quarters)


def images(x_ref, refs, last_ref, obs_ref, im_ref, xs):
    lay_out([x_ref], xs)
    quarter, fine = last_ref.shape
    rows = fine // CUTS
    for i in range(CUTS):
        some = pl.ds(i * rows, rows)
        if len(refs) > 1:
            turned = dot(xs[:, 3 * quarter :], last_ref[:, some])
            for n, m in enumerate(refs):
                turned = turned + dot(xs[:, n * quarter : (n + 1) * quarter], m[:, some])
        else:
            turned = dot(xs[...], last_ref[:, some]) + refs[0][:, some]
        im = turned.T
        im_ref[some, :] = im
        yield some, im, obs_ref[some, :].astype(F32) * im


def image_kernel(parts, first, x_ref, *refs):
    part_refs, refs = refs[:parts], refs[parts:]
    far_ref, obs_ref, g_ref, im_ref, sum_ref, *refs = refs
    if first:
        v_ref, out_ref, xs = refs
    else:
        (xs,) = refs
    sums = g_ref[...]
    row = lax.broadcasted_iota(jnp.int32, sums.shape, 0)
    for some, im, v in images(x_ref, part_refs, far_ref, obs_ref, im_ref, xs):
        if first:
            v_ref[some, :] = v.astype(BF)
        sums = sums + jnp.where(row == 1, fold(v * im), 0.0)
    sum_ref[...] = sums
    if first:
        rows = far_ref.shape[0]
        out_ref[pl.ds(0, rows), :] = dot(far_ref[...], v_ref[...])
        out_ref[pl.ds(rows, 8), :] = sums


def image_of(xs, quarters, far, obs, g_sums, first):
    quarter, fine = far.shape
    width = obs.shape[1]
    whole = len(xs) == 1
    part = quarters if whole else [image_part(xs[:-1], quarters, width)]
    out = [shape((fine, width), F32), shape((8, width), F32)]
    if first:
        out += [shape((fine, width), BF)]
        out += [shape((quarter + 8, width), F32)]
    last = 4 * quarter if whole else quarter
    return pl.pallas_call(
        functools.partial(image_kernel, len(part), first),
        in_specs=[VMEM] * (4 + len(part)),
        out_specs=[VMEM] * len(out),
        out_shape=out,
        scratch_shapes=[pltpu.VMEM((width, last), BF)],
        compiler_params=params(16),
        cost_estimate=cost(4 * quarter * fine * width, 6e6),
        name="image_first" if first else "image_second",
    )(xs[-1], *part, far, obs, g_sums)


def back_kernel(at_ref, v_ref, *refs):
    refs[-1][...] = dot(at_ref[...], v_ref[...])


def back(at, v, name, *after):
    rows, fine = at.shape
    width = v.shape[1]
    return pl.pallas_call(
        back_kernel,
        in_specs=[VMEM] * (2 + len(after)),
        out_specs=VMEM,
        out_shape=shape((rows, width), F32),
        compiler_params=params(16),
        cost_estimate=cost(2 * rows * fine * width, 2e6),
        name=name,
    )(at, v, *after)


OUT_CUTS = 8


def result_kernel(count, l0_ref, *refs):
    sums = refs[0][...]
    for r in refs[1:count]:
        sums = sums + r[...]
    g0_ref, g1_ref, i0_ref, i1_ref, control_hbm, increment_hbm, c_s, i_s, sem = refs[count:]
    l0 = -l0_ref[0:1, 0:1]
    l1, _ = length_of(sums)
    lanes = c_s.shape[1] // OUT_CUTS
    rows = i_s.shape[0] // OUT_CUTS
    copies = []
    for i in range(OUT_CUTS):
        some = pl.ds(i * lanes, lanes)
        c_s[:, some] = l0 * g0_ref[:, some] - l1 * g1_ref[:, some]
        copies.append(
            pltpu.make_async_copy(c_s.at[:, some], control_hbm.at[:, some], sem.at[2 * i])
        )
        copies[-1].start()
        some = pl.ds(i * rows, rows)
        i_s[some, :] = l0 * i0_ref[some, :] - l1 * i1_ref[some, :]
        copies.append(
            pltpu.make_async_copy(i_s.at[some, :], increment_hbm.at[some, :], sem.at[2 * i + 1])
        )
        copies[-1].start()
    for copy in copies:
        copy.wait()


def result(l0, sums, g0, g1, im0, im1):
    return pl.pallas_call(
        functools.partial(result_kernel, len(sums)),
        in_specs=[VMEM] * (5 + len(sums)),
        out_specs=[ANY] * 2,
        out_shape=[shape(g0.shape, F32), shape(im0.shape, F32)],
        scratch_shapes=[
            pltpu.VMEM(g0.shape, F32),
            pltpu.VMEM(im0.shape, F32),
            pltpu.SemaphoreType.DMA((2 * OUT_CUTS,)),
        ],
        compiler_params=params(16),
        cost_estimate=cost(3 * g0.size, 1e7),
        name="result",
    )(l0, *sums, g0, g1, im0, im1)


def over_core(x):
    return lax.ppermute(x, "space", [(i, i ^ 1) for i in range(GROUP)])


def over_y(x):
    return lax.ppermute(x, "space", [(i, i ^ 2) for i in range(GROUP)])


def over_z(x, k):
    return lax.ppermute(x, "space", [(i, i ^ (4 * k)) for i in range(GROUP)])


def scatter_sums(parts, sums=None):
    near, far_y, near_c, far_yc = parts
    got_yc = over_core(far_yc)
    first, second, *s = merge_y(far_y, got_yc, sums)
    got_c = over_core(near_c(first))
    first, second = over_y(first), over_y(second)
    two, three, *s = merge_z(False, near, got_c, first, s[0] if s else None)
    got = [over_z(two, 2), over_z(three, 3)]
    one, own = merge_z(True, near, got_c, second, s[0] if s else None)
    return own, got + [over_z(one, 1)], (s[0] if s else None)


def gather_columns(x, work):
    four = shape((STEPS,) + x.shape, BF)
    a = copy_of(join_kernel, "join", four, *[over_z(x, k) for k in ORDER[:3]], x)
    ya, ca = over_y(a), over_core(a)
    done, token = work(a)
    ya = copy_of(relay_kernel, "relay", four, ya, token)
    return [a, ya, ca, over_core(ya)], done


def sum_all(x):
    x = x + over_core(x)
    x = x + over_y(x)
    return [x] + [over_z(x, k) for k in range(1, STEPS)]


def on_device(ensemble, innovation, obs_weight, interp_weight, slot_of, intersection_list):
    members, columns, width = ensemble.shape
    levels = width // VAR
    devices = lax.axis_size("space")
    capacity = intersection_list.shape[2]
    slots = devices * capacity
    grouped = devices == GROUP and capacity == columns == LANES

    taper = vertical_taper(levels)
    both = taper.astype(np.float64) @ taper.T.astype(np.float64)
    kern = np.tile(np.concatenate(host_halves(both), axis=0), (2, VAR))
    tall = np.tile(np.concatenate(host_halves(taper), axis=0), (2, 1))
    none = np.zeros_like(tall)
    taps = np.stack(
        [np.concatenate([tall, none], axis=1), np.concatenate([none, tall], axis=1)]
    )
    kern, taps = jnp.asarray(kern), jnp.asarray(taps)

    index = lax.axis_index("space").astype(jnp.int32)
    me = jnp.stack([index // 4, index // 2 % 2, index % 2, index])
    w = -(obs_weight.astype(F32) * innovation.astype(F32))
    high = lax.reduce_precision(w, 8, 7)
    wh, wl = high.astype(BF), (w - high).astype(BF)
    named = jnp.concatenate([slot_of.astype(F32), interp_weight], axis=0)
    if grouped:
        lists = exchange_lists(me, intersection_list[0])
        scatter, gather, add_up = scatter_sums, gather_columns, sum_all
    else:
        lists = intersection_list[0]
        hit = (lists.reshape(-1, 1) == jnp.arange(columns, dtype=jnp.int32)).astype(BF)

        def swap(x):
            x = x.reshape(devices, capacity, width)
            x = lax.all_to_all(x, "space", split_axis=0, concat_axis=0, tiled=True)
            return x.reshape(slots, width)

        def scatter(parts, sums=None):
            parts = [p(parts[0]) if callable(p) else p for p in parts]
            got = swap(jnp.concatenate([p[: slots // 4] for p in parts], axis=0))
            high = lax.reduce_precision(got, 8, 7)
            high, low = high.astype(BF), (got - high).astype(BF)
            if sums is not None:
                sums = lax.psum(sums, "space")
            return dot(hit.T, high) + dot(hit.T, low), [], sums

        def gather(x, work):
            return [swap(dot(hit, x.T).astype(BF)).T], work(x)[0]

        def add_up(x):
            return [lax.psum(x, "space")]

    ids, weight, far, c1 = adjoint_far(
        slots, [named, wh, wl], grouped, me, lists if grouped else []
    )
    built = [ids, weight, wh, wl]
    near, n1 = adjoint_near(slots, built, slots // 4)
    stay, n0 = adjoint_near(slots, built, 0)
    quarters = [stay, near]

    def first_side(after):
        side, c0 = adjoint_near(slots, built + [after], slots // 2)
        quarters.append(side)
        return c0

    own, got, _ = scatter([n0, n1, first_side, c1])
    ens = jnp.transpose(ensemble, (1, 0, 2))
    x0, y0, g_sums = coarse_image(ensemble, kern, own, got, after=[ens])
    xs, g0 = gather(x0, lambda after: project(ens, y0, taps, after))
    im0, sums, v, c1 = image_of(xs, quarters, far, obs_weight, g_sums, True)
    c0 = lambda after: back(quarters[2], v, "back_side", after)
    n1, n0 = back(near, v, "back_near"), back(stay, v, "back_stay")
    own, got, sums = scatter([n0, n1, c0, c1], sums)
    x1, y1, l0, g_sums = coarse_image(ensemble, kern, own, got, y0, sums)
    xs, g1 = gather(x1, lambda after: project(ens, y1, taps, after))
    im1, sums = image_of(xs, quarters, far, obs_weight, g_sums, False)
    return tuple(result(l0, add_up(sums), g0, g1, im0, im1))


def solution(mesh):
    placed = (
        P("case", "space", None),
        P(("case", "space"), None),
        P(("case", "space"), None),
        P("case", "space"),
        P("case", "space"),
        P(("case", "space"), None, None),
    )
    return jax.shard_map(
        on_device,
        mesh=mesh,
        in_specs=placed,
        out_specs=(P("case", "space"), P(("case", "space"), None)),
        check_vma=False,
    )
```

```python
import functools

import jax
import jax.numpy as jnp
import ml_dtypes
import numpy as np
from jax import lax
from jax.experimental import pallas as pl
from jax.experimental.pallas import tpu as pltpu
from jax.sharding import PartitionSpec as P

VAR = 4
LOC_SCALE = 3.0
BF = jnp.bfloat16
F32 = jnp.float32
LANES = 128
GROUP = 16
VMEM = pl.BlockSpec(memory_space=pltpu.VMEM)
SMEM = pl.BlockSpec(memory_space=pltpu.SMEM)
ANY = pl.BlockSpec(memory_space=pl.ANY)


def vertical_taper(levels):
    heights = np.arange(levels).astype(np.float32)
    spread = (heights[:, None] - heights[None, :]) / np.float32(LOC_SCALE)
    return np.exp(np.float32(-0.5) * spread * spread)


def host_halves(x):
    high = x.astype(ml_dtypes.bfloat16)
    return [high, (x - high.astype(x.dtype)).astype(ml_dtypes.bfloat16)]


def params(mib):
    return pltpu.CompilerParams(vmem_limit_bytes=mib << 20)


def cost(flops, nbytes):
    return pl.CostEstimate(flops=int(flops), bytes_accessed=int(nbytes), transcendentals=0)


def dot(a, b):
    return jnp.dot(a, b, preferred_element_type=F32)


def halves(x):
    high = x.astype(BF)
    return high, (x - high.astype(F32)).astype(BF)


def shape(dims, dtype):
    return jax.ShapeDtypeStruct(dims, dtype)


STEPS = 4
ORDER = (2, 3, 1, 0)
LIST_ORDER = (1, 3, 0, 2)
PARTS = ((0, 0), (1, 0), (0, 1), (1, 1))
HEAD = 16
TOP = 32512.0


def owner_at(me_ref, i):
    dy, dc = PARTS[i // STEPS]
    z, y, c = me_ref[0], me_ref[1], me_ref[2]
    y = y if dy == 0 else 1 - y
    c = c if dc == 0 else 1 - c
    return (jnp.bitwise_xor(z, ORDER[i % STEPS]) * 2 + y) * 2 + c


def places(me_ref, list_refs, slots):
    slots = jnp.concatenate([slots, slots], axis=0)
    from_owner = jnp.right_shift(slots, 7)
    within = jnp.bitwise_and(slots, LANES - 1)
    rows = jnp.zeros(slots.shape, jnp.int32)
    for i in range(GROUP):
        o = owner_at(me_ref, i)
        dy, dc = PARTS[i // STEPS]
        k = ORDER[i % STEPS]
        row = k % 2 * STEPS + 2 * dy + dc
        row = jnp.broadcast_to(list_refs[k // 2][row : row + 1, :], slots.shape)
        column = jnp.take_along_axis(row, within, axis=1, mode="promise_in_bounds")
        rows = jnp.where(from_owner == o, column + i * LANES, rows)
    return rows[: slots.shape[0] // 2]


def build_rows(ids_ref, weight_ref, wh_ref, wl_ref, at_ref, y_refs, lo_s, base):
    sources, fine = ids_ref.shape
    rows = at_ref.shape[0] // len(y_refs)
    step = rows // 4
    row = lax.broadcasted_iota(jnp.int32, (step, LANES), 0)
    for n, y_ref in enumerate(y_refs):
        for m in range(4):
            start = n * rows + m * step
            for j in range(fine // LANES):
                lanes = pl.ds(j * LANES, LANES)
                total = None
                for b in range(sources):
                    ids = ids_ref[b : b + 1, lanes] - (base + start)
                    term = jnp.where(row == ids, weight_ref[b : b + 1, lanes], 0.0)
                    total = term if total is None else total + term
                high, low = halves(total)
                at_ref[pl.ds(start, step), lanes] = high
                lo_s[pl.ds(m * step, step), lanes] = low
        held = at_ref[pl.ds(n * rows, rows), :]
        y_ref[...] = dot(held, wh_ref[...]) + dot(held, wl_ref[...]) + dot(lo_s[...], wh_ref[...])


def far_kernel(grouped, me_ref, *refs):
    list_refs, refs = refs[: 2 * grouped], refs[2 * grouped :]
    both_ref, wh_ref, wl_ref, *refs = refs
    ids_ref, weight_ref, at_ref, y_ref, lo_s = refs
    sources = ids_ref.shape[0]
    for j in range(ids_ref.shape[1] // LANES):
        lanes = pl.ds(j * LANES, LANES)
        slots = both_ref[:sources, lanes].astype(jnp.int32)
        ids_ref[:, lanes] = places(me_ref, list_refs, slots) if grouped else slots
        weight_ref[:, lanes] = both_ref[sources:, lanes]
    base = 3 * at_ref.shape[0]
    build_rows(ids_ref, weight_ref, wh_ref, wl_ref, at_ref, [y_ref], lo_s, base)


def near_kernel(base, ids_ref, weight_ref, wh_ref, wl_ref, *refs):
    at_ref, y_ref, lo_s = refs[-3:]
    build_rows(ids_ref, weight_ref, wh_ref, wl_ref, at_ref, [y_ref], lo_s, base)


def adjoint_far(slots, args, grouped, me, lists):
    fine, width = args[-1].shape
    rows = slots // 4
    sources = args[0].shape[0] // 2
    out = [shape((sources, fine), jnp.int32), shape((sources, fine), F32)]
    out += [shape((rows, fine), BF), shape((rows, width), F32)]
    args = [me, *lists, *args]
    return pl.pallas_call(
        functools.partial(far_kernel, grouped),
        in_specs=[SMEM] + [VMEM] * (len(args) - 1),
        out_specs=[VMEM] * len(out),
        out_shape=out,
        scratch_shapes=[pltpu.VMEM((rows, fine), BF)],
        compiler_params=params(16),
        cost_estimate=cost(1.5 * slots * fine * width, 2e6),
        name="adjoint_far",
    )(*args)


def adjoint_near(slots, args, base):
    fine, width = args[2].shape
    rows = slots // 4
    return pl.pallas_call(
        functools.partial(near_kernel, base),
        in_specs=[VMEM] * len(args),
        out_specs=[VMEM] * 2,
        out_shape=[shape((rows, fine), BF), shape((rows, width), F32)],
        scratch_shapes=[pltpu.VMEM((rows, fine), BF)],
        compiler_params=params(16),
        cost_estimate=cost(1.5 * slots * fine * width, 2e6),
        name=("adjoint_stay", "adjoint_near", "adjoint_side")[base // rows],
    )(*args)


def pick_kernel(me_ref, lists_ref, near_ref, far_ref):
    z, y, c = me_ref[0], me_ref[1], me_ref[2]
    for dy in range(2):
        for p, k in enumerate(LIST_ORDER):
            there = (jnp.bitwise_xor(z, k) * 2 + (y if dy == 0 else 1 - y)) * 2
            row = slice(dy * STEPS + p, dy * STEPS + p + 1)
            near_ref[row, :] = lists_ref[pl.ds(there + c, 1), :]
            far_ref[row, :] = lists_ref[pl.ds(there + 1 - c, 1), :]


def mix_y_kernel(near_ref, got_ref, near_y_ref, far_y_ref):
    for i, held in enumerate((near_ref, got_ref)):
        rows = slice(i * STEPS, (i + 1) * STEPS)
        near_y_ref[rows, :] = held[:STEPS, :]
        far_y_ref[rows, :] = held[STEPS:, :]


def mix_z_kernel(near_ref, got_ref, near_z_ref, far_z_ref):
    for i, held in enumerate((near_ref, got_ref)):
        for c in range(2):
            rows = slice(4 * i + 2 * c, 4 * i + 2 * c + 2)
            far_z_ref[rows, :] = held[c * STEPS : c * STEPS + 2, :]
            near_z_ref[rows, :] = held[c * STEPS + 2 : c * STEPS + 4, :]


def mix_end_kernel(near_ref, got_ref, own_ref, sent_ref):
    for i, held in enumerate((near_ref, got_ref)):
        for n in range(STEPS):
            row = slice(i * STEPS + n, i * STEPS + n + 1)
            own_ref[row, :] = held[2 * n : 2 * n + 1, :]
            sent_ref[row, :] = held[2 * n + 1 : 2 * n + 2, :]


def small(kernel, n, name, *args, scalars=0):
    return pl.pallas_call(
        kernel,
        in_specs=[SMEM] * scalars + [VMEM] * (len(args) - scalars),
        out_specs=[VMEM] * n,
        out_shape=[shape((8, LANES), jnp.int32)] * n,
        compiler_params=params(8),
        cost_estimate=cost(1e4, 3e4),
        name=name,
    )(*args)


def exchange_lists(me, lists):
    near, far = small(pick_kernel, 2, "pick", me, lists, scalars=1)
    near, far = small(mix_y_kernel, 2, "mix_y", near, over_core(far))
    near, far = small(mix_z_kernel, 2, "mix_z", near, over_y(far))
    own, sent = small(mix_end_kernel, 2, "mix_end", near, over_z(far, 1))
    return [own, over_z(sent, 2)]


def exponent(m):
    return jnp.clip(jnp.ceil(jnp.log2(jnp.maximum(m, 1e-30))), -100.0, 100.0)


def whole16(x):
    return x.astype(jnp.int32).astype(jnp.int16)


def wide(x):
    return x.astype(jnp.int32).astype(F32)


def pack(out_ref, t, sums=None):
    rows, width = t.shape
    e = exponent(jnp.max(jnp.abs(t), axis=0, keepdims=True))
    out_ref[pl.ds(0, rows), :] = whole16(jnp.round(t * (jnp.exp2(-e) * TOP)))
    head = [e]
    if sums is not None:
        for i in range(2):
            v = sums[i : i + 1, :]
            f = exponent(v)
            v = v * (jnp.exp2(-f) * 16384.0)
            first = jnp.floor(v)
            head += [f, first, jnp.floor((v - first) * 16384.0)]
    row = lax.broadcasted_iota(jnp.int32, (HEAD, width), 0)
    total = jnp.zeros((HEAD, width), F32)
    for i, h in enumerate(head):
        total = jnp.where(row == i, h, total)
    out_ref[pl.ds(rows, HEAD), :] = whole16(total)


def unpack(ref):
    rows = ref.shape[0] - HEAD
    head = wide(ref[pl.ds(rows, HEAD), :])
    return wide(ref[pl.ds(0, rows), :]) * (jnp.exp2(head[0:1, :]) * (1.0 / TOP))


def unpack_sums(ref):
    head = wide(ref[pl.ds(ref.shape[0] - HEAD, HEAD), :])
    row = lax.broadcasted_iota(jnp.int32, (8, head.shape[1]), 0)
    total = jnp.zeros(row.shape, F32)
    for i in range(2):
        f, first, second = [head[1 + 3 * i + j : 2 + 3 * i + j, :] for j in range(3)]
        v = (first + second * (1.0 / 16384.0)) * (jnp.exp2(f) * (1.0 / 16384.0))
        total = jnp.where(row == i, v, total)
    return total


def merge_y_kernel(with_sums, *refs):
    if with_sums:
        a_ref, b_ref, mine_ref, first_ref, second_ref, s_ref = refs
        sums = mine_ref[...] + b_ref[pl.ds(a_ref.shape[0], 8), :]
        s_ref[...] = sums
    else:
        a_ref, b_ref, first_ref, second_ref = refs
        sums = None
    half = a_ref.shape[0] // 2
    pack(first_ref, a_ref[pl.ds(0, half), :] + b_ref[pl.ds(0, half), :], sums)
    pack(second_ref, a_ref[pl.ds(half, half), :] + b_ref[pl.ds(half, half), :])


def merge_y(a, b, sums):
    rows, width = a.shape
    out = [shape((rows // 2 + HEAD, width), jnp.int16)] * 2
    args = [a, b]
    if sums is not None:
        out.append(shape((8, width), F32))
        args.append(sums)
    return pl.pallas_call(
        functools.partial(merge_y_kernel, sums is not None),
        in_specs=[VMEM] * len(args),
        out_specs=[VMEM] * len(out),
        out_shape=out,
        compiler_params=params(8),
        cost_estimate=cost(5 * rows * width, 1e6),
        name="merge_y",
    )(*args)


def merge_z_kernel(last, with_sums, a_ref, b_ref, p_ref, *refs):
    half = a_ref.shape[0] // 2
    rows = pl.ds(half if last else 0, half)
    t = a_ref[rows, :] + b_ref[rows, :] + unpack(p_ref)
    sums = None
    if with_sums:
        sums = refs[0][...]
        refs = refs[1:]
        if not last:
            sums = sums + unpack_sums(p_ref)
            refs[2][...] = sums
    pack(refs[0], t[:LANES], sums)
    if last:
        refs[1][...] = t[LANES:]
    else:
        pack(refs[1], t[LANES:], sums)


def merge_z(last, a, b, p, sums):
    width = a.shape[1]
    sent = shape((LANES + HEAD, width), jnp.int16)
    out = [sent, shape((LANES, width), F32) if last else sent]
    args = [a, b, p]
    if sums is not None:
        args.append(sums)
        if not last:
            out.append(shape((8, width), F32))
    return pl.pallas_call(
        functools.partial(merge_z_kernel, last, sums is not None),
        in_specs=[VMEM] * len(args),
        out_specs=[VMEM] * len(out),
        out_shape=out,
        compiler_params=params(8),
        cost_estimate=cost(5 * a.size, 1e6),
        name="merge_z_last" if last else "merge_z_first",
    )(*args)


def join_kernel(*refs):
    for i, r in enumerate(refs[:-1]):
        refs[-1][i] = r[...]


def relay_kernel(x_ref, after_ref, out_ref):
    out_ref[...] = x_ref[...]


def copy_of(kernel, name, out, *args):
    return pl.pallas_call(
        kernel,
        in_specs=[VMEM] * len(args),
        out_specs=VMEM,
        out_shape=out,
        compiler_params=params(8),
        cost_estimate=cost(1e5, 5e5),
        name=name,
    )(*args)


def fold(a):
    return jnp.sum(a, axis=0, keepdims=True)


def length_of(sums):
    grad = jnp.sum(sums[0:1, :], axis=1, keepdims=True)
    image = jnp.sum(sums[1:2, :], axis=1, keepdims=True)
    return grad / (grad + image), image / (grad + image)


def products(e, y, held, rows):
    p = e.astype(F32) * y
    q = p[:, :LANES] + p[:, LANES:]
    q = q + pltpu.roll(q, LANES // 2, 1)
    high, low = halves(q)
    held[rows, :LANES] = high
    held[rows, LANES:] = low


BATCH = 16
SOME = 8


def coarse_kernel(packed, second, after, e_ref, k_ref, own_ref, *refs):
    refs = list(refs)
    got = [refs.pop(0) for _ in range(packed)]
    y = own_ref[...]
    for r in got:
        y = y + unpack(r)
    if second:
        y0_ref, s_ref = refs.pop(0), refs.pop(0)
        sums = s_ref[...]
        for r in got:
            sums = sums + unpack_sums(r)
        l0, keep = length_of(sums)
        y = keep * y0_ref[...] - l0 * y
        refs.pop(after + 2)[...] = jnp.broadcast_to(l0, (8, LANES))
    x_ref, y_ref, sum_ref, even_s, odd_s, x_s = refs[after:]
    members, columns, width = e_ref.shape
    y_ref[...] = y
    x_s[...] = jnp.zeros_like(x_s)

    def build(i, held):
        for m in range(SOME):
            products(e_ref[i * SOME + m], y_ref[...], held, pl.ds(m * columns, columns))

    def add_in(i, t):
        total = x_s[...]
        for m in range(SOME):
            total = total + t[m * columns : (m + 1) * columns] * e_ref[i * SOME + m].astype(F32)
        x_s[...] = total

    pairs = members // SOME // 2
    build(0, even_s)

    @pl.loop(0, pairs - 1)
    def _(i):
        t = dot(even_s[...], k_ref[...])
        build(2 * i + 1, odd_s)
        add_in(2 * i, t)
        t = dot(odd_s[...], k_ref[...])
        build(2 * i + 2, even_s)
        add_in(2 * i + 1, t)

    t = dot(even_s[...], k_ref[...])
    build(2 * pairs - 1, odd_s)
    add_in(2 * pairs - 2, t)
    add_in(2 * pairs - 1, dot(odd_s[...], k_ref[...]))

    x = x_s[...]
    x_ref[...] = x.T.astype(BF)
    sum_ref[...] = jnp.zeros_like(sum_ref)
    sum_ref[0:1, :] = fold(x * y_ref[...])


def coarse_image(ensemble, kern, own, got, y0=None, sums=None, after=()):
    members, columns, width = ensemble.shape
    second = y0 is not None
    args = [ensemble, kern, own, *got] + ([y0, sums] if second else []) + list(after)
    out = [shape((width, columns), BF), shape((columns, width), F32)]
    out += [shape((8, LANES), F32)] if second else []
    out += [shape((8, width), F32)]
    return pl.pallas_call(
        functools.partial(coarse_kernel, len(got), second, len(after)),
        in_specs=[VMEM] * (len(args) - len(after)) + [ANY] * len(after),
        out_specs=[VMEM] * len(out),
        out_shape=out,
        scratch_shapes=[
            pltpu.VMEM((SOME * columns, width), BF),
            pltpu.VMEM((SOME * columns, width), BF),
            pltpu.VMEM((columns, width), F32),
        ],
        compiler_params=params(16),
        cost_estimate=cost(2 * columns * members * width * width, 5e6),
        name="coarse_second" if second else "coarse_first",
    )(*args)


def project_kernel(e_ref, y_ref, t_ref, after_ref, g_ref, token_ref, even_s, odd_s):
    columns, members, width = e_ref.shape
    lanes = BATCH // 2 * LANES
    token_ref[...] = jnp.zeros_like(token_ref)

    @pl.loop(0, columns // BATCH)
    def _(i):
        base = pl.multiple_of(i * BATCH, BATCH)
        yb = y_ref[pl.ds(base, BATCH), :]
        for c in range(BATCH):
            held = odd_s if c % 2 else even_s
            rows = pl.ds((c // 2) * members, members)
            products(e_ref[base + c], yb[c : c + 1, :], held, rows)
        r = dot(even_s[...], t_ref[0]) + dot(odd_s[...], t_ref[1])
        for pair in range(BATCH // 2):
            at = pl.multiple_of(i * lanes + pair * LANES, LANES)
            g_ref[:, pl.ds(at, LANES)] = r[pair * members : (pair + 1) * members]


def project(ens, y, taps, after):
    columns, members, width = ens.shape
    levels = width // VAR
    return pl.pallas_call(
        project_kernel,
        in_specs=[VMEM] * 4,
        out_specs=[VMEM] * 2,
        out_shape=[shape((members, columns * levels), F32), shape((8, LANES), F32)],
        scratch_shapes=[pltpu.VMEM((BATCH // 2 * members, width), BF)] * 2,
        compiler_params=params(16),
        cost_estimate=cost(2 * columns * members * width * width, 8e6),
        name="project",
    )(ens, y, taps, after)


def lay_out(x_refs, xs):
    if len(x_refs[0].shape) == 2:
        xs[...] = x_refs[0][...]
        return
    for i, x in enumerate(x_refs):
        for n in range(STEPS):
            xs[:, pl.ds((i * STEPS + n) * LANES, LANES)] = x[n]


CUTS = 3


def part_kernel(*refs):
    *x_refs, a_ref, b_ref, c_ref, out_ref, xs = refs
    lay_out(x_refs, xs)
    quarter, fine = a_ref.shape
    rows = fine // CUTS
    for i in range(CUTS):
        some = pl.ds(i * rows, rows)
        total = None
        for n, m in enumerate((a_ref, b_ref, c_ref)):
            term = dot(xs[:, n * quarter : (n + 1) * quarter], m[:, some])
            total = term if total is None else total + term
        out_ref[:, some] = total


def image_part(xs, quarters, width):
    quarter, fine = quarters[0].shape
    return pl.pallas_call(
        part_kernel,
        in_specs=[VMEM] * 6,
        out_specs=VMEM,
        out_shape=shape((width, fine), F32),
        scratch_shapes=[pltpu.VMEM((width, 3 * quarter), BF)],
        compiler_params=params(16),
        cost_estimate=cost(6 * quarter * fine * width, 4e6),
        name="image_part",
    )(*xs, *quarters)


def images(x_ref, refs, last_ref, obs_ref, im_ref, xs):
    lay_out([x_ref], xs)
    quarter, fine = last_ref.shape
    rows = fine // CUTS
    for i in range(CUTS):
        some = pl.ds(i * rows, rows)
        if len(refs) > 1:
            turned = dot(xs[:, 3 * quarter :], last_ref[:, some])
            for n, m in enumerate(refs):
                turned = turned + dot(xs[:, n * quarter : (n + 1) * quarter], m[:, some])
        else:
            turned = dot(xs[...], last_ref[:, some]) + refs[0][:, some]
        im = turned.T
        im_ref[some, :] = im
        yield some, im, obs_ref[some, :].astype(F32) * im


def image_kernel(parts, first, x_ref, *refs):
    part_refs, refs = refs[:parts], refs[parts:]
    far_ref, obs_ref, g_ref, im_ref, sum_ref, *refs = refs
    if first:
        v_ref, out_ref, xs = refs
    else:
        (xs,) = refs
    sums = g_ref[...]
    row = lax.broadcasted_iota(jnp.int32, sums.shape, 0)
    for some, im, v in images(x_ref, part_refs, far_ref, obs_ref, im_ref, xs):
        if first:
            v_ref[some, :] = v.astype(BF)
        sums = sums + jnp.where(row == 1, fold(v * im), 0.0)
    sum_ref[...] = sums
    if first:
        rows = far_ref.shape[0]
        out_ref[pl.ds(0, rows), :] = dot(far_ref[...], v_ref[...])
        out_ref[pl.ds(rows, 8), :] = sums


def image_of(xs, quarters, far, obs, g_sums, first):
    quarter, fine = far.shape
    width = obs.shape[1]
    whole = len(xs) == 1
    part = quarters if whole else [image_part(xs[:-1], quarters, width)]
    out = [shape((fine, width), F32), shape((8, width), F32)]
    if first:
        out += [shape((fine, width), BF)]
        out += [shape((quarter + 8, width), F32)]
    last = 4 * quarter if whole else quarter
    return pl.pallas_call(
        functools.partial(image_kernel, len(part), first),
        in_specs=[VMEM] * (4 + len(part)),
        out_specs=[VMEM] * len(out),
        out_shape=out,
        scratch_shapes=[pltpu.VMEM((width, last), BF)],
        compiler_params=params(16),
        cost_estimate=cost(4 * quarter * fine * width, 6e6),
        name="image_first" if first else "image_second",
    )(xs[-1], *part, far, obs, g_sums)


def back_kernel(at_ref, v_ref, *refs):
    refs[-1][...] = dot(at_ref[...], v_ref[...])


def back(at, v, name, *after):
    rows, fine = at.shape
    width = v.shape[1]
    return pl.pallas_call(
        back_kernel,
        in_specs=[VMEM] * (2 + len(after)),
        out_specs=VMEM,
        out_shape=shape((rows, width), F32),
        compiler_params=params(16),
        cost_estimate=cost(2 * rows * fine * width, 2e6),
        name=name,
    )(at, v, *after)


OUT_CUTS = 4


def result_kernel(count, l0_ref, *refs):
    sums = refs[0][...]
    for r in refs[1:count]:
        sums = sums + r[...]
    g0_ref, g1_ref, i0_ref, i1_ref, control_hbm, increment_hbm, c_s, i_s, sem = refs[count:]
    l0 = -l0_ref[0:1, 0:1]
    l1, _ = length_of(sums)
    lanes = c_s.shape[1] // OUT_CUTS
    rows = i_s.shape[0] // OUT_CUTS
    copies = []
    for i in range(OUT_CUTS):
        some = pl.ds(i * lanes, lanes)
        c_s[:, some] = l0 * g0_ref[:, some] - l1 * g1_ref[:, some]
        copies.append(
            pltpu.make_async_copy(c_s.at[:, some], control_hbm.at[:, some], sem.at[2 * i])
        )
        copies[-1].start()
        some = pl.ds(i * rows, rows)
        i_s[some, :] = l0 * i0_ref[some, :] - l1 * i1_ref[some, :]
        copies.append(
            pltpu.make_async_copy(i_s.at[some, :], increment_hbm.at[some, :], sem.at[2 * i + 1])
        )
        copies[-1].start()
    for copy in copies:
        copy.wait()


def result(l0, sums, g0, g1, im0, im1):
    return pl.pallas_call(
        functools.partial(result_kernel, len(sums)),
        in_specs=[VMEM] * (5 + len(sums)),
        out_specs=[ANY] * 2,
        out_shape=[shape(g0.shape, F32), shape(im0.shape, F32)],
        scratch_shapes=[
            pltpu.VMEM(g0.shape, F32),
            pltpu.VMEM(im0.shape, F32),
            pltpu.SemaphoreType.DMA((2 * OUT_CUTS,)),
        ],
        compiler_params=params(16),
        cost_estimate=cost(3 * g0.size, 1e7),
        name="result",
    )(l0, *sums, g0, g1, im0, im1)


def over_core(x):
    return lax.ppermute(x, "space", [(i, i ^ 1) for i in range(GROUP)])


def over_y(x):
    return lax.ppermute(x, "space", [(i, i ^ 2) for i in range(GROUP)])


def over_z(x, k):
    return lax.ppermute(x, "space", [(i, i ^ (4 * k)) for i in range(GROUP)])


def scatter_sums(parts, sums=None):
    near, far_y, near_c, far_yc = parts
    got_yc = over_core(far_yc)
    first, second, *s = merge_y(far_y, got_yc, sums)
    got_c = over_core(near_c(first))
    first, second = over_y(first), over_y(second)
    two, three, *s = merge_z(False, near, got_c, first, s[0] if s else None)
    got = [over_z(two, 2), over_z(three, 3)]
    one, own = merge_z(True, near, got_c, second, s[0] if s else None)
    return own, got + [over_z(one, 1)], (s[0] if s else None)


def gather_columns(x, work):
    four = shape((STEPS,) + x.shape, BF)
    a = copy_of(join_kernel, "join", four, *[over_z(x, k) for k in ORDER[:3]], x)
    ya, ca = over_y(a), over_core(a)
    done, token = work(a)
    ya = copy_of(relay_kernel, "relay", four, ya, token)
    return [a, ya, ca, over_core(ya)], done


def sum_all(x):
    x = x + over_core(x)
    x = x + over_y(x)
    return [x] + [over_z(x, k) for k in range(1, STEPS)]


def on_device(ensemble, innovation, obs_weight, interp_weight, slot_of, intersection_list):
    members, columns, width = ensemble.shape
    levels = width // VAR
    devices = lax.axis_size("space")
    capacity = intersection_list.shape[2]
    slots = devices * capacity
    grouped = devices == GROUP and capacity == columns == LANES

    taper = vertical_taper(levels)
    both = taper.astype(np.float64) @ taper.T.astype(np.float64)
    kern = np.tile(np.concatenate(host_halves(both), axis=0), (2, VAR))
    tall = np.tile(np.concatenate(host_halves(taper), axis=0), (2, 1))
    none = np.zeros_like(tall)
    taps = np.stack(
        [np.concatenate([tall, none], axis=1), np.concatenate([none, tall], axis=1)]
    )
    kern, taps = jnp.asarray(kern), jnp.asarray(taps)

    index = lax.axis_index("space").astype(jnp.int32)
    me = jnp.stack([index // 4, index // 2 % 2, index % 2, index])
    w = -(obs_weight.astype(F32) * innovation.astype(F32))
    high = lax.reduce_precision(w, 8, 7)
    wh, wl = high.astype(BF), (w - high).astype(BF)
    named = jnp.concatenate([slot_of.astype(F32), interp_weight], axis=0)
    if grouped:
        lists = exchange_lists(me, intersection_list[0])
        scatter, gather, add_up = scatter_sums, gather_columns, sum_all
    else:
        lists = intersection_list[0]
        hit = (lists.reshape(-1, 1) == jnp.arange(columns, dtype=jnp.int32)).astype(BF)

        def swap(x):
            x = x.reshape(devices, capacity, width)
            x = lax.all_to_all(x, "space", split_axis=0, concat_axis=0, tiled=True)
            return x.reshape(slots, width)

        def scatter(parts, sums=None):
            parts = [p(parts[0]) if callable(p) else p for p in parts]
            got = swap(jnp.concatenate([p[: slots // 4] for p in parts], axis=0))
            high = lax.reduce_precision(got, 8, 7)
            high, low = high.astype(BF), (got - high).astype(BF)
            if sums is not None:
                sums = lax.psum(sums, "space")
            return dot(hit.T, high) + dot(hit.T, low), [], sums

        def gather(x, work):
            return [swap(dot(hit, x.T).astype(BF)).T], work(x)[0]

        def add_up(x):
            return [lax.psum(x, "space")]

    ids, weight, far, c1 = adjoint_far(
        slots, [named, wh, wl], grouped, me, lists if grouped else []
    )
    built = [ids, weight, wh, wl]
    near, n1 = adjoint_near(slots, built, slots // 4)
    stay, n0 = adjoint_near(slots, built, 0)
    quarters = [stay, near]

    def first_side(after):
        side, c0 = adjoint_near(slots, built + [after], slots // 2)
        quarters.append(side)
        return c0

    own, got, _ = scatter([n0, n1, first_side, c1])
    ens = jnp.transpose(ensemble, (1, 0, 2))
    x0, y0, g_sums = coarse_image(ensemble, kern, own, got, after=[ens])
    xs, g0 = gather(x0, lambda after: project(ens, y0, taps, after))
    im0, sums, v, c1 = image_of(xs, quarters, far, obs_weight, g_sums, True)
    c0 = lambda after: back(quarters[2], v, "back_side", after)
    n1, n0 = back(near, v, "back_near"), back(stay, v, "back_stay")
    own, got, sums = scatter([n0, n1, c0, c1], sums)
    x1, y1, l0, g_sums = coarse_image(ensemble, kern, own, got, y0, sums)
    xs, g1 = gather(x1, lambda after: project(ens, y1, taps, after))
    im1, sums = image_of(xs, quarters, far, obs_weight, g_sums, False)
    return tuple(result(l0, add_up(sums), g0, g1, im0, im1))


def solution(mesh):
    placed = (
        P("case", "space", None),
        P(("case", "space"), None),
        P(("case", "space"), None),
        P("case", "space"),
        P("case", "space"),
        P(("case", "space"), None, None),
    )
    return jax.shard_map(
        on_device,
        mesh=mesh,
        in_specs=placed,
        out_specs=(P("case", "space"), P(("case", "space"), None)),
        check_vma=False,
    )
```
